32 devices in a mesh: dp: 8 (over z, y), fsdp: 4 (over x, core).
Axes of the slice: x: 2, y: 2, z: 4, core: 2. Of those that a mesh axis runs over, the one named last changes fastest.
Arguments:
- inputs: bfloat16 [2, 8, 1024, 1280], P(None, 'dp', 'fsdp'), may hold values from -6 to 6
- positions: int32 [2, 8, 1024], P(None, 'dp', 'fsdp'), may hold values from 0 to 799, as said below
- cotangent: bfloat16 [2, 8, 1024, 1280], P(None, 'dp', 'fsdp'), may hold values from -6 to 6
- attn_gain: bfloat16 [1280], P(('dp', 'fsdp')), may hold values from 0.5 to 1.5
- w_query: bfloat16 [1280, 1280], P(('dp', 'fsdp')), may hold values from -0.15625 to 0.15625
- key_matrix: bfloat16 [1280, 320], P(('dp', 'fsdp')), may hold values from -0.15625 to 0.15625
- value_matrix: bfloat16 [1280, 320], P(('dp', 'fsdp')), may hold values from -0.15625 to 0.15625
- w_out: bfloat16 [1280, 1280], P(('dp', 'fsdp')), may hold values from -1.5 to 1.5
- mlp_gain: bfloat16 [1280], P(('dp', 'fsdp')), may hold values from 0.5 to 1.5
- w_gate: bfloat16 [1280, 3584], P(('dp', 'fsdp')), may hold values from -0.15625 to 0.15625
- w_up: bfloat16 [1280, 3584], P(('dp', 'fsdp')), may hold values from -0.15625 to 0.15625
- w_down: bfloat16 [3584, 1280], P(('dp', 'fsdp')), may hold values from -0.09375 to 0.09375
Outputs:
- result: bfloat16 [2, 8, 1024, 1280], P(None, 'dp', 'fsdp')
- input_grad: bfloat16 [2, 8, 1024, 1280], P(None, 'dp', 'fsdp')
- grad_attn_gain: float32 [1280], P(('dp', 'fsdp'))
- grad_query: float32 [1280, 1280], P(('dp', 'fsdp'))
- grad_key: float32 [1280, 320], P(('dp', 'fsdp'))
- grad_value: float32 [1280, 320], P(('dp', 'fsdp'))
- grad_out: float32 [1280, 1280], P(('dp', 'fsdp'))
- grad_mlp_gain: float32 [1280], P(('dp', 'fsdp'))
- grad_gate: float32 [1280, 3584], P(('dp', 'fsdp'))
- grad_up: float32 [1280, 3584], P(('dp', 'fsdp'))
- grad_down: float32 [3584, 1280], P(('dp', 'fsdp'))
The draws below stay inside these ranges and needn't reach their ends.
Inputs may be any that keep to these rules, and one draw needn't show every extreme that they name: `positions`: positions count 0, 1, 2, ... within each document and restart at 0 where a document begins; the first token of every sequence has position 0. Every sequence holds a document of exactly 800 tokens that starts within its first 65 tokens.
All inputs are finite; a program needn't handle non-finite values.
Results may differ from the reference program's by a relative error of at most 0.015.
Values may be sent and summed in bfloat16 or wider, within the bound.
A program may use at most 384 MiB of HBM per device.

```python
import jax
import jax.numpy as jnp
from jax import lax

MODEL_DIMENSION = 1280
HEADS = 20
KV_HEADS = 5
HD = 64
FF = 3584
LEN_DEV = 256
MB = 2
HQ = 1280
KEY_FEATURES = 320
GROUP = 4
LEN = 1024
SEQS = 8
MAXDOC = 800


def draw_positions(key, part):
    key = jax.random.fold_in(key, 11)
    first_key, tail_key = jax.random.split(key)
    seq_count = MB * SEQS
    first_end = jax.random.randint(first_key, (seq_count, 1), 1, LEN_DEV // 4 + 1)
    long_end = first_end + MAXDOC
    tail_start = long_end + jax.random.randint(tail_key, (seq_count, 1), 1, LEN - long_end)
    token_index = jnp.arange(LEN, dtype=jnp.int32)[None, :]
    doc_start = jnp.where(token_index >= tail_start, tail_start, jnp.where(token_index >= long_end, long_end, jnp.where(token_index >= first_end, first_end, 0)))
    return (token_index - doc_start).reshape(MB, SEQS, LEN).astype(jnp.int32)


def block_scale(key, extent, cuts, low, top_value):
    factor_of, own = 1.0, jax.random.fold_in(key, 6)
    for axis_at, blocks in cuts:
        draws = jnp.exp(jax.random.uniform(jax.random.fold_in(own, axis_at), (blocks,), jnp.float32, low / len(cuts), top_value / len(cuts)))
        factor_of = factor_of * jnp.repeat(draws, extent[axis_at] // blocks).reshape([-1 if axis == axis_at else 1 for axis in range(len(extent))])
    return factor_of


def noise(own_key, extent, spread, bound, cuts=(), kind=jnp.bfloat16):
    level = block_scale(own_key, extent, cuts, -0.22, 0.18) if cuts else 1.0
    result = jax.random.normal(own_key, extent, jnp.float32) * spread * level
    return jnp.minimum(jnp.maximum(result, -bound), bound).astype(kind)


def setup_inputs(seed: int = 0) -> dict:
    key_list = jax.random.split(jax.random.key(seed), 13)
    return {
        "inputs": noise(key_list[0], (MB, SEQS, LEN, MODEL_DIMENSION), 1.0, 6.0, ((1, 8), (2, 4))),
        "positions": draw_positions(jax.random.fold_in(key_list[12], 71), 0),
        "cotangent": noise(key_list[2], (MB, SEQS, LEN, MODEL_DIMENSION), 1.0, 6.0, ((1, 8), (2, 4))),
        "attn_gain": jnp.clip(1.0 + 0.1 * jax.random.normal(key_list[3], (MODEL_DIMENSION,), jnp.float32), 0.5, 1.5).astype(jnp.bfloat16),
        "w_query": noise(key_list[4], (MODEL_DIMENSION, HQ), MODEL_DIMENSION ** -0.5, 0.15625, ((0, 32),)),
        "key_matrix": noise(key_list[5], (MODEL_DIMENSION, KEY_FEATURES), MODEL_DIMENSION ** -0.5, 0.15625, ((0, 32),)),
        "value_matrix": noise(key_list[6], (MODEL_DIMENSION, KEY_FEATURES), MODEL_DIMENSION ** -0.5, 0.15625, ((0, 32),)),
        "w_out": noise(key_list[7], (HQ, MODEL_DIMENSION), (HD // 4) ** -0.5, 1.5, ((0, 32),)),
        "mlp_gain": jnp.clip(1.0 + 0.1 * jax.random.normal(key_list[8], (MODEL_DIMENSION,), jnp.float32), 0.5, 1.5).astype(jnp.bfloat16),
        "w_gate": noise(key_list[9], (MODEL_DIMENSION, FF), MODEL_DIMENSION ** -0.5, 0.15625, ((0, 32),)),
        "w_up": noise(key_list[10], (MODEL_DIMENSION, FF), MODEL_DIMENSION ** -0.5, 0.15625, ((0, 32),)),
        "w_down": noise(key_list[11], (FF, MODEL_DIMENSION), FF ** -0.5, 0.09375, ((0, 32),)),
    }


EPSILON = 1e-05
NEGATIVE = -1e+30
ROPE_BASE = 10000.0

@jax.custom_vjp
def low(v):
    return lax.optimization_barrier(v.astype(jnp.bfloat16)).astype(jnp.float32)

@jax.custom_vjp
def low_back(v):
    return v

def low_keep(v):
    return (low(v), None)

def low_pass(kept, grad):
    return (grad,)

def back_keep(v):
    return (v, None)

def back_low(kept, grad):
    return (low(grad),)
low.defvjp(low_keep, low_pass)
low_back.defvjp(back_keep, back_low)

def matmul_high(left, right):
    return jnp.dot(left, right, precision=lax.Precision.HIGHEST, preferred_element_type=jnp.float32)

def rope_tables(places):
    half = HD // 2
    freqs = ROPE_BASE ** (-jnp.arange(half).astype(jnp.float32) / half)
    angles = places.astype(jnp.float32)[:, None] * freqs[None, :]
    return (jnp.cos(angles), jnp.sin(angles))

def rotate(field, cos_table, sin_table, head_count):
    tokens_here = field.shape[0]
    shaped = field.reshape(tokens_here, head_count, HD)
    first_half = shaped[..., :HD // 2]
    second_half = shaped[..., HD // 2:]
    cos_heads = cos_table[:, None, :]
    sin_heads = sin_table[:, None, :]
    turned = jnp.concatenate([first_half * cos_heads - second_half * sin_heads, second_half * cos_heads + first_half * sin_heads], -1)
    return turned.reshape(tokens_here, head_count * HD)

def block_forward(parameters, x_float, cos_table, sin_table, allowed):
    attn_gain, w_query, key_matrix, value_matrix, w_out, mlp_gain, w_gate, w_up, w_down = parameters
    attn_inverse = lax.rsqrt(lax.optimization_barrier(jnp.mean(x_float * x_float, -1, keepdims=True)) + EPSILON)
    normed = low(x_float * attn_inverse * attn_gain)
    queries = low(rotate(low_back(matmul_high(normed, w_query)), cos_table, sin_table, HEADS) * HD ** (-0.5))
    key_rows = low(rotate(low_back(matmul_high(normed, key_matrix)), cos_table, sin_table, KV_HEADS))
    value_rows = low(low_back(matmul_high(normed, value_matrix)))
    grouped = queries.reshape(LEN, KV_HEADS, GROUP, HD)
    key_heads = key_rows.reshape(LEN, KV_HEADS, HD)
    value_heads = value_rows.reshape(LEN, KV_HEADS, HD)
    scores = jnp.einsum('qkgd,skd->kgqs', grouped, key_heads, precision=lax.Precision.HIGHEST)
    scores = jnp.where(allowed[None, None], low_back(scores), NEGATIVE)
    probabilities = jax.nn.softmax(scores, -1)
    attended = jnp.einsum('kgqs,skd->qkgd', low(probabilities), value_heads, precision=lax.Precision.HIGHEST)
    attended = low(low_back(attended.reshape(LEN, HQ)))
    mixed = x_float + low_back(matmul_high(attended, w_out))
    mlp_inverse = lax.rsqrt(lax.optimization_barrier(jnp.mean(mixed * mixed, -1, keepdims=True)) + EPSILON)
    normed_mlp = low(mixed * mlp_inverse * mlp_gain)
    gate_pre = low_back(matmul_high(normed_mlp, w_gate))
    up_proj = low_back(matmul_high(normed_mlp, w_up))
    hidden = low(jax.nn.silu(gate_pre) * up_proj)
    return mixed + matmul_high(hidden, w_down)

def reference(inputs, positions, cotangent, attn_gain, w_query, key_matrix, value_matrix, w_out, mlp_gain, w_gate, w_up, w_down):
    parameters = tuple((w.astype(jnp.float32) for w in (attn_gain, w_query, key_matrix, value_matrix, w_out, mlp_gain, w_gate, w_up, w_down)))
    seq_count = MB * SEQS
    x_all = inputs.reshape(seq_count, LEN, MODEL_DIMENSION).astype(jnp.float32)
    cot_all = cotangent.reshape(seq_count, LEN, MODEL_DIMENSION).astype(jnp.float32)
    place_all = positions.reshape(seq_count, LEN)
    token_index = jnp.arange(LEN).astype(jnp.int32)

    def per_sequence(grad_sums, scan_items):
        x_float, places, cot_float = scan_items
        cos_table, sin_table = rope_tables(places)
        doc_start = token_index - places
        allowed = (token_index[None, :] <= token_index[:, None]) & (token_index[None, :] >= doc_start[:, None])

        def forward_only(prm, x_in):
            return block_forward(prm, x_in, cos_table, sin_table, allowed)
        output, pullback = jax.vjp(forward_only, parameters, x_float)
        grad_params, grad_x = pullback(cot_float)
        grad_sums = jax.tree.map(lambda acc, new: acc + new, grad_sums, grad_params)
        return (grad_sums, (output.astype(jnp.bfloat16), grad_x.astype(jnp.bfloat16)))
    initial = tuple((jnp.zeros(w.shape, jnp.float32) for w in parameters))
    grad_sums, (outputs, grad_inputs) = lax.scan(per_sequence, initial, (x_all, place_all, cot_all))
    shape = inputs.shape
    return (outputs.reshape(shape), grad_inputs.reshape(shape), grad_sums[0], grad_sums[1], grad_sums[2], grad_sums[3], grad_sums[4], grad_sums[5], grad_sums[6], grad_sums[7], grad_sums[8])
```

```python
import jax
import jax.numpy as jnp
from jax import lax
from jax.sharding import PartitionSpec as P

HD = 64
EPSILON = 1e-05
NEGATIVE = -1e30
ROPE_BASE = 10000.0
BOTH = ("dp", "fsdp")


def rope_tables(places):
    half = HD // 2
    freqs = ROPE_BASE ** (-jnp.arange(half).astype(jnp.float32) / half)
    angles = places.astype(jnp.float32)[:, None] * freqs[None, :]
    return (jnp.cos(angles), jnp.sin(angles))


def rotate(field, cos_table, sin_table, sign):
    shaped = field.reshape(field.shape[0], -1, HD)
    first_half = shaped[..., : HD // 2]
    second_half = shaped[..., HD // 2 :]
    cos_heads = cos_table[:, None, :]
    sin_heads = sin_table[:, None, :] * sign
    turned = jnp.concatenate(
        [
            first_half * cos_heads - second_half * sin_heads,
            second_half * cos_heads + first_half * sin_heads,
        ],
        -1,
    )
    return turned.reshape(field.shape)


def plain_dot(left, right):
    return jnp.dot(left, right, preferred_element_type=jnp.float32)


def left_dot(left, right):
    return lax.dot_general(
        left, right, (((0,), (0,)), ((), ())), preferred_element_type=jnp.float32
    )


def right_dot(left, right):
    return lax.dot_general(
        left, right, (((1,), (1,)), ((), ())), preferred_element_type=jnp.float32
    )


def norm_back(grad_normed, inputs_float, inverse):
    return inverse * (
        grad_normed
        - inputs_float * inverse * inverse * jnp.mean(grad_normed * inputs_float, -1, keepdims=True)
    )


def einsum32(spec, a, b):
    return jnp.einsum(spec, a, b, preferred_element_type=jnp.float32)


def gather_rows(shard):
    return lax.all_gather(shard, BOTH, axis=0, tiled=True)


def scatter_rows(full):
    return lax.psum_scatter(
        full.astype(jnp.bfloat16), BOTH, scatter_dimension=0, tiled=True
    ).astype(jnp.float32)


def on_device(
    inputs,
    positions,
    cotangent,
    attn_gain,
    w_query,
    key_matrix,
    value_matrix,
    w_out,
    mlp_gain,
    w_gate,
    w_up,
    w_down,
):
    batches, _, rows, width = inputs.shape
    shard = w_query.shape[0]
    query_features = w_query.shape[1]
    key_features = key_matrix.shape[1]
    kv_heads = key_features // HD
    group = query_features // key_features
    tokens = batches * rows
    length = rows * lax.axis_size("fsdp")
    first_row = lax.axis_index("fsdp") * rows
    query_index = first_row + jnp.arange(rows, dtype=jnp.int32)
    key_index = jnp.arange(length, dtype=jnp.int32)
    score_scale = HD ** (-0.5)

    extras = jnp.zeros((shard, 128), jnp.bfloat16)
    extras = extras.at[:, 0].set(attn_gain).at[:, 1].set(mlp_gain)
    first_pack = gather_rows(
        jnp.concatenate([w_query, key_matrix, value_matrix, extras], axis=1)
    )
    projection = first_pack[:, : query_features + 2 * key_features]
    gains = first_pack[:, query_features + 2 * key_features :][:, :2].astype(jnp.float32).T
    out_full = gather_rows(w_out)
    gate_full = gather_rows(w_gate)
    up_full = gather_rows(w_up)
    down_full = gather_rows(w_down)

    x_float = inputs.reshape(tokens, width).astype(jnp.float32)
    places = positions.reshape(batches, rows)
    cos_table, sin_table = rope_tables(places.reshape(tokens))
    doc_start = query_index[None, :] - places
    allowed = (key_index[None, None, :] <= query_index[None, :, None]) & (
        key_index[None, None, :] >= doc_start[:, :, None]
    )
    attn_inverse = lax.rsqrt(jnp.mean(x_float * x_float, -1, keepdims=True) + EPSILON)
    attn_gain_f = gains[0]
    mlp_gain_f = gains[1]
    normed = (x_float * attn_inverse * attn_gain_f).astype(jnp.bfloat16)
    projected = plain_dot(normed, projection)
    queries = (
        rotate(projected[:, :query_features], cos_table, sin_table, 1.0) * score_scale
    ).astype(jnp.bfloat16)
    key_rows = rotate(
        projected[:, query_features : query_features + key_features], cos_table, sin_table, 1.0
    ).astype(jnp.bfloat16)
    value_rows = projected[:, query_features + key_features :].astype(jnp.bfloat16)
    both_rows = jnp.concatenate([key_rows, value_rows], -1).reshape(batches, rows, -1)
    both_all = lax.all_gather(both_rows, "fsdp", axis=1, tiled=True)
    key_heads = both_all[..., :key_features].reshape(batches, length, kv_heads, HD)
    value_heads = both_all[..., key_features:].reshape(batches, length, kv_heads, HD)
    grouped = queries.reshape(batches, rows, kv_heads, group, HD)
    mask = allowed[:, None, None]
    scores = einsum32("bqkgd,bskd->bkgqs", grouped, key_heads)
    scores = jnp.where(mask, scores, NEGATIVE)
    row_max = jnp.max(scores, -1, keepdims=True)
    row_total = jnp.sum(jnp.exp(scores - row_max), -1, keepdims=True)
    log_total = row_max + jnp.log(row_total)
    probs_low = jnp.exp(scores - log_total).astype(jnp.bfloat16)
    attended = einsum32("bkgqs,bskd->bqkgd", probs_low, value_heads)
    attended = attended.reshape(tokens, query_features).astype(jnp.bfloat16)

    mixed = x_float + plain_dot(attended, out_full)
    mlp_inverse = lax.rsqrt(jnp.mean(mixed * mixed, -1, keepdims=True) + EPSILON)
    normed_mlp = (mixed * mlp_inverse * mlp_gain_f).astype(jnp.bfloat16)
    gate_pre = plain_dot(normed_mlp, gate_full)
    up_proj = plain_dot(normed_mlp, up_full)
    gate_sig = jax.nn.sigmoid(gate_pre)
    hidden = (gate_pre * gate_sig * up_proj).astype(jnp.bfloat16)
    output = (mixed + plain_dot(hidden, down_full)).astype(jnp.bfloat16)

    cot_low = cotangent.reshape(tokens, width)
    cot_float = cot_low.astype(jnp.float32)
    grad_down = scatter_rows(left_dot(hidden, cot_low))
    grad_hidden = right_dot(cot_low, down_full)
    sig_slope = gate_sig * (1.0 + gate_pre * (1.0 - gate_sig))
    grad_gate_pre = (grad_hidden * up_proj * sig_slope).astype(jnp.bfloat16)
    grad_up_pre = (grad_hidden * gate_pre * gate_sig).astype(jnp.bfloat16)
    grad_gate = scatter_rows(left_dot(normed_mlp, grad_gate_pre))
    grad_up = scatter_rows(left_dot(normed_mlp, grad_up_pre))
    grad_normed_mlp = right_dot(grad_gate_pre, gate_full) + right_dot(grad_up_pre, up_full)
    grad_mlp_gain = jnp.sum(grad_normed_mlp * mixed * mlp_inverse, 0)
    grad_mixed = cot_float + norm_back(grad_normed_mlp * mlp_gain_f, mixed, mlp_inverse)
    grad_mixed_low = grad_mixed.astype(jnp.bfloat16)
    grad_out = scatter_rows(left_dot(attended, grad_mixed_low))
    grad_attended = right_dot(grad_mixed_low, out_full).astype(jnp.bfloat16)
    grad_attended = grad_attended.reshape(batches, rows, kv_heads, group, HD)

    scores_again = einsum32("bqkgd,bskd->bkgqs", grouped, key_heads)
    scores_again = jnp.where(mask, scores_again, NEGATIVE)
    probabilities = jnp.exp(scores_again - log_total)
    grad_probs = einsum32("bqkgd,bskd->bkgqs", grad_attended, value_heads)
    row_dot = jnp.sum(probabilities * grad_probs, -1, keepdims=True)
    grad_scores = (probabilities * (grad_probs - row_dot)).astype(jnp.bfloat16)
    grad_query_rot = einsum32("bkgqs,bskd->bqkgd", grad_scores, key_heads)
    key_portion = einsum32("bkgqs,bqkgd->bskd", grad_scores, grouped)
    value_portion = einsum32(
        "bkgqs,bqkgd->bskd", probabilities.astype(jnp.bfloat16), grad_attended
    )
    portions = jnp.concatenate(
        [
            key_portion.reshape(batches, length, key_features),
            value_portion.reshape(batches, length, key_features),
        ],
        -1,
    ).astype(jnp.bfloat16)
    sums = lax.psum_scatter(portions, "fsdp", scatter_dimension=1, tiled=True)
    sums = sums.astype(jnp.float32).reshape(tokens, 2 * key_features)
    grad_query_pre = rotate(
        grad_query_rot.reshape(tokens, query_features) * score_scale, cos_table, sin_table, -1.0
    ).astype(jnp.bfloat16)
    grad_key_pre = rotate(sums[:, :key_features], cos_table, sin_table, -1.0).astype(jnp.bfloat16)
    grad_value_pre = sums[:, key_features:].astype(jnp.bfloat16)
    grad_pre = jnp.concatenate([grad_query_pre, grad_key_pre, grad_value_pre], -1)
    grad_projection = left_dot(normed, grad_pre)
    grad_normed = right_dot(grad_pre, projection)
    grad_attn_gain = jnp.sum(grad_normed * x_float * attn_inverse, 0)
    grad_input = grad_mixed + norm_back(grad_normed * attn_gain_f, x_float, attn_inverse)
    gain_columns = jnp.stack([grad_attn_gain, grad_mlp_gain], -1)
    gain_columns = jnp.pad(gain_columns, ((0, 0), (0, 126)))
    last = scatter_rows(jnp.concatenate([grad_projection, gain_columns], 1))
    split = query_features + key_features
    return (
        output.reshape(inputs.shape),
        grad_input.astype(jnp.bfloat16).reshape(inputs.shape),
        last[:, split + key_features],
        last[:, :query_features],
        last[:, query_features:split],
        last[:, split : split + key_features],
        grad_out,
        last[:, split + key_features + 1],
        grad_gate,
        grad_up,
        grad_down,
    )


def solution(mesh):
    tokens = P(None, "dp", "fsdp", None)
    vector = P(BOTH)
    matrix = P(BOTH, None)
    weights = (vector, matrix, matrix, matrix, matrix, vector, matrix, matrix, matrix)
    return jax.shard_map(
        on_device,
        mesh=mesh,
        in_specs=(tokens, P(None, "dp", "fsdp"), tokens) + weights,
        out_specs=(tokens, tokens) + weights,
        check_vma=False,
    )
```

```python
import functools

import jax
import jax.numpy as jnp
from jax import lax
from jax.experimental import pallas as pl
from jax.experimental.pallas import tpu as pltpu
from jax.sharding import PartitionSpec as P

HD = 64
EPSILON = 1e-05
NEGATIVE = -1e30
ROPE_BASE = 10000.0
BOTH = ("dp", "fsdp")


def rope_tables(places):
    half = HD // 2
    freqs = ROPE_BASE ** (-jnp.arange(half).astype(jnp.float32) / half)
    angles = places.astype(jnp.float32)[:, None] * freqs[None, :]
    return (jnp.cos(angles), jnp.sin(angles))


def rotate(field, cos_table, sin_table, sign):
    shaped = field.reshape(field.shape[0], -1, HD)
    first_half = shaped[..., : HD // 2]
    second_half = shaped[..., HD // 2 :]
    cos_heads = cos_table[:, None, :]
    sin_heads = sin_table[:, None, :] * sign
    turned = jnp.concatenate(
        [
            first_half * cos_heads - second_half * sin_heads,
            second_half * cos_heads + first_half * sin_heads,
        ],
        -1,
    )
    return turned.reshape(field.shape)


def plain_dot(left, right):
    return jnp.dot(left, right, preferred_element_type=jnp.float32)


def left_dot(left, right):
    return lax.dot_general(
        left, right, (((0,), (0,)), ((), ())), preferred_element_type=jnp.float32
    )


def right_dot(left, right):
    return lax.dot_general(
        left, right, (((1,), (1,)), ((), ())), preferred_element_type=jnp.float32
    )


def norm_back(grad_normed, inputs_float, inverse):
    return inverse * (
        grad_normed
        - inputs_float * inverse * inverse * jnp.mean(grad_normed * inputs_float, -1, keepdims=True)
    )


def einsum32(spec, a, b):
    return jnp.einsum(spec, a, b, preferred_element_type=jnp.float32)


class Place:
    def __init__(self):
        self.Z=lax.axis_size("dp")//2; self.X=lax.axis_size("fsdp")//2
        dp=lax.axis_index("dp"); fs=lax.axis_index("fsdp")
        self.z=dp//2; self.y=dp%2; self.x=fs//2; self.c=fs%2
    def device(self,s=0,dy=0,dx=0,dc=0):
        return (lax.rem(self.z+s,self.Z)*2+lax.rem(self.y+dy,2), lax.rem(self.x+dx,self.X)*2+lax.rem(self.c+dc,2))
    def slot(self,s,dy,dx,dc):
        return ((lax.rem(self.z+self.Z-s,self.Z)*2+lax.rem(self.y+dy,2))*self.X+lax.rem(self.x+dx,self.X))*2+lax.rem(self.c+dc,2)

MESH = pl.DeviceIdType.MESH

def greet(me):
    barrier=pltpu.get_barrier_semaphore()
    friends=[me.device(s=s) for s in range(1,me.Z)]+[me.device(dy=1),me.device(dx=1),me.device(dc=1)]
    for f in friends:
        pl.semaphore_signal(barrier,inc=1,device_id=f,device_id_type=MESH)
    pl.semaphore_wait(barrier,len(friends))

def gather_kernel(Z, orders, ahead, *refs):
    K=len(orders)
    shards=refs[:K]; outs=refs[K:2*K]; local,send,recv=refs[2*K:]
    me=Place()
    greet(me)
    dims={"y":1,"x":2,"c":3}
    def sem(rel):
        return ((rel[0]*2+rel[1])*2+rel[2])*2+rel[3]
    started=[]
    def start(k,rel,to):
        if isinstance(to,int):
            target=me.device(s=to); landed=(to,0,0,0)
        else:
            landed=list(rel); landed[dims[to]]=1; landed=tuple(landed)
            target=me.device(**{"d"+to:1})
        slot=me.slot(*rel)
        src=shards[k] if rel==(0,0,0,0) else outs[k].at[slot]
        cp=pltpu.make_async_remote_copy(src_ref=src,dst_ref=outs[k].at[slot],send_sem=send.at[k,sem(landed)],recv_sem=recv.at[k,sem(landed)],device_id=target,device_id_type=MESH)
        cp.start()
        table[(k,landed)]=cp
    table={}
    own=[]
    def first(k):
        cp=pltpu.make_async_copy(shards[k],outs[k].at[me.slot(0,0,0,0)],local.at[k]); cp.start(); own.append(cp)
        for s in range(1,Z): start(k,(0,0,0,0),s)
        for d in orders[k]: start(k,(0,0,0,0),d)
    def arrive(k,rel,rest):
        table[(k,rel)].wait_recv()
        for d in rest: start(k,rel,d)
    def rel_of(s,o,a,b=0,c=0):
        r=[s,0,0,0]; r[dims[o[0]]]=a; r[dims[o[1]]]=b; r[dims[o[2]]]=c
        return tuple(r)
    for k in range(min(ahead,K)): first(k)
    for t in range(K+3):
        if t+ahead<K: first(t+ahead)
        k=t
        if k<K:
            o=orders[k]
            for s in range(1,Z): arrive(k,rel_of(s,o,0),o)
        k=t-1
        if 0<=k<K:
            o=orders[k]
            for s in range(Z): arrive(k,rel_of(s,o,1),o[1:])
        k=t-2
        if 0<=k<K:
            o=orders[k]
            for s in range(Z):
                for a in range(2): arrive(k,rel_of(s,o,a,1),o[2:])
        k=t-3
        if 0<=k<K:
            o=orders[k]
            for s in range(Z):
                for a in range(2):
                    for b in range(2): arrive(k,rel_of(s,o,a,b,1),"")
    for cp in own: cp.wait()
    for cp in table.values(): cp.wait_send()

def gather(shards, orders, cid, ahead=2):
    n=lax.axis_size("dp")*lax.axis_size("fsdp"); Z=lax.axis_size("dp")//2; K=len(shards)
    return pl.pallas_call(functools.partial(gather_kernel,Z,orders,ahead),
        out_shape=[jax.ShapeDtypeStruct((n,)+s.shape,s.dtype) for s in shards],
        in_specs=[pl.BlockSpec(memory_space=pl.ANY)]*K,
        out_specs=[pl.BlockSpec(memory_space=pl.ANY)]*K,
        scratch_shapes=[pltpu.SemaphoreType.DMA((K,)),pltpu.SemaphoreType.DMA((K,8*Z)),pltpu.SemaphoreType.DMA((K,8*Z))],
        compiler_params=pltpu.CompilerParams(collective_id=cid,has_side_effects=True))(*shards)


def tile_of(N):
    for t in (512,384,256,128):
        if N%t==0: return t
    return N

def scatter_kernel(Z, orders, ahead, dims_, *refs):
    K=len(orders)
    parts=refs[:K]; outs=refs[K:2*K]
    sc=refs[2*K:]
    first_buf=sc[:K]; one_buf=sc[K:2*K]; two_buf=sc[2*K:3*K]; last_buf=sc[3*K:4*K]
    shapes=sorted(set(dims_))
    stage=[sc[4*K+shapes.index(d)] for d in dims_]
    local,send,recv=sc[4*K+len(shapes):]
    me=Place()
    greet(me)
    copies={}
    def ship(k,name,index,src,dst,target):
        cp=pltpu.make_async_remote_copy(src_ref=src,dst_ref=dst,send_sem=send.at[k,index],recv_sem=recv.at[k,index],device_id=target,device_id_type=MESH)
        cp.start(); copies[(k,name)]=cp
    def part(k,a,b,other):
        o=orders[k]
        rel={o[0]:a,o[1]:b}
        y=lax.rem(me.y+rel["y"],2); x=lax.rem(me.x+rel["x"],me.X); c=lax.rem(me.c+other,2)
        return parts[k].at[:,y,x,c]
    order4=((1,1),(1,0),(0,1),(0,0))
    locals_={}
    def first(k):
        for i,(a,b) in enumerate(order4):
            ship(k,("c",a,b),i,part(k,a,b,1),first_buf[k].at[a,b],me.device(dc=1))
    def bring(k,i):
        a,b=order4[i]
        cp=pltpu.make_async_copy(part(k,a,b,0),stage[k].at[i%2],local.at[k,i%2]); cp.start(); locals_[(k,i)]=cp
    def add(dst,src,k):
        _,r,N=dims_[k]
        t=tile_of(N)
        def body(i,_):
            zi=i//(N//t); j=i%(N//t)
            cols=pl.ds(pl.multiple_of(j*t,128),t)
            dst[zi,:,cols]=dst[zi,:,cols]+src[zi,:,cols]
            return 0
        lax.fori_loop(0,Z*(N//t),body,0)
    def step_c(k):
        bring(k,0); bring(k,1)
        for i,(a,b) in enumerate(order4):
            copies[(k,("c",a,b))].wait_recv()
            locals_[(k,i)].wait()
            add(first_buf[k].at[a,b],stage[k].at[i%2],k)
            if i+2<4: bring(k,i+2)
            if a==1:
                ship(k,("1",b),4+b,first_buf[k].at[1,b],one_buf[k].at[b],me.device(**{"d"+orders[k][0]:1}))
    def step_1(k):
        for b in (1,0):
            copies[(k,("1",b))].wait_recv()
            add(first_buf[k].at[0,b],one_buf[k].at[b],k)
            if b==1:
                ship(k,"2",6,first_buf[k].at[0,1],two_buf[k],me.device(**{"d"+orders[k][1]:1}))
    def step_2(k):
        copies[(k,"2")].wait_recv()
        add(first_buf[k].at[0,0],two_buf[k],k)
        for s in range(1,Z):
            ship(k,("z",s),6+s,first_buf[k].at[0,0,lax.rem(me.z+s,Z)],last_buf[k].at[s-1],me.device(s=s))
    def step_z(k):
        _,r,N=dims_[k]
        for s in range(1,Z): copies[(k,("z",s))].wait_recv()
        t=tile_of(N)
        mine=first_buf[k].at[0,0,me.z]
        def body(j,_):
            cols=pl.ds(pl.multiple_of(j*t,128),t)
            total=mine[:,cols].astype(jnp.float32)
            for s in range(1,Z): total=total+last_buf[k][s-1,:,cols].astype(jnp.float32)
            outs[k][:,cols]=total
            return 0
        lax.fori_loop(0,N//t,body,0)
    for k in range(min(ahead,K)): first(k)
    for t in range(K+3):
        if t+ahead<K: first(t+ahead)
        if t<K: step_c(t)
        if 0<=t-1<K: step_1(t-1)
        if 0<=t-2<K: step_2(t-2)
        if 0<=t-3<K: step_z(t-3)
    for cp in copies.values(): cp.wait_send()

def scatter(parts, orders, cid, ahead=2):
    n=lax.axis_size("dp")*lax.axis_size("fsdp"); Z=lax.axis_size("dp")//2; X=lax.axis_size("fsdp")//2; K=len(parts)
    dims_=[(n,p.shape[0]//n,p.shape[1]) for p in parts]
    parts=[p.reshape(Z,2,X,2,p.shape[0]//n,p.shape[1]) for p in parts]
    bf=jnp.bfloat16
    sc=[pltpu.VMEM((2,2,Z,r,N),bf) for _,r,N in dims_]+[pltpu.VMEM((2,Z,r,N),bf) for _,r,N in dims_]+[pltpu.VMEM((Z,r,N),bf) for _,r,N in dims_]+[pltpu.VMEM((Z-1,r,N),bf) for _,r,N in dims_]+[pltpu.VMEM((2,Z,r,N),bf) for _,r,N in sorted(set(dims_))]
    return pl.pallas_call(functools.partial(scatter_kernel,Z,orders,ahead,dims_),
        out_shape=[jax.ShapeDtypeStruct((r,N),jnp.float32) for _,r,N in dims_],
        in_specs=[pl.BlockSpec(memory_space=pl.ANY)]*K,
        out_specs=[pl.BlockSpec(memory_space=pltpu.VMEM)]*K,
        scratch_shapes=sc+[pltpu.SemaphoreType.DMA((K,2)),pltpu.SemaphoreType.DMA((K,6+Z)),pltpu.SemaphoreType.DMA((K,6+Z))],
        compiler_params=pltpu.CompilerParams(collective_id=cid,has_side_effects=True,vmem_limit_bytes=63*2**20))(*parts)


def half_of(full):
    return full.astype(jnp.bfloat16)


def on_device(
    inputs,
    positions,
    cotangent,
    attn_gain,
    w_query,
    key_matrix,
    value_matrix,
    w_out,
    mlp_gain,
    w_gate,
    w_up,
    w_down,
):
    batches, _, rows, width = inputs.shape
    shard = w_query.shape[0]
    query_features = w_query.shape[1]
    key_features = key_matrix.shape[1]
    kv_heads = key_features // HD
    group = query_features // key_features
    tokens = batches * rows
    length = rows * lax.axis_size("fsdp")
    first_row = lax.axis_index("fsdp") * rows
    query_index = first_row + jnp.arange(rows, dtype=jnp.int32)
    key_index = jnp.arange(length, dtype=jnp.int32)
    score_scale = HD ** (-0.5)

    extras = jnp.zeros((shard, 128), jnp.bfloat16)
    extras = extras.at[:, 0].set(attn_gain).at[:, 1].set(mlp_gain)
    first_shard = jnp.concatenate([w_query, key_matrix, value_matrix, extras], axis=1)
    fulls = gather(
        (first_shard, w_out, w_gate, w_up, w_down), ("yxc", "xyc", "yxc", "xyc", "yxc"), 1, 5
    )
    first_pack, out_full, gate_full, up_full, down_full = (
        f.reshape(-1, f.shape[-1]) for f in fulls
    )
    projection = first_pack[:, : query_features + 2 * key_features]
    gains = first_pack[:, query_features + 2 * key_features :][:, :2].astype(jnp.float32).T

    x_float = inputs.reshape(tokens, width).astype(jnp.float32)
    places = positions.reshape(batches, rows)
    cos_table, sin_table = rope_tables(places.reshape(tokens))
    doc_start = query_index[None, :] - places
    allowed = (key_index[None, None, :] <= query_index[None, :, None]) & (
        key_index[None, None, :] >= doc_start[:, :, None]
    )
    attn_inverse = lax.rsqrt(jnp.mean(x_float * x_float, -1, keepdims=True) + EPSILON)
    attn_gain_f = gains[0]
    mlp_gain_f = gains[1]
    normed = (x_float * attn_inverse * attn_gain_f).astype(jnp.bfloat16)
    projected = plain_dot(normed, projection)
    queries = (
        rotate(projected[:, :query_features], cos_table, sin_table, 1.0) * score_scale
    ).astype(jnp.bfloat16)
    key_rows = rotate(
        projected[:, query_features : query_features + key_features], cos_table, sin_table, 1.0
    ).astype(jnp.bfloat16)
    value_rows = projected[:, query_features + key_features :].astype(jnp.bfloat16)
    both_rows = jnp.concatenate([key_rows, value_rows], -1).reshape(batches, rows, -1)
    both_all = lax.all_gather(both_rows, "fsdp", axis=1, tiled=True)
    key_heads = both_all[..., :key_features].reshape(batches, length, kv_heads, HD)
    value_heads = both_all[..., key_features:].reshape(batches, length, kv_heads, HD)
    grouped = queries.reshape(batches, rows, kv_heads, group, HD)
    mask = allowed[:, None, None]
    scores = einsum32("bqkgd,bskd->bkgqs", grouped, key_heads)
    scores = jnp.where(mask, scores, NEGATIVE)
    row_max = jnp.max(scores, -1, keepdims=True)
    row_total = jnp.sum(jnp.exp(scores - row_max), -1, keepdims=True)
    log_total = row_max + jnp.log(row_total)
    probs_low = jnp.exp(scores - log_total).astype(jnp.bfloat16)
    attended = einsum32("bkgqs,bskd->bqkgd", probs_low, value_heads)
    attended = attended.reshape(tokens, query_features).astype(jnp.bfloat16)

    mixed = x_float + plain_dot(attended, out_full)
    mlp_inverse = lax.rsqrt(jnp.mean(mixed * mixed, -1, keepdims=True) + EPSILON)
    normed_mlp = (mixed * mlp_inverse * mlp_gain_f).astype(jnp.bfloat16)
    gate_pre = plain_dot(normed_mlp, gate_full)
    up_proj = plain_dot(normed_mlp, up_full)
    gate_sig = jax.nn.sigmoid(gate_pre)
    hidden = (gate_pre * gate_sig * up_proj).astype(jnp.bfloat16)
    output = (mixed + plain_dot(hidden, down_full)).astype(jnp.bfloat16)

    cot_low = cotangent.reshape(tokens, width)
    cot_float = cot_low.astype(jnp.float32)
    grad_down = half_of(left_dot(hidden, cot_low))
    grad_hidden = right_dot(cot_low, down_full)
    sig_slope = gate_sig * (1.0 + gate_pre * (1.0 - gate_sig))
    grad_gate_pre = (grad_hidden * up_proj * sig_slope).astype(jnp.bfloat16)
    grad_up_pre = (grad_hidden * gate_pre * gate_sig).astype(jnp.bfloat16)
    grad_gate = half_of(left_dot(normed_mlp, grad_gate_pre))
    grad_up = half_of(left_dot(normed_mlp, grad_up_pre))
    grad_normed_mlp = right_dot(grad_gate_pre, gate_full) + right_dot(grad_up_pre, up_full)
    grad_mlp_gain = jnp.sum(grad_normed_mlp * mixed * mlp_inverse, 0)
    grad_mixed = cot_float + norm_back(grad_normed_mlp * mlp_gain_f, mixed, mlp_inverse)
    grad_mixed_low = grad_mixed.astype(jnp.bfloat16)
    grad_out = half_of(left_dot(attended, grad_mixed_low))
    grad_attended = right_dot(grad_mixed_low, out_full).astype(jnp.bfloat16)
    grad_attended = grad_attended.reshape(batches, rows, kv_heads, group, HD)

    scores_again = einsum32("bqkgd,bskd->bkgqs", grouped, key_heads)
    scores_again = jnp.where(mask, scores_again, NEGATIVE)
    probabilities = jnp.exp(scores_again - log_total)
    grad_probs = einsum32("bqkgd,bskd->bkgqs", grad_attended, value_heads)
    row_dot = jnp.sum(probabilities * grad_probs, -1, keepdims=True)
    grad_scores = (probabilities * (grad_probs - row_dot)).astype(jnp.bfloat16)
    grad_query_rot = einsum32("bkgqs,bskd->bqkgd", grad_scores, key_heads)
    key_portion = einsum32("bkgqs,bqkgd->bskd", grad_scores, grouped)
    value_portion = einsum32(
        "bkgqs,bqkgd->bskd", probabilities.astype(jnp.bfloat16), grad_attended
    )
    portions = jnp.concatenate(
        [
            key_portion.reshape(batches, length, key_features),
            value_portion.reshape(batches, length, key_features),
        ],
        -1,
    ).astype(jnp.bfloat16)
    sums = lax.psum_scatter(portions, "fsdp", scatter_dimension=1, tiled=True)
    sums = sums.astype(jnp.float32).reshape(tokens, 2 * key_features)
    grad_query_pre = rotate(
        grad_query_rot.reshape(tokens, query_features) * score_scale, cos_table, sin_table, -1.0
    ).astype(jnp.bfloat16)
    grad_key_pre = rotate(sums[:, :key_features], cos_table, sin_table, -1.0).astype(jnp.bfloat16)
    grad_value_pre = sums[:, key_features:].astype(jnp.bfloat16)
    grad_pre = jnp.concatenate([grad_query_pre, grad_key_pre, grad_value_pre], -1)
    grad_projection = left_dot(normed, grad_pre)
    grad_normed = right_dot(grad_pre, projection)
    grad_attn_gain = jnp.sum(grad_normed * x_float * attn_inverse, 0)
    grad_input = grad_mixed + norm_back(grad_normed * attn_gain_f, x_float, attn_inverse)
    gain_columns = jnp.stack([grad_attn_gain, grad_mlp_gain], -1)
    gain_columns = jnp.pad(gain_columns, ((0, 0), (0, 126)))
    grad_first = half_of(jnp.concatenate([grad_projection, gain_columns], 1))
    grad_down, grad_gate, grad_up, grad_out, last = scatter(
        (grad_down, grad_gate, grad_up, grad_out, grad_first), ("xy", "yx", "xy", "yx", "xy"), 2
    )
    split = query_features + key_features
    return (
        output.reshape(inputs.shape),
        grad_input.astype(jnp.bfloat16).reshape(inputs.shape),
        last[:, split + key_features],
        last[:, :query_features],
        last[:, query_features:split],
        last[:, split : split + key_features],
        grad_out,
        last[:, split + key_features + 1],
        grad_gate,
        grad_up,
        grad_down,
    )


def solution(mesh):
    tokens = P(None, "dp", "fsdp", None)
    vector = P(BOTH)
    matrix = P(BOTH, None)
    weights = (vector, matrix, matrix, matrix, matrix, vector, matrix, matrix, matrix)
    return jax.shard_map(
        on_device,
        mesh=mesh,
        in_specs=(tokens, P(None, "dp", "fsdp"), tokens) + weights,
        out_specs=(tokens, tokens) + weights,
        check_vma=False,
    )
```

```python
import functools

import jax
import jax.numpy as jnp
from jax import lax
from jax.experimental import pallas as pl
from jax.experimental.pallas import tpu as pltpu
from jax.sharding import PartitionSpec as P

HD = 64
EPSILON = 1e-05
NEGATIVE = -1e30
ROPE_BASE = 10000.0
BOTH = ("dp", "fsdp")


def rope_tables(places):
    half = HD // 2
    freqs = ROPE_BASE ** (-jnp.arange(half).astype(jnp.float32) / half)
    angles = places.astype(jnp.float32)[:, None] * freqs[None, :]
    return (jnp.cos(angles), jnp.sin(angles))


def plain_dot(left, right):
    return jnp.dot(left, right, preferred_element_type=jnp.float32)


def left_dot(left, right):
    return lax.dot_general(
        left, right, (((0,), (0,)), ((), ())), preferred_element_type=jnp.float32
    )


def right_dot(left, right):
    return lax.dot_general(
        left, right, (((1,), (1,)), ((), ())), preferred_element_type=jnp.float32
    )


def norm_back(grad_normed, inputs_float, inverse):
    return inverse * (
        grad_normed
        - inputs_float * inverse * inverse * jnp.mean(grad_normed * inputs_float, -1, keepdims=True)
    )


class Place:
    def __init__(self):
        self.Z=lax.axis_size("dp")//2; self.X=lax.axis_size("fsdp")//2
        dp=lax.axis_index("dp"); fs=lax.axis_index("fsdp")
        self.z=dp//2; self.y=dp%2; self.x=fs//2; self.c=fs%2
    def device(self,s=0,dy=0,dx=0,dc=0):
        return (lax.rem(self.z+s,self.Z)*2+lax.rem(self.y+dy,2), lax.rem(self.x+dx,self.X)*2+lax.rem(self.c+dc,2))
    def slot(self,s,dy,dx,dc):
        return ((lax.rem(self.z+self.Z-s,self.Z)*2+lax.rem(self.y+dy,2))*self.X+lax.rem(self.x+dx,self.X))*2+lax.rem(self.c+dc,2)

MESH = pl.DeviceIdType.MESH

def greet(me):
    barrier=pltpu.get_barrier_semaphore()
    friends=[me.device(s=s) for s in range(1,me.Z)]+[me.device(dy=1),me.device(dx=1),me.device(dc=1)]
    for f in friends:
        pl.semaphore_signal(barrier,inc=1,device_id=f,device_id_type=MESH)
    pl.semaphore_wait(barrier,len(friends))

def gather_kernel(Z, orders, ahead, *refs):
    K=len(orders)
    shards=refs[:K]; outs=refs[K:2*K]; local,send,recv=refs[2*K:]
    me=Place()
    greet(me)
    dims={"y":1,"x":2,"c":3}
    def sem(rel):
        return ((rel[0]*2+rel[1])*2+rel[2])*2+rel[3]
    started=[]
    def start(k,rel,to):
        if isinstance(to,int):
            target=me.device(s=to); landed=(to,0,0,0)
        else:
            landed=list(rel); landed[dims[to]]=1; landed=tuple(landed)
            target=me.device(**{"d"+to:1})
        slot=me.slot(*rel)
        src=shards[k] if rel==(0,0,0,0) else outs[k].at[slot]
        cp=pltpu.make_async_remote_copy(src_ref=src,dst_ref=outs[k].at[slot],send_sem=send.at[k,sem(landed)],recv_sem=recv.at[k,sem(landed)],device_id=target,device_id_type=MESH)
        cp.start()
        table[(k,landed)]=cp
    table={}
    own=[]
    def first(k):
        cp=pltpu.make_async_copy(shards[k],outs[k].at[me.slot(0,0,0,0)],local.at[k]); cp.start(); own.append(cp)
        for s in range(1,Z): start(k,(0,0,0,0),s)
        for d in orders[k]: start(k,(0,0,0,0),d)
    def arrive(k,rel,rest):
        table[(k,rel)].wait_recv()
        for d in rest: start(k,rel,d)
    def rel_of(s,o,a,b=0,c=0):
        r=[s,0,0,0]; r[dims[o[0]]]=a; r[dims[o[1]]]=b; r[dims[o[2]]]=c
        return tuple(r)
    for k in range(min(ahead,K)): first(k)
    for t in range(K+3):
        if t+ahead<K: first(t+ahead)
        k=t
        if k<K:
            o=orders[k]
            for s in range(1,Z): arrive(k,rel_of(s,o,0),o)
        k=t-1
        if 0<=k<K:
            o=orders[k]
            for s in range(Z): arrive(k,rel_of(s,o,1),o[1:])
        k=t-2
        if 0<=k<K:
            o=orders[k]
            for s in range(Z):
                for a in range(2): arrive(k,rel_of(s,o,a,1),o[2:])
        k=t-3
        if 0<=k<K:
            o=orders[k]
            for s in range(Z):
                for a in range(2):
                    for b in range(2): arrive(k,rel_of(s,o,a,b,1),"")
    for cp in own: cp.wait()
    for cp in table.values(): cp.wait_send()

def gather(shards, orders, cid, ahead=2):
    n=lax.axis_size("dp")*lax.axis_size("fsdp"); Z=lax.axis_size("dp")//2; K=len(shards)
    return pl.pallas_call(functools.partial(gather_kernel,Z,orders,ahead),
        out_shape=[jax.ShapeDtypeStruct((n,)+s.shape,s.dtype) for s in shards],
        in_specs=[pl.BlockSpec(memory_space=pl.ANY)]*K,
        out_specs=[pl.BlockSpec(memory_space=pl.ANY)]*K,
        scratch_shapes=[pltpu.SemaphoreType.DMA((K,)),pltpu.SemaphoreType.DMA((K,8*Z)),pltpu.SemaphoreType.DMA((K,8*Z))],
        compiler_params=pltpu.CompilerParams(collective_id=cid,has_side_effects=True))(*shards)


def tile_of(N):
    for t in (512,384,256,128):
        if N%t==0: return t
    return N

def scatter_kernel(Z, orders, ahead, dims_, *refs):
    K=len(orders)
    parts=refs[:K]; outs=refs[K:2*K]
    sc=refs[2*K:]
    first_buf=sc[:K]; one_buf=sc[K:2*K]; two_buf=sc[2*K:3*K]; last_buf=sc[3*K:4*K]
    shapes=sorted(set(dims_))
    stage=[sc[4*K+shapes.index(d)] for d in dims_]
    local,send,recv=sc[4*K+len(shapes):]
    me=Place()
    greet(me)
    copies={}
    def ship(k,name,index,src,dst,target):
        cp=pltpu.make_async_remote_copy(src_ref=src,dst_ref=dst,send_sem=send.at[k,index],recv_sem=recv.at[k,index],device_id=target,device_id_type=MESH)
        cp.start(); copies[(k,name)]=cp
    def part(k,a,b,other):
        o=orders[k]
        rel={o[0]:a,o[1]:b}
        y=lax.rem(me.y+rel["y"],2); x=lax.rem(me.x+rel["x"],me.X); c=lax.rem(me.c+other,2)
        return parts[k].at[:,y,x,c]
    order4=((1,1),(1,0),(0,1),(0,0))
    locals_={}
    def first(k):
        for i,(a,b) in enumerate(order4):
            ship(k,("c",a,b),i,part(k,a,b,1),first_buf[k].at[a,b],me.device(dc=1))
    def bring(k,i):
        a,b=order4[i]
        cp=pltpu.make_async_copy(part(k,a,b,0),stage[k].at[i%2],local.at[k,i%2]); cp.start(); locals_[(k,i)]=cp
    def add(dst,src,k):
        _,r,N=dims_[k]
        t=tile_of(N)
        def body(i,_):
            zi=i//(N//t); j=i%(N//t)
            cols=pl.ds(pl.multiple_of(j*t,128),t)
            dst[zi,:,cols]=dst[zi,:,cols]+src[zi,:,cols]
            return 0
        lax.fori_loop(0,Z*(N//t),body,0)
    def step_c(k):
        bring(k,0); bring(k,1)
        for i,(a,b) in enumerate(order4):
            copies[(k,("c",a,b))].wait_recv()
            locals_[(k,i)].wait()
            add(first_buf[k].at[a,b],stage[k].at[i%2],k)
            if i+2<4: bring(k,i+2)
            if a==1:
                ship(k,("1",b),4+b,first_buf[k].at[1,b],one_buf[k].at[b],me.device(**{"d"+orders[k][0]:1}))
    def step_1(k):
        for b in (1,0):
            copies[(k,("1",b))].wait_recv()
            add(first_buf[k].at[0,b],one_buf[k].at[b],k)
            if b==1:
                ship(k,"2",6,first_buf[k].at[0,1],two_buf[k],me.device(**{"d"+orders[k][1]:1}))
    def step_2(k):
        copies[(k,"2")].wait_recv()
        add(first_buf[k].at[0,0],two_buf[k],k)
        for s in range(1,Z):
            ship(k,("z",s),6+s,first_buf[k].at[0,0,lax.rem(me.z+s,Z)],last_buf[k].at[s-1],me.device(s=s))
    def step_z(k):
        _,r,N=dims_[k]
        for s in range(1,Z): copies[(k,("z",s))].wait_recv()
        t=tile_of(N)
        mine=first_buf[k].at[0,0,me.z]
        def body(j,_):
            cols=pl.ds(pl.multiple_of(j*t,128),t)
            total=mine[:,cols].astype(jnp.float32)
            for s in range(1,Z): total=total+last_buf[k][s-1,:,cols].astype(jnp.float32)
            outs[k][:,cols]=total
            return 0
        lax.fori_loop(0,N//t,body,0)
    for k in range(min(ahead,K)): first(k)
    for t in range(K+3):
        if t+ahead<K: first(t+ahead)
        if t<K: step_c(t)
        if 0<=t-1<K: step_1(t-1)
        if 0<=t-2<K: step_2(t-2)
        if 0<=t-3<K: step_z(t-3)
    for cp in copies.values(): cp.wait_send()

def scatter(parts, orders, cid, ahead=2):
    n=lax.axis_size("dp")*lax.axis_size("fsdp"); Z=lax.axis_size("dp")//2; X=lax.axis_size("fsdp")//2; K=len(parts)
    dims_=[(n,p.shape[0]//n,p.shape[1]) for p in parts]
    parts=[p.reshape(Z,2,X,2,p.shape[0]//n,p.shape[1]) for p in parts]
    bf=jnp.bfloat16
    sc=[pltpu.VMEM((2,2,Z,r,N),bf) for _,r,N in dims_]+[pltpu.VMEM((2,Z,r,N),bf) for _,r,N in dims_]+[pltpu.VMEM((Z,r,N),bf) for _,r,N in dims_]+[pltpu.VMEM((Z-1,r,N),bf) for _,r,N in dims_]+[pltpu.VMEM((2,Z,r,N),bf) for _,r,N in sorted(set(dims_))]
    return pl.pallas_call(functools.partial(scatter_kernel,Z,orders,ahead,dims_),
        out_shape=[jax.ShapeDtypeStruct((r,N),jnp.float32) for _,r,N in dims_],
        in_specs=[pl.BlockSpec(memory_space=pl.ANY)]*K,
        out_specs=[pl.BlockSpec(memory_space=pltpu.VMEM)]*K,
        scratch_shapes=sc+[pltpu.SemaphoreType.DMA((K,2)),pltpu.SemaphoreType.DMA((K,6+Z)),pltpu.SemaphoreType.DMA((K,6+Z))],
        compiler_params=pltpu.CompilerParams(collective_id=cid,has_side_effects=True,vmem_limit_bytes=63*2**20))(*parts)


def dot_t(left, right):
    return lax.dot_general(
        left, right, (((1,), (1,)), ((), ())), preferred_element_type=jnp.float32
    )


def swap_halves(u):
    lane = lax.broadcasted_iota(jnp.int32, u.shape, 1)
    down = pltpu.roll(u, 32, 1)
    up = pltpu.roll(u, 96, 1)
    return jnp.where(lax.rem(lane, 64) < 32, up, down)


def project_kernel(h_ref, w_ref, cos_ref, sin_ref, out_ref):
    u = plain_dot(h_ref[...], w_ref[...])
    for j in range(u.shape[1] // 128):
        piece = u[:, j * 128 : (j + 1) * 128]
        turned = piece * cos_ref[0] + swap_halves(piece) * sin_ref[0]
        out_ref[:, j * 128 : (j + 1) * 128] = turned.astype(jnp.bfloat16)


def project(normed, weight, cos_tables, sin_tables, width):
    tokens, depth = normed.shape
    steps = weight.shape[1] // width
    return pl.pallas_call(
        project_kernel,
        grid=(steps,),
        in_specs=[
            pl.BlockSpec((tokens, depth), lambda j: (0, 0)),
            pl.BlockSpec((depth, width), lambda j: (0, j)),
            pl.BlockSpec((1, tokens, 128), lambda j: (j // (steps - 1), 0, 0)),
            pl.BlockSpec((1, tokens, 128), lambda j: (j // (steps - 1), 0, 0)),
        ],
        out_specs=pl.BlockSpec((tokens, width), lambda j: (0, j)),
        out_shape=jax.ShapeDtypeStruct((tokens, steps * width), jnp.bfloat16),
        compiler_params=pltpu.CompilerParams(vmem_limit_bytes=48 * 2**20),
        cost_estimate=pl.CostEstimate(
            flops=2 * tokens * depth * weight.shape[1],
            bytes_accessed=2 * depth * weight.shape[1],
            transcendentals=0,
        ),
    )(normed, weight, cos_tables, sin_tables)


def lane_masks(rows):
    lane = lax.broadcasted_iota(jnp.int32, (rows, 128), 1)
    low_side = (lane < 64).astype(jnp.float32)
    return low_side.astype(jnp.bfloat16), (1.0 - low_side).astype(jnp.bfloat16)


def swapped(kv):
    return pltpu.roll(kv.astype(jnp.float32), 64, 1).astype(jnp.bfloat16)


def attend_kernel(group, q_ref, kv_ref, bias_ref, o_ref, log_ref):
    kv = kv_ref[0]
    sides = (kv, swapped(kv))
    rows = q_ref.shape[0]
    masks = lane_masks(rows)
    lane = lax.broadcasted_iota(jnp.int32, (rows, 128), 1)
    logs = jnp.zeros((rows, 128), jnp.float32)
    bias = bias_ref[0]
    for pair in range(group // 2):
        cols = slice(pair * 128, pair * 128 + 128)
        q = q_ref[:, cols]
        found = []
        for half in range(2):
            scores = dot_t(q * masks[half], sides[half]) + bias
            top = jnp.max(scores, -1, keepdims=True)
            powers = jnp.exp(scores - top)
            total = jnp.sum(powers, -1, keepdims=True)
            probs = (powers * (1.0 / total)).astype(jnp.bfloat16)
            found.append(plain_dot(probs, sides[1 - half]))
            logs = jnp.where(lane == pair * 2 + half, top + jnp.log(total), logs)
        o_ref[:, cols] = jnp.where(lane < 64, found[0], found[1]).astype(jnp.bfloat16)
    log_ref[...] = logs


def attend(projected, both_all, bias, kv_heads, group):
    batches, length, _ = both_all.shape
    rows = projected.shape[0] // batches
    wide = group * HD
    return pl.pallas_call(
        functools.partial(attend_kernel, group),
        grid=(batches, kv_heads),
        in_specs=[
            pl.BlockSpec((rows, wide), lambda b, h: (b, h)),
            pl.BlockSpec((1, length, 128), lambda b, h: (b, 0, h)),
            pl.BlockSpec((1, rows, length), lambda b, h: (b, 0, 0)),
        ],
        out_specs=[
            pl.BlockSpec((rows, wide), lambda b, h: (b, h)),
            pl.BlockSpec((rows, 128), lambda b, h: (b, h)),
        ],
        out_shape=[
            jax.ShapeDtypeStruct((batches * rows, kv_heads * wide), jnp.bfloat16),
            jax.ShapeDtypeStruct((batches * rows, kv_heads * 128), jnp.float32),
        ],
        compiler_params=pltpu.CompilerParams(vmem_limit_bytes=48 * 2**20),
    )(projected, both_all, bias)


def attend_back_kernel(
    group, q_ref, do_ref, kv_ref, bias_ref, log_ref, cos_ref, sin_ref, dq_ref, dkv_ref
):
    kv = kv_ref[0]
    sides = (kv, swapped(kv))
    rows = q_ref.shape[0]
    length = kv.shape[0]
    masks = lane_masks(rows)
    lane = lax.broadcasted_iota(jnp.int32, (rows, 128), 1)
    bias = bias_ref[0]
    key_sum = jnp.zeros((128, length), jnp.float32)
    value_sum = jnp.zeros((128, length), jnp.float32)
    for pair in range(group // 2):
        cols = slice(pair * 128, pair * 128 + 128)
        q = q_ref[:, cols]
        do = do_ref[:, cols]
        found = []
        for half in range(2):
            q_half = q * masks[half]
            do_half = do * masks[half]
            at = pair * 2 + half
            log_total = log_ref[:, at : at + 1]
            probs = jnp.exp(dot_t(q_half, sides[half]) + bias - log_total)
            grad_probs = dot_t(do_half, sides[1 - half])
            row_dot = jnp.sum(probs * grad_probs, -1, keepdims=True)
            grad_scores = (probs * (grad_probs - row_dot)).astype(jnp.bfloat16)
            found.append(plain_dot(grad_scores, sides[half]))
            key_sum = key_sum + left_dot(q_half, grad_scores)
            value_sum = value_sum + left_dot(do_half, probs.astype(jnp.bfloat16))
        dq = jnp.where(lane < 64, found[0], found[1])
        dq = dq * cos_ref[0] - swap_halves(dq) * sin_ref[0]
        dq_ref[:, cols] = dq.astype(jnp.bfloat16)
    both = jnp.concatenate(
        [key_sum[:64] + key_sum[64:], value_sum[:64] + value_sum[64:]], 0
    )
    dkv_ref[0] = both.T.astype(jnp.bfloat16)


def attend_back(projected, grad_attended, both_all, bias, logs, cos_tables, sin_tables, group):
    batches, length, _ = both_all.shape
    rows = projected.shape[0] // batches
    wide = group * HD
    kv_heads = both_all.shape[2] // 128
    return pl.pallas_call(
        functools.partial(attend_back_kernel, group),
        grid=(batches, kv_heads),
        in_specs=[
            pl.BlockSpec((rows, wide), lambda b, h: (b, h)),
            pl.BlockSpec((rows, wide), lambda b, h: (b, h)),
            pl.BlockSpec((1, length, 128), lambda b, h: (b, 0, h)),
            pl.BlockSpec((1, rows, length), lambda b, h: (b, 0, 0)),
            pl.BlockSpec((rows, 128), lambda b, h: (b, h)),
            pl.BlockSpec((1, rows, 128), lambda b, h: (0, b, 0)),
            pl.BlockSpec((1, rows, 128), lambda b, h: (0, b, 0)),
        ],
        out_specs=[
            pl.BlockSpec((rows, wide), lambda b, h: (b, h)),
            pl.BlockSpec((1, length, 128), lambda b, h: (b, 0, h)),
        ],
        out_shape=[
            jax.ShapeDtypeStruct((batches * rows, kv_heads * wide), jnp.bfloat16),
            jax.ShapeDtypeStruct((batches, length, kv_heads * 128), jnp.bfloat16),
        ],
        compiler_params=pltpu.CompilerParams(vmem_limit_bytes=48 * 2**20),
    )(projected, grad_attended, both_all, bias, logs, cos_tables, sin_tables)


def half_of(full):
    return full.astype(jnp.bfloat16)


def on_device(
    inputs,
    positions,
    cotangent,
    attn_gain,
    w_query,
    key_matrix,
    value_matrix,
    w_out,
    mlp_gain,
    w_gate,
    w_up,
    w_down,
):
    batches, _, rows, width = inputs.shape
    shard = w_query.shape[0]
    query_features = w_query.shape[1]
    key_features = key_matrix.shape[1]
    kv_heads = key_features // HD
    group = query_features // key_features
    tokens = batches * rows
    length = rows * lax.axis_size("fsdp")
    first_row = lax.axis_index("fsdp") * rows
    query_index = first_row + jnp.arange(rows, dtype=jnp.int32)
    key_index = jnp.arange(length, dtype=jnp.int32)
    score_scale = HD ** (-0.5)

    extras = jnp.zeros((shard, 128), jnp.bfloat16)
    extras = extras.at[:, 0].set(attn_gain).at[:, 1].set(mlp_gain)
    pairs = jnp.concatenate(
        [key_matrix.reshape(shard, kv_heads, HD), value_matrix.reshape(shard, kv_heads, HD)], -1
    )
    first_shard = jnp.concatenate([w_query, pairs.reshape(shard, -1), extras], axis=1)
    fulls = gather(
        (first_shard, w_out, w_gate, w_up, w_down), ("yxc", "xyc", "yxc", "xyc", "yxc"), 1, 5
    )
    first_pack, out_full, gate_full, up_full, down_full = (
        f.reshape(-1, f.shape[-1]) for f in fulls
    )
    used = query_features + 2 * key_features
    projection = first_pack[:, :used]
    gains = first_pack[:, used : used + 2].astype(jnp.float32).T

    x_float = inputs.reshape(tokens, width).astype(jnp.float32)
    places = positions.reshape(batches, rows)
    cos_table, sin_table = rope_tables(places.reshape(tokens))
    ones, zeros = jnp.ones((tokens, HD), jnp.float32), jnp.zeros((tokens, HD), jnp.float32)
    cos_pair = jnp.concatenate([cos_table, cos_table], -1)
    sin_pair = jnp.concatenate([-sin_table, sin_table], -1)
    cos_tables = jnp.stack(
        [
            jnp.concatenate([cos_pair, cos_pair], -1) * score_scale,
            jnp.concatenate([cos_pair, ones], -1),
        ]
    )
    sin_tables = jnp.stack(
        [
            jnp.concatenate([sin_pair, sin_pair], -1) * score_scale,
            jnp.concatenate([sin_pair, zeros], -1),
        ]
    )
    doc_start = query_index[None, :] - places
    allowed = (key_index[None, None, :] <= query_index[None, :, None]) & (
        key_index[None, None, :] >= doc_start[:, :, None]
    )
    bias = jnp.where(allowed, 0.0, NEGATIVE)
    attn_inverse = lax.rsqrt(jnp.mean(x_float * x_float, -1, keepdims=True) + EPSILON)
    attn_gain_f = gains[0]
    mlp_gain_f = gains[1]
    normed = (x_float * attn_inverse * attn_gain_f).astype(jnp.bfloat16)
    projected = project(normed, projection, cos_tables, sin_tables, 2 * key_features)
    both_rows = projected[:, query_features:].reshape(batches, rows, -1)
    both_all = lax.all_gather(both_rows, "fsdp", axis=1, tiled=True)
    attended, logs = attend(projected, both_all, bias, kv_heads, group)

    mixed = x_float + plain_dot(attended, out_full)
    mlp_inverse = lax.rsqrt(jnp.mean(mixed * mixed, -1, keepdims=True) + EPSILON)
    normed_mlp = (mixed * mlp_inverse * mlp_gain_f).astype(jnp.bfloat16)
    gate_pre = plain_dot(normed_mlp, gate_full)
    up_proj = plain_dot(normed_mlp, up_full)
    gate_sig = jax.nn.sigmoid(gate_pre)
    hidden = (gate_pre * gate_sig * up_proj).astype(jnp.bfloat16)
    output = (mixed + plain_dot(hidden, down_full)).astype(jnp.bfloat16)

    cot_low = cotangent.reshape(tokens, width)
    cot_float = cot_low.astype(jnp.float32)
    grad_down = half_of(left_dot(hidden, cot_low))
    grad_hidden = right_dot(cot_low, down_full)
    sig_slope = gate_sig * (1.0 + gate_pre * (1.0 - gate_sig))
    grad_gate_pre = (grad_hidden * up_proj * sig_slope).astype(jnp.bfloat16)
    grad_up_pre = (grad_hidden * gate_pre * gate_sig).astype(jnp.bfloat16)
    grad_gate = half_of(left_dot(normed_mlp, grad_gate_pre))
    grad_up = half_of(left_dot(normed_mlp, grad_up_pre))
    grad_normed_mlp = right_dot(grad_gate_pre, gate_full) + right_dot(grad_up_pre, up_full)
    grad_mlp_gain = jnp.sum(grad_normed_mlp * mixed * mlp_inverse, 0)
    grad_mixed = cot_float + norm_back(grad_normed_mlp * mlp_gain_f, mixed, mlp_inverse)
    grad_mixed_low = grad_mixed.astype(jnp.bfloat16)
    grad_out = half_of(left_dot(attended, grad_mixed_low))
    grad_attended = right_dot(grad_mixed_low, out_full).astype(jnp.bfloat16)
    grad_query_pre, portions = attend_back(
        projected, grad_attended, both_all, bias, logs, cos_tables, sin_tables, group
    )
    sums = lax.psum_scatter(portions, "fsdp", scatter_dimension=1, tiled=True)
    sums = sums.astype(jnp.float32).reshape(tokens, kv_heads, 128)
    turned = jnp.concatenate([sums[..., 32:64], sums[..., :32], sums[..., 64:]], -1)
    grad_pair_pre = (sums * cos_tables[1][:, None] - turned * sin_tables[1][:, None]).astype(
        jnp.bfloat16
    )
    grad_pre = jnp.concatenate(
        [grad_query_pre, grad_pair_pre.reshape(tokens, 2 * key_features)], -1
    )
    grad_projection = left_dot(normed, grad_pre)
    grad_normed = right_dot(grad_pre, projection)
    grad_attn_gain = jnp.sum(grad_normed * x_float * attn_inverse, 0)
    grad_input = grad_mixed + norm_back(grad_normed * attn_gain_f, x_float, attn_inverse)
    gain_columns = jnp.stack([grad_attn_gain, grad_mlp_gain], -1)
    gain_columns = jnp.pad(gain_columns, ((0, 0), (0, 126)))
    grad_first = half_of(jnp.concatenate([grad_projection, gain_columns], 1))
    grad_down, grad_gate, grad_up, grad_out, last = scatter(
        (grad_down, grad_gate, grad_up, grad_out, grad_first), ("xy", "yx", "xy", "yx", "xy"), 2
    )
    last_pairs = last[:, query_features:used].reshape(shard, kv_heads, 2, HD)
    return (
        output.reshape(inputs.shape),
        grad_input.astype(jnp.bfloat16).reshape(inputs.shape),
        last[:, used],
        last[:, :query_features],
        last_pairs[:, :, 0].reshape(shard, key_features),
        last_pairs[:, :, 1].reshape(shard, key_features),
        grad_out,
        last[:, used + 1],
        grad_gate,
        grad_up,
        grad_down,
    )


def solution(mesh):
    tokens = P(None, "dp", "fsdp", None)
    vector = P(BOTH)
    matrix = P(BOTH, None)
    weights = (vector, matrix, matrix, matrix, matrix, vector, matrix, matrix, matrix)
    return jax.shard_map(
        on_device,
        mesh=mesh,
        in_specs=(tokens, P(None, "dp", "fsdp"), tokens) + weights,
        out_specs=(tokens, tokens) + weights,
        check_vma=False,
    )
```

```python
import functools

import jax
import jax.numpy as jnp
from jax import lax
from jax.experimental import pallas as pl
from jax.experimental.pallas import tpu as pltpu
from jax.sharding import PartitionSpec as P

HD = 64
EPSILON = 1e-05
NEGATIVE = -1e30
ROPE_BASE = 10000.0
BOTH = ("dp", "fsdp")


def rope_tables(places):
    half = HD // 2
    freqs = ROPE_BASE ** (-jnp.arange(half).astype(jnp.float32) / half)
    angles = places.astype(jnp.float32)[:, None] * freqs[None, :]
    return (jnp.cos(angles), jnp.sin(angles))


def plain_dot(left, right):
    return jnp.dot(left, right, preferred_element_type=jnp.float32)


def left_dot(left, right):
    return lax.dot_general(
        left, right, (((0,), (0,)), ((), ())), preferred_element_type=jnp.float32
    )


def right_dot(left, right):
    return lax.dot_general(
        left, right, (((1,), (1,)), ((), ())), preferred_element_type=jnp.float32
    )


def norm_back(grad_normed, inputs_float, inverse):
    return inverse * (
        grad_normed
        - inputs_float * inverse * inverse * jnp.mean(grad_normed * inputs_float, -1, keepdims=True)
    )


class Place:
    def __init__(self):
        self.Z=lax.axis_size("dp")//2; self.X=lax.axis_size("fsdp")//2
        dp=lax.axis_index("dp"); fs=lax.axis_index("fsdp")
        self.z=dp//2; self.y=dp%2; self.x=fs//2; self.c=fs%2
    def device(self,s=0,dy=0,dx=0,dc=0):
        return (lax.rem(self.z+s,self.Z)*2+lax.rem(self.y+dy,2), lax.rem(self.x+dx,self.X)*2+lax.rem(self.c+dc,2))
    def slot(self,s,dy,dx,dc):
        return ((lax.rem(self.z+self.Z-s,self.Z)*2+lax.rem(self.y+dy,2))*self.X+lax.rem(self.x+dx,self.X))*2+lax.rem(self.c+dc,2)

MESH = pl.DeviceIdType.MESH

def greet(me):
    barrier=pltpu.get_barrier_semaphore()
    friends=[me.device(s=s) for s in range(1,me.Z)]+[me.device(dy=1),me.device(dx=1),me.device(dc=1)]
    for f in friends:
        pl.semaphore_signal(barrier,inc=1,device_id=f,device_id_type=MESH)
    pl.semaphore_wait(barrier,len(friends))

def gather_kernel(Z, orders, ahead, *refs):
    K=len(orders)
    shards=refs[:K]; outs=refs[K:2*K]; local,send,recv=refs[2*K:]
    me=Place()
    greet(me)
    dims={"y":1,"x":2,"c":3}
    def sem(rel):
        return ((rel[0]*2+rel[1])*2+rel[2])*2+rel[3]
    started=[]
    def start(k,rel,to):
        if isinstance(to,int):
            target=me.device(s=to); landed=(to,0,0,0)
        else:
            landed=list(rel); landed[dims[to]]=1; landed=tuple(landed)
            target=me.device(**{"d"+to:1})
        slot=me.slot(*rel)
        src=shards[k] if rel==(0,0,0,0) else outs[k].at[slot]
        cp=pltpu.make_async_remote_copy(src_ref=src,dst_ref=outs[k].at[slot],send_sem=send.at[k,sem(landed)],recv_sem=recv.at[k,sem(landed)],device_id=target,device_id_type=MESH)
        cp.start()
        table[(k,landed)]=cp
    table={}
    own=[]
    def first(k):
        cp=pltpu.make_async_copy(shards[k],outs[k].at[me.slot(0,0,0,0)],local.at[k]); cp.start(); own.append(cp)
        for s in range(1,Z): start(k,(0,0,0,0),s)
        for d in orders[k]: start(k,(0,0,0,0),d)
    def arrive(k,rel,rest):
        table[(k,rel)].wait_recv()
        for d in rest: start(k,rel,d)
    def rel_of(s,o,a,b=0,c=0):
        r=[s,0,0,0]; r[dims[o[0]]]=a; r[dims[o[1]]]=b; r[dims[o[2]]]=c
        return tuple(r)
    for k in range(min(ahead,K)): first(k)
    for t in range(K+3):
        if t+ahead<K: first(t+ahead)
        k=t
        if k<K:
            o=orders[k]
            for s in range(1,Z): arrive(k,rel_of(s,o,0),o)
        k=t-1
        if 0<=k<K:
            o=orders[k]
            for s in range(Z): arrive(k,rel_of(s,o,1),o[1:])
        k=t-2
        if 0<=k<K:
            o=orders[k]
            for s in range(Z):
                for a in range(2): arrive(k,rel_of(s,o,a,1),o[2:])
        k=t-3
        if 0<=k<K:
            o=orders[k]
            for s in range(Z):
                for a in range(2):
                    for b in range(2): arrive(k,rel_of(s,o,a,b,1),"")
    for cp in own: cp.wait()
    for cp in table.values(): cp.wait_send()

def gather(shards, orders, cid, ahead=2):
    n=lax.axis_size("dp")*lax.axis_size("fsdp"); Z=lax.axis_size("dp")//2; K=len(shards)
    return pl.pallas_call(functools.partial(gather_kernel,Z,orders,ahead),
        out_shape=[jax.ShapeDtypeStruct((n,)+s.shape,s.dtype) for s in shards],
        in_specs=[pl.BlockSpec(memory_space=pl.ANY)]*K,
        out_specs=[pl.BlockSpec(memory_space=pl.ANY)]*K,
        scratch_shapes=[pltpu.SemaphoreType.DMA((K,)),pltpu.SemaphoreType.DMA((K,8*Z)),pltpu.SemaphoreType.DMA((K,8*Z))],
        compiler_params=pltpu.CompilerParams(collective_id=cid,has_side_effects=True))(*shards)


class Gathering:
    def __init__(self, me, chunks, local, send, recv):
        self.me, self.chunks = me, chunks
        self.local, self.send, self.recv = local, send, recv
        self.table, self.own = {}, []

    def start(self, k, rel, to):
        shard, full, cols, _ = self.chunks[k]
        me = self.me
        if isinstance(to, int):
            target, landed = me.device(s=to), (to, 0, 0, 0)
        else:
            landed = list(rel)
            landed["zyxc".index(to)] = 1
            landed = tuple(landed)
            target = me.device(**{"d" + to: 1})
        slot = me.slot(*rel)
        here = full.at[slot, :, cols]
        at = ((landed[0] * 2 + landed[1]) * 2 + landed[2]) * 2 + landed[3]
        copy = pltpu.make_async_remote_copy(
            src_ref=shard.at[:, cols] if rel == (0, 0, 0, 0) else here,
            dst_ref=here,
            send_sem=self.send.at[k, at],
            recv_sem=self.recv.at[k, at],
            device_id=target,
            device_id_type=MESH,
        )
        copy.start()
        self.table[(k, landed)] = copy

    def begin(self, k):
        shard, full, cols, order = self.chunks[k]
        copy = pltpu.make_async_copy(
            shard.at[:, cols], full.at[self.me.slot(0, 0, 0, 0), :, cols], self.local.at[k]
        )
        copy.start()
        self.own.append((k, copy))
        for s in range(1, self.me.Z):
            self.start(k, (0, 0, 0, 0), s)
        for d in order:
            self.start(k, (0, 0, 0, 0), d)

    def step(self, k, stage):
        order = self.chunks[k][3]
        where = ["zyxc".index(d) for d in order]
        for s in range(1 if stage == 0 else 0, self.me.Z):
            for bits in range(1 << max(stage - 1, 0)):
                rel = [s, 0, 0, 0]
                for i in range(stage - 1):
                    rel[where[i]] = bits >> i & 1
                if stage:
                    rel[where[stage - 1]] = 1
                rel = tuple(rel)
                self.table[(k, rel)].wait_recv()
                for d in order[stage:]:
                    self.start(k, rel, d)
        if stage == 3:
            for at, copy in self.own:
                if at == k:
                    copy.wait()

    def finish(self):
        for copy in self.table.values():
            copy.wait_send()


def forward_kernel(sizes, *refs):
    batches, rows, kv_heads, group, used = sizes
    (first_s, out_s, gate_s, up_s, down_s, x_ref, place_ref, freq_ref) = refs[:8]
    (first_w, out_w, gate_w, up_w, down_w, q_out, kv_out, o_out, log_out) = refs[8:17]
    (mixed_out, h2_out, hidden_out, slope_out, silu_out, bias_out, cos_out, sin_out) = refs[17:25]
    (raw_a, raw_b, w_a, w_b, normed, queries, kv_all, attended, logs, mixed, h2) = refs[25:36]
    (hidden, slope, silu, bias, cos_t, sin_t, gains) = refs[36:43]
    (local, send, recv, kv_send, kv_recv, load_sem, store_sem) = refs[43:]
    me = Place()
    greet(me)
    whole = slice(None)
    half = down_w.shape[2] // 2
    comm = Gathering(
        me,
        (
            (first_s, first_w, whole, "yxc"),
            (out_s, out_w, whole, "xyc"),
            (gate_s, gate_w, whole, "yxc"),
            (up_s, up_w, whole, "xyc"),
            (down_s, down_w, pl.ds(0, half), "yxc"),
            (down_s, down_w, pl.ds(half, half), "xyc"),
        ),
        local,
        send,
        recv,
    )
    tokens, width = x_ref.shape
    length = kv_all.shape[1]
    stores = []

    def store(i, src, dst):
        copy = pltpu.make_async_copy(src, dst, store_sem.at[i])
        copy.start()
        stores.append(copy)

    def over_rows(body, step=64):
        def one(i, carry):
            body(pl.ds(pl.multiple_of(i * step, step), step))
            return carry

        lax.fori_loop(0, tokens // step, one, 0)

    def load(full, raw, col, size, i):
        return pltpu.make_async_copy(
            full.at[:, :, pl.ds(col, size)], raw.at[:, :, pl.ds(0, size)], load_sem.at[i]
        )

    def assemble(raw, flat, size):
        n, r, _ = raw.shape
        pair = 2 * r

        def one(i, carry):
            piece = raw[pl.ds(2 * i, 2), :, pl.ds(0, size)].astype(jnp.float32)
            flat[pl.ds(pl.multiple_of(pair * i, 16), pair), pl.ds(0, size)] = piece.reshape(
                pair, size
            ).astype(jnp.bfloat16)
            return carry

        lax.fori_loop(0, n // 2, one, 0)

    comm.begin(0)
    comm.begin(1)

    scale = HD**-0.5
    lane = lax.broadcasted_iota(jnp.int32, (64, 128), 1)
    second = lax.rem(lane, HD) >= HD // 2
    is_value = lane >= HD

    def tables(at):
        angle = place_ref[at, :].astype(jnp.float32) * freq_ref[...]
        c, s = jnp.cos(angle), jnp.sin(angle)
        s = jnp.where(second, s, -s)
        cos_t[0, at, :] = c * scale
        sin_t[0, at, :] = s * scale
        cos_t[1, at, :] = jnp.where(is_value, 1.0, c)
        sin_t[1, at, :] = jnp.where(is_value, 0.0, s)

    over_rows(tables)
    first_row = lax.axis_index("fsdp") * rows

    def masks(at):
        token = at.start
        inside = lax.rem(token, rows)
        query = first_row + inside + lax.broadcasted_iota(jnp.int32, (64, length), 0)
        key = lax.broadcasted_iota(jnp.int32, (64, length), 1)
        start = query - place_ref[at, :]
        allowed = (key <= query) & (key >= start)
        bias[at, :] = jnp.where(allowed, 0.0, NEGATIVE)

    over_rows(masks)
    store(0, bias, bias_out)
    store(1, cos_t, cos_out)
    store(2, sin_t, sin_out)

    comm.step(0, 0)
    comm.begin(2)
    comm.step(1, 0)
    comm.step(0, 1)
    comm.step(1, 1)
    comm.step(0, 2)
    comm.begin(3)
    comm.step(1, 2)
    comm.step(0, 3)

    tile = raw_a.shape[2]
    load(first_w, raw_a, used, 128, 0).start()
    load(first_w, raw_b, 0, tile, 1).start()
    load(first_w, raw_a, used, 128, 0).wait()
    assemble(raw_a, w_a, 128)
    gains[...] = w_a[:, :128].astype(jnp.float32).T[:8]
    load(first_w, raw_a, used - tile, tile, 0).start()

    def norm_one(at):
        x = x_ref[at, :].astype(jnp.float32)
        inverse = lax.rsqrt(jnp.mean(x * x, -1, keepdims=True) + EPSILON)
        normed[at, :] = (x * inverse * gains[0:1, :]).astype(jnp.bfloat16)

    over_rows(norm_one)

    def turn(flat, kind, put, step=128):
        def body(at):
            u = plain_dot(normed[at, :], flat[...])
            for j in range(tile // 128):
                piece = u[:, j * 128 : (j + 1) * 128]
                piece = piece * cos_t[kind, at, :] + swap_halves(piece) * sin_t[kind, at, :]
                put(at, j, piece.astype(jnp.bfloat16))

        over_rows(body, step)

    slot = (me.x * 2 + me.c) * rows

    def put_pair(at, j, piece):
        token = at.start
        b = token // rows
        row = pl.multiple_of(slot + lax.rem(token, rows), 128)
        kv_all[b, pl.ds(row, 128), j * 128 : (j + 1) * 128] = piece

    load(first_w, raw_a, used - tile, tile, 0).wait()
    assemble(raw_a, w_a, tile)
    turn(w_a, 1, put_pair)

    def share(i, dx, to):
        row = (lax.rem(me.x + dx, 2) * 2 + me.c) * rows
        block = kv_all.at[:, pl.ds(pl.multiple_of(row, 256), rows), :]
        copy = pltpu.make_async_remote_copy(
            src_ref=block,
            dst_ref=block,
            send_sem=kv_send.at[i],
            recv_sem=kv_recv.at[i],
            device_id=me.device(**{"d" + to: 1}),
            device_id_type=MESH,
        )
        copy.start()
        return copy

    to_x = share(0, 0, "x")
    to_c = share(1, 0, "c")
    for j in range(queries.shape[1] // tile):
        raw, flat = ((raw_b, w_b), (raw_a, w_a))[j % 2]
        if (j + 1) * tile < queries.shape[1]:
            load(first_w, (raw_a, raw_b)[j % 2], (j + 1) * tile, tile, j % 2).start()
        load(first_w, raw, j * tile, tile, 1 - j % 2).wait()
        assemble(raw, flat, tile)

        def put_query(at, i, piece, j=j):
            queries[at, j * tile + i * 128 : j * tile + (i + 1) * 128] = piece

        turn(flat, 0, put_query)
    store(3, queries, q_out)
    comm.step(2, 0)
    comm.step(1, 3)
    comm.begin(4)
    comm.step(3, 0)
    comm.step(2, 1)
    to_x.wait_recv()
    to_far = share(2, 1, "c")
    to_c.wait_recv()
    to_far.wait_recv()
    store(4, kv_all, kv_out)

    lanes = lax.broadcasted_iota(jnp.int32, (rows, 128), 1)
    sides_mask = lane_masks(rows)

    def head(i, carry):
        b = i // kv_heads
        h = lax.rem(i, kv_heads)
        at = pl.ds(pl.multiple_of(b * rows, 256), rows)
        kv = kv_all[b, :, pl.ds(pl.multiple_of(h * 128, 128), 128)]
        sides = (kv, swapped(kv))
        shift = bias[at, :]
        log_piece = jnp.zeros((rows, 128), jnp.float32)
        for pair in range(group // 2):
            cols = pl.ds(pl.multiple_of(h * group * HD + pair * 128, 128), 128)
            q = queries[at, cols]
            found = []
            for side in range(2):
                scores = dot_t(q * sides_mask[side], sides[side]) + shift
                top = jnp.max(scores, -1, keepdims=True)
                powers = jnp.exp(scores - top)
                total = jnp.sum(powers, -1, keepdims=True)
                probs = (powers * (1.0 / total)).astype(jnp.bfloat16)
                found.append(plain_dot(probs, sides[1 - side]))
                log_piece = jnp.where(
                    lanes == pair * 2 + side, top + jnp.log(total), log_piece
                )
            attended[at, cols] = jnp.where(lanes < HD, found[0], found[1]).astype(jnp.bfloat16)
        logs[at, pl.ds(pl.multiple_of(h * 128, 128), 128)] = log_piece
        return carry

    count = batches * kv_heads
    pumps = [(3, 1), (2, 2), (4, 0), (3, 2)]
    done = 0
    for i in range(5):
        upto = count * (i + 1) // 5
        lax.fori_loop(done, upto, head, 0)
        done = upto
        if i == 0:
            comm.begin(5)
        if i < len(pumps):
            comm.step(*pumps[i])
    store(5, attended, o_out)
    store(6, logs, log_out)

    steps = width // tile
    load(out_w, raw_a, 0, tile, 0).start()
    for j in range(steps):
        raw, flat = ((raw_a, w_a), (raw_b, w_b))[j % 2]
        if j + 1 < steps:
            load(out_w, (raw_b, raw_a)[j % 2], (j + 1) * tile, tile, 1 - j % 2).start()
        load(out_w, raw, j * tile, tile, j % 2).wait()
        assemble(raw, flat, tile)

        def add_in(at, flat=flat, j=j):
            cols = slice(j * tile, (j + 1) * tile)
            mixed[at, cols] = x_ref[at, cols].astype(jnp.float32) + plain_dot(
                attended[at, :], flat[...]
            )

        over_rows(add_in, 128)

    def norm_two(at):
        y = mixed[at, :]
        inverse = lax.rsqrt(jnp.mean(y * y, -1, keepdims=True) + EPSILON)
        h2[at, :] = (y * inverse * gains[1:2, :]).astype(jnp.bfloat16)

    over_rows(norm_two)
    store(7, mixed, mixed_out)
    store(8, h2, h2_out)

    comm.step(5, 0)
    comm.step(4, 1)
    comm.step(2, 3)
    comm.step(3, 3)

    wide = 512
    features = hidden.shape[1]
    pumps = {1: (5, 1), 3: (4, 2), 5: (5, 2)}
    load(gate_w, raw_a, 0, wide, 0).start()
    load(up_w, raw_b, 0, wide, 1).start()
    for j in range(features // wide):
        load(gate_w, raw_a, j * wide, wide, 0).wait()
        assemble(raw_a, w_a, wide)
        load(up_w, raw_b, j * wide, wide, 1).wait()
        assemble(raw_b, w_b, wide)
        if (j + 1) * wide < features:
            load(gate_w, raw_a, (j + 1) * wide, wide, 0).start()
            load(up_w, raw_b, (j + 1) * wide, wide, 1).start()

        def units(at, j=j):
            cols = slice(j * wide, (j + 1) * wide)
            g = plain_dot(h2[at, :], w_a[:, :wide])
            u = plain_dot(h2[at, :], w_b[:, :wide])
            sig = jax.nn.sigmoid(g)
            soft = g * sig
            hidden[at, cols] = (soft * u).astype(jnp.bfloat16)
            silu[at, cols] = soft.astype(jnp.bfloat16)
            slope[at, cols] = (u * (sig * (1.0 + g * (1.0 - sig)))).astype(jnp.bfloat16)

        over_rows(units, 128)
        if j in pumps:
            comm.step(*pumps[j])
    store(9, hidden, hidden_out)
    store(10, silu, silu_out)
    store(11, slope, slope_out)
    comm.step(4, 3)
    comm.step(5, 3)
    for copy in (to_x, to_c, to_far):
        copy.wait_send()
    comm.finish()
    for copy in stores:
        copy.wait()


def forward(shards, x, places, kv_heads, group, batches):
    first_s, out_s, gate_s, up_s, down_s = shards
    n = lax.axis_size("dp") * lax.axis_size("fsdp")
    Z = lax.axis_size("dp") // 2
    tokens, width = x.shape
    rows = tokens // batches
    length = rows * lax.axis_size("fsdp")
    key_wide = kv_heads * 128
    query_wide = kv_heads * group * HD
    used = query_wide + key_wide
    features = gate_s.shape[1]
    r = first_s.shape[0]
    freqs = ROPE_BASE ** (-jnp.arange(HD // 2).astype(jnp.float32) / (HD // 2))
    freqs = jnp.tile(freqs, 4)[None]
    bf, f32 = jnp.bfloat16, jnp.float32
    shape = jax.ShapeDtypeStruct
    outs = [shape((n,) + s.shape, s.dtype) for s in shards] + [
        shape((tokens, query_wide), bf),
        shape((batches, length, key_wide), bf),
        shape((tokens, query_wide), bf),
        shape((tokens, key_wide), f32),
        shape((tokens, width), f32),
        shape((tokens, width), bf),
        shape((tokens, features), bf),
        shape((tokens, features), bf),
        shape((tokens, features), bf),
        shape((tokens, length), f32),
        shape((2, tokens, 128), f32),
        shape((2, tokens, 128), f32),
    ]
    vmem = pltpu.VMEM
    scratch = [
        vmem((n, r, key_wide), bf),
        vmem((n, r, key_wide), bf),
        vmem((width, key_wide), bf),
        vmem((width, key_wide), bf),
        vmem((tokens, width), bf),
        vmem((tokens, query_wide), bf),
        vmem((batches, length, key_wide), bf),
        vmem((tokens, query_wide), bf),
        vmem((tokens, key_wide), f32),
        vmem((tokens, width), f32),
        vmem((tokens, width), bf),
        vmem((tokens, features), bf),
        vmem((tokens, features), bf),
        vmem((tokens, features), bf),
        vmem((tokens, length), f32),
        vmem((2, tokens, 128), f32),
        vmem((2, tokens, 128), f32),
        vmem((8, width), f32),
        pltpu.SemaphoreType.DMA((6,)),
        pltpu.SemaphoreType.DMA((6, 8 * Z)),
        pltpu.SemaphoreType.DMA((6, 8 * Z)),
        pltpu.SemaphoreType.DMA((3,)),
        pltpu.SemaphoreType.DMA((3,)),
        pltpu.SemaphoreType.DMA((2,)),
        pltpu.SemaphoreType.DMA((12,)),
    ]
    any_space = pl.BlockSpec(memory_space=pl.ANY)
    in_vmem = pl.BlockSpec(memory_space=pltpu.VMEM)
    return pl.pallas_call(
        functools.partial(forward_kernel, (batches, rows, kv_heads, group, used)),
        out_shape=outs,
        in_specs=[any_space] * 5 + [in_vmem] * 3,
        out_specs=[any_space] * len(outs),
        scratch_shapes=scratch,
        compiler_params=pltpu.CompilerParams(
            collective_id=1, has_side_effects=True, vmem_limit_bytes=63 * 2**20
        ),
        cost_estimate=pl.CostEstimate(
            flops=2 * tokens * width * (used + width + 2 * features),
            bytes_accessed=4 * n * r * (used + width + 3 * features),
            transcendentals=tokens * features,
        ),
    )(*shards, x, places, freqs)


def tile_of(N):
    for t in (512,384,256,128):
        if N%t==0: return t
    return N

def scatter_kernel(Z, orders, ahead, dims_, *refs):
    K=len(orders)
    parts=refs[:K]; outs=refs[K:2*K]
    sc=refs[2*K:]
    first_buf=sc[:K]; one_buf=sc[K:2*K]; two_buf=sc[2*K:3*K]; last_buf=sc[3*K:4*K]
    shapes=sorted(set(dims_))
    stage=[sc[4*K+shapes.index(d)] for d in dims_]
    local,send,recv=sc[4*K+len(shapes):]
    me=Place()
    greet(me)
    copies={}
    def ship(k,name,index,src,dst,target):
        cp=pltpu.make_async_remote_copy(src_ref=src,dst_ref=dst,send_sem=send.at[k,index],recv_sem=recv.at[k,index],device_id=target,device_id_type=MESH)
        cp.start(); copies[(k,name)]=cp
    def part(k,a,b,other):
        o=orders[k]
        rel={o[0]:a,o[1]:b}
        y=lax.rem(me.y+rel["y"],2); x=lax.rem(me.x+rel["x"],me.X); c=lax.rem(me.c+other,2)
        return parts[k].at[:,y,x,c]
    order4=((1,1),(1,0),(0,1),(0,0))
    locals_={}
    def first(k):
        for i,(a,b) in enumerate(order4):
            ship(k,("c",a,b),i,part(k,a,b,1),first_buf[k].at[a,b],me.device(dc=1))
    def bring(k,i):
        a,b=order4[i]
        cp=pltpu.make_async_copy(part(k,a,b,0),stage[k].at[i%2],local.at[k,i%2]); cp.start(); locals_[(k,i)]=cp
    def add(dst,src,k):
        _,r,N=dims_[k]
        t=tile_of(N)
        def body(i,_):
            zi=i//(N//t); j=i%(N//t)
            cols=pl.ds(pl.multiple_of(j*t,128),t)
            dst[zi,:,cols]=dst[zi,:,cols]+src[zi,:,cols]
            return 0
        lax.fori_loop(0,Z*(N//t),body,0)
    def step_c(k):
        bring(k,0); bring(k,1)
        for i,(a,b) in enumerate(order4):
            copies[(k,("c",a,b))].wait_recv()
            locals_[(k,i)].wait()
            add(first_buf[k].at[a,b],stage[k].at[i%2],k)
            if i+2<4: bring(k,i+2)
            if a==1:
                ship(k,("1",b),4+b,first_buf[k].at[1,b],one_buf[k].at[b],me.device(**{"d"+orders[k][0]:1}))
    def step_1(k):
        for b in (1,0):
            copies[(k,("1",b))].wait_recv()
            add(first_buf[k].at[0,b],one_buf[k].at[b],k)
            if b==1:
                ship(k,"2",6,first_buf[k].at[0,1],two_buf[k],me.device(**{"d"+orders[k][1]:1}))
    def step_2(k):
        copies[(k,"2")].wait_recv()
        add(first_buf[k].at[0,0],two_buf[k],k)
        for s in range(1,Z):
            ship(k,("z",s),6+s,first_buf[k].at[0,0,lax.rem(me.z+s,Z)],last_buf[k].at[s-1],me.device(s=s))
    def step_z(k):
        _,r,N=dims_[k]
        for s in range(1,Z): copies[(k,("z",s))].wait_recv()
        t=tile_of(N)
        mine=first_buf[k].at[0,0,me.z]
        def body(j,_):
            cols=pl.ds(pl.multiple_of(j*t,128),t)
            total=mine[:,cols].astype(jnp.float32)
            for s in range(1,Z): total=total+last_buf[k][s-1,:,cols].astype(jnp.float32)
            outs[k][:,cols]=total
            return 0
        lax.fori_loop(0,N//t,body,0)
    for k in range(min(ahead,K)): first(k)
    for t in range(K+3):
        if t+ahead<K: first(t+ahead)
        if t<K: step_c(t)
        if 0<=t-1<K: step_1(t-1)
        if 0<=t-2<K: step_2(t-2)
        if 0<=t-3<K: step_z(t-3)
    for cp in copies.values(): cp.wait_send()

def scatter(parts, orders, cid, ahead=2):
    n=lax.axis_size("dp")*lax.axis_size("fsdp"); Z=lax.axis_size("dp")//2; X=lax.axis_size("fsdp")//2; K=len(parts)
    dims_=[(n,p.shape[0]//n,p.shape[1]) for p in parts]
    parts=[p.reshape(Z,2,X,2,p.shape[0]//n,p.shape[1]) for p in parts]
    bf=jnp.bfloat16
    sc=[pltpu.VMEM((2,2,Z,r,N),bf) for _,r,N in dims_]+[pltpu.VMEM((2,Z,r,N),bf) for _,r,N in dims_]+[pltpu.VMEM((Z,r,N),bf) for _,r,N in dims_]+[pltpu.VMEM((Z-1,r,N),bf) for _,r,N in dims_]+[pltpu.VMEM((2,Z,r,N),bf) for _,r,N in sorted(set(dims_))]
    return pl.pallas_call(functools.partial(scatter_kernel,Z,orders,ahead,dims_),
        out_shape=[jax.ShapeDtypeStruct((r,N),jnp.float32) for _,r,N in dims_],
        in_specs=[pl.BlockSpec(memory_space=pl.ANY)]*K,
        out_specs=[pl.BlockSpec(memory_space=pltpu.VMEM)]*K,
        scratch_shapes=sc+[pltpu.SemaphoreType.DMA((K,2)),pltpu.SemaphoreType.DMA((K,6+Z)),pltpu.SemaphoreType.DMA((K,6+Z))],
        compiler_params=pltpu.CompilerParams(collective_id=cid,has_side_effects=True,vmem_limit_bytes=63*2**20))(*parts)


def dot_t(left, right):
    return lax.dot_general(
        left, right, (((1,), (1,)), ((), ())), preferred_element_type=jnp.float32
    )


def swap_halves(u):
    lane = lax.broadcasted_iota(jnp.int32, u.shape, 1)
    down = pltpu.roll(u, 32, 1)
    up = pltpu.roll(u, 96, 1)
    return jnp.where(lax.rem(lane, 64) < 32, up, down)


def project_kernel(h_ref, w_ref, cos_ref, sin_ref, out_ref):
    u = plain_dot(h_ref[...], w_ref[...])
    for j in range(u.shape[1] // 128):
        piece = u[:, j * 128 : (j + 1) * 128]
        turned = piece * cos_ref[0] + swap_halves(piece) * sin_ref[0]
        out_ref[:, j * 128 : (j + 1) * 128] = turned.astype(jnp.bfloat16)


def project(normed, weight, cos_tables, sin_tables, width):
    tokens, depth = normed.shape
    steps = weight.shape[1] // width
    return pl.pallas_call(
        project_kernel,
        grid=(steps,),
        in_specs=[
            pl.BlockSpec((tokens, depth), lambda j: (0, 0)),
            pl.BlockSpec((depth, width), lambda j: (0, j)),
            pl.BlockSpec((1, tokens, 128), lambda j: (j // (steps - 1), 0, 0)),
            pl.BlockSpec((1, tokens, 128), lambda j: (j // (steps - 1), 0, 0)),
        ],
        out_specs=pl.BlockSpec((tokens, width), lambda j: (0, j)),
        out_shape=jax.ShapeDtypeStruct((tokens, steps * width), jnp.bfloat16),
        compiler_params=pltpu.CompilerParams(vmem_limit_bytes=48 * 2**20),
        cost_estimate=pl.CostEstimate(
            flops=2 * tokens * depth * weight.shape[1],
            bytes_accessed=2 * depth * weight.shape[1],
            transcendentals=0,
        ),
    )(normed, weight, cos_tables, sin_tables)


def lane_masks(rows):
    lane = lax.broadcasted_iota(jnp.int32, (rows, 128), 1)
    low_side = (lane < 64).astype(jnp.float32)
    return low_side.astype(jnp.bfloat16), (1.0 - low_side).astype(jnp.bfloat16)


def swapped(kv):
    return pltpu.roll(kv.astype(jnp.float32), 64, 1).astype(jnp.bfloat16)


def attend_kernel(group, q_ref, kv_ref, bias_ref, o_ref, log_ref):
    kv = kv_ref[0]
    sides = (kv, swapped(kv))
    rows = q_ref.shape[0]
    masks = lane_masks(rows)
    lane = lax.broadcasted_iota(jnp.int32, (rows, 128), 1)
    logs = jnp.zeros((rows, 128), jnp.float32)
    bias = bias_ref[0]
    for pair in range(group // 2):
        cols = slice(pair * 128, pair * 128 + 128)
        q = q_ref[:, cols]
        found = []
        for half in range(2):
            scores = dot_t(q * masks[half], sides[half]) + bias
            top = jnp.max(scores, -1, keepdims=True)
            powers = jnp.exp(scores - top)
            total = jnp.sum(powers, -1, keepdims=True)
            probs = (powers * (1.0 / total)).astype(jnp.bfloat16)
            found.append(plain_dot(probs, sides[1 - half]))
            logs = jnp.where(lane == pair * 2 + half, top + jnp.log(total), logs)
        o_ref[:, cols] = jnp.where(lane < 64, found[0], found[1]).astype(jnp.bfloat16)
    log_ref[...] = logs


def attend(projected, both_all, bias, kv_heads, group):
    batches, length, _ = both_all.shape
    rows = projected.shape[0] // batches
    wide = group * HD
    return pl.pallas_call(
        functools.partial(attend_kernel, group),
        grid=(batches, kv_heads),
        in_specs=[
            pl.BlockSpec((rows, wide), lambda b, h: (b, h)),
            pl.BlockSpec((1, length, 128), lambda b, h: (b, 0, h)),
            pl.BlockSpec((1, rows, length), lambda b, h: (b, 0, 0)),
        ],
        out_specs=[
            pl.BlockSpec((rows, wide), lambda b, h: (b, h)),
            pl.BlockSpec((rows, 128), lambda b, h: (b, h)),
        ],
        out_shape=[
            jax.ShapeDtypeStruct((batches * rows, kv_heads * wide), jnp.bfloat16),
            jax.ShapeDtypeStruct((batches * rows, kv_heads * 128), jnp.float32),
        ],
        compiler_params=pltpu.CompilerParams(vmem_limit_bytes=48 * 2**20),
    )(projected, both_all, bias)


def attend_back_kernel(
    group, q_ref, do_ref, kv_ref, bias_ref, log_ref, cos_ref, sin_ref, dq_ref, dkv_ref
):
    kv = kv_ref[0]
    sides = (kv, swapped(kv))
    rows = q_ref.shape[0]
    length = kv.shape[0]
    masks = lane_masks(rows)
    lane = lax.broadcasted_iota(jnp.int32, (rows, 128), 1)
    bias = bias_ref[0]
    key_sum = jnp.zeros((128, length), jnp.float32)
    value_sum = jnp.zeros((128, length), jnp.float32)
    for pair in range(group // 2):
        cols = slice(pair * 128, pair * 128 + 128)
        q = q_ref[:, cols]
        do = do_ref[:, cols]
        found = []
        for half in range(2):
            q_half = q * masks[half]
            do_half = do * masks[half]
            at = pair * 2 + half
            log_total = log_ref[:, at : at + 1]
            probs = jnp.exp(dot_t(q_half, sides[half]) + bias - log_total)
            grad_probs = dot_t(do_half, sides[1 - half])
            row_dot = jnp.sum(probs * grad_probs, -1, keepdims=True)
            grad_scores = (probs * (grad_probs - row_dot)).astype(jnp.bfloat16)
            found.append(plain_dot(grad_scores, sides[half]))
            key_sum = key_sum + left_dot(q_half, grad_scores)
            value_sum = value_sum + left_dot(do_half, probs.astype(jnp.bfloat16))
        dq = jnp.where(lane < 64, found[0], found[1])
        dq = dq * cos_ref[0] - swap_halves(dq) * sin_ref[0]
        dq_ref[:, cols] = dq.astype(jnp.bfloat16)
    both = jnp.concatenate(
        [key_sum[:64] + key_sum[64:], value_sum[:64] + value_sum[64:]], 0
    )
    dkv_ref[0] = both.T.astype(jnp.bfloat16)


def attend_back(projected, grad_attended, both_all, bias, logs, cos_tables, sin_tables, group):
    batches, length, _ = both_all.shape
    rows = projected.shape[0] // batches
    wide = group * HD
    kv_heads = both_all.shape[2] // 128
    return pl.pallas_call(
        functools.partial(attend_back_kernel, group),
        grid=(batches, kv_heads),
        in_specs=[
            pl.BlockSpec((rows, wide), lambda b, h: (b, h)),
            pl.BlockSpec((rows, wide), lambda b, h: (b, h)),
            pl.BlockSpec((1, length, 128), lambda b, h: (b, 0, h)),
            pl.BlockSpec((1, rows, length), lambda b, h: (b, 0, 0)),
            pl.BlockSpec((rows, 128), lambda b, h: (b, h)),
            pl.BlockSpec((1, rows, 128), lambda b, h: (0, b, 0)),
            pl.BlockSpec((1, rows, 128), lambda b, h: (0, b, 0)),
        ],
        out_specs=[
            pl.BlockSpec((rows, wide), lambda b, h: (b, h)),
            pl.BlockSpec((1, length, 128), lambda b, h: (b, 0, h)),
        ],
        out_shape=[
            jax.ShapeDtypeStruct((batches * rows, kv_heads * wide), jnp.bfloat16),
            jax.ShapeDtypeStruct((batches, length, kv_heads * 128), jnp.bfloat16),
        ],
        compiler_params=pltpu.CompilerParams(vmem_limit_bytes=48 * 2**20),
    )(projected, grad_attended, both_all, bias, logs, cos_tables, sin_tables)


def half_of(full):
    return full.astype(jnp.bfloat16)


def rotary_pairs(places, tokens, score_scale):
    cos_table, sin_table = rope_tables(places.reshape(tokens))
    ones, zeros = jnp.ones((tokens, HD), jnp.float32), jnp.zeros((tokens, HD), jnp.float32)
    cos_pair = jnp.concatenate([cos_table, cos_table], -1)
    sin_pair = jnp.concatenate([-sin_table, sin_table], -1)
    cos_tables = jnp.stack(
        [
            jnp.concatenate([cos_pair, cos_pair], -1) * score_scale,
            jnp.concatenate([cos_pair, ones], -1),
        ]
    )
    sin_tables = jnp.stack(
        [
            jnp.concatenate([sin_pair, sin_pair], -1) * score_scale,
            jnp.concatenate([sin_pair, zeros], -1),
        ]
    )
    return cos_tables, sin_tables


def forward_plain(shards, x, places, kv_heads, group, batches):
    tokens = x.shape[0]
    rows = tokens // batches
    length = rows * lax.axis_size("fsdp")
    query_features = kv_heads * group * HD
    used = query_features + kv_heads * 128
    fulls = gather(shards, ("yxc", "xyc", "yxc", "xyc", "yxc"), 1, 5)
    first_pack, out_full, gate_full, up_full, _ = (f.reshape(-1, f.shape[-1]) for f in fulls)
    gains = first_pack[:, used : used + 2].astype(jnp.float32).T
    query_index = lax.axis_index("fsdp") * rows + jnp.arange(rows, dtype=jnp.int32)
    key_index = jnp.arange(length, dtype=jnp.int32)
    x_float = x.astype(jnp.float32)
    cos_tables, sin_tables = rotary_pairs(places, tokens, HD**-0.5)
    doc_start = query_index[None, :] - places.reshape(batches, rows)
    allowed = (key_index[None, None, :] <= query_index[None, :, None]) & (
        key_index[None, None, :] >= doc_start[:, :, None]
    )
    bias = jnp.where(allowed, 0.0, NEGATIVE)
    attn_inverse = lax.rsqrt(jnp.mean(x_float * x_float, -1, keepdims=True) + EPSILON)
    normed = (x_float * attn_inverse * gains[0]).astype(jnp.bfloat16)
    projected = project(normed, first_pack[:, :used], cos_tables, sin_tables, kv_heads * 128)
    both_rows = projected[:, query_features:].reshape(batches, rows, -1)
    both_all = lax.all_gather(both_rows, "fsdp", axis=1, tiled=True)
    attended, logs = attend(projected, both_all, bias, kv_heads, group)
    mixed = x_float + plain_dot(attended, out_full)
    mlp_inverse = lax.rsqrt(jnp.mean(mixed * mixed, -1, keepdims=True) + EPSILON)
    normed_mlp = (mixed * mlp_inverse * gains[1]).astype(jnp.bfloat16)
    gate_pre = plain_dot(normed_mlp, gate_full)
    up_proj = plain_dot(normed_mlp, up_full)
    gate_sig = jax.nn.sigmoid(gate_pre)
    silu = gate_pre * gate_sig
    slope = up_proj * gate_sig * (1.0 + gate_pre * (1.0 - gate_sig))
    low = jnp.bfloat16
    return list(fulls) + [
        projected[:, :query_features],
        both_all,
        attended,
        logs,
        mixed,
        normed_mlp,
        (silu * up_proj).astype(low),
        slope.astype(low),
        silu.astype(low),
        bias.reshape(tokens, length),
        cos_tables,
        sin_tables,
    ]


def on_device(
    inputs,
    positions,
    cotangent,
    attn_gain,
    w_query,
    key_matrix,
    value_matrix,
    w_out,
    mlp_gain,
    w_gate,
    w_up,
    w_down,
):
    batches, _, rows, width = inputs.shape
    shard = w_query.shape[0]
    query_features = w_query.shape[1]
    key_features = key_matrix.shape[1]
    kv_heads = key_features // HD
    group = query_features // key_features
    tokens = batches * rows
    used = query_features + 2 * key_features

    extras = jnp.zeros((shard, 128), jnp.bfloat16)
    extras = extras.at[:, 0].set(attn_gain).at[:, 1].set(mlp_gain)
    pairs = jnp.concatenate(
        [key_matrix.reshape(shard, kv_heads, HD), value_matrix.reshape(shard, kv_heads, HD)], -1
    )
    first_shard = jnp.concatenate([w_query, pairs.reshape(shard, -1), extras], axis=1)
    shards = (first_shard, w_out, w_gate, w_up, w_down)
    x_low = inputs.reshape(tokens, width)
    x_float = x_low.astype(jnp.float32)
    fits = shard % 8 == 0 and lax.axis_size("fsdp") == 4 and rows % 256 == 0
    saved = (forward if fits else forward_plain)(
        shards, x_low, positions.reshape(tokens, 1), kv_heads, group, batches
    )
    first_pack, out_full, gate_full, up_full, down_full = (
        f.reshape(-1, f.shape[-1]) for f in saved[:5]
    )
    queries, both_all, attended, logs, mixed, normed_mlp = saved[5:11]
    hidden, slope, silu, bias, cos_tables, sin_tables = saved[11:]
    projection = first_pack[:, :used]
    gains = first_pack[:, used : used + 2].astype(jnp.float32).T
    attn_gain_f = gains[0]
    mlp_gain_f = gains[1]
    attn_inverse = lax.rsqrt(jnp.mean(x_float * x_float, -1, keepdims=True) + EPSILON)
    normed = (x_float * attn_inverse * attn_gain_f).astype(jnp.bfloat16)
    mlp_inverse = lax.rsqrt(jnp.mean(mixed * mixed, -1, keepdims=True) + EPSILON)
    output = (mixed + plain_dot(hidden, down_full)).astype(jnp.bfloat16)

    cot_low = cotangent.reshape(tokens, width)
    cot_float = cot_low.astype(jnp.float32)
    grad_down = half_of(left_dot(hidden, cot_low))
    grad_hidden = right_dot(cot_low, down_full)
    grad_gate_pre = (grad_hidden * slope.astype(jnp.float32)).astype(jnp.bfloat16)
    grad_up_pre = (grad_hidden * silu.astype(jnp.float32)).astype(jnp.bfloat16)
    grad_gate = half_of(left_dot(normed_mlp, grad_gate_pre))
    grad_up = half_of(left_dot(normed_mlp, grad_up_pre))
    grad_normed_mlp = right_dot(grad_gate_pre, gate_full) + right_dot(grad_up_pre, up_full)
    grad_mlp_gain = jnp.sum(grad_normed_mlp * mixed * mlp_inverse, 0)
    grad_mixed = cot_float + norm_back(grad_normed_mlp * mlp_gain_f, mixed, mlp_inverse)
    grad_mixed_low = grad_mixed.astype(jnp.bfloat16)
    grad_out = half_of(left_dot(attended, grad_mixed_low))
    grad_attended = right_dot(grad_mixed_low, out_full).astype(jnp.bfloat16)
    grad_query_pre, portions = attend_back(
        queries,
        grad_attended,
        both_all,
        bias.reshape(batches, rows, -1),
        logs,
        cos_tables,
        sin_tables,
        group,
    )
    sums = lax.psum_scatter(portions, "fsdp", scatter_dimension=1, tiled=True)
    sums = sums.astype(jnp.float32).reshape(tokens, kv_heads, 128)
    turned = jnp.concatenate([sums[..., 32:64], sums[..., :32], sums[..., 64:]], -1)
    grad_pair_pre = (sums * cos_tables[1][:, None] - turned * sin_tables[1][:, None]).astype(
        jnp.bfloat16
    )
    grad_pre = jnp.concatenate(
        [grad_query_pre, grad_pair_pre.reshape(tokens, 2 * key_features)], -1
    )
    grad_projection = left_dot(normed, grad_pre)
    grad_normed = right_dot(grad_pre, projection)
    grad_attn_gain = jnp.sum(grad_normed * x_float * attn_inverse, 0)
    grad_input = grad_mixed + norm_back(grad_normed * attn_gain_f, x_float, attn_inverse)
    gain_columns = jnp.stack([grad_attn_gain, grad_mlp_gain], -1)
    gain_columns = jnp.pad(gain_columns, ((0, 0), (0, 126)))
    grad_first = half_of(jnp.concatenate([grad_projection, gain_columns], 1))
    grad_down, grad_gate, grad_up, grad_out, last = scatter(
        (grad_down, grad_gate, grad_up, grad_out, grad_first), ("xy", "yx", "xy", "yx", "xy"), 2
    )
    last_pairs = last[:, query_features:used].reshape(shard, kv_heads, 2, HD)
    return (
        output.reshape(inputs.shape),
        grad_input.astype(jnp.bfloat16).reshape(inputs.shape),
        last[:, used],
        last[:, :query_features],
        last_pairs[:, :, 0].reshape(shard, key_features),
        last_pairs[:, :, 1].reshape(shard, key_features),
        grad_out,
        last[:, used + 1],
        grad_gate,
        grad_up,
        grad_down,
    )


def solution(mesh):
    tokens = P(None, "dp", "fsdp", None)
    vector = P(BOTH)
    matrix = P(BOTH, None)
    weights = (vector, matrix, matrix, matrix, matrix, vector, matrix, matrix, matrix)
    return jax.shard_map(
        on_device,
        mesh=mesh,
        in_specs=(tokens, P(None, "dp", "fsdp"), tokens) + weights,
        out_specs=(tokens, tokens) + weights,
        check_vma=False,
    )
```

```python
import functools

import jax
import jax.numpy as jnp
from jax import lax
from jax.experimental import pallas as pl
from jax.experimental.pallas import tpu as pltpu
from jax.sharding import PartitionSpec as P

HD = 64
EPSILON = 1e-05
NEGATIVE = -1e30
ROPE_BASE = 10000.0
BOTH = ("dp", "fsdp")


def rope_tables(places):
    half = HD // 2
    freqs = ROPE_BASE ** (-jnp.arange(half).astype(jnp.float32) / half)
    angles = places.astype(jnp.float32)[:, None] * freqs[None, :]
    return (jnp.cos(angles), jnp.sin(angles))


def plain_dot(left, right):
    return jnp.dot(left, right, preferred_element_type=jnp.float32)


def left_dot(left, right):
    return lax.dot_general(
        left, right, (((0,), (0,)), ((), ())), preferred_element_type=jnp.float32
    )


def right_dot(left, right):
    return lax.dot_general(
        left, right, (((1,), (1,)), ((), ())), preferred_element_type=jnp.float32
    )


def norm_back(grad_normed, inputs_float, inverse):
    return inverse * (
        grad_normed
        - inputs_float * inverse * inverse * jnp.mean(grad_normed * inputs_float, -1, keepdims=True)
    )


class Place:
    def __init__(self):
        self.Z=lax.axis_size("dp")//2; self.X=lax.axis_size("fsdp")//2
        dp=lax.axis_index("dp"); fs=lax.axis_index("fsdp")
        self.z=dp//2; self.y=dp%2; self.x=fs//2; self.c=fs%2
    def device(self,s=0,dy=0,dx=0,dc=0):
        return (lax.rem(self.z+s,self.Z)*2+lax.rem(self.y+dy,2), lax.rem(self.x+dx,self.X)*2+lax.rem(self.c+dc,2))
    def slot(self,s,dy,dx,dc):
        return ((lax.rem(self.z+self.Z-s,self.Z)*2+lax.rem(self.y+dy,2))*self.X+lax.rem(self.x+dx,self.X))*2+lax.rem(self.c+dc,2)

MESH = pl.DeviceIdType.MESH

def greet(me):
    barrier=pltpu.get_barrier_semaphore()
    friends=[me.device(s=s) for s in range(1,me.Z)]+[me.device(dy=1),me.device(dx=1),me.device(dc=1)]
    for f in friends:
        pl.semaphore_signal(barrier,inc=1,device_id=f,device_id_type=MESH)
    pl.semaphore_wait(barrier,len(friends))

def gather_kernel(Z, orders, ahead, *refs):
    K=len(orders)
    shards=refs[:K]; outs=refs[K:2*K]; local,send,recv=refs[2*K:]
    me=Place()
    greet(me)
    dims={"y":1,"x":2,"c":3}
    def sem(rel):
        return ((rel[0]*2+rel[1])*2+rel[2])*2+rel[3]
    started=[]
    def start(k,rel,to):
        if isinstance(to,int):
            target=me.device(s=to); landed=(to,0,0,0)
        else:
            landed=list(rel); landed[dims[to]]=1; landed=tuple(landed)
            target=me.device(**{"d"+to:1})
        slot=me.slot(*rel)
        src=shards[k] if rel==(0,0,0,0) else outs[k].at[slot]
        cp=pltpu.make_async_remote_copy(src_ref=src,dst_ref=outs[k].at[slot],send_sem=send.at[k,sem(landed)],recv_sem=recv.at[k,sem(landed)],device_id=target,device_id_type=MESH)
        cp.start()
        table[(k,landed)]=cp
    table={}
    own=[]
    def first(k):
        cp=pltpu.make_async_copy(shards[k],outs[k].at[me.slot(0,0,0,0)],local.at[k]); cp.start(); own.append(cp)
        for s in range(1,Z): start(k,(0,0,0,0),s)
        for d in orders[k]: start(k,(0,0,0,0),d)
    def arrive(k,rel,rest):
        table[(k,rel)].wait_recv()
        for d in rest: start(k,rel,d)
    def rel_of(s,o,a,b=0,c=0):
        r=[s,0,0,0]; r[dims[o[0]]]=a; r[dims[o[1]]]=b; r[dims[o[2]]]=c
        return tuple(r)
    for k in range(min(ahead,K)): first(k)
    for t in range(K+3):
        if t+ahead<K: first(t+ahead)
        k=t
        if k<K:
            o=orders[k]
            for s in range(1,Z): arrive(k,rel_of(s,o,0),o)
        k=t-1
        if 0<=k<K:
            o=orders[k]
            for s in range(Z): arrive(k,rel_of(s,o,1),o[1:])
        k=t-2
        if 0<=k<K:
            o=orders[k]
            for s in range(Z):
                for a in range(2): arrive(k,rel_of(s,o,a,1),o[2:])
        k=t-3
        if 0<=k<K:
            o=orders[k]
            for s in range(Z):
                for a in range(2):
                    for b in range(2): arrive(k,rel_of(s,o,a,b,1),"")
    for cp in own: cp.wait()
    for cp in table.values(): cp.wait_send()

def gather(shards, orders, cid, ahead=2):
    n=lax.axis_size("dp")*lax.axis_size("fsdp"); Z=lax.axis_size("dp")//2; K=len(shards)
    return pl.pallas_call(functools.partial(gather_kernel,Z,orders,ahead),
        out_shape=[jax.ShapeDtypeStruct((n,)+s.shape,s.dtype) for s in shards],
        in_specs=[pl.BlockSpec(memory_space=pl.ANY)]*K,
        out_specs=[pl.BlockSpec(memory_space=pl.ANY)]*K,
        scratch_shapes=[pltpu.SemaphoreType.DMA((K,)),pltpu.SemaphoreType.DMA((K,8*Z)),pltpu.SemaphoreType.DMA((K,8*Z))],
        compiler_params=pltpu.CompilerParams(collective_id=cid,has_side_effects=True))(*shards)


class Gathering:
    def __init__(self, me, chunks, local, send, recv):
        self.me, self.chunks = me, chunks
        self.local, self.send, self.recv = local, send, recv
        self.table, self.own = {}, []

    def start(self, k, rel, to):
        shard, full, cols, _ = self.chunks[k]
        me = self.me
        if isinstance(to, int):
            target, landed = me.device(s=to), (to, 0, 0, 0)
        else:
            landed = list(rel)
            landed["zyxc".index(to)] = 1
            landed = tuple(landed)
            target = me.device(**{"d" + to: 1})
        slot = me.slot(*rel)
        here = full.at[slot, :, cols]
        at = ((landed[0] * 2 + landed[1]) * 2 + landed[2]) * 2 + landed[3]
        copy = pltpu.make_async_remote_copy(
            src_ref=shard.at[:, cols] if rel == (0, 0, 0, 0) else here,
            dst_ref=here,
            send_sem=self.send.at[k, at],
            recv_sem=self.recv.at[k, at],
            device_id=target,
            device_id_type=MESH,
        )
        copy.start()
        self.table[(k, landed)] = copy

    def begin(self, k):
        shard, full, cols, order = self.chunks[k]
        copy = pltpu.make_async_copy(
            shard.at[:, cols], full.at[self.me.slot(0, 0, 0, 0), :, cols], self.local.at[k]
        )
        copy.start()
        self.own.append((k, copy))
        for s in range(1, self.me.Z):
            self.start(k, (0, 0, 0, 0), s)
        for d in order:
            self.start(k, (0, 0, 0, 0), d)

    def step(self, k, stage):
        order = self.chunks[k][3]
        where = ["zyxc".index(d) for d in order]
        for s in range(1 if stage == 0 else 0, self.me.Z):
            for bits in range(1 << max(stage - 1, 0)):
                rel = [s, 0, 0, 0]
                for i in range(stage - 1):
                    rel[where[i]] = bits >> i & 1
                if stage:
                    rel[where[stage - 1]] = 1
                rel = tuple(rel)
                self.table[(k, rel)].wait_recv()
                for d in order[stage:]:
                    self.start(k, rel, d)
        if stage == 3:
            for at, copy in self.own:
                if at == k:
                    copy.wait()

    def finish(self):
        for copy in self.table.values():
            copy.wait_send()


def forward_kernel(sizes, *refs):
    batches, rows, kv_heads, group, used = sizes
    (first_s, out_s, gate_s, up_s, down_s, x_ref, place_ref, freq_ref) = refs[:8]
    (first_w, out_w, gate_w, up_w, down_w, q_out, kv_out, o_out, log_out) = refs[8:17]
    (mixed_out, h2_out, hidden_out, slope_out, silu_out, bias_out, cos_out, sin_out) = refs[17:25]
    (raw_a, raw_b, w_a, w_b, normed, queries, kv_all, attended, logs, mixed, h2) = refs[25:36]
    (hidden, slope, silu, bias, cos_t, sin_t, gains) = refs[36:43]
    (local, send, recv, kv_send, kv_recv, load_sem, store_sem) = refs[43:]
    me = Place()
    greet(me)
    whole = slice(None)
    half = down_w.shape[2] // 2
    comm = Gathering(
        me,
        (
            (first_s, first_w, whole, "yxc"),
            (out_s, out_w, whole, "xyc"),
            (gate_s, gate_w, whole, "yxc"),
            (up_s, up_w, whole, "xyc"),
            (down_s, down_w, pl.ds(0, half), "yxc"),
            (down_s, down_w, pl.ds(half, half), "xyc"),
        ),
        local,
        send,
        recv,
    )
    tokens, width = x_ref.shape
    length = kv_all.shape[1]
    stores = []

    def store(i, src, dst):
        copy = pltpu.make_async_copy(src, dst, store_sem.at[i])
        copy.start()
        stores.append(copy)

    def over_rows(body, step=64):
        def one(i, carry):
            body(pl.ds(pl.multiple_of(i * step, step), step))
            return carry

        lax.fori_loop(0, tokens // step, one, 0)

    def load(full, raw, col, size, i):
        return pltpu.make_async_copy(
            full.at[:, :, pl.ds(col, size)], raw.at[:, :, pl.ds(0, size)], load_sem.at[i]
        )

    def assemble(raw, flat, size):
        n, r, _ = raw.shape
        pair = 2 * r

        def one(i, carry):
            piece = raw[pl.ds(2 * i, 2), :, pl.ds(0, size)].astype(jnp.float32)
            flat[pl.ds(pl.multiple_of(pair * i, 16), pair), pl.ds(0, size)] = piece.reshape(
                pair, size
            ).astype(jnp.bfloat16)
            return carry

        lax.fori_loop(0, n // 2, one, 0)

    comm.begin(0)
    comm.begin(1)

    scale = HD**-0.5
    lane = lax.broadcasted_iota(jnp.int32, (64, 128), 1)
    second = lax.rem(lane, HD) >= HD // 2
    is_value = lane >= HD

    def tables(at):
        angle = place_ref[at, :].astype(jnp.float32) * freq_ref[...]
        c, s = jnp.cos(angle), jnp.sin(angle)
        s = jnp.where(second, s, -s)
        cos_t[0, at, :] = c * scale
        sin_t[0, at, :] = s * scale
        cos_t[1, at, :] = jnp.where(is_value, 1.0, c)
        sin_t[1, at, :] = jnp.where(is_value, 0.0, s)

    over_rows(tables)
    first_row = lax.axis_index("fsdp") * rows

    def masks(at):
        token = at.start
        inside = lax.rem(token, rows)
        query = first_row + inside + lax.broadcasted_iota(jnp.int32, (64, length), 0)
        key = lax.broadcasted_iota(jnp.int32, (64, length), 1)
        start = query - place_ref[at, :]
        allowed = (key <= query) & (key >= start)
        bias[at, :] = jnp.where(allowed, 0.0, NEGATIVE).astype(jnp.bfloat16)

    over_rows(masks)
    store(0, bias, bias_out)
    store(1, cos_t, cos_out)
    store(2, sin_t, sin_out)

    comm.step(0, 0)
    comm.begin(2)
    comm.step(1, 0)
    comm.step(0, 1)
    comm.step(1, 1)
    comm.step(0, 2)
    comm.begin(3)
    comm.step(1, 2)
    comm.step(0, 3)

    tile = raw_a.shape[2]
    load(first_w, raw_a, used, 128, 0).start()
    load(first_w, raw_b, 0, tile, 1).start()
    load(first_w, raw_a, used, 128, 0).wait()
    assemble(raw_a, w_a, 128)
    gains[...] = w_a[:, :128].astype(jnp.float32).T[:8]
    load(first_w, raw_a, used - tile, tile, 0).start()

    def norm_one(at):
        x = x_ref[at, :].astype(jnp.float32)
        inverse = lax.rsqrt(jnp.mean(x * x, -1, keepdims=True) + EPSILON)
        normed[at, :] = (x * inverse * gains[0:1, :]).astype(jnp.bfloat16)

    over_rows(norm_one)

    def turn(flat, kind, put, step=128):
        def body(at):
            u = plain_dot(normed[at, :], flat[...])
            for j in range(tile // 128):
                piece = u[:, j * 128 : (j + 1) * 128]
                piece = piece * cos_t[kind, at, :] + swap_halves(piece) * sin_t[kind, at, :]
                put(at, j, piece.astype(jnp.bfloat16))

        over_rows(body, step)

    slot = (me.x * 2 + me.c) * rows

    def put_pair(at, j, piece):
        token = at.start
        b = token // rows
        row = pl.multiple_of(slot + lax.rem(token, rows), 128)
        kv_all[b, pl.ds(row, 128), j * 128 : (j + 1) * 128] = piece

    load(first_w, raw_a, used - tile, tile, 0).wait()
    assemble(raw_a, w_a, tile)
    turn(w_a, 1, put_pair)

    def share(i, dx, to):
        row = (lax.rem(me.x + dx, 2) * 2 + me.c) * rows
        block = kv_all.at[:, pl.ds(pl.multiple_of(row, 256), rows), :]
        copy = pltpu.make_async_remote_copy(
            src_ref=block,
            dst_ref=block,
            send_sem=kv_send.at[i],
            recv_sem=kv_recv.at[i],
            device_id=me.device(**{"d" + to: 1}),
            device_id_type=MESH,
        )
        copy.start()
        return copy

    to_x = share(0, 0, "x")
    to_c = share(1, 0, "c")
    for j in range(queries.shape[1] // tile):
        raw, flat = ((raw_b, w_b), (raw_a, w_a))[j % 2]
        if (j + 1) * tile < queries.shape[1]:
            load(first_w, (raw_a, raw_b)[j % 2], (j + 1) * tile, tile, j % 2).start()
        load(first_w, raw, j * tile, tile, 1 - j % 2).wait()
        assemble(raw, flat, tile)

        def put_query(at, i, piece, j=j):
            queries[at, j * tile + i * 128 : j * tile + (i + 1) * 128] = piece

        turn(flat, 0, put_query)
    store(3, queries, q_out)
    comm.step(2, 0)
    comm.step(1, 3)
    comm.begin(4)
    comm.step(3, 0)
    comm.step(2, 1)
    to_x.wait_recv()
    to_far = share(2, 1, "c")
    to_c.wait_recv()
    to_far.wait_recv()
    store(4, kv_all, kv_out)

    logs[...] = jnp.zeros_like(logs)
    lanes = lax.broadcasted_iota(jnp.int32, (rows, 128), 1)
    sides_mask = lane_masks(rows)

    def head(i, carry):
        b = i // kv_heads
        h = lax.rem(i, kv_heads)
        at = pl.ds(pl.multiple_of(b * rows, 256), rows)
        kv = kv_all[b, :, pl.ds(pl.multiple_of(h * 128, 128), 128)]
        sides = (kv, swapped(kv))
        shift = bias[at, :].astype(jnp.float32)
        log_piece = logs[at, :]
        for pair in range(group // 2):
            cols = pl.ds(pl.multiple_of(h * group * HD + pair * 128, 128), 128)
            q = queries[at, cols]
            found = []
            for side in range(2):
                scores = dot_t(q * sides_mask[side], sides[side]) + shift
                top = jnp.max(scores, -1, keepdims=True)
                powers = jnp.exp(scores - top)
                total = jnp.sum(powers, -1, keepdims=True)
                probs = (powers * (1.0 / total)).astype(jnp.bfloat16)
                found.append(plain_dot(probs, sides[1 - side]))
                log_piece = jnp.where(
                    lanes == h * group + pair * 2 + side, top + jnp.log(total), log_piece
                )
            attended[at, cols] = jnp.where(lanes < HD, found[0], found[1]).astype(jnp.bfloat16)
        logs[at, :] = log_piece
        return carry

    count = batches * kv_heads
    pumps = [(3, 1), (2, 2), (4, 0), (3, 2)]
    done = 0
    for i in range(5):
        upto = count * (i + 1) // 5
        lax.fori_loop(done, upto, head, 0)
        done = upto
        if i == 0:
            comm.begin(5)
        if i < len(pumps):
            comm.step(*pumps[i])
    store(5, attended, o_out)
    store(6, logs, log_out)

    steps = width // tile
    load(out_w, raw_a, 0, tile, 0).start()
    for j in range(steps):
        raw, flat = ((raw_a, w_a), (raw_b, w_b))[j % 2]
        if j + 1 < steps:
            load(out_w, (raw_b, raw_a)[j % 2], (j + 1) * tile, tile, 1 - j % 2).start()
        load(out_w, raw, j * tile, tile, j % 2).wait()
        assemble(raw, flat, tile)

        def add_in(at, flat=flat, j=j):
            cols = slice(j * tile, (j + 1) * tile)
            mixed[at, cols] = x_ref[at, cols].astype(jnp.float32) + plain_dot(
                attended[at, :], flat[...]
            )

        over_rows(add_in, 128)

    def norm_two(at):
        y = mixed[at, :]
        inverse = lax.rsqrt(jnp.mean(y * y, -1, keepdims=True) + EPSILON)
        h2[at, :] = (y * inverse * gains[1:2, :]).astype(jnp.bfloat16)

    over_rows(norm_two)
    store(7, mixed, mixed_out)
    store(8, h2, h2_out)

    comm.step(5, 0)
    comm.step(4, 1)
    comm.step(2, 3)
    comm.step(3, 3)

    wide = 512
    features = hidden.shape[1]
    pumps = {1: (5, 1), 3: (4, 2), 5: (5, 2)}
    load(gate_w, raw_a, 0, wide, 0).start()
    load(up_w, raw_b, 0, wide, 1).start()
    for j in range(features // wide):
        load(gate_w, raw_a, j * wide, wide, 0).wait()
        assemble(raw_a, w_a, wide)
        load(up_w, raw_b, j * wide, wide, 1).wait()
        assemble(raw_b, w_b, wide)
        if (j + 1) * wide < features:
            load(gate_w, raw_a, (j + 1) * wide, wide, 0).start()
            load(up_w, raw_b, (j + 1) * wide, wide, 1).start()

        def units(at, j=j):
            cols = slice(j * wide, (j + 1) * wide)
            g = plain_dot(h2[at, :], w_a[:, :wide])
            u = plain_dot(h2[at, :], w_b[:, :wide])
            sig = jax.nn.sigmoid(g)
            soft = g * sig
            hidden[at, cols] = (soft * u).astype(jnp.bfloat16)
            silu[at, cols] = soft.astype(jnp.bfloat16)
            slope[at, cols] = (u * (sig * (1.0 + g * (1.0 - sig)))).astype(jnp.bfloat16)

        over_rows(units, 128)
        if j in pumps:
            comm.step(*pumps[j])
    store(9, hidden, hidden_out)
    store(10, silu, silu_out)
    store(11, slope, slope_out)
    comm.step(4, 3)
    comm.step(5, 3)
    for copy in (to_x, to_c, to_far):
        copy.wait_send()
    comm.finish()
    for copy in stores:
        copy.wait()


def forward(shards, x, places, kv_heads, group, batches):
    first_s, out_s, gate_s, up_s, down_s = shards
    n = lax.axis_size("dp") * lax.axis_size("fsdp")
    Z = lax.axis_size("dp") // 2
    tokens, width = x.shape
    rows = tokens // batches
    length = rows * lax.axis_size("fsdp")
    key_wide = kv_heads * 128
    query_wide = kv_heads * group * HD
    used = query_wide + key_wide
    features = gate_s.shape[1]
    r = first_s.shape[0]
    freqs = ROPE_BASE ** (-jnp.arange(HD // 2).astype(jnp.float32) / (HD // 2))
    freqs = jnp.tile(freqs, 4)[None]
    bf, f32 = jnp.bfloat16, jnp.float32
    shape = jax.ShapeDtypeStruct
    outs = [shape((n,) + s.shape, s.dtype) for s in shards] + [
        shape((tokens, query_wide), bf),
        shape((batches, length, key_wide), bf),
        shape((tokens, query_wide), bf),
        shape((tokens, 128), f32),
        shape((tokens, width), f32),
        shape((tokens, width), bf),
        shape((tokens, features), bf),
        shape((tokens, features), bf),
        shape((tokens, features), bf),
        shape((tokens, length), bf),
        shape((2, tokens, 128), f32),
        shape((2, tokens, 128), f32),
    ]
    vmem = pltpu.VMEM
    scratch = [
        vmem((n, r, key_wide), bf),
        vmem((n, r, key_wide), bf),
        vmem((width, key_wide), bf),
        vmem((width, key_wide), bf),
        vmem((tokens, width), bf),
        vmem((tokens, query_wide), bf),
        vmem((batches, length, key_wide), bf),
        vmem((tokens, query_wide), bf),
        vmem((tokens, 128), f32),
        vmem((tokens, width), f32),
        vmem((tokens, width), bf),
        vmem((tokens, features), bf),
        vmem((tokens, features), bf),
        vmem((tokens, features), bf),
        vmem((tokens, length), bf),
        vmem((2, tokens, 128), f32),
        vmem((2, tokens, 128), f32),
        vmem((8, width), f32),
        pltpu.SemaphoreType.DMA((6,)),
        pltpu.SemaphoreType.DMA((6, 8 * Z)),
        pltpu.SemaphoreType.DMA((6, 8 * Z)),
        pltpu.SemaphoreType.DMA((3,)),
        pltpu.SemaphoreType.DMA((3,)),
        pltpu.SemaphoreType.DMA((2,)),
        pltpu.SemaphoreType.DMA((12,)),
    ]
    any_space = pl.BlockSpec(memory_space=pl.ANY)
    in_vmem = pl.BlockSpec(memory_space=pltpu.VMEM)
    return pl.pallas_call(
        functools.partial(forward_kernel, (batches, rows, kv_heads, group, used)),
        out_shape=outs,
        in_specs=[any_space] * 5 + [in_vmem] * 3,
        out_specs=[any_space] * len(outs),
        scratch_shapes=scratch,
        compiler_params=pltpu.CompilerParams(
            collective_id=1, has_side_effects=True, vmem_limit_bytes=63 * 2**20
        ),
        cost_estimate=pl.CostEstimate(
            flops=2 * tokens * width * (used + width + 2 * features),
            bytes_accessed=4 * n * r * (used + width + 3 * features),
            transcendentals=tokens * features,
        ),
    )(*shards, x, places, freqs)


def tile_of(N):
    for t in (512,384,256,128):
        if N%t==0: return t
    return N

def scatter_kernel(Z, orders, ahead, dims_, *refs):
    K=len(orders)
    parts=refs[:K]; outs=refs[K:2*K]
    sc=refs[2*K:]
    first_buf=sc[:K]; one_buf=sc[K:2*K]; two_buf=sc[2*K:3*K]; last_buf=sc[3*K:4*K]
    shapes=sorted(set(dims_))
    stage=[sc[4*K+shapes.index(d)] for d in dims_]
    local,send,recv=sc[4*K+len(shapes):]
    me=Place()
    greet(me)
    copies={}
    def ship(k,name,index,src,dst,target):
        cp=pltpu.make_async_remote_copy(src_ref=src,dst_ref=dst,send_sem=send.at[k,index],recv_sem=recv.at[k,index],device_id=target,device_id_type=MESH)
        cp.start(); copies[(k,name)]=cp
    def part(k,a,b,other):
        o=orders[k]
        rel={o[0]:a,o[1]:b}
        y=lax.rem(me.y+rel["y"],2); x=lax.rem(me.x+rel["x"],me.X); c=lax.rem(me.c+other,2)
        return parts[k].at[:,y,x,c]
    order4=((1,1),(1,0),(0,1),(0,0))
    locals_={}
    def first(k):
        for i,(a,b) in enumerate(order4):
            ship(k,("c",a,b),i,part(k,a,b,1),first_buf[k].at[a,b],me.device(dc=1))
    def bring(k,i):
        a,b=order4[i]
        cp=pltpu.make_async_copy(part(k,a,b,0),stage[k].at[i%2],local.at[k,i%2]); cp.start(); locals_[(k,i)]=cp
    def add(dst,src,k):
        _,r,N=dims_[k]
        t=tile_of(N)
        def body(i,_):
            zi=i//(N//t); j=i%(N//t)
            cols=pl.ds(pl.multiple_of(j*t,128),t)
            dst[zi,:,cols]=dst[zi,:,cols]+src[zi,:,cols]
            return 0
        lax.fori_loop(0,Z*(N//t),body,0)
    def step_c(k):
        bring(k,0); bring(k,1)
        for i,(a,b) in enumerate(order4):
            copies[(k,("c",a,b))].wait_recv()
            locals_[(k,i)].wait()
            add(first_buf[k].at[a,b],stage[k].at[i%2],k)
            if i+2<4: bring(k,i+2)
            if a==1:
                ship(k,("1",b),4+b,first_buf[k].at[1,b],one_buf[k].at[b],me.device(**{"d"+orders[k][0]:1}))
    def step_1(k):
        for b in (1,0):
            copies[(k,("1",b))].wait_recv()
            add(first_buf[k].at[0,b],one_buf[k].at[b],k)
            if b==1:
                ship(k,"2",6,first_buf[k].at[0,1],two_buf[k],me.device(**{"d"+orders[k][1]:1}))
    def step_2(k):
        copies[(k,"2")].wait_recv()
        add(first_buf[k].at[0,0],two_buf[k],k)
        for s in range(1,Z):
            ship(k,("z",s),6+s,first_buf[k].at[0,0,lax.rem(me.z+s,Z)],last_buf[k].at[s-1],me.device(s=s))
    def step_z(k):
        _,r,N=dims_[k]
        for s in range(1,Z): copies[(k,("z",s))].wait_recv()
        t=tile_of(N)
        mine=first_buf[k].at[0,0,me.z]
        def body(j,_):
            cols=pl.ds(pl.multiple_of(j*t,128),t)
            total=mine[:,cols].astype(jnp.float32)
            for s in range(1,Z): total=total+last_buf[k][s-1,:,cols].astype(jnp.float32)
            outs[k][:,cols]=total
            return 0
        lax.fori_loop(0,N//t,body,0)
    for k in range(min(ahead,K)): first(k)
    for t in range(K+3):
        if t+ahead<K: first(t+ahead)
        if t<K: step_c(t)
        if 0<=t-1<K: step_1(t-1)
        if 0<=t-2<K: step_2(t-2)
        if 0<=t-3<K: step_z(t-3)
    for cp in copies.values(): cp.wait_send()

def scatter(parts, orders, cid, ahead=2):
    n=lax.axis_size("dp")*lax.axis_size("fsdp"); Z=lax.axis_size("dp")//2; X=lax.axis_size("fsdp")//2; K=len(parts)
    dims_=[(n,p.shape[0]//n,p.shape[1]) for p in parts]
    parts=[p.reshape(Z,2,X,2,p.shape[0]//n,p.shape[1]) for p in parts]
    bf=jnp.bfloat16
    sc=[pltpu.VMEM((2,2,Z,r,N),bf) for _,r,N in dims_]+[pltpu.VMEM((2,Z,r,N),bf) for _,r,N in dims_]+[pltpu.VMEM((Z,r,N),bf) for _,r,N in dims_]+[pltpu.VMEM((Z-1,r,N),bf) for _,r,N in dims_]+[pltpu.VMEM((2,Z,r,N),bf) for _,r,N in sorted(set(dims_))]
    return pl.pallas_call(functools.partial(scatter_kernel,Z,orders,ahead,dims_),
        out_shape=[jax.ShapeDtypeStruct((r,N),jnp.float32) for _,r,N in dims_],
        in_specs=[pl.BlockSpec(memory_space=pl.ANY)]*K,
        out_specs=[pl.BlockSpec(memory_space=pltpu.VMEM)]*K,
        scratch_shapes=sc+[pltpu.SemaphoreType.DMA((K,2)),pltpu.SemaphoreType.DMA((K,6+Z)),pltpu.SemaphoreType.DMA((K,6+Z))],
        compiler_params=pltpu.CompilerParams(collective_id=cid,has_side_effects=True,vmem_limit_bytes=63*2**20))(*parts)


def dot_t(left, right):
    return lax.dot_general(
        left, right, (((1,), (1,)), ((), ())), preferred_element_type=jnp.float32
    )


def swap_halves(u):
    lane = lax.broadcasted_iota(jnp.int32, u.shape, 1)
    down = pltpu.roll(u, 32, 1)
    up = pltpu.roll(u, 96, 1)
    return jnp.where(lax.rem(lane, 64) < 32, up, down)


def project_kernel(h_ref, w_ref, cos_ref, sin_ref, out_ref):
    u = plain_dot(h_ref[...], w_ref[...])
    for j in range(u.shape[1] // 128):
        piece = u[:, j * 128 : (j + 1) * 128]
        turned = piece * cos_ref[0] + swap_halves(piece) * sin_ref[0]
        out_ref[:, j * 128 : (j + 1) * 128] = turned.astype(jnp.bfloat16)


def project(normed, weight, cos_tables, sin_tables, width):
    tokens, depth = normed.shape
    steps = weight.shape[1] // width
    return pl.pallas_call(
        project_kernel,
        grid=(steps,),
        in_specs=[
            pl.BlockSpec((tokens, depth), lambda j: (0, 0)),
            pl.BlockSpec((depth, width), lambda j: (0, j)),
            pl.BlockSpec((1, tokens, 128), lambda j: (j // (steps - 1), 0, 0)),
            pl.BlockSpec((1, tokens, 128), lambda j: (j // (steps - 1), 0, 0)),
        ],
        out_specs=pl.BlockSpec((tokens, width), lambda j: (0, j)),
        out_shape=jax.ShapeDtypeStruct((tokens, steps * width), jnp.bfloat16),
        compiler_params=pltpu.CompilerParams(vmem_limit_bytes=48 * 2**20),
        cost_estimate=pl.CostEstimate(
            flops=2 * tokens * depth * weight.shape[1],
            bytes_accessed=2 * depth * weight.shape[1],
            transcendentals=0,
        ),
    )(normed, weight, cos_tables, sin_tables)


def lane_masks(rows):
    lane = lax.broadcasted_iota(jnp.int32, (rows, 128), 1)
    low_side = (lane < 64).astype(jnp.float32)
    return low_side.astype(jnp.bfloat16), (1.0 - low_side).astype(jnp.bfloat16)


def swapped(kv):
    return pltpu.roll(kv.astype(jnp.float32), 64, 1).astype(jnp.bfloat16)


def attend_kernel(group, q_ref, kv_ref, bias_ref, o_ref, log_ref):
    kv = kv_ref[0]
    sides = (kv, swapped(kv))
    rows = q_ref.shape[0]
    masks = lane_masks(rows)
    lane = lax.broadcasted_iota(jnp.int32, (rows, 128), 1)
    logs = jnp.zeros((rows, 128), jnp.float32)
    bias = bias_ref[0]
    for pair in range(group // 2):
        cols = slice(pair * 128, pair * 128 + 128)
        q = q_ref[:, cols]
        found = []
        for half in range(2):
            scores = dot_t(q * masks[half], sides[half]) + bias
            top = jnp.max(scores, -1, keepdims=True)
            powers = jnp.exp(scores - top)
            total = jnp.sum(powers, -1, keepdims=True)
            probs = (powers * (1.0 / total)).astype(jnp.bfloat16)
            found.append(plain_dot(probs, sides[1 - half]))
            logs = jnp.where(lane == pair * 2 + half, top + jnp.log(total), logs)
        o_ref[:, cols] = jnp.where(lane < 64, found[0], found[1]).astype(jnp.bfloat16)
    log_ref[...] = logs


def attend(projected, both_all, bias, kv_heads, group):
    batches, length, _ = both_all.shape
    rows = projected.shape[0] // batches
    wide = group * HD
    return pl.pallas_call(
        functools.partial(attend_kernel, group),
        grid=(batches, kv_heads),
        in_specs=[
            pl.BlockSpec((rows, wide), lambda b, h: (b, h)),
            pl.BlockSpec((1, length, 128), lambda b, h: (b, 0, h)),
            pl.BlockSpec((1, rows, length), lambda b, h: (b, 0, 0)),
        ],
        out_specs=[
            pl.BlockSpec((rows, wide), lambda b, h: (b, h)),
            pl.BlockSpec((rows, 128), lambda b, h: (b, h)),
        ],
        out_shape=[
            jax.ShapeDtypeStruct((batches * rows, kv_heads * wide), jnp.bfloat16),
            jax.ShapeDtypeStruct((batches * rows, kv_heads * 128), jnp.float32),
        ],
        compiler_params=pltpu.CompilerParams(vmem_limit_bytes=48 * 2**20),
    )(projected, both_all, bias)


def attend_back_kernel(
    group, q_ref, do_ref, kv_ref, bias_ref, log_ref, cos_ref, sin_ref, dq_ref, dkv_ref
):
    kv = kv_ref[0]
    sides = (kv, swapped(kv))
    rows = q_ref.shape[0]
    length = kv.shape[0]
    masks = lane_masks(rows)
    lane = lax.broadcasted_iota(jnp.int32, (rows, 128), 1)
    bias = bias_ref[0]
    key_sum = jnp.zeros((128, length), jnp.float32)
    value_sum = jnp.zeros((128, length), jnp.float32)
    for pair in range(group // 2):
        cols = slice(pair * 128, pair * 128 + 128)
        q = q_ref[:, cols]
        do = do_ref[:, cols]
        found = []
        for half in range(2):
            q_half = q * masks[half]
            do_half = do * masks[half]
            at = pair * 2 + half
            log_total = log_ref[:, at : at + 1]
            probs = jnp.exp(dot_t(q_half, sides[half]) + bias - log_total)
            grad_probs = dot_t(do_half, sides[1 - half])
            row_dot = jnp.sum(probs * grad_probs, -1, keepdims=True)
            grad_scores = (probs * (grad_probs - row_dot)).astype(jnp.bfloat16)
            found.append(plain_dot(grad_scores, sides[half]))
            key_sum = key_sum + left_dot(q_half, grad_scores)
            value_sum = value_sum + left_dot(do_half, probs.astype(jnp.bfloat16))
        dq = jnp.where(lane < 64, found[0], found[1])
        dq = dq * cos_ref[0] - swap_halves(dq) * sin_ref[0]
        dq_ref[:, cols] = dq.astype(jnp.bfloat16)
    both = jnp.concatenate(
        [key_sum[:64] + key_sum[64:], value_sum[:64] + value_sum[64:]], 0
    )
    dkv_ref[0] = both.T.astype(jnp.bfloat16)


def attend_back(projected, grad_attended, both_all, bias, logs, cos_tables, sin_tables, group):
    batches, length, _ = both_all.shape
    rows = projected.shape[0] // batches
    wide = group * HD
    kv_heads = both_all.shape[2] // 128
    return pl.pallas_call(
        functools.partial(attend_back_kernel, group),
        grid=(batches, kv_heads),
        in_specs=[
            pl.BlockSpec((rows, wide), lambda b, h: (b, h)),
            pl.BlockSpec((rows, wide), lambda b, h: (b, h)),
            pl.BlockSpec((1, length, 128), lambda b, h: (b, 0, h)),
            pl.BlockSpec((1, rows, length), lambda b, h: (b, 0, 0)),
            pl.BlockSpec((rows, 128), lambda b, h: (b, h)),
            pl.BlockSpec((1, rows, 128), lambda b, h: (0, b, 0)),
            pl.BlockSpec((1, rows, 128), lambda b, h: (0, b, 0)),
        ],
        out_specs=[
            pl.BlockSpec((rows, wide), lambda b, h: (b, h)),
            pl.BlockSpec((1, length, 128), lambda b, h: (b, 0, h)),
        ],
        out_shape=[
            jax.ShapeDtypeStruct((batches * rows, kv_heads * wide), jnp.bfloat16),
            jax.ShapeDtypeStruct((batches, length, kv_heads * 128), jnp.bfloat16),
        ],
        compiler_params=pltpu.CompilerParams(vmem_limit_bytes=48 * 2**20),
    )(projected, grad_attended, both_all, bias, logs, cos_tables, sin_tables)


class Scattering:
    def __init__(self, me, chunks, send, recv, free):
        self.me, self.chunks = me, chunks
        self.send, self.recv, self.free = send, recv, free
        self.copies = {}
        self.friends = [me.device(s=s) for s in range(1, me.Z)]
        self.friends += [me.device(dy=1), me.device(dx=1), me.device(dc=1)]

    def ship(self, k, name, index, src, dst, target):
        copy = pltpu.make_async_remote_copy(
            src_ref=src,
            dst_ref=dst,
            send_sem=self.send.at[k, index],
            recv_sem=self.recv.at[k, index],
            device_id=target,
            device_id_type=MESH,
        )
        copy.start()
        self.copies[(k, name)] = copy

    def add(self, dst, src, wide):
        depth = dst.shape[0]
        t = tile_of(wide)
        count = wide // t

        def body(i, carry):
            at = i // count
            cols = pl.ds(pl.multiple_of(lax.rem(i, count) * t, 128), t)
            dst[at, :, cols] = dst[at, :, cols] + src[at, :, cols]
            return carry

        lax.fori_loop(0, depth * count, body, 0)

    def buffers(self, k):
        own, one, two, last, wide = self.chunks[k][:5]
        cols = pl.ds(0, wide)
        return own, one, two, last, wide, cols

    def begin(self, k):
        own, one, two, last, wide, cols = self.buffers(k)
        order = self.chunks[k][5]
        for b in (1, 0):
            self.ship(
                k,
                ("1", b),
                b,
                own.at[1, b, :, :, cols],
                one.at[b, :, :, cols],
                self.me.device(**{"d" + order[0]: 1}),
            )

    def first(self, k):
        own, one, two, last, wide, cols = self.buffers(k)
        order = self.chunks[k][5]
        for b in (1, 0):
            self.copies[(k, ("1", b))].wait_recv()
            self.add(own.at[0, b], one.at[b], wide)
            if b == 1:
                self.ship(
                    k,
                    "2",
                    2,
                    own.at[0, 1, :, :, cols],
                    two.at[:, :, cols],
                    self.me.device(**{"d" + order[1]: 1}),
                )

    def second(self, k):
        own, one, two, last, wide, cols = self.buffers(k)
        me = self.me
        self.copies[(k, "2")].wait_recv()
        self.add(own.at[0, 0], two, wide)
        for s in range(1, me.Z):
            self.ship(
                k,
                ("z", s),
                2 + s,
                own.at[0, 0, lax.rem(me.z + s, me.Z), :, cols],
                last.at[s - 1, :, cols],
                me.device(s=s),
            )

    def third(self, k):
        own, one, two, last, wide, cols = self.buffers(k)
        me = self.me
        _, out, base, group = self.chunks[k][5:]
        for s in range(1, me.Z):
            self.copies[(k, ("z", s))].wait_recv()
        t = tile_of(wide)

        def body(j, carry):
            here = pl.ds(pl.multiple_of(j * t, 128), t)
            there = pl.ds(pl.multiple_of(base + j * t, 128), t)
            total = own[0, 0, me.z, :, here].astype(jnp.float32)
            for s in range(1, me.Z):
                total = total + last[s - 1, :, here].astype(jnp.float32)
            out[:, there] = total
            return carry

        lax.fori_loop(0, wide // t, body, 0)
        for (at, _), copy in self.copies.items():
            if at == k:
                copy.wait_send()
        if group is not None:
            for friend in self.friends:
                pl.semaphore_signal(
                    self.free.at[group], inc=1, device_id=friend, device_id_type=MESH
                )

    def reuse(self, group):
        pl.semaphore_wait(self.free.at[group], len(self.friends))


def backward_kernel(sizes, *refs):
    batches, rows, kv_heads, group, used = sizes
    (dy_ref, first_w, out_w, gate_w, up_w, down_w) = refs[:6]
    (q_in, kv_in, log_in, mixed_in, hidden_in, slope_in, silu_in, bias_in, cos_in, sin_in) = refs[6:16]
    (hid_t, h2_t, att_t, nor_t, x_in) = refs[16:21]
    outs = refs[21:36]
    (result_out, grad_out, g_first, g_out, g_gate, g_up, g_down) = outs[:7]
    (hid_s, h2_s, att_s, nor_s, dy_p, gate_p, up_p, dm_p) = outs[7:]
    pre_p, dy1_h = refs[36:38]
    sc = list(refs[38:])
    take = lambda n: [sc.pop(0) for _ in range(n)]
    sets = [take(4) for _ in range(3)]
    down_sets = [take(4) for _ in range(2)]
    gain_set = take(4)
    (lhs_d, lhs, lraw, rhs, acc, part, cot, low_t, queries, grads, pre) = take(11)
    (kv_all, dkv, bias, logs, cos_t, sin_t, dkv_r, dkv_x) = take(8)
    (raw_a, raw_b, w_a, w_b, wd, fac_a, fac_b, dgt, dut, gains, gsum, gcol) = take(12)
    (send, recv, free, x_send, x_recv, t_send, t_recv, load_sem, lhs_sem, store_sem, own_sem, part_sem) = take(12)
    me = Place()
    greet(me)
    tokens, width = cot.shape
    length = kv_all.shape[1]
    features = hidden_in.shape[1]
    wide = dgt.shape[2]
    tiles = features // wide
    scale = HD**-0.5
    sibling = me.device(dc=1)
    f32, bf = jnp.float32, jnp.bfloat16
    r = lhs.shape[0] // (4 * me.Z)
    rd = lhs_d.shape[0] // me.Z
    big = sets[0][0].shape[-1]
    half = features // 2
    d_wide = down_sets[0][0].shape[-1]
    d_rest = width - 2 * d_wide
    chunks = (
        (*down_sets[0], d_wide, "xy", g_down, 0, 4),
        (*down_sets[1], d_wide, "yx", g_down, d_wide, None),
        (*sets[0], half, "xy", g_gate, 0, 0),
        (*sets[1], half, "yx", g_gate, half, 1),
        (*sets[2], half, "xy", g_up, 0, 2),
        (*sets[0], half, "yx", g_up, half, 3),
        (*sets[1], width, "xy", g_out, 0, None),
        (*sets[2], pre.shape[1] - kv_heads * 128, "yx", g_first, 0, None),
        (*sets[0], kv_heads * 128, "xy", g_first, pre.shape[1] - kv_heads * 128, None),
        (*gain_set, 128, "yx", g_first, pre.shape[1], None),
        (*down_sets[0], d_rest, "yx", g_down, 2 * d_wide, None),
    )
    D0, D1, G0, G1, U0, U1, O, Q, KV, GAIN, D2 = range(11)
    comm = Scattering(me, chunks, send, recv, free)

    def over_rows(body, step=64):
        def one(i, carry):
            body(pl.ds(pl.multiple_of(i * step, step), step))
            return carry

        lax.fori_loop(0, tokens // step, one, 0)

    passes = []

    def hand(i, src, dst):
        copy = pltpu.make_async_remote_copy(
            src_ref=src,
            dst_ref=dst,
            send_sem=x_send.at[i],
            recv_sem=x_recv.at[i],
            device_id=sibling,
            device_id_type=MESH,
        )
        copy.start()
        passes.append(copy)
        return copy

    other = lax.rem(me.c + 1, 2)
    got_hid = hand(0, hid_t.at[:, :, :, other], hid_s)
    got_dy = hand(1, dy_ref, dy_p.at[1])
    got_h2 = hand(2, h2_t.at[:, :, :, other], h2_s)
    got_att = hand(3, att_t.at[:, :, :, other], att_s)
    got_nor = hand(4, nor_t.at[:, :, :, other], nor_s)

    def fetch(i, src, dst):
        copy = pltpu.make_async_copy(src, dst, load_sem.at[i])
        copy.start()
        return copy

    stores = []

    def store(i, src, dst):
        copy = pltpu.make_async_copy(src, dst, store_sem.at[i])
        copy.start()
        stores.append(copy)
        return copy

    need_cot = fetch(0, dy_ref, cot)
    own_dy = store(0, dy_ref, dy_p.at[0])
    def block(ref, a, b, order, c=None):
        rel = {order[0]: a, order[1]: b}
        y = lax.rem(me.y + rel["y"], 2)
        x = lax.rem(me.x + rel["x"], 2)
        return ref.at[:, y, x] if c is None else ref.at[:, y, x, c]

    def left_rows(own_t, sib_t, order):
        for side, ref in ((0, own_t), (1, sib_t)):
            loads = []
            for i in range(4):
                src = block(ref, i // 2, i % 2, order, me.c if side == 0 else None)
                copy = pltpu.make_async_copy(src, lraw.at[i], lhs_sem.at[i])
                copy.start()
                loads.append(copy)
            for copy in loads:
                copy.wait()

            def one(i, carry, side=side):
                for j in range(me.Z // 2):
                    piece = lraw[i, 2 * j : 2 * j + 2].astype(f32).reshape(2 * r, tokens)
                    at = pl.multiple_of((i * me.Z + 2 * j) * r, 16)
                    lhs[pl.ds(at, 2 * r), side * tokens : (side + 1) * tokens] = piece.astype(bf)
                return carry

            lax.fori_loop(0, 4, one, 0)

    def product_down(k, base):
        order = chunks[k][5]
        for i in (3, 2, 1, 0):
            loads = []
            for side, ref in ((0, hid_t), (1, hid_s)):
                src = block(ref, i // 2, i % 2, order, me.c if side == 0 else None)
                for z in range(me.Z):
                    copy = pltpu.make_async_copy(
                        src.at[z],
                        lhs_d.at[pl.ds(z * rd, rd), pl.ds(side * tokens, tokens)],
                        lhs_sem.at[side * me.Z + z],
                    )
                    copy.start()
                    loads.append(copy)
            for copy in loads:
                copy.wait()
            product(k, dy_p, base, lhs_d, rd, (i,))
        comm.begin(k)

    def product(k, pair, base, left, depth, blocks=(0, 1, 2, 3)):
        own, wide_k = chunks[k][0], chunks[k][4]
        t = rhs.shape[3] if wide_k % rhs.shape[3] == 0 else 128
        count = wide_k // t
        span = len(blocks)

        def tile(j, slot):
            cols = pl.ds(pl.multiple_of(base + j * t, 128), t)
            return [
                pltpu.make_async_copy(
                    pair.at[side, :, cols],
                    rhs.at[slot, side, :, pl.ds(0, t)],
                    own_sem.at[slot, side],
                )
                for side in range(2)
            ]

        for copy in tile(0, 0):
            copy.start()

        def body(j, carry):
            slot = lax.rem(j, 2)

            @pl.when(j + 1 < count)
            def _():
                for copy in tile(j + 1, lax.rem(j + 1, 2)):
                    copy.start()

            for copy in tile(j, slot):
                copy.wait()
            cols = pl.ds(pl.multiple_of(j * t, 128), t)
            total = plain_dot(left[:, :tokens], rhs[slot, 0, :, :t]) + plain_dot(
                left[:, tokens:], rhs[slot, 1, :, :t]
            )
            total = total.reshape(span, me.Z, depth, t).astype(bf)
            for q, at in enumerate(blocks):
                own[at // 2, at % 2, :, :, cols] = total[q]
            return carry

        lax.fori_loop(0, count, body, 0)

    def load3(i, full, raw, col, size):
        return pltpu.make_async_copy(
            full.at[:, :, pl.ds(col, size)], raw.at[:, :, pl.ds(0, size)], load_sem.at[i]
        )

    def assemble(raw, flat, size):
        n, depth, _ = raw.shape
        pair = 2 * depth

        def one(i, carry):
            piece = raw[pl.ds(2 * i, 2), :, pl.ds(0, size)].astype(f32)
            flat[pl.ds(pl.multiple_of(pair * i, 16), pair), pl.ds(0, size)] = piece.reshape(
                pair, size
            ).astype(bf)
            return carry

        lax.fori_loop(0, n // 2, one, 0)

    def tile_loads(j):
        at = pl.ds(j * wide, wide)
        return [
            pltpu.make_async_copy(down_w.at[at, :], wd, load_sem.at[2]),
            pltpu.make_async_copy(slope_in.at[:, at], fac_a, load_sem.at[3]),
            pltpu.make_async_copy(silu_in.at[:, at], fac_b, load_sem.at[4]),
        ]

    gather_tiles = lambda j: [
        load3(5, gate_w, raw_a, j * wide, wide),
        load3(6, up_w, raw_b, j * wide, wide),
    ]
    head_pack = load3(7, first_w, raw_a, used, 128)
    head_pack.start()
    head_pack.wait()
    assemble(raw_a, w_a, 128)
    gains[...] = w_a[:, :128].astype(f32).T[:8]
    for copy in tile_loads(0) + gather_tiles(0):
        copy.start()
    need_cot.wait()
    own_dy.wait()
    tile_sends = [None] * tiles
    for j in range(tiles):
        slot = j % 2
        for copy in tile_loads(j):
            copy.wait()
        if j >= 2:
            for copy in tile_sends[j - 2]:
                copy.wait()
        for copy in gather_tiles(j):
            copy.wait()
        assemble(raw_a, w_a, wide)
        assemble(raw_b, w_b, wide)
        if j + 1 < tiles:
            for copy in gather_tiles(j + 1):
                copy.start()

        def units(at, slot=slot, j=j):
            grad_hidden = dot_t(cot[at, :], wd[...])
            dg = (grad_hidden * fac_a[at, :].astype(f32)).astype(bf)
            du = (grad_hidden * fac_b[at, :].astype(f32)).astype(bf)
            dgt[slot, at, :] = dg
            dut[slot, at, :] = du
            piece = dot_t(dg, w_a[:, :wide]) + dot_t(du, w_b[:, :wide])
            acc[at, :] = piece if j == 0 else acc[at, :] + piece

        over_rows(units, 256)
        if j + 1 < tiles:
            for copy in tile_loads(j + 1):
                copy.start()
        cols = pl.ds(j * wide, wide)
        sends = []
        for i, (src, dst) in enumerate(((dgt, gate_p), (dut, up_p))):
            here = pltpu.make_async_copy(
                src.at[slot], dst.at[0, :, cols], store_sem.at[1 + 2 * slot + i]
            )
            there = pltpu.make_async_remote_copy(
                src_ref=src.at[slot],
                dst_ref=dst.at[1, :, cols],
                send_sem=t_send.at[2 * j + i],
                recv_sem=t_recv.at[2 * j + i],
                device_id=sibling,
                device_id_type=MESH,
            )
            here.start()
            there.start()
            passes.append(there)
            sends.append(here)
        tile_sends[j] = [_Both(here, there) for here, there in zip(sends, passes[-2:])]
        if j == 1:
            got_hid.wait_recv()
            got_dy.wait_recv()
            product_down(D0, 0)
        if j == 3:
            product_down(D1, d_wide)
    for j in (tiles - 2, tiles - 1):
        for copy in tile_sends[j]:
            copy.wait()
    arrived = [p for p in passes[5:]]
    for copy in arrived:
        copy.wait_recv()
    got_h2.wait_recv()
    left_rows(h2_t, h2_s, "xy")
    product(G0, gate_p, 0, lhs, r)
    comm.begin(G0)
    product(U0, up_p, 0, lhs, r)
    comm.begin(U0)
    comm.first(D0)
    left_rows(h2_t, h2_s, "yx")
    product(G1, gate_p, half, lhs, r)
    comm.begin(G1)
    comm.first(D1)

    gsum[...] = jnp.zeros_like(gsum)

    def stream(src, body):
        def piece(i, slot):
            at = pl.ds(pl.multiple_of(i * 64, 64), 64)
            return pltpu.make_async_copy(src.at[at, :], part.at[slot], part_sem.at[slot])

        piece(0, 0).start()

        def one(i, carry):
            slot = lax.rem(i, 2)

            @pl.when(i + 1 < tokens // 64)
            def _():
                piece(i + 1, lax.rem(i + 1, 2)).start()

            piece(i, slot).wait()
            body(pl.ds(pl.multiple_of(i * 64, 64), 64), part[slot])
            return carry

        lax.fori_loop(0, tokens // 64, one, 0)

    def norm_two(at, y):
        inverse = lax.rsqrt(jnp.mean(y * y, -1, keepdims=True) + EPSILON)
        grad = acc[at, :]
        gsum[1:2, :] += jnp.sum(grad * (y * inverse), 0, keepdims=True)
        e = grad * gains[1:2, :]
        dy1 = cot[at, :].astype(f32) + inverse * (
            e - y * (inverse * inverse) * jnp.mean(e * y, -1, keepdims=True)
        )
        acc[at, :] = dy1
        low_t[at, :] = dy1.astype(bf)

    stream(mixed_in, norm_two)
    keep_dy1 = pltpu.make_async_copy(acc, dy1_h, part_sem.at[2])
    keep_dy1.start()
    own_low = store(5, low_t, dm_p.at[0])
    got_low = hand(5, low_t, dm_p.at[1])

    need_q = fetch(0, q_in, queries)
    need_kv = fetch(1, kv_in, kv_all)
    need = [
        fetch(8, bias_in, bias),
        fetch(9, log_in, logs),
        fetch(10, cos_in, cos_t),
        fetch(11, sin_in, sin_t),
    ]
    tile_w = raw_a.shape[2]
    steps = width // tile_w
    load3(5, out_w, raw_a, 0, tile_w).start()
    for j in range(steps):
        raw, flat = ((raw_a, w_a), (raw_b, w_b))[j % 2]
        if j + 1 < steps:
            load3(5 + (j + 1) % 2, out_w, (raw_b, raw_a)[j % 2], (j + 1) * tile_w, tile_w).start()
        load3(5 + j % 2, out_w, raw, j * tile_w, tile_w).wait()
        assemble(raw, flat, tile_w)

    def back_out(at):
        grads[at, :] = (
            dot_t(low_t[at, :tile_w], w_a[...]) + dot_t(low_t[at, tile_w:], w_b[...])
        ).astype(bf)

    over_rows(back_out, 256)
    comm.second(D0)
    comm.first(G0)
    comm.second(D1)

    need_q.wait()
    need_kv.wait()
    for copy in need:
        copy.wait()
    lanes = lax.broadcasted_iota(jnp.int32, (rows, 128), 1)
    sides_mask = lane_masks(rows)

    def head(i, carry):
        b = i // kv_heads
        h = lax.rem(i, kv_heads)
        at = pl.ds(pl.multiple_of(b * rows, 256), rows)
        here = pl.ds(pl.multiple_of(h * 128, 128), 128)
        kv = kv_all[b, :, here]
        sides = (kv, swapped(kv))
        shift = bias[at, :].astype(f32)
        key_sum = jnp.zeros((128, length), f32)
        value_sum = jnp.zeros((128, length), f32)
        log_piece = logs[at, :]
        for pair in range(group // 2):
            cols = pl.ds(pl.multiple_of(h * group * HD + pair * 128, 128), 128)
            q = queries[at, cols]
            do = grads[at, cols]
            found = []
            for side in range(2):
                q_half = q * sides_mask[side]
                do_half = do * sides_mask[side]
                head_at = pair * 2 + side
                log_total = jnp.sum(
                    jnp.where(lanes == h * group + head_at, log_piece, 0.0), -1, keepdims=True
                )
                probs = jnp.exp(dot_t(q_half, sides[side]) + shift - log_total)
                grad_probs = dot_t(do_half, sides[1 - side])
                row_dot = jnp.sum(probs * grad_probs, -1, keepdims=True)
                grad_scores = (probs * (grad_probs - row_dot)).astype(bf)
                found.append(plain_dot(grad_scores, sides[side]))
                key_sum = key_sum + left_dot(q_half, grad_scores)
                value_sum = value_sum + left_dot(do_half, probs.astype(bf))
            dq = jnp.where(lanes < HD, found[0], found[1])
            dq = dq * cos_t[0, at, :] - swap_halves(dq) * sin_t[0, at, :]
            pre[at, cols] = dq.astype(bf)
        both = jnp.concatenate(
            [key_sum[:HD] + key_sum[HD:], value_sum[:HD] + value_sum[HD:]], 0
        )
        dkv[b, :, here] = both.T.astype(bf)
        return carry

    count = batches * kv_heads
    lax.fori_loop(0, 2, head, 0)
    own_low.wait()
    got_low.wait_recv()
    comm.first(U0)
    comm.second(G0)
    comm.third(D0)
    lax.fori_loop(2, 4, head, 0)
    comm.first(G1)
    comm.third(D1)
    comm.third(G0)
    lax.fori_loop(4, 6, head, 0)
    comm.reuse(4)
    product_down(D2, 2 * d_wide)
    comm.reuse(0)
    left_rows(h2_t, h2_s, "yx")
    product(U1, up_p, half, lhs, r)
    comm.begin(U1)
    comm.second(U0)
    comm.second(G1)
    lax.fori_loop(6, 8, head, 0)
    comm.third(U0)
    comm.third(G1)
    lax.fori_loop(8, count, head, 0)
    comm.first(D2)

    def portion(dx, c):
        row = (lax.rem(me.x + dx, 2) * 2 + c) * rows
        return pl.ds(pl.multiple_of(row, 256), rows)

    to_c = [hand(6 + dx, dkv.at[:, portion(dx, other), :], dkv_r.at[dx]) for dx in (1, 0)]
    comm.reuse(1)
    got_att.wait_recv()
    left_rows(att_t, att_s, "xy")
    product(O, dm_p, 0, lhs, r)
    comm.begin(O)

    def gather_portion(dx):
        place = portion(dx, me.c)
        for b in range(batches):

            def body(j, carry, b=b):
                at = pl.ds(pl.multiple_of(j * 64, 64), 64)
                there = pl.ds(pl.multiple_of(place.start + j * 64, 64), 64)
                total = dkv_r[dx, b, at, :].astype(f32) + dkv[b, there, :].astype(f32)
                dkv_r[dx, b, at, :] = total.astype(bf)
                return carry

            lax.fori_loop(0, rows // 64, body, 0)

    to_c[0].wait_recv()
    gather_portion(1)
    to_x = pltpu.make_async_remote_copy(
        src_ref=dkv_r.at[1],
        dst_ref=dkv_x,
        send_sem=x_send.at[8],
        recv_sem=x_recv.at[8],
        device_id=me.device(dx=1),
        device_id_type=MESH,
    )
    to_x.start()
    passes.append(to_x)
    query_wide = pre.shape[1] - kv_heads * 128
    own_q = store(6, pre.at[:, pl.ds(0, query_wide)], pre_p.at[0, :, pl.ds(0, query_wide)])
    got_q = hand(9, pre.at[:, pl.ds(0, query_wide)], pre_p.at[1, :, pl.ds(0, query_wide)])
    to_c[1].wait_recv()
    gather_portion(0)
    comm.first(U1)
    comm.second(D2)
    comm.reuse(2)
    got_nor.wait_recv()
    left_rows(nor_t, nor_s, "yx")
    own_q.wait()
    got_q.wait_recv()
    product(Q, pre_p, 0, lhs, r)
    comm.begin(Q)
    comm.first(O)
    comm.second(U1)
    to_x.wait_recv()
    for b in range(batches):

        def merge(j, carry, b=b):
            at = pl.ds(pl.multiple_of(j * 64, 64), 64)
            token = pl.ds(pl.multiple_of(b * rows + j * 64, 64), 64)
            for h in range(kv_heads):
                cols = slice(h * 128, (h + 1) * 128)
                total = dkv_r[0, b, at, cols].astype(f32) + dkv_x[b, at, cols].astype(f32)
                total = total * cos_t[1, token, :] - swap_halves(total) * sin_t[1, token, :]
                pre[token, query_wide + h * 128 : query_wide + (h + 1) * 128] = total.astype(bf)
            return carry

        lax.fori_loop(0, rows // 64, merge, 0)
    rest = pl.ds(query_wide, kv_heads * 128)
    own_kv = store(7, pre.at[:, rest], pre_p.at[0, :, rest])
    got_kv = hand(10, pre.at[:, rest], pre_p.at[1, :, rest])

    need_x = fetch(0, x_in, cot)
    keep_dy1.wait()
    steps = pre.shape[1] // tile_w
    load3(5, first_w, raw_a, 0, tile_w).start()
    for j in range(steps):
        raw, flat = ((raw_a, w_a), (raw_b, w_b))[j % 2]
        if j + 1 < steps:
            load3(5 + (j + 1) % 2, first_w, (raw_b, raw_a)[j % 2], (j + 1) * tile_w, tile_w).start()
        load3(5 + j % 2, first_w, raw, j * tile_w, tile_w).wait()
        assemble(raw, flat, tile_w)

        def back_in(at, j=j, flat=flat):
            piece = dot_t(pre[at, j * tile_w : (j + 1) * tile_w], flat[...])
            acc[at, :] = piece if j == 0 else acc[at, :] + piece

        over_rows(back_in, 256)
    comm.third(U1)
    comm.third(D2)
    comm.reuse(3)
    own_kv.wait()
    got_kv.wait_recv()
    left_rows(nor_t, nor_s, "xy")
    product(KV, pre_p, query_wide, lhs, r)
    comm.begin(KV)
    need_x.wait()

    def norm_one(at, dy1):
        x = cot[at, :].astype(f32)
        inverse = lax.rsqrt(jnp.mean(x * x, -1, keepdims=True) + EPSILON)
        grad = acc[at, :]
        gsum[0:1, :] += jnp.sum(grad * (x * inverse), 0, keepdims=True)
        e = grad * gains[0:1, :]
        total = dy1 + inverse * (
            e - x * (inverse * inverse) * jnp.mean(e * x, -1, keepdims=True)
        )
        queries[at, :] = total.astype(bf)

    stream(dy1_h, norm_one)
    store(8, queries, grad_out)
    comm.first(Q)
    comm.second(O)

    gsib = gain_set[0]
    columns = jnp.concatenate([gsum[...], jnp.zeros((120, width), f32)], 0).T
    gcol[0] = columns.reshape(gcol.shape[1:]).astype(bf)
    got_gain = hand(11, gcol.at[0], gcol.at[1])
    comm.first(KV)
    got_gain.wait_recv()
    for a in range(2):
        for b in range(2):
            y = lax.rem(me.y + b, 2)
            x = lax.rem(me.x + a, 2)
            if chunks[GAIN][5] == "yx":
                y, x = lax.rem(me.y + a, 2), lax.rem(me.x + b, 2)
            for z in range(me.Z):
                at = ((z * 2 + y) * 2 + x) * 2 + me.c
                gsib[a, b, z] = gcol[0, at] + gcol[1, at]
    comm.begin(GAIN)
    comm.second(Q)

    need_mixed = fetch(1, mixed_in, acc)
    need_mixed.wait()
    for j in range(tiles):
        at = pl.ds(j * wide, wide)
        wd_load = pltpu.make_async_copy(down_w.at[at, :], wd, load_sem.at[2])
        hidden_load = pltpu.make_async_copy(hidden_in.at[:, at], fac_a, load_sem.at[3])
        wd_load.start()
        hidden_load.start()
        wd_load.wait()
        hidden_load.wait()

        def add_down(at):
            acc[at, :] = acc[at, :] + plain_dot(fac_a[at, :], wd[...])

        over_rows(add_down, 256)
        if j == 1:
            comm.first(GAIN)
            comm.third(O)
        if j == 2:
            comm.second(KV)
        if j == 4:
            comm.third(Q)
            comm.second(GAIN)

    def round_result(at):
        low_t[at, :] = acc[at, :].astype(bf)

    got_low.wait_send()
    over_rows(round_result)
    store(9, low_t, result_out)
    comm.third(KV)
    comm.third(GAIN)
    for copy in passes:
        if copy is not got_low and not any(copy is p for p in arrived):
            copy.wait_send()
    for copy in stores:
        if not any(copy is p for p in (own_dy, own_low, own_q, own_kv)):
            copy.wait()


class _Both:
    def __init__(self, here, there):
        self.here, self.there = here, there

    def wait(self):
        self.here.wait()
        self.there.wait_send()


def backward(saved, transposed, dy, x, kv_heads, group, batches):
    first_w, out_w, gate_w, up_w, down_w = saved[:5]
    queries, both_all, _, logs, mixed, _ = saved[5:11]
    hidden, slope, silu, bias, cos_tables, sin_tables = saved[11:]
    tokens, width = x.shape
    rows = tokens // batches
    Z = lax.axis_size("dp") // 2
    X = lax.axis_size("fsdp") // 2
    n, r, first_wide = first_w.shape
    rd = down_w.shape[1]
    key_wide = kv_heads * 128
    query_wide = kv_heads * group * HD
    used = query_wide + key_wide
    length = both_all.shape[1]
    features = hidden.shape[1]
    half = features // 2
    d_wide = width * 2 // 5 // 256 * 256
    wide, t = 512, 256
    bf, f32 = jnp.bfloat16, jnp.float32
    shape = jax.ShapeDtypeStruct
    vmem, dma = pltpu.VMEM, pltpu.SemaphoreType.DMA

    def four(depth, size):
        return [
            vmem((2, 2, Z, depth, size), bf),
            vmem((2, Z, depth, size), bf),
            vmem((Z, depth, size), bf),
            vmem((Z - 1, depth, size), bf),
        ]

    outs = [
        shape((tokens, width), bf),
        shape((tokens, width), bf),
        shape((r, first_wide), f32),
        shape((r, width), f32),
        shape((r, features), f32),
        shape((r, features), f32),
        shape((rd, width), f32),
        shape((Z, 2, X, rd, tokens), bf),
        shape((Z, 2, X, r, tokens), bf),
        shape((Z, 2, X, r, tokens), bf),
        shape((Z, 2, X, r, tokens), bf),
        shape((2, tokens, width), bf),
        shape((2, tokens, features), bf),
        shape((2, tokens, features), bf),
        shape((2, tokens, width), bf),
        shape((2, tokens, used), bf),
        shape((tokens, width), f32),
    ]
    any_space = pl.BlockSpec(memory_space=pl.ANY)
    in_vmem = pl.BlockSpec(memory_space=pltpu.VMEM)
    scratch = sum([four(r, half) for _ in range(3)], [])
    scratch += four(rd, d_wide) + four(rd, d_wide) + four(r, 128)
    scratch += [
        vmem((Z * rd, 2 * tokens), bf),
        vmem((4 * Z * r, 2 * tokens), bf),
        vmem((4, Z, r, tokens), bf),
        vmem((2, 2, tokens, t), bf),
        vmem((tokens, width), f32),
        vmem((2, 64, width), f32),
        vmem((tokens, width), bf),
        vmem((tokens, width), bf),
        vmem((tokens, query_wide), bf),
        vmem((tokens, query_wide), bf),
        vmem((tokens, used), bf),
        vmem((batches, length, key_wide), bf),
        vmem((batches, length, key_wide), bf),
        vmem((tokens, length), bias.dtype),
        vmem((tokens, 128), f32),
        vmem((2, tokens, 128), f32),
        vmem((2, tokens, 128), f32),
        vmem((2, batches, rows, key_wide), bf),
        vmem((batches, rows, key_wide), bf),
        vmem((n, r, key_wide), bf),
        vmem((n, r, key_wide), bf),
        vmem((width, key_wide), bf),
        vmem((width, key_wide), bf),
        vmem((wide, width), bf),
        vmem((tokens, wide), bf),
        vmem((tokens, wide), bf),
        vmem((2, tokens, wide), bf),
        vmem((2, tokens, wide), bf),
        vmem((8, width), f32),
        vmem((8, width), f32),
        vmem((2, n, r, 128), bf),
        dma((11, 2 + Z)),
        dma((11, 2 + Z)),
        pltpu.SemaphoreType.REGULAR((5,)),
        dma((12,)),
        dma((12,)),
        dma((2 * (features // wide),)),
        dma((2 * (features // wide),)),
        dma((12,)),
        dma((8 * Z,)),
        dma((10,)),
        dma((2, 2)),
        dma((3,)),
    ]
    return pl.pallas_call(
        functools.partial(backward_kernel, (batches, rows, kv_heads, group, used)),
        out_shape=outs,
        in_specs=[any_space] * 21,
        out_specs=[any_space] * 2 + [in_vmem] * 5 + [any_space] * 10,
        scratch_shapes=scratch,
        compiler_params=pltpu.CompilerParams(
            collective_id=2, has_side_effects=True, vmem_limit_bytes=63 * 2**20
        ),
    )(
        dy,
        first_w,
        out_w,
        gate_w,
        up_w,
        down_w.reshape(-1, width),
        queries,
        both_all,
        logs,
        mixed,
        hidden,
        slope,
        silu,
        bias,
        cos_tables,
        sin_tables,
        *transposed,
        x,
    )


def half_of(full):
    return full.astype(jnp.bfloat16)


def rotary_pairs(places, tokens, score_scale):
    cos_table, sin_table = rope_tables(places.reshape(tokens))
    ones, zeros = jnp.ones((tokens, HD), jnp.float32), jnp.zeros((tokens, HD), jnp.float32)
    cos_pair = jnp.concatenate([cos_table, cos_table], -1)
    sin_pair = jnp.concatenate([-sin_table, sin_table], -1)
    cos_tables = jnp.stack(
        [
            jnp.concatenate([cos_pair, cos_pair], -1) * score_scale,
            jnp.concatenate([cos_pair, ones], -1),
        ]
    )
    sin_tables = jnp.stack(
        [
            jnp.concatenate([sin_pair, sin_pair], -1) * score_scale,
            jnp.concatenate([sin_pair, zeros], -1),
        ]
    )
    return cos_tables, sin_tables


def forward_plain(shards, x, places, kv_heads, group, batches):
    tokens = x.shape[0]
    rows = tokens // batches
    length = rows * lax.axis_size("fsdp")
    query_features = kv_heads * group * HD
    used = query_features + kv_heads * 128
    fulls = gather(shards, ("yxc", "xyc", "yxc", "xyc", "yxc"), 1, 5)
    first_pack, out_full, gate_full, up_full, _ = (f.reshape(-1, f.shape[-1]) for f in fulls)
    gains = first_pack[:, used : used + 2].astype(jnp.float32).T
    query_index = lax.axis_index("fsdp") * rows + jnp.arange(rows, dtype=jnp.int32)
    key_index = jnp.arange(length, dtype=jnp.int32)
    x_float = x.astype(jnp.float32)
    cos_tables, sin_tables = rotary_pairs(places, tokens, HD**-0.5)
    doc_start = query_index[None, :] - places.reshape(batches, rows)
    allowed = (key_index[None, None, :] <= query_index[None, :, None]) & (
        key_index[None, None, :] >= doc_start[:, :, None]
    )
    bias = jnp.where(allowed, 0.0, NEGATIVE)
    attn_inverse = lax.rsqrt(jnp.mean(x_float * x_float, -1, keepdims=True) + EPSILON)
    normed = (x_float * attn_inverse * gains[0]).astype(jnp.bfloat16)
    projected = project(normed, first_pack[:, :used], cos_tables, sin_tables, kv_heads * 128)
    both_rows = projected[:, query_features:].reshape(batches, rows, -1)
    both_all = lax.all_gather(both_rows, "fsdp", axis=1, tiled=True)
    attended, logs = attend(projected, both_all, bias, kv_heads, group)
    mixed = x_float + plain_dot(attended, out_full)
    mlp_inverse = lax.rsqrt(jnp.mean(mixed * mixed, -1, keepdims=True) + EPSILON)
    normed_mlp = (mixed * mlp_inverse * gains[1]).astype(jnp.bfloat16)
    gate_pre = plain_dot(normed_mlp, gate_full)
    up_proj = plain_dot(normed_mlp, up_full)
    gate_sig = jax.nn.sigmoid(gate_pre)
    silu = gate_pre * gate_sig
    slope = up_proj * gate_sig * (1.0 + gate_pre * (1.0 - gate_sig))
    low = jnp.bfloat16
    return list(fulls) + [
        projected[:, :query_features],
        both_all,
        attended,
        logs,
        mixed,
        normed_mlp,
        (silu * up_proj).astype(low),
        slope.astype(low),
        silu.astype(low),
        bias.reshape(tokens, length),
        cos_tables,
        sin_tables,
    ]


def backward_plain(saved, cotangent, x_low, kv_heads, group, batches):
    tokens, width = x_low.shape
    rows = tokens // batches
    key_features = kv_heads * HD
    query_features = kv_heads * group * HD
    used = query_features + 2 * key_features
    x_float = x_low.astype(jnp.float32)
    first_pack, out_full, gate_full, up_full, down_full = (
        f.reshape(-1, f.shape[-1]) for f in saved[:5]
    )
    queries, both_all, attended, logs, mixed, normed_mlp = saved[5:11]
    hidden, slope, silu, bias, cos_tables, sin_tables = saved[11:]
    projection = first_pack[:, :used]
    gains = first_pack[:, used : used + 2].astype(jnp.float32).T
    attn_gain_f = gains[0]
    mlp_gain_f = gains[1]
    attn_inverse = lax.rsqrt(jnp.mean(x_float * x_float, -1, keepdims=True) + EPSILON)
    normed = (x_float * attn_inverse * attn_gain_f).astype(jnp.bfloat16)
    mlp_inverse = lax.rsqrt(jnp.mean(mixed * mixed, -1, keepdims=True) + EPSILON)
    output = (mixed + plain_dot(hidden, down_full)).astype(jnp.bfloat16)

    cot_low = cotangent
    cot_float = cot_low.astype(jnp.float32)
    grad_down = half_of(left_dot(hidden, cot_low))
    grad_hidden = right_dot(cot_low, down_full)
    grad_gate_pre = (grad_hidden * slope.astype(jnp.float32)).astype(jnp.bfloat16)
    grad_up_pre = (grad_hidden * silu.astype(jnp.float32)).astype(jnp.bfloat16)
    grad_gate = half_of(left_dot(normed_mlp, grad_gate_pre))
    grad_up = half_of(left_dot(normed_mlp, grad_up_pre))
    grad_normed_mlp = right_dot(grad_gate_pre, gate_full) + right_dot(grad_up_pre, up_full)
    grad_mlp_gain = jnp.sum(grad_normed_mlp * mixed * mlp_inverse, 0)
    grad_mixed = cot_float + norm_back(grad_normed_mlp * mlp_gain_f, mixed, mlp_inverse)
    grad_mixed_low = grad_mixed.astype(jnp.bfloat16)
    grad_out = half_of(left_dot(attended, grad_mixed_low))
    grad_attended = right_dot(grad_mixed_low, out_full).astype(jnp.bfloat16)
    grad_query_pre, portions = attend_back(
        queries,
        grad_attended,
        both_all,
        bias.reshape(batches, rows, -1),
        logs,
        cos_tables,
        sin_tables,
        group,
    )
    sums = lax.psum_scatter(portions, "fsdp", scatter_dimension=1, tiled=True)
    sums = sums.astype(jnp.float32).reshape(tokens, kv_heads, 128)
    turned = jnp.concatenate([sums[..., 32:64], sums[..., :32], sums[..., 64:]], -1)
    grad_pair_pre = (sums * cos_tables[1][:, None] - turned * sin_tables[1][:, None]).astype(
        jnp.bfloat16
    )
    grad_pre = jnp.concatenate(
        [grad_query_pre, grad_pair_pre.reshape(tokens, 2 * key_features)], -1
    )
    grad_projection = left_dot(normed, grad_pre)
    grad_normed = right_dot(grad_pre, projection)
    grad_attn_gain = jnp.sum(grad_normed * x_float * attn_inverse, 0)
    grad_input = grad_mixed + norm_back(grad_normed * attn_gain_f, x_float, attn_inverse)
    gain_columns = jnp.stack([grad_attn_gain, grad_mlp_gain], -1)
    gain_columns = jnp.pad(gain_columns, ((0, 0), (0, 126)))
    grad_first = half_of(jnp.concatenate([grad_projection, gain_columns], 1))
    grad_down, grad_gate, grad_up, grad_out, last = scatter(
        (grad_down, grad_gate, grad_up, grad_out, grad_first), ("xy", "yx", "xy", "yx", "xy"), 2
    )
    return (
        output,
        grad_input.astype(jnp.bfloat16),
        last,
        grad_out,
        grad_gate,
        grad_up,
        grad_down,
    )


def on_device(
    inputs,
    positions,
    cotangent,
    attn_gain,
    w_query,
    key_matrix,
    value_matrix,
    w_out,
    mlp_gain,
    w_gate,
    w_up,
    w_down,
):
    batches, _, rows, width = inputs.shape
    shard = w_query.shape[0]
    query_features = w_query.shape[1]
    key_features = key_matrix.shape[1]
    kv_heads = key_features // HD
    group = query_features // key_features
    tokens = batches * rows
    used = query_features + 2 * key_features

    extras = jnp.zeros((shard, 128), jnp.bfloat16)
    extras = extras.at[:, 0].set(attn_gain).at[:, 1].set(mlp_gain)
    pairs = jnp.concatenate(
        [key_matrix.reshape(shard, kv_heads, HD), value_matrix.reshape(shard, kv_heads, HD)], -1
    )
    first_shard = jnp.concatenate([w_query, pairs.reshape(shard, -1), extras], axis=1)
    shards = (first_shard, w_out, w_gate, w_up, w_down)
    x_low = inputs.reshape(tokens, width)
    cot_low = cotangent.reshape(tokens, width)
    fits = shard % 8 == 0 and lax.axis_size("fsdp") == 4 and rows % 256 == 0
    saved = (forward if fits else forward_plain)(
        shards, x_low, positions.reshape(tokens, 1), kv_heads, group, batches
    )
    if fits:
        x_float = x_low.astype(jnp.float32)
        attn_inverse = lax.rsqrt(jnp.mean(x_float * x_float, -1, keepdims=True) + EPSILON)
        gain = saved[0].reshape(width, -1)[:, used].astype(jnp.float32)
        normed = (x_float * attn_inverse * gain).astype(jnp.bfloat16)
        by_place = (lax.axis_size("dp") // 2, 2, lax.axis_size("fsdp") // 2, 2, -1, tokens)
        transposed = [
            t.T.reshape(by_place) for t in (saved[11], saved[10], saved[7], normed)
        ]
        found = backward(saved, transposed, cot_low, x_low, kv_heads, group, batches)
    else:
        found = backward_plain(saved, cot_low, x_low, kv_heads, group, batches)
    output, grad_input, last, grad_out, grad_gate, grad_up, grad_down = found[:7]
    last_pairs = last[:, query_features:used].reshape(shard, kv_heads, 2, HD)
    return (
        output.reshape(inputs.shape),
        grad_input.reshape(inputs.shape),
        last[:, used],
        last[:, :query_features],
        last_pairs[:, :, 0].reshape(shard, key_features),
        last_pairs[:, :, 1].reshape(shard, key_features),
        grad_out,
        last[:, used + 1],
        grad_gate,
        grad_up,
        grad_down,
    )


def solution(mesh):
    tokens = P(None, "dp", "fsdp", None)
    vector = P(BOTH)
    matrix = P(BOTH, None)
    weights = (vector, matrix, matrix, matrix, matrix, vector, matrix, matrix, matrix)
    return jax.shard_map(
        on_device,
        mesh=mesh,
        in_specs=(tokens, P(None, "dp", "fsdp"), tokens) + weights,
        out_specs=(tokens, tokens) + weights,
        check_vma=False,
    )
```

```python
import functools

import jax
import jax.numpy as jnp
from jax import lax
from jax.experimental import pallas as pl
from jax.experimental.pallas import tpu as pltpu
from jax.sharding import PartitionSpec as P

HD = 64
EPSILON = 1e-05
NEGATIVE = -1e30
ROPE_BASE = 10000.0
BOTH = ("dp", "fsdp")


def rope_tables(places):
    half = HD // 2
    freqs = ROPE_BASE ** (-jnp.arange(half).astype(jnp.float32) / half)
    angles = places.astype(jnp.float32)[:, None] * freqs[None, :]
    return (jnp.cos(angles), jnp.sin(angles))


def plain_dot(left, right):
    return jnp.dot(left, right, preferred_element_type=jnp.float32)


def left_dot(left, right):
    return lax.dot_general(
        left, right, (((0,), (0,)), ((), ())), preferred_element_type=jnp.float32
    )


def right_dot(left, right):
    return lax.dot_general(
        left, right, (((1,), (1,)), ((), ())), preferred_element_type=jnp.float32
    )


def norm_back(grad_normed, inputs_float, inverse):
    return inverse * (
        grad_normed
        - inputs_float * inverse * inverse * jnp.mean(grad_normed * inputs_float, -1, keepdims=True)
    )


class Place:
    def __init__(self):
        self.Z=lax.axis_size("dp")//2; self.X=lax.axis_size("fsdp")//2
        dp=lax.axis_index("dp"); fs=lax.axis_index("fsdp")
        self.z=dp//2; self.y=dp%2; self.x=fs//2; self.c=fs%2
    def device(self,s=0,dy=0,dx=0,dc=0):
        return (lax.rem(self.z+s,self.Z)*2+lax.rem(self.y+dy,2), lax.rem(self.x+dx,self.X)*2+lax.rem(self.c+dc,2))
    def slot(self,s,dy,dx,dc):
        return ((lax.rem(self.z+self.Z-s,self.Z)*2+lax.rem(self.y+dy,2))*self.X+lax.rem(self.x+dx,self.X))*2+lax.rem(self.c+dc,2)

MESH = pl.DeviceIdType.MESH

def greet(me):
    barrier=pltpu.get_barrier_semaphore()
    friends=[me.device(s=s) for s in range(1,me.Z)]+[me.device(dy=1),me.device(dx=1),me.device(dc=1)]
    for f in friends:
        pl.semaphore_signal(barrier,inc=1,device_id=f,device_id_type=MESH)
    pl.semaphore_wait(barrier,len(friends))

def gather_kernel(Z, orders, ahead, *refs):
    K=len(orders)
    shards=refs[:K]; outs=refs[K:2*K]; local,send,recv=refs[2*K:]
    me=Place()
    greet(me)
    dims={"y":1,"x":2,"c":3}
    def sem(rel):
        return ((rel[0]*2+rel[1])*2+rel[2])*2+rel[3]
    started=[]
    def start(k,rel,to):
        if isinstance(to,int):
            target=me.device(s=to); landed=(to,0,0,0)
        else:
            landed=list(rel); landed[dims[to]]=1; landed=tuple(landed)
            target=me.device(**{"d"+to:1})
        slot=me.slot(*rel)
        src=shards[k] if rel==(0,0,0,0) else outs[k].at[slot]
        cp=pltpu.make_async_remote_copy(src_ref=src,dst_ref=outs[k].at[slot],send_sem=send.at[k,sem(landed)],recv_sem=recv.at[k,sem(landed)],device_id=target,device_id_type=MESH)
        cp.start()
        table[(k,landed)]=cp
    table={}
    own=[]
    def first(k):
        cp=pltpu.make_async_copy(shards[k],outs[k].at[me.slot(0,0,0,0)],local.at[k]); cp.start(); own.append(cp)
        for s in range(1,Z): start(k,(0,0,0,0),s)
        for d in orders[k]: start(k,(0,0,0,0),d)
    def arrive(k,rel,rest):
        table[(k,rel)].wait_recv()
        for d in rest: start(k,rel,d)
    def rel_of(s,o,a,b=0,c=0):
        r=[s,0,0,0]; r[dims[o[0]]]=a; r[dims[o[1]]]=b; r[dims[o[2]]]=c
        return tuple(r)
    for k in range(min(ahead,K)): first(k)
    for t in range(K+3):
        if t+ahead<K: first(t+ahead)
        k=t
        if k<K:
            o=orders[k]
            for s in range(1,Z): arrive(k,rel_of(s,o,0),o)
        k=t-1
        if 0<=k<K:
            o=orders[k]
            for s in range(Z): arrive(k,rel_of(s,o,1),o[1:])
        k=t-2
        if 0<=k<K:
            o=orders[k]
            for s in range(Z):
                for a in range(2): arrive(k,rel_of(s,o,a,1),o[2:])
        k=t-3
        if 0<=k<K:
            o=orders[k]
            for s in range(Z):
                for a in range(2):
                    for b in range(2): arrive(k,rel_of(s,o,a,b,1),"")
    for cp in own: cp.wait()
    for cp in table.values(): cp.wait_send()

def gather(shards, orders, cid, ahead=2):
    n=lax.axis_size("dp")*lax.axis_size("fsdp"); Z=lax.axis_size("dp")//2; K=len(shards)
    return pl.pallas_call(functools.partial(gather_kernel,Z,orders,ahead),
        out_shape=[jax.ShapeDtypeStruct((n,)+s.shape,s.dtype) for s in shards],
        in_specs=[pl.BlockSpec(memory_space=pl.ANY)]*K,
        out_specs=[pl.BlockSpec(memory_space=pl.ANY)]*K,
        scratch_shapes=[pltpu.SemaphoreType.DMA((K,)),pltpu.SemaphoreType.DMA((K,8*Z)),pltpu.SemaphoreType.DMA((K,8*Z))],
        compiler_params=pltpu.CompilerParams(collective_id=cid,has_side_effects=True))(*shards)


class Gathering:
    def __init__(self, me, chunks, local, send, recv):
        self.me, self.chunks = me, chunks
        self.local, self.send, self.recv = local, send, recv
        self.table, self.own = {}, []

    def start(self, k, rel, to):
        shard, full, cols, _ = self.chunks[k]
        me = self.me
        if isinstance(to, int):
            target, landed = me.device(s=to), (to, 0, 0, 0)
        else:
            landed = list(rel)
            landed["zyxc".index(to)] = 1
            landed = tuple(landed)
            target = me.device(**{"d" + to: 1})
        slot = me.slot(*rel)
        here = full.at[slot, :, cols]
        at = ((landed[0] * 2 + landed[1]) * 2 + landed[2]) * 2 + landed[3]
        copy = pltpu.make_async_remote_copy(
            src_ref=shard.at[:, cols] if rel == (0, 0, 0, 0) else here,
            dst_ref=here,
            send_sem=self.send.at[k, at],
            recv_sem=self.recv.at[k, at],
            device_id=target,
            device_id_type=MESH,
        )
        copy.start()
        self.table[(k, landed)] = copy

    def begin(self, k):
        shard, full, cols, order = self.chunks[k]
        copy = pltpu.make_async_copy(
            shard.at[:, cols], full.at[self.me.slot(0, 0, 0, 0), :, cols], self.local.at[k]
        )
        copy.start()
        self.own.append((k, copy))
        for s in range(1, self.me.Z):
            self.start(k, (0, 0, 0, 0), s)
        for d in order:
            self.start(k, (0, 0, 0, 0), d)

    def step(self, k, stage):
        order = self.chunks[k][3]
        where = ["zyxc".index(d) for d in order]
        for s in range(1 if stage == 0 else 0, self.me.Z):
            for bits in range(1 << max(stage - 1, 0)):
                rel = [s, 0, 0, 0]
                for i in range(stage - 1):
                    rel[where[i]] = bits >> i & 1
                if stage:
                    rel[where[stage - 1]] = 1
                rel = tuple(rel)
                self.table[(k, rel)].wait_recv()
                for d in order[stage:]:
                    self.start(k, rel, d)
        if stage == 3:
            for at, copy in self.own:
                if at == k:
                    copy.wait()

    def finish(self):
        for copy in self.table.values():
            copy.wait_send()


def forward_kernel(sizes, *refs):
    batches, rows, kv_heads, group, used = sizes
    (first_s, out_s, gate_s, up_s, down_s, x_ref, place_ref, freq_ref) = refs[:8]
    (first_w, out_w, gate_w, up_w, down_w, q_out, kv_out, o_out, log_out) = refs[8:17]
    (mixed_out, h2_out, hidden_out, slope_out, silu_out, bias_out, cos_out, sin_out) = refs[17:25]
    (hid_turned, h2_turned, att_turned, nor_turned) = refs[25:29]
    (raw_a, raw_b, w_a, w_b, normed, queries, kv_all, attended, logs, mixed, h2) = refs[29:40]
    (hidden, slope, silu, bias, cos_t, sin_t, gains) = refs[40:47]
    (hid_t, h2_t, att_t, nor_t) = refs[47:51]
    (local, send, recv, kv_send, kv_recv, load_sem, store_sem) = refs[51:]
    me = Place()
    greet(me)
    whole = slice(None)
    half = down_w.shape[2] // 2
    comm = Gathering(
        me,
        (
            (first_s, first_w, whole, "yxc"),
            (out_s, out_w, whole, "xyc"),
            (gate_s, gate_w, whole, "yxc"),
            (up_s, up_w, whole, "xyc"),
            (down_s, down_w, pl.ds(0, half), "yxc"),
            (down_s, down_w, pl.ds(half, half), "xyc"),
        ),
        local,
        send,
        recv,
    )
    tokens, width = x_ref.shape
    length = kv_all.shape[1]
    stores = []

    def store(i, src, dst):
        copy = pltpu.make_async_copy(src, dst, store_sem.at[i])
        copy.start()
        stores.append(copy)

    def over_rows(body, step=64):
        def one(i, carry):
            body(pl.ds(pl.multiple_of(i * step, step), step))
            return carry

        lax.fori_loop(0, tokens // step, one, 0)

    def load(full, raw, col, size, i):
        return pltpu.make_async_copy(
            full.at[:, :, pl.ds(col, size)], raw.at[:, :, pl.ds(0, size)], load_sem.at[i]
        )

    def assemble(raw, flat, size):
        n, r, _ = raw.shape
        pair = 2 * r

        def one(i, carry):
            piece = raw[pl.ds(2 * i, 2), :, pl.ds(0, size)].astype(jnp.float32)
            flat[pl.ds(pl.multiple_of(pair * i, 16), pair), pl.ds(0, size)] = piece.reshape(
                pair, size
            ).astype(jnp.bfloat16)
            return carry

        lax.fori_loop(0, n // 2, one, 0)

    def turn_rows(src, dst, base, size):
        for i in range(size // 256):
            at = slice(base + i * 256, base + (i + 1) * 256)
            dst[at, :] = src[:, at].astype(jnp.float32).T.astype(jnp.bfloat16)

    comm.begin(0)
    comm.begin(1)
    comm.begin(2)

    scale = HD**-0.5
    lane = lax.broadcasted_iota(jnp.int32, (64, 128), 1)
    second = lax.rem(lane, HD) >= HD // 2
    is_value = lane >= HD

    def tables(at):
        angle = place_ref[at, :].astype(jnp.float32) * freq_ref[...]
        c, s = jnp.cos(angle), jnp.sin(angle)
        s = jnp.where(second, s, -s)
        cos_t[0, at, :] = c * scale
        sin_t[0, at, :] = s * scale
        cos_t[1, at, :] = jnp.where(is_value, 1.0, c)
        sin_t[1, at, :] = jnp.where(is_value, 0.0, s)

    over_rows(tables)
    first_row = lax.axis_index("fsdp") * rows

    def masks(at):
        token = at.start
        inside = lax.rem(token, rows)
        query = first_row + inside + lax.broadcasted_iota(jnp.int32, (64, length), 0)
        key = lax.broadcasted_iota(jnp.int32, (64, length), 1)
        start = query - place_ref[at, :]
        allowed = (key <= query) & (key >= start)
        bias[at, :] = jnp.where(allowed, 0.0, NEGATIVE).astype(jnp.bfloat16)

    over_rows(masks)
    store(0, bias, bias_out)
    store(1, cos_t, cos_out)
    store(2, sin_t, sin_out)

    comm.step(0, 0)
    comm.begin(3)
    comm.step(1, 0)
    comm.step(0, 1)
    comm.begin(4)
    comm.step(2, 0)
    comm.step(1, 1)
    comm.step(0, 2)
    comm.begin(5)
    comm.step(3, 0)
    comm.step(2, 1)
    comm.step(1, 2)
    comm.step(0, 3)

    tile = raw_a.shape[2]
    load(first_w, raw_a, used, 128, 0).start()
    load(first_w, raw_b, 0, tile, 1).start()
    load(first_w, raw_a, used, 128, 0).wait()
    assemble(raw_a, w_a, 128)
    gains[...] = w_a[:, :128].astype(jnp.float32).T[:8]
    load(first_w, raw_a, used - tile, tile, 0).start()

    def norm_one(at):
        x = x_ref[at, :].astype(jnp.float32)
        inverse = lax.rsqrt(jnp.mean(x * x, -1, keepdims=True) + EPSILON)
        normed[at, :] = (x * inverse * gains[0:1, :]).astype(jnp.bfloat16)

    over_rows(norm_one)
    comm.step(4, 0)

    def turn(flat, kind, put, step=256):
        def body(at):
            u = plain_dot(normed[at, :], flat[...])
            for j in range(tile // 128):
                piece = u[:, j * 128 : (j + 1) * 128]
                piece = piece * cos_t[kind, at, :] + swap_halves(piece) * sin_t[kind, at, :]
                put(at, j, piece.astype(jnp.bfloat16))

        over_rows(body, step)

    slot = (me.x * 2 + me.c) * rows

    def put_pair(at, j, piece):
        token = at.start
        b = token // rows
        row = pl.multiple_of(slot + lax.rem(token, rows), 256)
        kv_all[b, pl.ds(row, 256), j * 128 : (j + 1) * 128] = piece

    load(first_w, raw_a, used - tile, tile, 0).wait()
    assemble(raw_a, w_a, tile)
    turn(w_a, 1, put_pair)

    def share(i, dx, to):
        row = (lax.rem(me.x + dx, 2) * 2 + me.c) * rows
        block = kv_all.at[:, pl.ds(pl.multiple_of(row, 256), rows), :]
        copy = pltpu.make_async_remote_copy(
            src_ref=block,
            dst_ref=block,
            send_sem=kv_send.at[i],
            recv_sem=kv_recv.at[i],
            device_id=me.device(**{"d" + to: 1}),
            device_id_type=MESH,
        )
        copy.start()
        return copy

    to_x = share(0, 0, "x")
    to_c = share(1, 0, "c")
    comm.step(3, 1)
    for j in range(queries.shape[1] // tile):
        raw, flat = ((raw_b, w_b), (raw_a, w_a))[j % 2]
        if (j + 1) * tile < queries.shape[1]:
            load(first_w, (raw_a, raw_b)[j % 2], (j + 1) * tile, tile, j % 2).start()
        load(first_w, raw, j * tile, tile, 1 - j % 2).wait()
        assemble(raw, flat, tile)

        def put_query(at, i, piece, j=j):
            queries[at, j * tile + i * 128 : j * tile + (i + 1) * 128] = piece

        turn(flat, 0, put_query)
        if j == 0:
            comm.step(2, 2)
    store(3, queries, q_out)
    turn_rows(normed, nor_t, 0, width)
    store(12, nor_t, nor_turned)
    comm.step(1, 3)
    to_x.wait_recv()
    to_far = share(2, 1, "c")
    to_c.wait_recv()
    to_far.wait_recv()
    store(4, kv_all, kv_out)

    logs[...] = jnp.zeros_like(logs)
    lanes = lax.broadcasted_iota(jnp.int32, (rows, 128), 1)
    sides_mask = lane_masks(rows)

    def head(i, carry):
        b = i // kv_heads
        h = lax.rem(i, kv_heads)
        at = pl.ds(pl.multiple_of(b * rows, 256), rows)
        kv = kv_all[b, :, pl.ds(pl.multiple_of(h * 128, 128), 128)]
        sides = (kv, swapped(kv))
        shift = bias[at, :].astype(jnp.float32)
        log_piece = logs[at, :]
        for pair in range(group // 2):
            cols = pl.ds(pl.multiple_of(h * group * HD + pair * 128, 128), 128)
            q = queries[at, cols]
            found = []
            for side in range(2):
                scores = dot_t(q * sides_mask[side], sides[side]) + shift
                top = jnp.max(scores, -1, keepdims=True)
                powers = jnp.exp(scores - top)
                total = jnp.sum(powers, -1, keepdims=True)
                probs = (powers * (1.0 / total)).astype(jnp.bfloat16)
                found.append(plain_dot(probs, sides[1 - side]))
                log_piece = jnp.where(
                    lanes == h * group + pair * 2 + side, top + jnp.log(total), log_piece
                )
            attended[at, cols] = jnp.where(lanes < HD, found[0], found[1]).astype(jnp.bfloat16)
        logs[at, :] = log_piece
        return carry

    count = batches * kv_heads
    pumps = [(5, 0), (4, 1), (3, 2), (2, 3), (5, 1), (4, 2)]
    done = 0
    for i in range(6):
        upto = (2, 4, 6, 8, 9, 10)[i] * count // 10
        lax.fori_loop(done, upto, head, 0)
        done = upto
        comm.step(*pumps[i])
    store(5, attended, o_out)
    store(6, logs, log_out)

    steps = width // tile
    load(out_w, raw_a, 0, tile, 0).start()
    for j in range(steps):
        raw, flat = ((raw_a, w_a), (raw_b, w_b))[j % 2]
        if j + 1 < steps:
            load(out_w, (raw_b, raw_a)[j % 2], (j + 1) * tile, tile, 1 - j % 2).start()
        load(out_w, raw, j * tile, tile, j % 2).wait()
        assemble(raw, flat, tile)

        def add_in(at, flat=flat, j=j):
            cols = slice(j * tile, (j + 1) * tile)
            mixed[at, cols] = x_ref[at, cols].astype(jnp.float32) + plain_dot(
                attended[at, :], flat[...]
            )

        over_rows(add_in, 256)

    def norm_two(at):
        y = mixed[at, :]
        inverse = lax.rsqrt(jnp.mean(y * y, -1, keepdims=True) + EPSILON)
        h2[at, :] = (y * inverse * gains[1:2, :]).astype(jnp.bfloat16)

    over_rows(norm_two)
    store(7, mixed, mixed_out)
    store(8, h2, h2_out)
    turn_rows(attended, att_t, 0, attended.shape[1])
    store(13, att_t, att_turned)
    turn_rows(h2, h2_t, 0, width)
    store(14, h2_t, h2_turned)
    comm.step(3, 3)

    wide = 512
    features = hidden.shape[1]
    pumps = {2: (5, 2), 5: (4, 3)}
    load(gate_w, raw_a, 0, wide, 0).start()
    load(up_w, raw_b, 0, wide, 1).start()
    for j in range(features // wide):
        load(gate_w, raw_a, j * wide, wide, 0).wait()
        assemble(raw_a, w_a, wide)
        load(up_w, raw_b, j * wide, wide, 1).wait()
        assemble(raw_b, w_b, wide)
        if (j + 1) * wide < features:
            load(gate_w, raw_a, (j + 1) * wide, wide, 0).start()
            load(up_w, raw_b, (j + 1) * wide, wide, 1).start()

        def units(at, j=j):
            cols = slice(j * wide, (j + 1) * wide)
            g = plain_dot(h2[at, :], w_a[:, :wide])
            u = plain_dot(h2[at, :], w_b[:, :wide])
            sig = jax.nn.sigmoid(g)
            soft = g * sig
            hidden[at, cols] = (soft * u).astype(jnp.bfloat16)
            silu[at, cols] = soft.astype(jnp.bfloat16)
            slope[at, cols] = (u * (sig * (1.0 + g * (1.0 - sig)))).astype(jnp.bfloat16)

        over_rows(units, 256)
        turn_rows(hidden, hid_t, j * wide, wide)
        if j in pumps:
            comm.step(*pumps[j])
    store(9, hidden, hidden_out)
    store(10, silu, silu_out)
    store(11, slope, slope_out)
    store(15, hid_t, hid_turned)
    comm.step(5, 3)
    for copy in (to_x, to_c, to_far):
        copy.wait_send()
    comm.finish()
    for copy in stores:
        copy.wait()


def forward(shards, x, places, kv_heads, group, batches):
    first_s, out_s, gate_s, up_s, down_s = shards
    n = lax.axis_size("dp") * lax.axis_size("fsdp")
    Z = lax.axis_size("dp") // 2
    tokens, width = x.shape
    rows = tokens // batches
    length = rows * lax.axis_size("fsdp")
    key_wide = kv_heads * 128
    query_wide = kv_heads * group * HD
    used = query_wide + key_wide
    features = gate_s.shape[1]
    r = first_s.shape[0]
    freqs = ROPE_BASE ** (-jnp.arange(HD // 2).astype(jnp.float32) / (HD // 2))
    freqs = jnp.tile(freqs, 4)[None]
    bf, f32 = jnp.bfloat16, jnp.float32
    shape = jax.ShapeDtypeStruct
    outs = [shape((n,) + s.shape, s.dtype) for s in shards] + [
        shape((tokens, query_wide), bf),
        shape((batches, length, key_wide), bf),
        shape((tokens, query_wide), bf),
        shape((tokens, 128), f32),
        shape((tokens, width), f32),
        shape((tokens, width), bf),
        shape((tokens, features), bf),
        shape((tokens, features), bf),
        shape((tokens, features), bf),
        shape((tokens, length), bf),
        shape((2, tokens, 128), f32),
        shape((2, tokens, 128), f32),
        shape((features, tokens), bf),
        shape((width, tokens), bf),
        shape((query_wide, tokens), bf),
        shape((width, tokens), bf),
    ]
    vmem = pltpu.VMEM
    scratch = [
        vmem((n, r, key_wide), bf),
        vmem((n, r, key_wide), bf),
        vmem((width, key_wide), bf),
        vmem((width, key_wide), bf),
        vmem((tokens, width), bf),
        vmem((tokens, query_wide), bf),
        vmem((batches, length, key_wide), bf),
        vmem((tokens, query_wide), bf),
        vmem((tokens, 128), f32),
        vmem((tokens, width), f32),
        vmem((tokens, width), bf),
        vmem((tokens, features), bf),
        vmem((tokens, features), bf),
        vmem((tokens, features), bf),
        vmem((tokens, length), bf),
        vmem((2, tokens, 128), f32),
        vmem((2, tokens, 128), f32),
        vmem((8, width), f32),
        vmem((features, tokens), bf),
        vmem((width, tokens), bf),
        vmem((query_wide, tokens), bf),
        vmem((width, tokens), bf),
        pltpu.SemaphoreType.DMA((6,)),
        pltpu.SemaphoreType.DMA((6, 8 * Z)),
        pltpu.SemaphoreType.DMA((6, 8 * Z)),
        pltpu.SemaphoreType.DMA((3,)),
        pltpu.SemaphoreType.DMA((3,)),
        pltpu.SemaphoreType.DMA((2,)),
        pltpu.SemaphoreType.DMA((16,)),
    ]
    any_space = pl.BlockSpec(memory_space=pl.ANY)
    in_vmem = pl.BlockSpec(memory_space=pltpu.VMEM)
    return pl.pallas_call(
        functools.partial(forward_kernel, (batches, rows, kv_heads, group, used)),
        out_shape=outs,
        in_specs=[any_space] * 5 + [in_vmem] * 3,
        out_specs=[any_space] * len(outs),
        scratch_shapes=scratch,
        compiler_params=pltpu.CompilerParams(
            collective_id=1, has_side_effects=True, vmem_limit_bytes=63 * 2**20
        ),
        cost_estimate=pl.CostEstimate(
            flops=2 * tokens * width * (used + width + 2 * features),
            bytes_accessed=4 * n * r * (used + width + 3 * features),
            transcendentals=tokens * features,
        ),
    )(*shards, x, places, freqs)


def tile_of(N):
    for t in (512,384,256,128):
        if N%t==0: return t
    return N

def scatter_kernel(Z, orders, ahead, dims_, *refs):
    K=len(orders)
    parts=refs[:K]; outs=refs[K:2*K]
    sc=refs[2*K:]
    first_buf=sc[:K]; one_buf=sc[K:2*K]; two_buf=sc[2*K:3*K]; last_buf=sc[3*K:4*K]
    shapes=sorted(set(dims_))
    stage=[sc[4*K+shapes.index(d)] for d in dims_]
    local,send,recv=sc[4*K+len(shapes):]
    me=Place()
    greet(me)
    copies={}
    def ship(k,name,index,src,dst,target):
        cp=pltpu.make_async_remote_copy(src_ref=src,dst_ref=dst,send_sem=send.at[k,index],recv_sem=recv.at[k,index],device_id=target,device_id_type=MESH)
        cp.start(); copies[(k,name)]=cp
    def part(k,a,b,other):
        o=orders[k]
        rel={o[0]:a,o[1]:b}
        y=lax.rem(me.y+rel["y"],2); x=lax.rem(me.x+rel["x"],me.X); c=lax.rem(me.c+other,2)
        return parts[k].at[:,y,x,c]
    order4=((1,1),(1,0),(0,1),(0,0))
    locals_={}
    def first(k):
        for i,(a,b) in enumerate(order4):
            ship(k,("c",a,b),i,part(k,a,b,1),first_buf[k].at[a,b],me.device(dc=1))
    def bring(k,i):
        a,b=order4[i]
        cp=pltpu.make_async_copy(part(k,a,b,0),stage[k].at[i%2],local.at[k,i%2]); cp.start(); locals_[(k,i)]=cp
    def add(dst,src,k):
        _,r,N=dims_[k]
        t=tile_of(N)
        def body(i,_):
            zi=i//(N//t); j=i%(N//t)
            cols=pl.ds(pl.multiple_of(j*t,128),t)
            dst[zi,:,cols]=dst[zi,:,cols]+src[zi,:,cols]
            return 0
        lax.fori_loop(0,Z*(N//t),body,0)
    def step_c(k):
        bring(k,0); bring(k,1)
        for i,(a,b) in enumerate(order4):
            copies[(k,("c",a,b))].wait_recv()
            locals_[(k,i)].wait()
            add(first_buf[k].at[a,b],stage[k].at[i%2],k)
            if i+2<4: bring(k,i+2)
            if a==1:
                ship(k,("1",b),4+b,first_buf[k].at[1,b],one_buf[k].at[b],me.device(**{"d"+orders[k][0]:1}))
    def step_1(k):
        for b in (1,0):
            copies[(k,("1",b))].wait_recv()
            add(first_buf[k].at[0,b],one_buf[k].at[b],k)
            if b==1:
                ship(k,"2",6,first_buf[k].at[0,1],two_buf[k],me.device(**{"d"+orders[k][1]:1}))
    def step_2(k):
        copies[(k,"2")].wait_recv()
        add(first_buf[k].at[0,0],two_buf[k],k)
        for s in range(1,Z):
            ship(k,("z",s),6+s,first_buf[k].at[0,0,lax.rem(me.z+s,Z)],last_buf[k].at[s-1],me.device(s=s))
    def step_z(k):
        _,r,N=dims_[k]
        for s in range(1,Z): copies[(k,("z",s))].wait_recv()
        t=tile_of(N)
        mine=first_buf[k].at[0,0,me.z]
        def body(j,_):
            cols=pl.ds(pl.multiple_of(j*t,128),t)
            total=mine[:,cols].astype(jnp.float32)
            for s in range(1,Z): total=total+last_buf[k][s-1,:,cols].astype(jnp.float32)
            outs[k][:,cols]=total
            return 0
        lax.fori_loop(0,N//t,body,0)
    for k in range(min(ahead,K)): first(k)
    for t in range(K+3):
        if t+ahead<K: first(t+ahead)
        if t<K: step_c(t)
        if 0<=t-1<K: step_1(t-1)
        if 0<=t-2<K: step_2(t-2)
        if 0<=t-3<K: step_z(t-3)
    for cp in copies.values(): cp.wait_send()

def scatter(parts, orders, cid, ahead=2):
    n=lax.axis_size("dp")*lax.axis_size("fsdp"); Z=lax.axis_size("dp")//2; X=lax.axis_size("fsdp")//2; K=len(parts)
    dims_=[(n,p.shape[0]//n,p.shape[1]) for p in parts]
    parts=[p.reshape(Z,2,X,2,p.shape[0]//n,p.shape[1]) for p in parts]
    bf=jnp.bfloat16
    sc=[pltpu.VMEM((2,2,Z,r,N),bf) for _,r,N in dims_]+[pltpu.VMEM((2,Z,r,N),bf) for _,r,N in dims_]+[pltpu.VMEM((Z,r,N),bf) for _,r,N in dims_]+[pltpu.VMEM((Z-1,r,N),bf) for _,r,N in dims_]+[pltpu.VMEM((2,Z,r,N),bf) for _,r,N in sorted(set(dims_))]
    return pl.pallas_call(functools.partial(scatter_kernel,Z,orders,ahead,dims_),
        out_shape=[jax.ShapeDtypeStruct((r,N),jnp.float32) for _,r,N in dims_],
        in_specs=[pl.BlockSpec(memory_space=pl.ANY)]*K,
        out_specs=[pl.BlockSpec(memory_space=pltpu.VMEM)]*K,
        scratch_shapes=sc+[pltpu.SemaphoreType.DMA((K,2)),pltpu.SemaphoreType.DMA((K,6+Z)),pltpu.SemaphoreType.DMA((K,6+Z))],
        compiler_params=pltpu.CompilerParams(collective_id=cid,has_side_effects=True,vmem_limit_bytes=63*2**20))(*parts)


def dot_t(left, right):
    return lax.dot_general(
        left, right, (((1,), (1,)), ((), ())), preferred_element_type=jnp.float32
    )


def swap_halves(u):
    lane = lax.broadcasted_iota(jnp.int32, u.shape, 1)
    down = pltpu.roll(u, 32, 1)
    up = pltpu.roll(u, 96, 1)
    return jnp.where(lax.rem(lane, 64) < 32, up, down)


def project_kernel(h_ref, w_ref, cos_ref, sin_ref, out_ref):
    u = plain_dot(h_ref[...], w_ref[...])
    for j in range(u.shape[1] // 128):
        piece = u[:, j * 128 : (j + 1) * 128]
        turned = piece * cos_ref[0] + swap_halves(piece) * sin_ref[0]
        out_ref[:, j * 128 : (j + 1) * 128] = turned.astype(jnp.bfloat16)


def project(normed, weight, cos_tables, sin_tables, width):
    tokens, depth = normed.shape
    steps = weight.shape[1] // width
    return pl.pallas_call(
        project_kernel,
        grid=(steps,),
        in_specs=[
            pl.BlockSpec((tokens, depth), lambda j: (0, 0)),
            pl.BlockSpec((depth, width), lambda j: (0, j)),
            pl.BlockSpec((1, tokens, 128), lambda j: (j // (steps - 1), 0, 0)),
            pl.BlockSpec((1, tokens, 128), lambda j: (j // (steps - 1), 0, 0)),
        ],
        out_specs=pl.BlockSpec((tokens, width), lambda j: (0, j)),
        out_shape=jax.ShapeDtypeStruct((tokens, steps * width), jnp.bfloat16),
        compiler_params=pltpu.CompilerParams(vmem_limit_bytes=48 * 2**20),
        cost_estimate=pl.CostEstimate(
            flops=2 * tokens * depth * weight.shape[1],
            bytes_accessed=2 * depth * weight.shape[1],
            transcendentals=0,
        ),
    )(normed, weight, cos_tables, sin_tables)


def lane_masks(rows):
    lane = lax.broadcasted_iota(jnp.int32, (rows, 128), 1)
    low_side = (lane < 64).astype(jnp.float32)
    return low_side.astype(jnp.bfloat16), (1.0 - low_side).astype(jnp.bfloat16)


def swapped(kv):
    return pltpu.roll(kv.astype(jnp.float32), 64, 1).astype(jnp.bfloat16)


def attend_kernel(group, q_ref, kv_ref, bias_ref, o_ref, log_ref):
    kv = kv_ref[0]
    sides = (kv, swapped(kv))
    rows = q_ref.shape[0]
    masks = lane_masks(rows)
    lane = lax.broadcasted_iota(jnp.int32, (rows, 128), 1)
    logs = jnp.zeros((rows, 128), jnp.float32)
    bias = bias_ref[0]
    for pair in range(group // 2):
        cols = slice(pair * 128, pair * 128 + 128)
        q = q_ref[:, cols]
        found = []
        for half in range(2):
            scores = dot_t(q * masks[half], sides[half]) + bias
            top = jnp.max(scores, -1, keepdims=True)
            powers = jnp.exp(scores - top)
            total = jnp.sum(powers, -1, keepdims=True)
            probs = (powers * (1.0 / total)).astype(jnp.bfloat16)
            found.append(plain_dot(probs, sides[1 - half]))
            logs = jnp.where(lane == pair * 2 + half, top + jnp.log(total), logs)
        o_ref[:, cols] = jnp.where(lane < 64, found[0], found[1]).astype(jnp.bfloat16)
    log_ref[...] = logs


def attend(projected, both_all, bias, kv_heads, group):
    batches, length, _ = both_all.shape
    rows = projected.shape[0] // batches
    wide = group * HD
    return pl.pallas_call(
        functools.partial(attend_kernel, group),
        grid=(batches, kv_heads),
        in_specs=[
            pl.BlockSpec((rows, wide), lambda b, h: (b, h)),
            pl.BlockSpec((1, length, 128), lambda b, h: (b, 0, h)),
            pl.BlockSpec((1, rows, length), lambda b, h: (b, 0, 0)),
        ],
        out_specs=[
            pl.BlockSpec((rows, wide), lambda b, h: (b, h)),
            pl.BlockSpec((rows, 128), lambda b, h: (b, h)),
        ],
        out_shape=[
            jax.ShapeDtypeStruct((batches * rows, kv_heads * wide), jnp.bfloat16),
            jax.ShapeDtypeStruct((batches * rows, kv_heads * 128), jnp.float32),
        ],
        compiler_params=pltpu.CompilerParams(vmem_limit_bytes=48 * 2**20),
    )(projected, both_all, bias)


def attend_back_kernel(
    group, q_ref, do_ref, kv_ref, bias_ref, log_ref, cos_ref, sin_ref, dq_ref, dkv_ref
):
    kv = kv_ref[0]
    sides = (kv, swapped(kv))
    rows = q_ref.shape[0]
    length = kv.shape[0]
    masks = lane_masks(rows)
    lane = lax.broadcasted_iota(jnp.int32, (rows, 128), 1)
    bias = bias_ref[0]
    key_sum = jnp.zeros((128, length), jnp.float32)
    value_sum = jnp.zeros((128, length), jnp.float32)
    for pair in range(group // 2):
        cols = slice(pair * 128, pair * 128 + 128)
        q = q_ref[:, cols]
        do = do_ref[:, cols]
        found = []
        for half in range(2):
            q_half = q * masks[half]
            do_half = do * masks[half]
            at = pair * 2 + half
            log_total = log_ref[:, at : at + 1]
            probs = jnp.exp(dot_t(q_half, sides[half]) + bias - log_total)
            grad_probs = dot_t(do_half, sides[1 - half])
            row_dot = jnp.sum(probs * grad_probs, -1, keepdims=True)
            grad_scores = (probs * (grad_probs - row_dot)).astype(jnp.bfloat16)
            found.append(plain_dot(grad_scores, sides[half]))
            key_sum = key_sum + left_dot(q_half, grad_scores)
            value_sum = value_sum + left_dot(do_half, probs.astype(jnp.bfloat16))
        dq = jnp.where(lane < 64, found[0], found[1])
        dq = dq * cos_ref[0] - swap_halves(dq) * sin_ref[0]
        dq_ref[:, cols] = dq.astype(jnp.bfloat16)
    both = jnp.concatenate(
        [key_sum[:64] + key_sum[64:], value_sum[:64] + value_sum[64:]], 0
    )
    dkv_ref[0] = both.T.astype(jnp.bfloat16)


def attend_back(projected, grad_attended, both_all, bias, logs, cos_tables, sin_tables, group):
    batches, length, _ = both_all.shape
    rows = projected.shape[0] // batches
    wide = group * HD
    kv_heads = both_all.shape[2] // 128
    return pl.pallas_call(
        functools.partial(attend_back_kernel, group),
        grid=(batches, kv_heads),
        in_specs=[
            pl.BlockSpec((rows, wide), lambda b, h: (b, h)),
            pl.BlockSpec((rows, wide), lambda b, h: (b, h)),
            pl.BlockSpec((1, length, 128), lambda b, h: (b, 0, h)),
            pl.BlockSpec((1, rows, length), lambda b, h: (b, 0, 0)),
            pl.BlockSpec((rows, 128), lambda b, h: (b, h)),
            pl.BlockSpec((1, rows, 128), lambda b, h: (0, b, 0)),
            pl.BlockSpec((1, rows, 128), lambda b, h: (0, b, 0)),
        ],
        out_specs=[
            pl.BlockSpec((rows, wide), lambda b, h: (b, h)),
            pl.BlockSpec((1, length, 128), lambda b, h: (b, 0, h)),
        ],
        out_shape=[
            jax.ShapeDtypeStruct((batches * rows, kv_heads * wide), jnp.bfloat16),
            jax.ShapeDtypeStruct((batches, length, kv_heads * 128), jnp.bfloat16),
        ],
        compiler_params=pltpu.CompilerParams(vmem_limit_bytes=48 * 2**20),
    )(projected, grad_attended, both_all, bias, logs, cos_tables, sin_tables)


class Scattering:
    def __init__(self, me, chunks, send, recv, free):
        self.me, self.chunks = me, chunks
        self.send, self.recv, self.free = send, recv, free
        self.copies = {}
        self.friends = [me.device(s=s) for s in range(1, me.Z)]
        self.friends += [me.device(dy=1), me.device(dx=1), me.device(dc=1)]

    def ship(self, k, name, index, src, dst, target):
        copy = pltpu.make_async_remote_copy(
            src_ref=src,
            dst_ref=dst,
            send_sem=self.send.at[k, index],
            recv_sem=self.recv.at[k, index],
            device_id=target,
            device_id_type=MESH,
        )
        copy.start()
        self.copies[(k, name)] = copy

    def add(self, dst, src, wide):
        depth = dst.shape[0]
        t = tile_of(wide)
        count = wide // t

        def body(i, carry):
            at = i // count
            cols = pl.ds(pl.multiple_of(lax.rem(i, count) * t, 128), t)
            dst[at, :, cols] = dst[at, :, cols] + src[at, :, cols]
            return carry

        lax.fori_loop(0, depth * count, body, 0)

    def buffers(self, k):
        own, one, two, last, wide = self.chunks[k][:5]
        cols = pl.ds(0, wide)
        return own, one, two, last, wide, cols

    def begin(self, k):
        own, one, two, last, wide, cols = self.buffers(k)
        order = self.chunks[k][5]
        for b in (1, 0):
            self.ship(
                k,
                ("1", b),
                b,
                own.at[1, b, :, :, cols],
                one.at[b, :, :, cols],
                self.me.device(**{"d" + order[0]: 1}),
            )

    def first(self, k):
        own, one, two, last, wide, cols = self.buffers(k)
        order = self.chunks[k][5]
        for b in (1, 0):
            self.copies[(k, ("1", b))].wait_recv()
            self.add(own.at[0, b], one.at[b], wide)
            if b == 1:
                self.ship(
                    k,
                    "2",
                    2,
                    own.at[0, 1, :, :, cols],
                    two.at[:, :, cols],
                    self.me.device(**{"d" + order[1]: 1}),
                )

    def second(self, k):
        own, one, two, last, wide, cols = self.buffers(k)
        me = self.me
        self.copies[(k, "2")].wait_recv()
        self.add(own.at[0, 0], two, wide)
        for s in range(1, me.Z):
            self.ship(
                k,
                ("z", s),
                2 + s,
                own.at[0, 0, lax.rem(me.z + s, me.Z), :, cols],
                last.at[s - 1, :, cols],
                me.device(s=s),
            )

    def third(self, k):
        own, one, two, last, wide, cols = self.buffers(k)
        me = self.me
        _, out, base, group = self.chunks[k][5:]
        for s in range(1, me.Z):
            self.copies[(k, ("z", s))].wait_recv()
        t = tile_of(wide)

        def body(j, carry):
            here = pl.ds(pl.multiple_of(j * t, 128), t)
            there = pl.ds(pl.multiple_of(base + j * t, 128), t)
            total = own[0, 0, me.z, :, here].astype(jnp.float32)
            for s in range(1, me.Z):
                total = total + last[s - 1, :, here].astype(jnp.float32)
            out[:, there] = total
            return carry

        lax.fori_loop(0, wide // t, body, 0)
        for (at, _), copy in self.copies.items():
            if at == k:
                copy.wait_send()
        if group is not None:
            for friend in self.friends:
                pl.semaphore_signal(
                    self.free.at[group], inc=1, device_id=friend, device_id_type=MESH
                )

    def reuse(self, group):
        pl.semaphore_wait(self.free.at[group], len(self.friends))


def backward_kernel(sizes, *refs):
    batches, rows, kv_heads, group, used = sizes
    (dy_ref, first_w, out_w, gate_w, up_w, down_w) = refs[:6]
    (q_in, kv_in, log_in, mixed_in, hidden_in, slope_in, silu_in, bias_in, cos_in, sin_in) = refs[6:16]
    (hid_t, h2_t, att_t, nor_t, x_in) = refs[16:21]
    outs = refs[21:36]
    (result_out, grad_out, g_first, g_out, g_gate, g_up, g_down) = outs[:7]
    (hid_s, h2_s, att_s, nor_s, dy_p, gate_p, up_p, dm_p) = outs[7:]
    pre_p, dy1_h = refs[36:38]
    sc = list(refs[38:])
    take = lambda n: [sc.pop(0) for _ in range(n)]
    sets = [take(4) for _ in range(3)]
    down_sets = [take(4) for _ in range(2)]
    gain_set = take(4)
    (lhs_d, lhs, lraw, rhs, acc, part, cot, low_t, queries, grads, pre) = take(11)
    (kv_all, dkv, bias, logs, cos_t, sin_t, dkv_r, dkv_x) = take(8)
    (raw_a, w_a, wd, fac_a, fac_b, dgt, dut, gains, gsum, gcol) = take(10)
    (send, recv, free, x_send, x_recv, t_send, t_recv, load_sem, lhs_sem, store_sem, own_sem, part_sem) = take(12)
    me = Place()
    greet(me)
    tokens, width = cot.shape
    length = kv_all.shape[1]
    features = hidden_in.shape[1]
    wide = dgt.shape[1]
    tiles = features // wide
    scale = HD**-0.5
    sibling = me.device(dc=1)
    f32, bf = jnp.float32, jnp.bfloat16
    r = lhs.shape[0] // (4 * me.Z)
    rd = lhs_d.shape[1] // me.Z
    big = sets[0][0].shape[-1]
    half = features // 2
    key_wide = kv_heads * 128
    query_wide = pre.shape[1] - key_wide
    d_wide = down_sets[0][0].shape[-1]
    d_rest = width - 2 * d_wide
    chunks = (
        (*down_sets[0], d_wide, "xy", g_down, 0, 4),
        (*down_sets[1], d_wide, "yx", g_down, d_wide, None),
        (*sets[0], half, "xy", g_gate, 0, 0),
        (*sets[1], half, "yx", g_up, 0, 1),
        (*sets[2], half, "xy", g_gate, half, 2),
        (*sets[0], half, "yx", g_up, half, 3),
        (*sets[1], width, "xy", g_out, 0, None),
        (*sets[2], query_wide, "yx", g_first, 0, None),
        (*sets[0], key_wide, "xy", g_first, query_wide, None),
        (*gain_set, 128, "yx", g_first, query_wide + key_wide, None),
        (*down_sets[0], d_rest, "xy", g_down, 2 * d_wide, None),
    )
    D0, D1, G0, U0, G1, U1, O, Q, KV, GAIN, D2 = range(11)
    comm = Scattering(me, chunks, send, recv, free)

    def over_rows(body, step=64):
        def one(i, carry):
            body(pl.ds(pl.multiple_of(i * step, step), step))
            return carry

        lax.fori_loop(0, tokens // step, one, 0)

    passes = []

    def hand(i, src, dst):
        copy = pltpu.make_async_remote_copy(
            src_ref=src,
            dst_ref=dst,
            send_sem=x_send.at[i],
            recv_sem=x_recv.at[i],
            device_id=sibling,
            device_id_type=MESH,
        )
        copy.start()
        passes.append(copy)
        return copy

    other = lax.rem(me.c + 1, 2)
    got_hid = hand(0, hid_t.at[:, :, :, other], hid_s)
    got_dy = hand(1, dy_ref, dy_p.at[1])
    got_h2 = hand(2, h2_t.at[:, :, :, other], h2_s)
    got_att = hand(3, att_t.at[:, :, :, other], att_s)
    got_nor = hand(4, nor_t.at[:, :, :, other], nor_s)

    def fetch(i, src, dst):
        copy = pltpu.make_async_copy(src, dst, load_sem.at[i])
        copy.start()
        return copy

    stores = []

    def store(i, src, dst):
        copy = pltpu.make_async_copy(src, dst, store_sem.at[i])
        copy.start()
        stores.append(copy)
        return copy

    need_cot = fetch(0, dy_ref, cot)
    own_dy = store(0, dy_ref, dy_p.at[0])
    def block(ref, a, b, order, c=None):
        rel = {order[0]: a, order[1]: b}
        y = lax.rem(me.y + rel["y"], 2)
        x = lax.rem(me.x + rel["x"], 2)
        return ref.at[:, y, x] if c is None else ref.at[:, y, x, c]

    def left_rows(own_t, sib_t):
        for side, ref in ((0, own_t), (1, sib_t)):
            loads = []
            for i in range(4):
                src = block(ref, i // 2, i % 2, "xy", me.c if side == 0 else None)
                copy = pltpu.make_async_copy(src, lraw.at[i], lhs_sem.at[i])
                copy.start()
                loads.append(copy)
            for copy in loads:
                copy.wait()

            def one(i, carry, side=side):
                for j in range(me.Z // 2):
                    piece = lraw[i, 2 * j : 2 * j + 2].astype(f32).reshape(2 * r, tokens)
                    at = pl.multiple_of((i * me.Z + 2 * j) * r, 16)
                    lhs[pl.ds(at, 2 * r), side * tokens : (side + 1) * tokens] = piece.astype(bf)
                return carry

            lax.fori_loop(0, 4, one, 0)

    def down_rows(k, i, slot):
        copies = []
        for side, ref in ((0, hid_t), (1, hid_s)):
            src = block(ref, i // 2, i % 2, chunks[k][5], me.c if side == 0 else None)
            for z in range(me.Z):
                copies.append(
                    pltpu.make_async_copy(
                        src.at[z],
                        lhs_d.at[slot, pl.ds(z * rd, rd), pl.ds(side * tokens, tokens)],
                        lhs_sem.at[(slot * 2 + side) * me.Z + z],
                    )
                )
        return copies

    def product_down(k, base, right=None):
        own, wide_k = chunks[k][0], chunks[k][4]
        for copy in down_rows(k, 3, 0):
            copy.start()
        for n, i in enumerate((3, 2, 1, 0)):
            slot = n % 2
            if i > 0:
                for copy in down_rows(k, i - 1, 1 - slot):
                    copy.start()
            for copy in down_rows(k, i, slot):
                copy.wait()
            left = lhs_d.at[slot]
            if right is None:
                product(k, dy_p, base, left, rd, (i,))
            else:

                def body(j, carry, i=i, left=left):
                    cols = pl.ds(pl.multiple_of(base + j * 256, 256), 256)
                    here = pl.ds(pl.multiple_of(j * 256, 256), 256)
                    total = plain_dot(left[:, :tokens], right[0][:, cols]) + plain_dot(
                        left[:, tokens:], right[1][:, cols]
                    )
                    own[i // 2, i % 2, :, :, here] = total.reshape(me.Z, rd, 256).astype(bf)
                    return carry

                lax.fori_loop(0, wide_k // 256, body, 0)
        comm.begin(k)

    def product(k, pair, base, left, depth, blocks=(0, 1, 2, 3)):
        own, wide_k = chunks[k][0], chunks[k][4]
        t = rhs.shape[3] if wide_k % rhs.shape[3] == 0 else 128
        count = wide_k // t
        span = len(blocks)

        def tile(j, slot):
            cols = pl.ds(pl.multiple_of(base + j * t, 128), t)
            return [
                pltpu.make_async_copy(
                    pair.at[side, :, cols],
                    rhs.at[slot, side, :, pl.ds(0, t)],
                    own_sem.at[slot, side],
                )
                for side in range(2)
            ]

        depth_of = rhs.shape[0]
        for j in range(min(depth_of - 1, count)):
            for copy in tile(j, j):
                copy.start()

        def body(j, carry):
            slot = lax.rem(j, depth_of)
            ahead = j + depth_of - 1

            @pl.when(ahead < count)
            def _():
                for copy in tile(ahead, lax.rem(ahead, depth_of)):
                    copy.start()

            for copy in tile(j, slot):
                copy.wait()
            cols = pl.ds(pl.multiple_of(j * t, 128), t)
            total = plain_dot(left[:, :tokens], rhs[slot, 0, :, :t]) + plain_dot(
                left[:, tokens:], rhs[slot, 1, :, :t]
            )
            total = total.reshape(span, me.Z, depth, t).astype(bf)
            for q, at in enumerate(blocks):
                if chunks[k][5] == "xy" or span == 1:
                    own[at // 2, at % 2, :, :, cols] = total[q]
                else:
                    own[at % 2, at // 2, :, :, cols] = total[q]
            return carry

        lax.fori_loop(0, count, body, 0)

    def load3(i, full, raw, col, size):
        return pltpu.make_async_copy(
            full.at[:, :, pl.ds(col, size)], raw.at[:, :, pl.ds(0, size)], load_sem.at[i]
        )

    def assemble(raw, flat, size):
        n, depth, _ = raw.shape
        pair = 2 * depth

        def one(i, carry):
            piece = raw[pl.ds(2 * i, 2), :, pl.ds(0, size)].astype(f32)
            flat[pl.ds(pl.multiple_of(pair * i, 16), pair), pl.ds(0, size)] = piece.reshape(
                pair, size
            ).astype(bf)
            return carry

        lax.fori_loop(0, n // 2, one, 0)

    def tile_loads(j):
        at = pl.ds(j * wide, wide)
        return [
            pltpu.make_async_copy(down_w.at[at, :], wd.at[j % 2], load_sem.at[2]),
            pltpu.make_async_copy(slope_in.at[:, at], fac_a.at[j % 2], load_sem.at[3]),
            pltpu.make_async_copy(silu_in.at[:, at], fac_b.at[j % 2], load_sem.at[4]),
        ]

    gate_tile = lambda j: load3(5, gate_w, raw_a, j * wide, wide)
    up_tile = lambda j: load3(6, up_w, raw_a, j * wide, wide)
    head_pack = load3(7, first_w, raw_a, used, 128)
    head_pack.start()
    head_pack.wait()
    assemble(raw_a, w_a, 128)
    gains[...] = w_a[:, :128].astype(f32).T[:8]
    for copy in tile_loads(0) + [gate_tile(0)]:
        copy.start()
    need_cot.wait()
    own_dy.wait()
    tile_sends = [None] * tiles

    def arrive(low, high):
        for j in range(low, high):
            for copy in tile_sends[j]:
                copy.settle()

    for j in range(tiles):
        slot = j % 2
        for copy in tile_loads(j):
            copy.wait()
        if j + 1 < tiles:
            for copy in tile_loads(j + 1):
                copy.start()
        gate_tile(j).wait()
        assemble(raw_a, w_a, wide)
        up_tile(j).start()
        if j >= 1:
            for copy in tile_sends[j - 1]:
                copy.wait()

        def units(at, slot=slot, j=j):
            grad_hidden = dot_t(cot[at, :], wd[slot])
            dg = (grad_hidden * fac_a[slot, at, :].astype(f32)).astype(bf)
            du = (grad_hidden * fac_b[slot, at, :].astype(f32)).astype(bf)
            dgt[at, :] = dg
            dut[at, :] = du
            piece = dot_t(dg, w_a[:, :wide])
            acc[at, :] = piece if j == 0 else acc[at, :] + piece

        over_rows(units, 256)
        cols = pl.ds(j * wide, wide)
        sends = []
        for i, (src, dst) in enumerate(((dgt, gate_p), (dut, up_p))):
            here = pltpu.make_async_copy(
                src, dst.at[0, :, cols], store_sem.at[1 + i]
            )
            there = pltpu.make_async_remote_copy(
                src_ref=src,
                dst_ref=dst.at[1, :, cols],
                send_sem=t_send.at[2 * j + i],
                recv_sem=t_recv.at[2 * j + i],
                device_id=sibling,
                device_id_type=MESH,
            )
            here.start()
            there.start()
            sends.append(_Both(here, there))
        tile_sends[j] = sends
        up_tile(j).wait()
        assemble(raw_a, w_a, wide)
        if j + 1 < tiles:
            gate_tile(j + 1).start()

        def units_up(at):
            acc[at, :] = acc[at, :] + dot_t(dut[at, :], w_a[:, :wide])

        over_rows(units_up, 256)
        if j == 0:
            got_dy.wait_recv()
            need_sib = fetch(1, dy_p.at[1], low_t)
            got_hid.wait_recv()
            need_sib.wait()
            product_down(D0, 0, (cot, low_t))
        if j == 1:
            product_down(D1, d_wide, (cot, low_t))
        if j == 3:
            got_h2.wait_recv()
            left_rows(h2_t, h2_s)
            arrive(0, 4)
            product(G0, gate_p, 0, lhs, r)
            comm.begin(G0)
            product(U0, up_p, 0, lhs, r)
            comm.begin(U0)
        if j == 4:
            comm.first(D0)
        if j == 5:
            comm.first(D1)
    arrive(4, tiles)
    product(G1, gate_p, half, lhs, r)
    comm.begin(G1)
    comm.second(D0)
    comm.second(D1)

    gsum[...] = jnp.zeros_like(gsum)

    def stream(src, body):
        def piece(i, slot):
            at = pl.ds(pl.multiple_of(i * 64, 64), 64)
            return pltpu.make_async_copy(src.at[at, :], part.at[slot], part_sem.at[slot])

        piece(0, 0).start()

        def one(i, carry):
            slot = lax.rem(i, 2)

            @pl.when(i + 1 < tokens // 64)
            def _():
                piece(i + 1, lax.rem(i + 1, 2)).start()

            piece(i, slot).wait()
            body(pl.ds(pl.multiple_of(i * 64, 64), 64), part[slot])
            return carry

        lax.fori_loop(0, tokens // 64, one, 0)

    def norm_two(at, y):
        inverse = lax.rsqrt(jnp.mean(y * y, -1, keepdims=True) + EPSILON)
        grad = acc[at, :]
        gsum[1:2, :] += jnp.sum(grad * (y * inverse), 0, keepdims=True)
        e = grad * gains[1:2, :]
        dy1 = cot[at, :].astype(f32) + inverse * (
            e - y * (inverse * inverse) * jnp.mean(e * y, -1, keepdims=True)
        )
        acc[at, :] = dy1
        low_t[at, :] = dy1.astype(bf)

    stream(mixed_in, norm_two)
    keep_dy1 = pltpu.make_async_copy(acc, dy1_h, part_sem.at[2])
    keep_dy1.start()
    own_low = store(5, low_t, dm_p.at[0])
    got_low = hand(5, low_t, dm_p.at[1])

    need_q = fetch(0, q_in, queries)
    need_kv = fetch(1, kv_in, kv_all)
    need = [
        fetch(8, bias_in, bias),
        fetch(9, log_in, logs),
        fetch(10, cos_in, cos_t),
        fetch(11, sin_in, sin_t),
    ]
    tile_w = raw_a.shape[2]
    steps = width // tile_w
    load3(5, out_w, raw_a, 0, tile_w).start()
    keep_dy1.wait()
    for j in range(steps):
        load3(5, out_w, raw_a, j * tile_w, tile_w).wait()
        assemble(raw_a, w_a, tile_w)
        if j + 1 < steps:
            load3(5, out_w, raw_a, (j + 1) * tile_w, tile_w).start()

        def back_out(at, j=j):
            piece = dot_t(low_t[at, j * tile_w : (j + 1) * tile_w], w_a[...])
            if j > 0:
                piece = acc[at, :] + piece
            if j + 1 < steps:
                acc[at, :] = piece
            else:
                grads[at, :] = piece.astype(bf)

        over_rows(back_out, 256)
    comm.first(G0)
    comm.third(D0)
    comm.third(D1)

    need_q.wait()
    need_kv.wait()
    for copy in need:
        copy.wait()
    lanes = lax.broadcasted_iota(jnp.int32, (rows, 128), 1)
    sides_mask = lane_masks(rows)

    def head(i, carry):
        b = i // kv_heads
        h = lax.rem(i, kv_heads)
        at = pl.ds(pl.multiple_of(b * rows, 256), rows)
        here = pl.ds(pl.multiple_of(h * 128, 128), 128)
        kv = kv_all[b, :, here]
        sides = (kv, swapped(kv))
        shift = bias[at, :].astype(f32)
        key_sum = jnp.zeros((128, length), f32)
        value_sum = jnp.zeros((128, length), f32)
        log_piece = logs[at, :]
        for pair in range(group // 2):
            cols = pl.ds(pl.multiple_of(h * group * HD + pair * 128, 128), 128)
            q = queries[at, cols]
            do = grads[at, cols]
            found = []
            for side in range(2):
                q_half = q * sides_mask[side]
                do_half = do * sides_mask[side]
                head_at = pair * 2 + side
                log_total = jnp.sum(
                    jnp.where(lanes == h * group + head_at, log_piece, 0.0), -1, keepdims=True
                )
                probs = jnp.exp(dot_t(q_half, sides[side]) + shift - log_total)
                grad_probs = dot_t(do_half, sides[1 - side])
                row_dot = jnp.sum(probs * grad_probs, -1, keepdims=True)
                grad_scores = (probs * (grad_probs - row_dot)).astype(bf)
                found.append(plain_dot(grad_scores, sides[side]))
                key_sum = key_sum + left_dot(q_half, grad_scores)
                value_sum = value_sum + left_dot(do_half, probs.astype(bf))
            dq = jnp.where(lanes < HD, found[0], found[1])
            dq = dq * cos_t[0, at, :] - swap_halves(dq) * sin_t[0, at, :]
            pre[at, cols] = dq.astype(bf)
        both = jnp.concatenate(
            [key_sum[:HD] + key_sum[HD:], value_sum[:HD] + value_sum[HD:]], 0
        )
        dkv[b, :, here] = both.T.astype(bf)
        return carry

    count = batches * kv_heads
    lax.fori_loop(0, 2, head, 0)
    comm.first(U0)
    own_low.wait()
    got_low.wait_recv()
    comm.second(G0)
    lax.fori_loop(2, 4, head, 0)
    comm.second(U0)
    comm.first(G1)
    comm.third(G0)
    comm.reuse(0)
    product(U1, up_p, half, lhs, r)
    comm.begin(U1)
    lax.fori_loop(4, 6, head, 0)
    comm.third(U0)
    comm.second(G1)
    comm.reuse(1)
    got_att.wait_recv()
    left_rows(att_t, att_s)
    product(O, dm_p, 0, lhs, r)
    comm.begin(O)
    lax.fori_loop(6, 8, head, 0)
    comm.reuse(4)
    product_down(D2, 2 * d_wide)
    comm.third(G1)
    lax.fori_loop(8, count, head, 0)

    def portion(dx, c):
        row = (lax.rem(me.x + dx, 2) * 2 + c) * rows
        return pl.ds(pl.multiple_of(row, 256), rows)

    to_c = [hand(6 + dx, dkv.at[:, portion(dx, other), :], dkv_r.at[dx]) for dx in (1, 0)]
    def gather_portion(dx):
        place = portion(dx, me.c)
        for b in range(batches):

            def body(j, carry, b=b):
                at = pl.ds(pl.multiple_of(j * 64, 64), 64)
                there = pl.ds(pl.multiple_of(place.start + j * 64, 64), 64)
                total = dkv_r[dx, b, at, :].astype(f32) + dkv[b, there, :].astype(f32)
                dkv_r[dx, b, at, :] = total.astype(bf)
                return carry

            lax.fori_loop(0, rows // 64, body, 0)

    to_c[0].wait_recv()
    gather_portion(1)
    to_x = pltpu.make_async_remote_copy(
        src_ref=dkv_r.at[1],
        dst_ref=dkv_x,
        send_sem=x_send.at[8],
        recv_sem=x_recv.at[8],
        device_id=me.device(dx=1),
        device_id_type=MESH,
    )
    to_x.start()
    passes.append(to_x)
    own_q = store(6, pre.at[:, pl.ds(0, query_wide)], pre_p.at[0, :, pl.ds(0, query_wide)])
    got_q = hand(9, pre.at[:, pl.ds(0, query_wide)], pre_p.at[1, :, pl.ds(0, query_wide)])
    to_c[1].wait_recv()
    gather_portion(0)
    comm.first(U1)
    comm.reuse(2)
    got_nor.wait_recv()
    left_rows(nor_t, nor_s)
    own_q.wait()
    got_q.wait_recv()
    product(Q, pre_p, 0, lhs, r)
    comm.begin(Q)
    comm.first(O)
    comm.first(D2)
    comm.second(U1)
    to_x.wait_recv()
    for b in range(batches):

        def merge(j, carry, b=b):
            at = pl.ds(pl.multiple_of(j * 64, 64), 64)
            token = pl.ds(pl.multiple_of(b * rows + j * 64, 64), 64)
            for h in range(kv_heads):
                cols = slice(h * 128, (h + 1) * 128)
                total = dkv_r[0, b, at, cols].astype(f32) + dkv_x[b, at, cols].astype(f32)
                total = total * cos_t[1, token, :] - swap_halves(total) * sin_t[1, token, :]
                pre[token, query_wide + h * 128 : query_wide + (h + 1) * 128] = total.astype(bf)
            return carry

        lax.fori_loop(0, rows // 64, merge, 0)
    rest = pl.ds(query_wide, kv_heads * 128)
    own_kv = store(7, pre.at[:, rest], pre_p.at[0, :, rest])
    got_kv = hand(10, pre.at[:, rest], pre_p.at[1, :, rest])

    need_x = fetch(0, x_in, cot)
    steps = pre.shape[1] // tile_w
    load3(5, first_w, raw_a, 0, tile_w).start()
    for j in range(steps):
        load3(5, first_w, raw_a, j * tile_w, tile_w).wait()
        assemble(raw_a, w_a, tile_w)
        if j + 1 < steps:
            load3(5, first_w, raw_a, (j + 1) * tile_w, tile_w).start()

        def back_in(at, j=j):
            piece = dot_t(pre[at, j * tile_w : (j + 1) * tile_w], w_a[...])
            acc[at, :] = piece if j == 0 else acc[at, :] + piece

        over_rows(back_in, 256)
    comm.second(O)
    comm.second(D2)
    comm.third(U1)
    comm.reuse(3)
    own_kv.wait()
    got_kv.wait_recv()
    product(KV, pre_p, query_wide, lhs, r)
    comm.begin(KV)
    need_x.wait()

    def norm_one(at, dy1):
        x = cot[at, :].astype(f32)
        inverse = lax.rsqrt(jnp.mean(x * x, -1, keepdims=True) + EPSILON)
        grad = acc[at, :]
        gsum[0:1, :] += jnp.sum(grad * (x * inverse), 0, keepdims=True)
        e = grad * gains[0:1, :]
        total = dy1 + inverse * (
            e - x * (inverse * inverse) * jnp.mean(e * x, -1, keepdims=True)
        )
        queries[at, :] = total.astype(bf)

    stream(dy1_h, norm_one)
    store(8, queries, grad_out)
    comm.first(Q)

    gsib = gain_set[0]
    columns = jnp.concatenate([gsum[...], jnp.zeros((120, width), f32)], 0).T
    gcol[0] = columns.reshape(gcol.shape[1:]).astype(bf)
    got_gain = hand(11, gcol.at[0], gcol.at[1])
    comm.first(KV)
    got_gain.wait_recv()
    for a in range(2):
        for b in range(2):
            y = lax.rem(me.y + b, 2)
            x = lax.rem(me.x + a, 2)
            if chunks[GAIN][5] == "yx":
                y, x = lax.rem(me.y + a, 2), lax.rem(me.x + b, 2)
            for z in range(me.Z):
                at = ((z * 2 + y) * 2 + x) * 2 + me.c
                gsib[a, b, z] = gcol[0, at] + gcol[1, at]
    comm.begin(GAIN)
    comm.second(Q)

    need_mixed = fetch(1, mixed_in, acc)
    need_mixed.wait()
    last_loads = lambda j: [
        pltpu.make_async_copy(
            down_w.at[pl.ds(j * wide, wide), :], wd.at[j % 2], load_sem.at[2]
        ),
        pltpu.make_async_copy(
            hidden_in.at[:, pl.ds(j * wide, wide)], fac_a.at[j % 2], load_sem.at[3]
        ),
    ]
    for copy in last_loads(0):
        copy.start()
    for j in range(tiles):
        for copy in last_loads(j):
            copy.wait()
        if j + 1 < tiles:
            for copy in last_loads(j + 1):
                copy.start()

        def add_down(at, j=j):
            acc[at, :] = acc[at, :] + plain_dot(fac_a[j % 2, at, :], wd[j % 2])

        over_rows(add_down, 256)
        if j == 1:
            comm.first(GAIN)
            comm.third(O)
            comm.third(D2)
        if j == 2:
            comm.second(KV)
        if j == 4:
            comm.third(Q)
            comm.second(GAIN)

    def round_result(at):
        low_t[at, :] = acc[at, :].astype(bf)

    got_low.wait_send()
    over_rows(round_result)
    store(9, low_t, result_out)
    comm.third(KV)
    comm.third(GAIN)
    for copy in passes:
        if copy is not got_low:
            copy.wait_send()
    for copy in stores:
        if not any(copy is p for p in (own_dy, own_low, own_q, own_kv)):
            copy.wait()


class _Both:
    def __init__(self, here, there):
        self.here, self.there, self.sent, self.settled = here, there, False, False

    def wait(self):
        if not self.sent:
            self.here.wait()
            self.there.wait_send()
        self.sent = True

    def settle(self):
        self.wait()
        if not self.settled:
            self.there.wait_recv()
        self.settled = True


def backward(saved, transposed, dy, x, kv_heads, group, batches):
    first_w, out_w, gate_w, up_w, down_w = saved[:5]
    queries, both_all, _, logs, mixed, _ = saved[5:11]
    hidden, slope, silu, bias, cos_tables, sin_tables = saved[11:]
    tokens, width = x.shape
    rows = tokens // batches
    Z = lax.axis_size("dp") // 2
    X = lax.axis_size("fsdp") // 2
    n, r, first_wide = first_w.shape
    rd = down_w.shape[1]
    key_wide = kv_heads * 128
    query_wide = kv_heads * group * HD
    used = query_wide + key_wide
    length = both_all.shape[1]
    features = hidden.shape[1]
    half = features // 2
    d_wide = width * 2 // 5 // 256 * 256
    wide, t = 512, 256
    bf, f32 = jnp.bfloat16, jnp.float32
    shape = jax.ShapeDtypeStruct
    vmem, dma = pltpu.VMEM, pltpu.SemaphoreType.DMA

    def four(depth, size):
        return [
            vmem((2, 2, Z, depth, size), bf),
            vmem((2, Z, depth, size), bf),
            vmem((Z, depth, size), bf),
            vmem((Z - 1, depth, size), bf),
        ]

    outs = [
        shape((tokens, width), bf),
        shape((tokens, width), bf),
        shape((r, first_wide), f32),
        shape((r, width), f32),
        shape((r, features), f32),
        shape((r, features), f32),
        shape((rd, width), f32),
        shape((Z, 2, X, rd, tokens), bf),
        shape((Z, 2, X, r, tokens), bf),
        shape((Z, 2, X, r, tokens), bf),
        shape((Z, 2, X, r, tokens), bf),
        shape((2, tokens, width), bf),
        shape((2, tokens, features), bf),
        shape((2, tokens, features), bf),
        shape((2, tokens, width), bf),
        shape((2, tokens, used), bf),
        shape((tokens, width), f32),
    ]
    any_space = pl.BlockSpec(memory_space=pl.ANY)
    in_vmem = pl.BlockSpec(memory_space=pltpu.VMEM)
    scratch = sum([four(r, half) for _ in range(3)], [])
    scratch += four(rd, d_wide) + four(rd, d_wide) + four(r, 128)
    scratch += [
        vmem((2, Z * rd, 2 * tokens), bf),
        vmem((4 * Z * r, 2 * tokens), bf),
        vmem((4, Z, r, tokens), bf),
        vmem((3, 2, tokens, t), bf),
        vmem((tokens, width), f32),
        vmem((2, 64, width), f32),
        vmem((tokens, width), bf),
        vmem((tokens, width), bf),
        vmem((tokens, query_wide), bf),
        vmem((tokens, query_wide), bf),
        vmem((tokens, used), bf),
        vmem((batches, length, key_wide), bf),
        vmem((batches, length, key_wide), bf),
        vmem((tokens, length), bias.dtype),
        vmem((tokens, 128), f32),
        vmem((2, tokens, 128), f32),
        vmem((2, tokens, 128), f32),
        vmem((2, batches, rows, key_wide), bf),
        vmem((batches, rows, key_wide), bf),
        vmem((n, r, key_wide), bf),
        vmem((width, key_wide), bf),
        vmem((2, wide, width), bf),
        vmem((2, tokens, wide), bf),
        vmem((2, tokens, wide), bf),
        vmem((tokens, wide), bf),
        vmem((tokens, wide), bf),
        vmem((8, width), f32),
        vmem((8, width), f32),
        vmem((2, n, r, 128), bf),
        dma((11, 2 + Z)),
        dma((11, 2 + Z)),
        pltpu.SemaphoreType.REGULAR((5,)),
        dma((12,)),
        dma((12,)),
        dma((2 * (features // wide),)),
        dma((2 * (features // wide),)),
        dma((12,)),
        dma((8 * Z,)),
        dma((10,)),
        dma((3, 2)),
        dma((3,)),
    ]
    return pl.pallas_call(
        functools.partial(backward_kernel, (batches, rows, kv_heads, group, used)),
        out_shape=outs,
        in_specs=[any_space] * 21,
        out_specs=[any_space] * 2 + [in_vmem] * 5 + [any_space] * 10,
        scratch_shapes=scratch,
        compiler_params=pltpu.CompilerParams(
            collective_id=2, has_side_effects=True, vmem_limit_bytes=63 * 2**20
        ),
    )(
        dy,
        first_w,
        out_w,
        gate_w,
        up_w,
        down_w.reshape(-1, width),
        queries,
        both_all,
        logs,
        mixed,
        hidden,
        slope,
        silu,
        bias,
        cos_tables,
        sin_tables,
        *transposed,
        x,
    )


def half_of(full):
    return full.astype(jnp.bfloat16)


def rotary_pairs(places, tokens, score_scale):
    cos_table, sin_table = rope_tables(places.reshape(tokens))
    ones, zeros = jnp.ones((tokens, HD), jnp.float32), jnp.zeros((tokens, HD), jnp.float32)
    cos_pair = jnp.concatenate([cos_table, cos_table], -1)
    sin_pair = jnp.concatenate([-sin_table, sin_table], -1)
    cos_tables = jnp.stack(
        [
            jnp.concatenate([cos_pair, cos_pair], -1) * score_scale,
            jnp.concatenate([cos_pair, ones], -1),
        ]
    )
    sin_tables = jnp.stack(
        [
            jnp.concatenate([sin_pair, sin_pair], -1) * score_scale,
            jnp.concatenate([sin_pair, zeros], -1),
        ]
    )
    return cos_tables, sin_tables


def forward_plain(shards, x, places, kv_heads, group, batches):
    tokens = x.shape[0]
    rows = tokens // batches
    length = rows * lax.axis_size("fsdp")
    query_features = kv_heads * group * HD
    used = query_features + kv_heads * 128
    fulls = gather(shards, ("yxc", "xyc", "yxc", "xyc", "yxc"), 1, 5)
    first_pack, out_full, gate_full, up_full, _ = (f.reshape(-1, f.shape[-1]) for f in fulls)
    gains = first_pack[:, used : used + 2].astype(jnp.float32).T
    query_index = lax.axis_index("fsdp") * rows + jnp.arange(rows, dtype=jnp.int32)
    key_index = jnp.arange(length, dtype=jnp.int32)
    x_float = x.astype(jnp.float32)
    cos_tables, sin_tables = rotary_pairs(places, tokens, HD**-0.5)
    doc_start = query_index[None, :] - places.reshape(batches, rows)
    allowed = (key_index[None, None, :] <= query_index[None, :, None]) & (
        key_index[None, None, :] >= doc_start[:, :, None]
    )
    bias = jnp.where(allowed, 0.0, NEGATIVE)
    attn_inverse = lax.rsqrt(jnp.mean(x_float * x_float, -1, keepdims=True) + EPSILON)
    normed = (x_float * attn_inverse * gains[0]).astype(jnp.bfloat16)
    projected = project(normed, first_pack[:, :used], cos_tables, sin_tables, kv_heads * 128)
    both_rows = projected[:, query_features:].reshape(batches, rows, -1)
    both_all = lax.all_gather(both_rows, "fsdp", axis=1, tiled=True)
    attended, logs = attend(projected, both_all, bias, kv_heads, group)
    mixed = x_float + plain_dot(attended, out_full)
    mlp_inverse = lax.rsqrt(jnp.mean(mixed * mixed, -1, keepdims=True) + EPSILON)
    normed_mlp = (mixed * mlp_inverse * gains[1]).astype(jnp.bfloat16)
    gate_pre = plain_dot(normed_mlp, gate_full)
    up_proj = plain_dot(normed_mlp, up_full)
    gate_sig = jax.nn.sigmoid(gate_pre)
    silu = gate_pre * gate_sig
    slope = up_proj * gate_sig * (1.0 + gate_pre * (1.0 - gate_sig))
    low = jnp.bfloat16
    return list(fulls) + [
        projected[:, :query_features],
        both_all,
        attended,
        logs,
        mixed,
        normed_mlp,
        (silu * up_proj).astype(low),
        slope.astype(low),
        silu.astype(low),
        bias.reshape(tokens, length),
        cos_tables,
        sin_tables,
    ]


def backward_plain(saved, cotangent, x_low, kv_heads, group, batches):
    tokens, width = x_low.shape
    rows = tokens // batches
    key_features = kv_heads * HD
    query_features = kv_heads * group * HD
    used = query_features + 2 * key_features
    x_float = x_low.astype(jnp.float32)
    first_pack, out_full, gate_full, up_full, down_full = (
        f.reshape(-1, f.shape[-1]) for f in saved[:5]
    )
    queries, both_all, attended, logs, mixed, normed_mlp = saved[5:11]
    hidden, slope, silu, bias, cos_tables, sin_tables = saved[11:]
    projection = first_pack[:, :used]
    gains = first_pack[:, used : used + 2].astype(jnp.float32).T
    attn_gain_f = gains[0]
    mlp_gain_f = gains[1]
    attn_inverse = lax.rsqrt(jnp.mean(x_float * x_float, -1, keepdims=True) + EPSILON)
    normed = (x_float * attn_inverse * attn_gain_f).astype(jnp.bfloat16)
    mlp_inverse = lax.rsqrt(jnp.mean(mixed * mixed, -1, keepdims=True) + EPSILON)
    output = (mixed + plain_dot(hidden, down_full)).astype(jnp.bfloat16)

    cot_low = cotangent
    cot_float = cot_low.astype(jnp.float32)
    grad_down = half_of(left_dot(hidden, cot_low))
    grad_hidden = right_dot(cot_low, down_full)
    grad_gate_pre = (grad_hidden * slope.astype(jnp.float32)).astype(jnp.bfloat16)
    grad_up_pre = (grad_hidden * silu.astype(jnp.float32)).astype(jnp.bfloat16)
    grad_gate = half_of(left_dot(normed_mlp, grad_gate_pre))
    grad_up = half_of(left_dot(normed_mlp, grad_up_pre))
    grad_normed_mlp = right_dot(grad_gate_pre, gate_full) + right_dot(grad_up_pre, up_full)
    grad_mlp_gain = jnp.sum(grad_normed_mlp * mixed * mlp_inverse, 0)
    grad_mixed = cot_float + norm_back(grad_normed_mlp * mlp_gain_f, mixed, mlp_inverse)
    grad_mixed_low = grad_mixed.astype(jnp.bfloat16)
    grad_out = half_of(left_dot(attended, grad_mixed_low))
    grad_attended = right_dot(grad_mixed_low, out_full).astype(jnp.bfloat16)
    grad_query_pre, portions = attend_back(
        queries,
        grad_attended,
        both_all,
        bias.reshape(batches, rows, -1),
        logs,
        cos_tables,
        sin_tables,
        group,
    )
    sums = lax.psum_scatter(portions, "fsdp", scatter_dimension=1, tiled=True)
    sums = sums.astype(jnp.float32).reshape(tokens, kv_heads, 128)
    turned = jnp.concatenate([sums[..., 32:64], sums[..., :32], sums[..., 64:]], -1)
    grad_pair_pre = (sums * cos_tables[1][:, None] - turned * sin_tables[1][:, None]).astype(
        jnp.bfloat16
    )
    grad_pre = jnp.concatenate(
        [grad_query_pre, grad_pair_pre.reshape(tokens, 2 * key_features)], -1
    )
    grad_projection = left_dot(normed, grad_pre)
    grad_normed = right_dot(grad_pre, projection)
    grad_attn_gain = jnp.sum(grad_normed * x_float * attn_inverse, 0)
    grad_input = grad_mixed + norm_back(grad_normed * attn_gain_f, x_float, attn_inverse)
    gain_columns = jnp.stack([grad_attn_gain, grad_mlp_gain], -1)
    gain_columns = jnp.pad(gain_columns, ((0, 0), (0, 126)))
    grad_first = half_of(jnp.concatenate([grad_projection, gain_columns], 1))
    grad_down, grad_gate, grad_up, grad_out, last = scatter(
        (grad_down, grad_gate, grad_up, grad_out, grad_first), ("xy", "yx", "xy", "yx", "xy"), 2
    )
    return (
        output,
        grad_input.astype(jnp.bfloat16),
        last,
        grad_out,
        grad_gate,
        grad_up,
        grad_down,
    )


def on_device(
    inputs,
    positions,
    cotangent,
    attn_gain,
    w_query,
    key_matrix,
    value_matrix,
    w_out,
    mlp_gain,
    w_gate,
    w_up,
    w_down,
):
    batches, _, rows, width = inputs.shape
    shard = w_query.shape[0]
    query_features = w_query.shape[1]
    key_features = key_matrix.shape[1]
    kv_heads = key_features // HD
    group = query_features // key_features
    tokens = batches * rows
    used = query_features + 2 * key_features

    extras = jnp.zeros((shard, 128), jnp.bfloat16)
    extras = extras.at[:, 0].set(attn_gain).at[:, 1].set(mlp_gain)
    pairs = jnp.concatenate(
        [key_matrix.reshape(shard, kv_heads, HD), value_matrix.reshape(shard, kv_heads, HD)], -1
    )
    first_shard = jnp.concatenate([w_query, pairs.reshape(shard, -1), extras], axis=1)
    shards = (first_shard, w_out, w_gate, w_up, w_down)
    x_low = inputs.reshape(tokens, width)
    cot_low = cotangent.reshape(tokens, width)
    fits = shard % 8 == 0 and lax.axis_size("fsdp") == 4 and rows % 256 == 0
    saved = (forward if fits else forward_plain)(
        shards, x_low, positions.reshape(tokens, 1), kv_heads, group, batches
    )
    if fits:
        by_place = (lax.axis_size("dp") // 2, 2, lax.axis_size("fsdp") // 2, 2, -1, tokens)
        transposed = [t.reshape(by_place) for t in saved[17:]]
        found = backward(saved[:17], transposed, cot_low, x_low, kv_heads, group, batches)
    else:
        found = backward_plain(saved, cot_low, x_low, kv_heads, group, batches)
    output, grad_input, last, grad_out, grad_gate, grad_up, grad_down = found[:7]
    last_pairs = last[:, query_features:used].reshape(shard, kv_heads, 2, HD)
    return (
        output.reshape(inputs.shape),
        grad_input.reshape(inputs.shape),
        last[:, used],
        last[:, :query_features],
        last_pairs[:, :, 0].reshape(shard, key_features),
        last_pairs[:, :, 1].reshape(shard, key_features),
        grad_out,
        last[:, used + 1],
        grad_gate,
        grad_up,
        grad_down,
    )


def solution(mesh):
    tokens = P(None, "dp", "fsdp", None)
    vector = P(BOTH)
    matrix = P(BOTH, None)
    weights = (vector, matrix, matrix, matrix, matrix, vector, matrix, matrix, matrix)
    return jax.shard_map(
        on_device,
        mesh=mesh,
        in_specs=(tokens, P(None, "dp", "fsdp"), tokens) + weights,
        out_specs=(tokens, tokens) + weights,
        check_vma=False,
    )
```

```python
import functools

import jax
import jax.numpy as jnp
from jax import lax
from jax.experimental import pallas as pl
from jax.experimental.pallas import tpu as pltpu
from jax.sharding import PartitionSpec as P

HD = 64
EPSILON = 1e-05
NEGATIVE = -1e30
ROPE_BASE = 10000.0
BOTH = ("dp", "fsdp")


def rope_tables(places):
    half = HD // 2
    freqs = ROPE_BASE ** (-jnp.arange(half).astype(jnp.float32) / half)
    angles = places.astype(jnp.float32)[:, None] * freqs[None, :]
    return (jnp.cos(angles), jnp.sin(angles))


def plain_dot(left, right):
    return jnp.dot(left, right, preferred_element_type=jnp.float32)


def left_dot(left, right):
    return lax.dot_general(
        left, right, (((0,), (0,)), ((), ())), preferred_element_type=jnp.float32
    )


def right_dot(left, right):
    return lax.dot_general(
        left, right, (((1,), (1,)), ((), ())), preferred_element_type=jnp.float32
    )


def norm_back(grad_normed, inputs_float, inverse):
    return inverse * (
        grad_normed
        - inputs_float * inverse * inverse * jnp.mean(grad_normed * inputs_float, -1, keepdims=True)
    )


class Place:
    def __init__(self):
        self.Z=lax.axis_size("dp")//2; self.X=lax.axis_size("fsdp")//2
        dp=lax.axis_index("dp"); fs=lax.axis_index("fsdp")
        self.z=dp//2; self.y=dp%2; self.x=fs//2; self.c=fs%2
    def device(self,s=0,dy=0,dx=0,dc=0):
        return (lax.rem(self.z+s,self.Z)*2+lax.rem(self.y+dy,2), lax.rem(self.x+dx,self.X)*2+lax.rem(self.c+dc,2))
    def slot(self,s,dy,dx,dc):
        return ((lax.rem(self.z+self.Z-s,self.Z)*2+lax.rem(self.y+dy,2))*self.X+lax.rem(self.x+dx,self.X))*2+lax.rem(self.c+dc,2)

MESH = pl.DeviceIdType.MESH

def greet(me):
    barrier=pltpu.get_barrier_semaphore()
    friends=[me.device(s=s) for s in range(1,me.Z)]+[me.device(dy=1),me.device(dx=1),me.device(dc=1)]
    for f in friends:
        pl.semaphore_signal(barrier,inc=1,device_id=f,device_id_type=MESH)
    pl.semaphore_wait(barrier,len(friends))

def gather_kernel(Z, orders, ahead, *refs):
    K=len(orders)
    shards=refs[:K]; outs=refs[K:2*K]; local,send,recv=refs[2*K:]
    me=Place()
    greet(me)
    dims={"y":1,"x":2,"c":3}
    def sem(rel):
        return ((rel[0]*2+rel[1])*2+rel[2])*2+rel[3]
    started=[]
    def start(k,rel,to):
        if isinstance(to,int):
            target=me.device(s=to); landed=(to,0,0,0)
        else:
            landed=list(rel); landed[dims[to]]=1; landed=tuple(landed)
            target=me.device(**{"d"+to:1})
        slot=me.slot(*rel)
        src=shards[k] if rel==(0,0,0,0) else outs[k].at[slot]
        cp=pltpu.make_async_remote_copy(src_ref=src,dst_ref=outs[k].at[slot],send_sem=send.at[k,sem(landed)],recv_sem=recv.at[k,sem(landed)],device_id=target,device_id_type=MESH)
        cp.start()
        table[(k,landed)]=cp
    table={}
    own=[]
    def first(k):
        cp=pltpu.make_async_copy(shards[k],outs[k].at[me.slot(0,0,0,0)],local.at[k]); cp.start(); own.append(cp)
        for s in range(1,Z): start(k,(0,0,0,0),s)
        for d in orders[k]: start(k,(0,0,0,0),d)
    def arrive(k,rel,rest):
        table[(k,rel)].wait_recv()
        for d in rest: start(k,rel,d)
    def rel_of(s,o,a,b=0,c=0):
        r=[s,0,0,0]; r[dims[o[0]]]=a; r[dims[o[1]]]=b; r[dims[o[2]]]=c
        return tuple(r)
    for k in range(min(ahead,K)): first(k)
    for t in range(K+3):
        if t+ahead<K: first(t+ahead)
        k=t
        if k<K:
            o=orders[k]
            for s in range(1,Z): arrive(k,rel_of(s,o,0),o)
        k=t-1
        if 0<=k<K:
            o=orders[k]
            for s in range(Z): arrive(k,rel_of(s,o,1),o[1:])
        k=t-2
        if 0<=k<K:
            o=orders[k]
            for s in range(Z):
                for a in range(2): arrive(k,rel_of(s,o,a,1),o[2:])
        k=t-3
        if 0<=k<K:
            o=orders[k]
            for s in range(Z):
                for a in range(2):
                    for b in range(2): arrive(k,rel_of(s,o,a,b,1),"")
    for cp in own: cp.wait()
    for cp in table.values(): cp.wait_send()

def gather(shards, orders, cid, ahead=2):
    n=lax.axis_size("dp")*lax.axis_size("fsdp"); Z=lax.axis_size("dp")//2; K=len(shards)
    return pl.pallas_call(functools.partial(gather_kernel,Z,orders,ahead),
        out_shape=[jax.ShapeDtypeStruct((n,)+s.shape,s.dtype) for s in shards],
        in_specs=[pl.BlockSpec(memory_space=pl.ANY)]*K,
        out_specs=[pl.BlockSpec(memory_space=pl.ANY)]*K,
        scratch_shapes=[pltpu.SemaphoreType.DMA((K,)),pltpu.SemaphoreType.DMA((K,8*Z)),pltpu.SemaphoreType.DMA((K,8*Z))],
        compiler_params=pltpu.CompilerParams(collective_id=cid,has_side_effects=True))(*shards)


class Gathering:
    def __init__(self, me, chunks, local, send, recv):
        self.me, self.chunks = me, chunks
        self.local, self.send, self.recv = local, send, recv
        self.table, self.own = {}, []

    def start(self, k, rel, to):
        shard, full, cols, _ = self.chunks[k]
        me = self.me
        if isinstance(to, int):
            target, landed = me.device(s=to), (to, 0, 0, 0)
        else:
            landed = list(rel)
            landed["zyxc".index(to)] = 1
            landed = tuple(landed)
            target = me.device(**{"d" + to: 1})
        slot = me.slot(*rel)
        here = full.at[slot, :, cols]
        at = ((landed[0] * 2 + landed[1]) * 2 + landed[2]) * 2 + landed[3]
        copy = pltpu.make_async_remote_copy(
            src_ref=shard.at[:, cols] if rel == (0, 0, 0, 0) else here,
            dst_ref=here,
            send_sem=self.send.at[k, at],
            recv_sem=self.recv.at[k, at],
            device_id=target,
            device_id_type=MESH,
        )
        copy.start()
        self.table[(k, landed)] = copy

    def begin(self, k):
        shard, full, cols, order = self.chunks[k]
        copy = pltpu.make_async_copy(
            shard.at[:, cols], full.at[self.me.slot(0, 0, 0, 0), :, cols], self.local.at[k]
        )
        copy.start()
        self.own.append((k, copy))
        for s in range(1, self.me.Z):
            self.start(k, (0, 0, 0, 0), s)
        for d in order:
            self.start(k, (0, 0, 0, 0), d)

    def step(self, k, stage):
        order = self.chunks[k][3]
        where = ["zyxc".index(d) for d in order]
        for s in range(1 if stage == 0 else 0, self.me.Z):
            for bits in range(1 << max(stage - 1, 0)):
                rel = [s, 0, 0, 0]
                for i in range(stage - 1):
                    rel[where[i]] = bits >> i & 1
                if stage:
                    rel[where[stage - 1]] = 1
                rel = tuple(rel)
                self.table[(k, rel)].wait_recv()
                for d in order[stage:]:
                    self.start(k, rel, d)
        if stage == 3:
            for at, copy in self.own:
                if at == k:
                    copy.wait()

    def finish(self):
        for copy in self.table.values():
            copy.wait_send()


def forward_kernel(sizes, *refs):
    batches, rows, kv_heads, group, used = sizes
    (first_s, out_s, gate_s, up_s, down_s, x_ref, place_ref, freq_ref) = refs[:8]
    (first_w, out_w, gate_w, up_w, down_w, q_out, kv_out, o_out, log_out) = refs[8:17]
    (mixed_out, h2_out, hidden_out, slope_out, silu_out, bias_out, cos_out, sin_out) = refs[17:25]
    (hid_turned, h2_turned, att_turned, nor_turned) = refs[25:29]
    (raw_a, raw_b, w_a, w_b, normed, queries, kv_all, attended, logs, mixed, h2) = refs[29:40]
    (hidden, slope, silu, bias, cos_t, sin_t, gains) = refs[40:47]
    (hid_t, h2_t, att_t, nor_t) = refs[47:51]
    (local, send, recv, kv_send, kv_recv, load_sem, store_sem) = refs[51:]
    me = Place()
    greet(me)
    whole = slice(None)
    half = down_w.shape[2] // 2
    comm = Gathering(
        me,
        (
            (first_s, first_w, whole, "xyc"),
            (out_s, out_w, whole, "yxc"),
            (gate_s, gate_w, whole, "yxc"),
            (up_s, up_w, whole, "xyc"),
            (down_s, down_w, pl.ds(0, half), "yxc"),
            (down_s, down_w, pl.ds(half, half), "xyc"),
        ),
        local,
        send,
        recv,
    )
    tokens, width = x_ref.shape
    length = kv_all.shape[1]
    stores = []

    def store(i, src, dst):
        copy = pltpu.make_async_copy(src, dst, store_sem.at[i])
        copy.start()
        stores.append(copy)

    def over_rows(body, step=64):
        def one(i, carry):
            body(pl.ds(pl.multiple_of(i * step, step), step))
            return carry

        lax.fori_loop(0, tokens // step, one, 0)

    def load(full, raw, col, size, i):
        return pltpu.make_async_copy(
            full.at[:, :, pl.ds(col, size)], raw.at[:, :, pl.ds(0, size)], load_sem.at[i]
        )

    def assemble(raw, flat, size):
        n, r, _ = raw.shape
        pair = 2 * r

        def one(i, carry):
            piece = raw[pl.ds(2 * i, 2), :, pl.ds(0, size)].astype(jnp.float32)
            flat[pl.ds(pl.multiple_of(pair * i, 16), pair), pl.ds(0, size)] = piece.reshape(
                pair, size
            ).astype(jnp.bfloat16)
            return carry

        lax.fori_loop(0, n // 2, one, 0)

    def turn_rows(src, dst, base, size):
        for i in range(size // 256):
            at = slice(base + i * 256, base + (i + 1) * 256)
            dst[at, :] = src[:, at].astype(jnp.float32).T.astype(jnp.bfloat16)

    comm.begin(0)
    comm.begin(1)
    comm.begin(2)

    scale = HD**-0.5
    lane = lax.broadcasted_iota(jnp.int32, (64, 128), 1)
    second = lax.rem(lane, HD) >= HD // 2
    is_value = lane >= HD

    def tables(at):
        angle = place_ref[at, :].astype(jnp.float32) * freq_ref[...]
        c, s = jnp.cos(angle), jnp.sin(angle)
        s = jnp.where(second, s, -s)
        cos_t[0, at, :] = c * scale
        sin_t[0, at, :] = s * scale
        cos_t[1, at, :] = jnp.where(is_value, 1.0, c)
        sin_t[1, at, :] = jnp.where(is_value, 0.0, s)

    over_rows(tables)
    first_row = lax.axis_index("fsdp") * rows

    def masks(at):
        token = at.start
        inside = lax.rem(token, rows)
        query = first_row + inside + lax.broadcasted_iota(jnp.int32, (64, length), 0)
        key = lax.broadcasted_iota(jnp.int32, (64, length), 1)
        start = query - place_ref[at, :]
        allowed = (key <= query) & (key >= start)
        bias[at, :] = jnp.where(allowed, 0.0, NEGATIVE).astype(jnp.bfloat16)

    over_rows(masks)
    store(0, bias, bias_out)
    store(1, cos_t, cos_out)
    store(2, sin_t, sin_out)

    comm.step(0, 0)
    comm.begin(3)
    comm.step(1, 0)
    comm.step(0, 1)
    comm.step(2, 0)
    comm.step(1, 1)
    comm.step(0, 2)
    comm.begin(4)
    comm.step(3, 0)
    comm.step(2, 1)
    comm.step(1, 2)
    comm.step(0, 3)

    tile = raw_a.shape[2]
    load(first_w, raw_a, used, 128, 0).start()
    load(first_w, raw_b, 0, tile, 1).start()
    load(first_w, raw_a, used, 128, 0).wait()
    assemble(raw_a, w_a, 128)
    gains[...] = w_a[:, :128].astype(jnp.float32).T[:8]
    load(first_w, raw_a, used - tile, tile, 0).start()

    def norm_one(at):
        x = x_ref[at, :].astype(jnp.float32)
        inverse = lax.rsqrt(jnp.mean(x * x, -1, keepdims=True) + EPSILON)
        normed[at, :] = (x * inverse * gains[0:1, :]).astype(jnp.bfloat16)

    over_rows(norm_one)
    comm.step(4, 0)

    def turn(flat, kind, put, step=256):
        def body(at):
            u = plain_dot(normed[at, :], flat[...])
            for j in range(tile // 128):
                piece = u[:, j * 128 : (j + 1) * 128]
                piece = piece * cos_t[kind, at, :] + swap_halves(piece) * sin_t[kind, at, :]
                put(at, j, piece.astype(jnp.bfloat16))

        over_rows(body, step)

    slot = (me.x * 2 + me.c) * rows

    def put_pair(at, j, piece):
        token = at.start
        b = token // rows
        row = pl.multiple_of(slot + lax.rem(token, rows), 256)
        kv_all[b, pl.ds(row, 256), j * 128 : (j + 1) * 128] = piece

    load(first_w, raw_a, used - tile, tile, 0).wait()
    assemble(raw_a, w_a, tile)
    turn(w_a, 1, put_pair)

    def share(i, dx, to):
        row = (lax.rem(me.x + dx, 2) * 2 + me.c) * rows
        block = kv_all.at[:, pl.ds(pl.multiple_of(row, 256), rows), :]
        copy = pltpu.make_async_remote_copy(
            src_ref=block,
            dst_ref=block,
            send_sem=kv_send.at[i],
            recv_sem=kv_recv.at[i],
            device_id=me.device(**{"d" + to: 1}),
            device_id_type=MESH,
        )
        copy.start()
        return copy

    to_x = share(0, 0, "x")
    to_c = share(1, 0, "c")
    comm.step(3, 1)
    comm.begin(5)
    for j in range(queries.shape[1] // tile):
        raw, flat = ((raw_b, w_b), (raw_a, w_a))[j % 2]
        if (j + 1) * tile < queries.shape[1]:
            load(first_w, (raw_a, raw_b)[j % 2], (j + 1) * tile, tile, j % 2).start()
        load(first_w, raw, j * tile, tile, 1 - j % 2).wait()
        assemble(raw, flat, tile)

        def put_query(at, i, piece, j=j):
            queries[at, j * tile + i * 128 : j * tile + (i + 1) * 128] = piece

        turn(flat, 0, put_query)
        if j == 0:
            comm.step(2, 2)
    store(3, queries, q_out)
    turn_rows(normed, nor_t, 0, width)
    store(12, nor_t, nor_turned)
    comm.step(1, 3)
    to_x.wait_recv()
    to_far = share(2, 1, "c")
    to_c.wait_recv()
    to_far.wait_recv()
    store(4, kv_all, kv_out)

    logs[...] = jnp.zeros_like(logs)
    lanes = lax.broadcasted_iota(jnp.int32, (rows, 128), 1)
    sides_mask = lane_masks(rows)

    def head(i, carry):
        b = i // kv_heads
        h = lax.rem(i, kv_heads)
        at = pl.ds(pl.multiple_of(b * rows, 256), rows)
        kv = kv_all[b, :, pl.ds(pl.multiple_of(h * 128, 128), 128)]
        sides = (kv, swapped(kv))
        shift = bias[at, :].astype(jnp.float32)
        log_piece = logs[at, :]
        for pair in range(group // 2):
            cols = pl.ds(pl.multiple_of(h * group * HD + pair * 128, 128), 128)
            q = queries[at, cols]
            found = []
            for side in range(2):
                scores = dot_t(q * sides_mask[side], sides[side]) + shift
                top = jnp.max(scores, -1, keepdims=True)
                powers = jnp.exp(scores - top)
                total = jnp.sum(powers, -1, keepdims=True)
                probs = (powers * (1.0 / total)).astype(jnp.bfloat16)
                found.append(plain_dot(probs, sides[1 - side]))
                log_piece = jnp.where(
                    lanes == h * group + pair * 2 + side, top + jnp.log(total), log_piece
                )
            attended[at, cols] = jnp.where(lanes < HD, found[0], found[1]).astype(jnp.bfloat16)
        logs[at, :] = log_piece
        return carry

    count = batches * kv_heads
    pumps = [(5, 0), (4, 1), (3, 2), (2, 3), (5, 1), (4, 2)]
    done = 0
    for i in range(6):
        upto = (2, 4, 6, 8, 9, 10)[i] * count // 10
        lax.fori_loop(done, upto, head, 0)
        done = upto
        comm.step(*pumps[i])
    store(5, attended, o_out)
    store(6, logs, log_out)

    steps = width // tile
    load(out_w, raw_a, 0, tile, 0).start()
    for j in range(steps):
        raw, flat = ((raw_a, w_a), (raw_b, w_b))[j % 2]
        if j + 1 < steps:
            load(out_w, (raw_b, raw_a)[j % 2], (j + 1) * tile, tile, 1 - j % 2).start()
        load(out_w, raw, j * tile, tile, j % 2).wait()
        assemble(raw, flat, tile)

        def add_in(at, flat=flat, j=j):
            cols = slice(j * tile, (j + 1) * tile)
            mixed[at, cols] = x_ref[at, cols].astype(jnp.float32) + plain_dot(
                attended[at, :], flat[...]
            )

        over_rows(add_in, 256)

    def norm_two(at):
        y = mixed[at, :]
        inverse = lax.rsqrt(jnp.mean(y * y, -1, keepdims=True) + EPSILON)
        h2[at, :] = (y * inverse * gains[1:2, :]).astype(jnp.bfloat16)

    over_rows(norm_two)
    store(7, mixed, mixed_out)
    store(8, h2, h2_out)
    turn_rows(attended, att_t, 0, attended.shape[1])
    store(13, att_t, att_turned)
    turn_rows(h2, h2_t, 0, width)
    store(14, h2_t, h2_turned)
    comm.step(3, 3)

    wide = 512
    features = hidden.shape[1]
    pumps = {2: (5, 2), 5: (4, 3)}
    load(gate_w, raw_a, 0, wide, 0).start()
    load(up_w, raw_b, 0, wide, 1).start()
    for j in range(features // wide):
        load(gate_w, raw_a, j * wide, wide, 0).wait()
        assemble(raw_a, w_a, wide)
        load(up_w, raw_b, j * wide, wide, 1).wait()
        assemble(raw_b, w_b, wide)
        if (j + 1) * wide < features:
            load(gate_w, raw_a, (j + 1) * wide, wide, 0).start()
            load(up_w, raw_b, (j + 1) * wide, wide, 1).start()

        def units(at, j=j):
            cols = slice(j * wide, (j + 1) * wide)
            g = plain_dot(h2[at, :], w_a[:, :wide])
            u = plain_dot(h2[at, :], w_b[:, :wide])
            sig = jax.nn.sigmoid(g)
            soft = g * sig
            hidden[at, cols] = (soft * u).astype(jnp.bfloat16)
            silu[at, cols] = soft.astype(jnp.bfloat16)
            slope[at, cols] = (u * (sig * (1.0 + g * (1.0 - sig)))).astype(jnp.bfloat16)

        over_rows(units, 256)
        turn_rows(hidden, hid_t, j * wide, wide)
        if j in pumps:
            comm.step(*pumps[j])
    store(9, hidden, hidden_out)
    store(10, silu, silu_out)
    store(11, slope, slope_out)
    store(15, hid_t, hid_turned)
    comm.step(5, 3)
    for copy in (to_x, to_c, to_far):
        copy.wait_send()
    comm.finish()
    for copy in stores:
        copy.wait()


def forward(shards, x, places, kv_heads, group, batches):
    first_s, out_s, gate_s, up_s, down_s = shards
    n = lax.axis_size("dp") * lax.axis_size("fsdp")
    Z = lax.axis_size("dp") // 2
    tokens, width = x.shape
    rows = tokens // batches
    length = rows * lax.axis_size("fsdp")
    key_wide = kv_heads * 128
    query_wide = kv_heads * group * HD
    used = query_wide + key_wide
    features = gate_s.shape[1]
    r = first_s.shape[0]
    freqs = ROPE_BASE ** (-jnp.arange(HD // 2).astype(jnp.float32) / (HD // 2))
    freqs = jnp.tile(freqs, 4)[None]
    bf, f32 = jnp.bfloat16, jnp.float32
    shape = jax.ShapeDtypeStruct
    outs = [shape((n,) + s.shape, s.dtype) for s in shards] + [
        shape((tokens, query_wide), bf),
        shape((batches, length, key_wide), bf),
        shape((tokens, query_wide), bf),
        shape((tokens, 128), f32),
        shape((tokens, width), f32),
        shape((tokens, width), bf),
        shape((tokens, features), bf),
        shape((tokens, features), bf),
        shape((tokens, features), bf),
        shape((tokens, length), bf),
        shape((2, tokens, 128), f32),
        shape((2, tokens, 128), f32),
        shape((features, tokens), bf),
        shape((width, tokens), bf),
        shape((query_wide, tokens), bf),
        shape((width, tokens), bf),
    ]
    vmem = pltpu.VMEM
    scratch = [
        vmem((n, r, key_wide), bf),
        vmem((n, r, key_wide), bf),
        vmem((width, key_wide), bf),
        vmem((width, key_wide), bf),
        vmem((tokens, width), bf),
        vmem((tokens, query_wide), bf),
        vmem((batches, length, key_wide), bf),
        vmem((tokens, query_wide), bf),
        vmem((tokens, 128), f32),
        vmem((tokens, width), f32),
        vmem((tokens, width), bf),
        vmem((tokens, features), bf),
        vmem((tokens, features), bf),
        vmem((tokens, features), bf),
        vmem((tokens, length), bf),
        vmem((2, tokens, 128), f32),
        vmem((2, tokens, 128), f32),
        vmem((8, width), f32),
        vmem((features, tokens), bf),
        vmem((width, tokens), bf),
        vmem((query_wide, tokens), bf),
        vmem((width, tokens), bf),
        pltpu.SemaphoreType.DMA((6,)),
        pltpu.SemaphoreType.DMA((6, 8 * Z)),
        pltpu.SemaphoreType.DMA((6, 8 * Z)),
        pltpu.SemaphoreType.DMA((3,)),
        pltpu.SemaphoreType.DMA((3,)),
        pltpu.SemaphoreType.DMA((2,)),
        pltpu.SemaphoreType.DMA((16,)),
    ]
    any_space = pl.BlockSpec(memory_space=pl.ANY)
    in_vmem = pl.BlockSpec(memory_space=pltpu.VMEM)
    return pl.pallas_call(
        functools.partial(forward_kernel, (batches, rows, kv_heads, group, used)),
        out_shape=outs,
        in_specs=[any_space] * 5 + [in_vmem] * 3,
        out_specs=[any_space] * len(outs),
        scratch_shapes=scratch,
        compiler_params=pltpu.CompilerParams(
            collective_id=1, has_side_effects=True, vmem_limit_bytes=63 * 2**20
        ),
        cost_estimate=pl.CostEstimate(
            flops=2 * tokens * width * (used + width + 2 * features),
            bytes_accessed=4 * n * r * (used + width + 3 * features),
            transcendentals=tokens * features,
        ),
    )(*shards, x, places, freqs)


def tile_of(N):
    for t in (512,384,256,128):
        if N%t==0: return t
    return N

def scatter_kernel(Z, orders, ahead, dims_, *refs):
    K=len(orders)
    parts=refs[:K]; outs=refs[K:2*K]
    sc=refs[2*K:]
    first_buf=sc[:K]; one_buf=sc[K:2*K]; two_buf=sc[2*K:3*K]; last_buf=sc[3*K:4*K]
    shapes=sorted(set(dims_))
    stage=[sc[4*K+shapes.index(d)] for d in dims_]
    local,send,recv=sc[4*K+len(shapes):]
    me=Place()
    greet(me)
    copies={}
    def ship(k,name,index,src,dst,target):
        cp=pltpu.make_async_remote_copy(src_ref=src,dst_ref=dst,send_sem=send.at[k,index],recv_sem=recv.at[k,index],device_id=target,device_id_type=MESH)
        cp.start(); copies[(k,name)]=cp
    def part(k,a,b,other):
        o=orders[k]
        rel={o[0]:a,o[1]:b}
        y=lax.rem(me.y+rel["y"],2); x=lax.rem(me.x+rel["x"],me.X); c=lax.rem(me.c+other,2)
        return parts[k].at[:,y,x,c]
    order4=((1,1),(1,0),(0,1),(0,0))
    locals_={}
    def first(k):
        for i,(a,b) in enumerate(order4):
            ship(k,("c",a,b),i,part(k,a,b,1),first_buf[k].at[a,b],me.device(dc=1))
    def bring(k,i):
        a,b=order4[i]
        cp=pltpu.make_async_copy(part(k,a,b,0),stage[k].at[i%2],local.at[k,i%2]); cp.start(); locals_[(k,i)]=cp
    def add(dst,src,k):
        _,r,N=dims_[k]
        t=tile_of(N)
        def body(i,_):
            zi=i//(N//t); j=i%(N//t)
            cols=pl.ds(pl.multiple_of(j*t,128),t)
            dst[zi,:,cols]=dst[zi,:,cols]+src[zi,:,cols]
            return 0
        lax.fori_loop(0,Z*(N//t),body,0)
    def step_c(k):
        bring(k,0); bring(k,1)
        for i,(a,b) in enumerate(order4):
            copies[(k,("c",a,b))].wait_recv()
            locals_[(k,i)].wait()
            add(first_buf[k].at[a,b],stage[k].at[i%2],k)
            if i+2<4: bring(k,i+2)
            if a==1:
                ship(k,("1",b),4+b,first_buf[k].at[1,b],one_buf[k].at[b],me.device(**{"d"+orders[k][0]:1}))
    def step_1(k):
        for b in (1,0):
            copies[(k,("1",b))].wait_recv()
            add(first_buf[k].at[0,b],one_buf[k].at[b],k)
            if b==1:
                ship(k,"2",6,first_buf[k].at[0,1],two_buf[k],me.device(**{"d"+orders[k][1]:1}))
    def step_2(k):
        copies[(k,"2")].wait_recv()
        add(first_buf[k].at[0,0],two_buf[k],k)
        for s in range(1,Z):
            ship(k,("z",s),6+s,first_buf[k].at[0,0,lax.rem(me.z+s,Z)],last_buf[k].at[s-1],me.device(s=s))
    def step_z(k):
        _,r,N=dims_[k]
        for s in range(1,Z): copies[(k,("z",s))].wait_recv()
        t=tile_of(N)
        mine=first_buf[k].at[0,0,me.z]
        def body(j,_):
            cols=pl.ds(pl.multiple_of(j*t,128),t)
            total=mine[:,cols].astype(jnp.float32)
            for s in range(1,Z): total=total+last_buf[k][s-1,:,cols].astype(jnp.float32)
            outs[k][:,cols]=total
            return 0
        lax.fori_loop(0,N//t,body,0)
    for k in range(min(ahead,K)): first(k)
    for t in range(K+3):
        if t+ahead<K: first(t+ahead)
        if t<K: step_c(t)
        if 0<=t-1<K: step_1(t-1)
        if 0<=t-2<K: step_2(t-2)
        if 0<=t-3<K: step_z(t-3)
    for cp in copies.values(): cp.wait_send()

def scatter(parts, orders, cid, ahead=2):
    n=lax.axis_size("dp")*lax.axis_size("fsdp"); Z=lax.axis_size("dp")//2; X=lax.axis_size("fsdp")//2; K=len(parts)
    dims_=[(n,p.shape[0]//n,p.shape[1]) for p in parts]
    parts=[p.reshape(Z,2,X,2,p.shape[0]//n,p.shape[1]) for p in parts]
    bf=jnp.bfloat16
    sc=[pltpu.VMEM((2,2,Z,r,N),bf) for _,r,N in dims_]+[pltpu.VMEM((2,Z,r,N),bf) for _,r,N in dims_]+[pltpu.VMEM((Z,r,N),bf) for _,r,N in dims_]+[pltpu.VMEM((Z-1,r,N),bf) for _,r,N in dims_]+[pltpu.VMEM((2,Z,r,N),bf) for _,r,N in sorted(set(dims_))]
    return pl.pallas_call(functools.partial(scatter_kernel,Z,orders,ahead,dims_),
        out_shape=[jax.ShapeDtypeStruct((r,N),jnp.float32) for _,r,N in dims_],
        in_specs=[pl.BlockSpec(memory_space=pl.ANY)]*K,
        out_specs=[pl.BlockSpec(memory_space=pltpu.VMEM)]*K,
        scratch_shapes=sc+[pltpu.SemaphoreType.DMA((K,2)),pltpu.SemaphoreType.DMA((K,6+Z)),pltpu.SemaphoreType.DMA((K,6+Z))],
        compiler_params=pltpu.CompilerParams(collective_id=cid,has_side_effects=True,vmem_limit_bytes=63*2**20))(*parts)


def dot_t(left, right):
    return lax.dot_general(
        left, right, (((1,), (1,)), ((), ())), preferred_element_type=jnp.float32
    )


def swap_halves(u):
    lane = lax.broadcasted_iota(jnp.int32, u.shape, 1)
    down = pltpu.roll(u, 32, 1)
    up = pltpu.roll(u, 96, 1)
    return jnp.where(lax.rem(lane, 64) < 32, up, down)


def project_kernel(h_ref, w_ref, cos_ref, sin_ref, out_ref):
    u = plain_dot(h_ref[...], w_ref[...])
    for j in range(u.shape[1] // 128):
        piece = u[:, j * 128 : (j + 1) * 128]
        turned = piece * cos_ref[0] + swap_halves(piece) * sin_ref[0]
        out_ref[:, j * 128 : (j + 1) * 128] = turned.astype(jnp.bfloat16)


def project(normed, weight, cos_tables, sin_tables, width):
    tokens, depth = normed.shape
    steps = weight.shape[1] // width
    return pl.pallas_call(
        project_kernel,
        grid=(steps,),
        in_specs=[
            pl.BlockSpec((tokens, depth), lambda j: (0, 0)),
            pl.BlockSpec((depth, width), lambda j: (0, j)),
            pl.BlockSpec((1, tokens, 128), lambda j: (j // (steps - 1), 0, 0)),
            pl.BlockSpec((1, tokens, 128), lambda j: (j // (steps - 1), 0, 0)),
        ],
        out_specs=pl.BlockSpec((tokens, width), lambda j: (0, j)),
        out_shape=jax.ShapeDtypeStruct((tokens, steps * width), jnp.bfloat16),
        compiler_params=pltpu.CompilerParams(vmem_limit_bytes=48 * 2**20),
        cost_estimate=pl.CostEstimate(
            flops=2 * tokens * depth * weight.shape[1],
            bytes_accessed=2 * depth * weight.shape[1],
            transcendentals=0,
        ),
    )(normed, weight, cos_tables, sin_tables)


def lane_masks(rows):
    lane = lax.broadcasted_iota(jnp.int32, (rows, 128), 1)
    low_side = (lane < 64).astype(jnp.float32)
    return low_side.astype(jnp.bfloat16), (1.0 - low_side).astype(jnp.bfloat16)


def swapped(kv):
    return pltpu.roll(kv.astype(jnp.float32), 64, 1).astype(jnp.bfloat16)


def attend_kernel(group, q_ref, kv_ref, bias_ref, o_ref, log_ref):
    kv = kv_ref[0]
    sides = (kv, swapped(kv))
    rows = q_ref.shape[0]
    masks = lane_masks(rows)
    lane = lax.broadcasted_iota(jnp.int32, (rows, 128), 1)
    logs = jnp.zeros((rows, 128), jnp.float32)
    bias = bias_ref[0]
    for pair in range(group // 2):
        cols = slice(pair * 128, pair * 128 + 128)
        q = q_ref[:, cols]
        found = []
        for half in range(2):
            scores = dot_t(q * masks[half], sides[half]) + bias
            top = jnp.max(scores, -1, keepdims=True)
            powers = jnp.exp(scores - top)
            total = jnp.sum(powers, -1, keepdims=True)
            probs = (powers * (1.0 / total)).astype(jnp.bfloat16)
            found.append(plain_dot(probs, sides[1 - half]))
            logs = jnp.where(lane == pair * 2 + half, top + jnp.log(total), logs)
        o_ref[:, cols] = jnp.where(lane < 64, found[0], found[1]).astype(jnp.bfloat16)
    log_ref[...] = logs


def attend(projected, both_all, bias, kv_heads, group):
    batches, length, _ = both_all.shape
    rows = projected.shape[0] // batches
    wide = group * HD
    return pl.pallas_call(
        functools.partial(attend_kernel, group),
        grid=(batches, kv_heads),
        in_specs=[
            pl.BlockSpec((rows, wide), lambda b, h: (b, h)),
            pl.BlockSpec((1, length, 128), lambda b, h: (b, 0, h)),
            pl.BlockSpec((1, rows, length), lambda b, h: (b, 0, 0)),
        ],
        out_specs=[
            pl.BlockSpec((rows, wide), lambda b, h: (b, h)),
            pl.BlockSpec((rows, 128), lambda b, h: (b, h)),
        ],
        out_shape=[
            jax.ShapeDtypeStruct((batches * rows, kv_heads * wide), jnp.bfloat16),
            jax.ShapeDtypeStruct((batches * rows, kv_heads * 128), jnp.float32),
        ],
        compiler_params=pltpu.CompilerParams(vmem_limit_bytes=48 * 2**20),
    )(projected, both_all, bias)


def attend_back_kernel(
    group, q_ref, do_ref, kv_ref, bias_ref, log_ref, cos_ref, sin_ref, dq_ref, dkv_ref
):
    kv = kv_ref[0]
    sides = (kv, swapped(kv))
    rows = q_ref.shape[0]
    length = kv.shape[0]
    masks = lane_masks(rows)
    lane = lax.broadcasted_iota(jnp.int32, (rows, 128), 1)
    bias = bias_ref[0]
    key_sum = jnp.zeros((128, length), jnp.float32)
    value_sum = jnp.zeros((128, length), jnp.float32)
    for pair in range(group // 2):
        cols = slice(pair * 128, pair * 128 + 128)
        q = q_ref[:, cols]
        do = do_ref[:, cols]
        found = []
        for half in range(2):
            q_half = q * masks[half]
            do_half = do * masks[half]
            at = pair * 2 + half
            log_total = log_ref[:, at : at + 1]
            probs = jnp.exp(dot_t(q_half, sides[half]) + bias - log_total)
            grad_probs = dot_t(do_half, sides[1 - half])
            row_dot = jnp.sum(probs * grad_probs, -1, keepdims=True)
            grad_scores = (probs * (grad_probs - row_dot)).astype(jnp.bfloat16)
            found.append(plain_dot(grad_scores, sides[half]))
            key_sum = key_sum + left_dot(q_half, grad_scores)
            value_sum = value_sum + left_dot(do_half, probs.astype(jnp.bfloat16))
        dq = jnp.where(lane < 64, found[0], found[1])
        dq = dq * cos_ref[0] - swap_halves(dq) * sin_ref[0]
        dq_ref[:, cols] = dq.astype(jnp.bfloat16)
    both = jnp.concatenate(
        [key_sum[:64] + key_sum[64:], value_sum[:64] + value_sum[64:]], 0
    )
    dkv_ref[0] = both.T.astype(jnp.bfloat16)


def attend_back(projected, grad_attended, both_all, bias, logs, cos_tables, sin_tables, group):
    batches, length, _ = both_all.shape
    rows = projected.shape[0] // batches
    wide = group * HD
    kv_heads = both_all.shape[2] // 128
    return pl.pallas_call(
        functools.partial(attend_back_kernel, group),
        grid=(batches, kv_heads),
        in_specs=[
            pl.BlockSpec((rows, wide), lambda b, h: (b, h)),
            pl.BlockSpec((rows, wide), lambda b, h: (b, h)),
            pl.BlockSpec((1, length, 128), lambda b, h: (b, 0, h)),
            pl.BlockSpec((1, rows, length), lambda b, h: (b, 0, 0)),
            pl.BlockSpec((rows, 128), lambda b, h: (b, h)),
            pl.BlockSpec((1, rows, 128), lambda b, h: (0, b, 0)),
            pl.BlockSpec((1, rows, 128), lambda b, h: (0, b, 0)),
        ],
        out_specs=[
            pl.BlockSpec((rows, wide), lambda b, h: (b, h)),
            pl.BlockSpec((1, length, 128), lambda b, h: (b, 0, h)),
        ],
        out_shape=[
            jax.ShapeDtypeStruct((batches * rows, kv_heads * wide), jnp.bfloat16),
            jax.ShapeDtypeStruct((batches, length, kv_heads * 128), jnp.bfloat16),
        ],
        compiler_params=pltpu.CompilerParams(vmem_limit_bytes=48 * 2**20),
    )(projected, grad_attended, both_all, bias, logs, cos_tables, sin_tables)


class Scattering:
    def __init__(self, me, chunks, send, recv, free):
        self.me, self.chunks = me, chunks
        self.send, self.recv, self.free = send, recv, free
        self.copies = {}
        self.friends = [me.device(s=s) for s in range(1, me.Z)]
        self.friends += [me.device(dy=1), me.device(dx=1), me.device(dc=1)]

    def ship(self, k, name, index, src, dst, target):
        copy = pltpu.make_async_remote_copy(
            src_ref=src,
            dst_ref=dst,
            send_sem=self.send.at[k, index],
            recv_sem=self.recv.at[k, index],
            device_id=target,
            device_id_type=MESH,
        )
        copy.start()
        self.copies[(k, name)] = copy

    def add(self, dst, src, wide, base):
        depth = dst.shape[0]
        t = tile_of(wide)
        count = wide // t

        def body(i, carry):
            at = i // count
            cols = pl.ds(pl.multiple_of(base + lax.rem(i, count) * t, 128), t)
            dst[at, :, cols] = dst[at, :, cols] + src[at, :, cols]
            return carry

        lax.fori_loop(0, depth * count, body, 0)

    def buffers(self, k):
        own, one, two, last, wide = self.chunks[k][:5]
        cols = pl.ds(self.chunks[k][9], wide)
        return own, one, two, last, wide, cols

    def begin(self, k):
        own, one, two, last, wide, cols = self.buffers(k)
        order = self.chunks[k][5]
        for b in (1, 0):
            self.ship(
                k,
                ("1", b),
                b,
                own.at[1, b, :, :, cols],
                one.at[b, :, :, cols],
                self.me.device(**{"d" + order[0]: 1}),
            )

    def first(self, k):
        own, one, two, last, wide, cols = self.buffers(k)
        order = self.chunks[k][5]
        for b in (1, 0):
            self.copies[(k, ("1", b))].wait_recv()
            self.add(own.at[0, b], one.at[b], wide, self.chunks[k][9])
            if b == 1:
                self.ship(
                    k,
                    "2",
                    2,
                    own.at[0, 1, :, :, cols],
                    two.at[:, :, cols],
                    self.me.device(**{"d" + order[1]: 1}),
                )

    def second(self, k):
        own, one, two, last, wide, cols = self.buffers(k)
        me = self.me
        self.copies[(k, "2")].wait_recv()
        self.add(own.at[0, 0], two, wide, self.chunks[k][9])
        for s in range(1, me.Z):
            self.ship(
                k,
                ("z", s),
                2 + s,
                own.at[0, 0, lax.rem(me.z + s, me.Z), :, cols],
                last.at[s - 1, :, cols],
                me.device(s=s),
            )

    def third(self, k):
        own, one, two, last, wide, cols = self.buffers(k)
        me = self.me
        _, out, base, group, off = self.chunks[k][5:]
        for s in range(1, me.Z):
            self.copies[(k, ("z", s))].wait_recv()
        t = tile_of(wide)

        def body(j, carry):
            here = pl.ds(pl.multiple_of(off + j * t, 128), t)
            there = pl.ds(pl.multiple_of(base + j * t, 128), t)
            total = own[0, 0, me.z, :, here].astype(jnp.float32)
            for s in range(1, me.Z):
                total = total + last[s - 1, :, here].astype(jnp.float32)
            out[:, there] = total
            return carry

        lax.fori_loop(0, wide // t, body, 0)
        for (at, _), copy in self.copies.items():
            if at == k:
                copy.wait_send()
        if group is not None:
            for friend in self.friends:
                pl.semaphore_signal(
                    self.free.at[group], inc=1, device_id=friend, device_id_type=MESH
                )

    def reuse(self, group):
        pl.semaphore_wait(self.free.at[group], len(self.friends))


def backward_kernel(sizes, *refs):
    batches, rows, kv_heads, group, used = sizes
    (dy_ref, first_w, out_w, gate_w, up_w, down_w) = refs[:6]
    (q_in, kv_in, log_in, mixed_in, hidden_in, slope_in, silu_in, bias_in, cos_in, sin_in) = refs[6:16]
    (hid_t, h2_t, att_t, nor_t, x_in) = refs[16:21]
    outs = refs[21:36]
    (result_out, grad_out, g_first, g_out, g_gate, g_up, g_down) = outs[:7]
    (hid_s, h2_s, att_s, nor_s, dy_p, gate_p, up_p, dm_p) = outs[7:]
    pre_p, dy1_h = refs[36:38]
    sc = list(refs[38:])
    take = lambda n: [sc.pop(0) for _ in range(n)]
    sets = [take(4) for _ in range(3)]
    down_sets = [take(4) for _ in range(2)]
    gain_set = take(4)
    (lhs_d, lhs, lraw, rhs, acc, part, cot, low_t, queries, grads, pre) = take(11)
    (kv_all, dkv, bias, logs, cos_t, sin_t, dkv_r, dkv_x) = take(8)
    (raw_a, w_a, wd, fac_a, fac_b, dgt, dut, gains, gsum, gcol) = take(10)
    (send, recv, free, x_send, x_recv, t_send, t_recv, load_sem, lhs_sem, store_sem, own_sem, part_sem) = take(12)
    me = Place()
    greet(me)
    tokens, width = cot.shape
    length = kv_all.shape[1]
    features = hidden_in.shape[1]
    wide = dgt.shape[1]
    tiles = features // wide
    scale = HD**-0.5
    sibling = me.device(dc=1)
    f32, bf = jnp.float32, jnp.bfloat16
    r = lhs.shape[0] // (4 * me.Z)
    rd = lhs_d.shape[1] // me.Z
    big = sets[0][0].shape[-1]
    half = features // 2
    key_wide = kv_heads * 128
    query_wide = pre.shape[1] - key_wide
    d_wide = down_sets[0][0].shape[-1]
    d_rest = width - 2 * d_wide
    chunks = (
        (*down_sets[0], d_wide, "xy", g_down, 0, 4, 0),
        (*down_sets[1], d_wide, "yx", g_down, d_wide, None, 0),
        (*sets[0], half, "xy", g_gate, 0, 0, 0),
        (*sets[1], half, "yx", g_up, 0, 1, 0),
        (*sets[2], half, "xy", g_gate, half, 2, 0),
        (*sets[0], half, "yx", g_up, half, None, 0),
        (*sets[1], width, "xy", g_out, 0, None, 0),
        (*sets[2], query_wide, "yx", g_first, 0, None, 0),
        (*sets[2], key_wide - 128, "yx", g_first, query_wide, None, query_wide),
        (*gain_set, 256, "yx", g_first, query_wide + key_wide - 128, None, 0),
        (*down_sets[0], d_rest, "yx", g_down, 2 * d_wide, None, 0),
    )
    D0, D1, G0, U0, G1, U1, O, Q, KV, GAIN, D2 = range(11)
    comm = Scattering(me, chunks, send, recv, free)

    def over_rows(body, step=64):
        def one(i, carry):
            body(pl.ds(pl.multiple_of(i * step, step), step))
            return carry

        lax.fori_loop(0, tokens // step, one, 0)

    passes = []

    def hand(i, src, dst):
        copy = pltpu.make_async_remote_copy(
            src_ref=src,
            dst_ref=dst,
            send_sem=x_send.at[i],
            recv_sem=x_recv.at[i],
            device_id=sibling,
            device_id_type=MESH,
        )
        copy.start()
        passes.append(copy)
        return copy

    other = lax.rem(me.c + 1, 2)
    got_hid = hand(0, hid_t.at[:, :, :, other], hid_s)
    got_dy = hand(1, dy_ref, dy_p.at[1])
    got_h2 = hand(2, h2_t.at[:, :, :, other], h2_s)
    got_att = hand(3, att_t.at[:, :, :, other], att_s)
    got_nor = hand(4, nor_t.at[:, :, :, other], nor_s)

    def fetch(i, src, dst):
        copy = pltpu.make_async_copy(src, dst, load_sem.at[i])
        copy.start()
        return copy

    stores = []

    def store(i, src, dst):
        copy = pltpu.make_async_copy(src, dst, store_sem.at[i])
        copy.start()
        stores.append(copy)
        return copy

    need_cot = fetch(0, dy_ref, cot)
    own_dy = store(0, dy_ref, dy_p.at[0])
    def block(ref, a, b, order, c=None):
        rel = {order[0]: a, order[1]: b}
        y = lax.rem(me.y + rel["y"], 2)
        x = lax.rem(me.x + rel["x"], 2)
        return ref.at[:, y, x] if c is None else ref.at[:, y, x, c]

    def left_rows(own_t, sib_t):
        for side, ref in ((0, own_t), (1, sib_t)):
            loads = []
            for i in range(4):
                src = block(ref, i // 2, i % 2, "xy", me.c if side == 0 else None)
                copy = pltpu.make_async_copy(src, lraw.at[i], lhs_sem.at[i])
                copy.start()
                loads.append(copy)
            for copy in loads:
                copy.wait()

            def one(i, carry, side=side):
                for j in range(me.Z // 2):
                    piece = lraw[i, 2 * j : 2 * j + 2].astype(f32).reshape(2 * r, tokens)
                    at = pl.multiple_of((i * me.Z + 2 * j) * r, 16)
                    lhs[pl.ds(at, 2 * r), side * tokens : (side + 1) * tokens] = piece.astype(bf)
                return carry

            lax.fori_loop(0, 4, one, 0)

    def down_rows(k, i, slot):
        copies = []
        for side, ref in ((0, hid_t), (1, hid_s)):
            src = block(ref, i // 2, i % 2, chunks[k][5], me.c if side == 0 else None)
            for z in range(me.Z):
                copies.append(
                    pltpu.make_async_copy(
                        src.at[z],
                        lhs_d.at[slot, pl.ds(z * rd, rd), pl.ds(side * tokens, tokens)],
                        lhs_sem.at[(slot * 2 + side) * me.Z + z],
                    )
                )
        return copies

    def product_down(k, base, right=None):
        own, wide_k = chunks[k][0], chunks[k][4]
        for copy in down_rows(k, 3, 0):
            copy.start()
        for n, i in enumerate((3, 2, 1, 0)):
            slot = n % 2
            if i > 0:
                for copy in down_rows(k, i - 1, 1 - slot):
                    copy.start()
            for copy in down_rows(k, i, slot):
                copy.wait()
            left = lhs_d.at[slot]
            if right is None:
                product(k, dy_p, base, left, rd, (i,))
            else:

                def body(j, carry, i=i, left=left):
                    cols = pl.ds(pl.multiple_of(base + j * 256, 256), 256)
                    here = pl.ds(pl.multiple_of(j * 256, 256), 256)
                    total = plain_dot(left[:, :tokens], right[0][:, cols]) + plain_dot(
                        left[:, tokens:], right[1][:, cols]
                    )
                    own[i // 2, i % 2, :, :, here] = total.reshape(me.Z, rd, 256).astype(bf)
                    return carry

                lax.fori_loop(0, wide_k // 256, body, 0)
        comm.begin(k)

    def product(k, pair, base, left, depth, blocks=(0, 1, 2, 3), size=None):
        own, wide_k = chunks[k][0], size or chunks[k][4]
        t = rhs.shape[3] if wide_k % rhs.shape[3] == 0 else 128
        count = wide_k // t
        span = len(blocks)

        def tile(j, slot):
            cols = pl.ds(pl.multiple_of(base + j * t, 128), t)
            return [
                pltpu.make_async_copy(
                    pair.at[side, :, cols],
                    rhs.at[slot, side, :, pl.ds(0, t)],
                    own_sem.at[slot, side],
                )
                for side in range(2)
            ]

        depth_of = rhs.shape[0]
        for j in range(min(depth_of - 1, count)):
            for copy in tile(j, j):
                copy.start()

        def body(j, carry):
            slot = lax.rem(j, depth_of)
            ahead = j + depth_of - 1

            @pl.when(ahead < count)
            def _():
                for copy in tile(ahead, lax.rem(ahead, depth_of)):
                    copy.start()

            for copy in tile(j, slot):
                copy.wait()
            cols = pl.ds(pl.multiple_of(chunks[k][9] + j * t, 128), t)
            total = plain_dot(left[:, :tokens], rhs[slot, 0, :, :t]) + plain_dot(
                left[:, tokens:], rhs[slot, 1, :, :t]
            )
            total = total.reshape(span, me.Z, depth, t).astype(bf)
            for q, at in enumerate(blocks):
                if chunks[k][5] == "xy" or span == 1:
                    own[at // 2, at % 2, :, :, cols] = total[q]
                else:
                    own[at % 2, at // 2, :, :, cols] = total[q]
            return carry

        lax.fori_loop(0, count, body, 0)

    def load3(i, full, raw, col, size):
        return pltpu.make_async_copy(
            full.at[:, :, pl.ds(col, size)], raw.at[:, :, pl.ds(0, size)], load_sem.at[i]
        )

    def assemble(raw, flat, size):
        n, depth, _ = raw.shape
        pair = 2 * depth

        def one(i, carry):
            piece = raw[pl.ds(2 * i, 2), :, pl.ds(0, size)].astype(f32)
            flat[pl.ds(pl.multiple_of(pair * i, 16), pair), pl.ds(0, size)] = piece.reshape(
                pair, size
            ).astype(bf)
            return carry

        lax.fori_loop(0, n // 2, one, 0)

    def tile_loads(j):
        at = pl.ds(j * wide, wide)
        return [
            pltpu.make_async_copy(down_w.at[at, :], wd.at[j % 2], load_sem.at[2]),
            pltpu.make_async_copy(slope_in.at[:, at], fac_a.at[j % 2], load_sem.at[3]),
            pltpu.make_async_copy(silu_in.at[:, at], fac_b.at[j % 2], load_sem.at[4]),
        ]

    gate_tile = lambda j: load3(5, gate_w, raw_a, j * wide, wide)
    up_tile = lambda j: load3(6, up_w, raw_a, j * wide, wide)
    head_pack = load3(7, first_w, raw_a, used, 128)
    head_pack.start()
    head_pack.wait()
    assemble(raw_a, w_a, 128)
    gains[...] = w_a[:, :128].astype(f32).T[:8]
    for copy in tile_loads(0) + [gate_tile(0)]:
        copy.start()
    need_cot.wait()
    own_dy.wait()
    tile_sends = [None] * tiles

    def arrive(low, high):
        for j in range(low, high):
            for copy in tile_sends[j]:
                copy.settle()

    for j in range(tiles):
        slot = j % 2
        for copy in tile_loads(j):
            copy.wait()
        if j + 1 < tiles:
            for copy in tile_loads(j + 1):
                copy.start()
        gate_tile(j).wait()
        assemble(raw_a, w_a, wide)
        up_tile(j).start()
        if j >= 1:
            for copy in tile_sends[j - 1]:
                copy.wait()

        def units(at, slot=slot, j=j):
            grad_hidden = dot_t(cot[at, :], wd[slot])
            dg = (grad_hidden * fac_a[slot, at, :].astype(f32)).astype(bf)
            du = (grad_hidden * fac_b[slot, at, :].astype(f32)).astype(bf)
            dgt[at, :] = dg
            dut[at, :] = du
            piece = dot_t(dg, w_a[:, :wide])
            acc[at, :] = piece if j == 0 else acc[at, :] + piece

        over_rows(units, 256)
        cols = pl.ds(j * wide, wide)
        sends = []
        for i, (src, dst) in enumerate(((dgt, gate_p), (dut, up_p))):
            here = pltpu.make_async_copy(
                src, dst.at[0, :, cols], store_sem.at[1 + i]
            )
            there = pltpu.make_async_remote_copy(
                src_ref=src,
                dst_ref=dst.at[1, :, cols],
                send_sem=t_send.at[2 * j + i],
                recv_sem=t_recv.at[2 * j + i],
                device_id=sibling,
                device_id_type=MESH,
            )
            here.start()
            there.start()
            sends.append(_Both(here, there))
        tile_sends[j] = sends
        up_tile(j).wait()
        assemble(raw_a, w_a, wide)
        if j + 1 < tiles:
            gate_tile(j + 1).start()

        def units_up(at):
            acc[at, :] = acc[at, :] + dot_t(dut[at, :], w_a[:, :wide])

        over_rows(units_up, 256)
        if j == 0:
            got_dy.wait_recv()
            need_sib = fetch(1, dy_p.at[1], low_t)
            got_hid.wait_recv()
            need_sib.wait()
            product_down(D0, 0, (cot, low_t))
        if j == 1:
            product_down(D1, d_wide, (cot, low_t))
        if j == 3:
            got_h2.wait_recv()
            left_rows(h2_t, h2_s)
            arrive(0, 4)
            product(G0, gate_p, 0, lhs, r)
            comm.begin(G0)
            product(U0, up_p, 0, lhs, r)
            comm.begin(U0)
        if j == 4:
            comm.first(D0)
        if j == 5:
            comm.first(D1)
    arrive(4, tiles)
    product(G1, gate_p, half, lhs, r)
    comm.begin(G1)

    gsum[...] = jnp.zeros_like(gsum)

    def stream(src, body):
        def piece(i, slot):
            at = pl.ds(pl.multiple_of(i * 64, 64), 64)
            return pltpu.make_async_copy(src.at[at, :], part.at[slot], part_sem.at[slot])

        piece(0, 0).start()

        def one(i, carry):
            slot = lax.rem(i, 2)

            @pl.when(i + 1 < tokens // 64)
            def _():
                piece(i + 1, lax.rem(i + 1, 2)).start()

            piece(i, slot).wait()
            body(pl.ds(pl.multiple_of(i * 64, 64), 64), part[slot])
            return carry

        lax.fori_loop(0, tokens // 64, one, 0)

    def norm_two(at, y):
        inverse = lax.rsqrt(jnp.mean(y * y, -1, keepdims=True) + EPSILON)
        grad = acc[at, :]
        gsum[1:2, :] += jnp.sum(grad * (y * inverse), 0, keepdims=True)
        e = grad * gains[1:2, :]
        dy1 = cot[at, :].astype(f32) + inverse * (
            e - y * (inverse * inverse) * jnp.mean(e * y, -1, keepdims=True)
        )
        acc[at, :] = dy1
        low_t[at, :] = dy1.astype(bf)

    stream(mixed_in, norm_two)
    keep_dy1 = pltpu.make_async_copy(acc, dy1_h, part_sem.at[2])
    keep_dy1.start()
    own_low = store(5, low_t, dm_p.at[0])
    got_low = hand(5, low_t, dm_p.at[1])

    need_q = fetch(0, q_in, queries)
    need_kv = fetch(1, kv_in, kv_all)
    need = [
        fetch(8, bias_in, bias),
        fetch(9, log_in, logs),
        fetch(10, cos_in, cos_t),
        fetch(11, sin_in, sin_t),
    ]
    tile_w = raw_a.shape[2]
    steps = width // tile_w
    load3(5, out_w, raw_a, 0, tile_w).start()
    keep_dy1.wait()
    for j in range(steps):
        load3(5, out_w, raw_a, j * tile_w, tile_w).wait()
        assemble(raw_a, w_a, tile_w)
        if j + 1 < steps:
            load3(5, out_w, raw_a, (j + 1) * tile_w, tile_w).start()

        def back_out(at, j=j):
            piece = dot_t(low_t[at, j * tile_w : (j + 1) * tile_w], w_a[...])
            if j > 0:
                piece = acc[at, :] + piece
            if j + 1 < steps:
                acc[at, :] = piece
            else:
                grads[at, :] = piece.astype(bf)

        over_rows(back_out, 256)
    comm.second(D0)
    comm.first(G0)
    comm.second(D1)

    need_q.wait()
    need_kv.wait()
    for copy in need:
        copy.wait()
    def portion(dx, c):
        row = (lax.rem(me.x + dx, 2) * 2 + c) * rows
        return pl.ds(pl.multiple_of(row, 256), rows)

    def to_sibling(b):
        return [
            hand(6 + 2 * b + dx, dkv.at[b, portion(dx, other), :], dkv_r.at[dx, b])
            for dx in (1, 0)
        ]

    def gather_portion(b, dx):
        place = portion(dx, me.c)

        def body(j, carry):
            at = pl.ds(pl.multiple_of(j * 64, 64), 64)
            there = pl.ds(pl.multiple_of(place.start + j * 64, 64), 64)
            total = dkv_r[dx, b, at, :].astype(f32) + dkv[b, there, :].astype(f32)
            dkv_r[dx, b, at, :] = total.astype(bf)
            return carry

        lax.fori_loop(0, rows // 64, body, 0)

    def to_neighbour(b, handed):
        handed[0].wait_recv()
        gather_portion(b, 1)
        copy = pltpu.make_async_remote_copy(
            src_ref=dkv_r.at[1, b],
            dst_ref=dkv_x.at[b],
            send_sem=x_send.at[10 + b],
            recv_sem=x_recv.at[10 + b],
            device_id=me.device(dx=1),
            device_id_type=MESH,
        )
        copy.start()
        passes.append(copy)
        handed[1].wait_recv()
        gather_portion(b, 0)
        return copy

    def merge_portion(b, copy):
        copy.wait_recv()

        def merge(j, carry):
            at = pl.ds(pl.multiple_of(j * 64, 64), 64)
            token = pl.ds(pl.multiple_of(b * rows + j * 64, 64), 64)
            for h in range(kv_heads):
                cols = slice(h * 128, (h + 1) * 128)
                total = dkv_r[0, b, at, cols].astype(f32) + dkv_x[b, at, cols].astype(f32)
                total = total * cos_t[1, token, :] - swap_halves(total) * sin_t[1, token, :]
                pre[token, query_wide + h * 128 : query_wide + (h + 1) * 128] = total.astype(bf)
            return carry

        lax.fori_loop(0, rows // 64, merge, 0)

    to_x = [None] * batches
    lanes = lax.broadcasted_iota(jnp.int32, (rows, 128), 1)
    sides_mask = lane_masks(rows)

    def head(i, carry):
        b = i // kv_heads
        h = lax.rem(i, kv_heads)
        at = pl.ds(pl.multiple_of(b * rows, 256), rows)
        here = pl.ds(pl.multiple_of(h * 128, 128), 128)
        kv = kv_all[b, :, here]
        sides = (kv, swapped(kv))
        shift = bias[at, :].astype(f32)
        key_sum = jnp.zeros((128, length), f32)
        value_sum = jnp.zeros((128, length), f32)
        log_piece = logs[at, :]
        for pair in range(group // 2):
            cols = pl.ds(pl.multiple_of(h * group * HD + pair * 128, 128), 128)
            q = queries[at, cols]
            do = grads[at, cols]
            found = []
            for side in range(2):
                q_half = q * sides_mask[side]
                do_half = do * sides_mask[side]
                head_at = pair * 2 + side
                log_total = jnp.sum(
                    jnp.where(lanes == h * group + head_at, log_piece, 0.0), -1, keepdims=True
                )
                probs = jnp.exp(dot_t(q_half, sides[side]) + shift - log_total)
                grad_probs = dot_t(do_half, sides[1 - side])
                row_dot = jnp.sum(probs * grad_probs, -1, keepdims=True)
                grad_scores = (probs * (grad_probs - row_dot)).astype(bf)
                found.append(plain_dot(grad_scores, sides[side]))
                key_sum = key_sum + left_dot(q_half, grad_scores)
                value_sum = value_sum + left_dot(do_half, probs.astype(bf))
            dq = jnp.where(lanes < HD, found[0], found[1])
            dq = dq * cos_t[0, at, :] - swap_halves(dq) * sin_t[0, at, :]
            pre[at, cols] = dq.astype(bf)
        both = jnp.concatenate(
            [key_sum[:HD] + key_sum[HD:], value_sum[:HD] + value_sum[HD:]], 0
        )
        dkv[b, :, here] = both.T.astype(bf)
        return carry

    count = batches * kv_heads
    lax.fori_loop(0, 2, head, 0)
    comm.first(U0)
    comm.third(D0)
    own_low.wait()
    got_low.wait_recv()
    lax.fori_loop(2, 5, head, 0)
    comm.third(D1)
    comm.second(G0)
    handed = to_sibling(0)
    comm.first(G1)
    lax.fori_loop(5, 8, head, 0)
    comm.second(U0)
    comm.third(G0)
    comm.reuse(0)
    product(U1, up_p, half, lhs, r)
    comm.begin(U1)
    to_x[0] = to_neighbour(0, handed)
    lax.fori_loop(8, count, head, 0)
    comm.third(U0)
    comm.second(G1)
    merge_portion(0, to_x[0])
    comm.reuse(1)
    got_att.wait_recv()
    left_rows(att_t, att_s)
    product(O, dm_p, 0, lhs, r)
    comm.begin(O)
    handed = to_sibling(1)
    own_q = store(6, pre.at[:, pl.ds(0, query_wide)], pre_p.at[0, :, pl.ds(0, query_wide)])
    got_q = hand(12, pre.at[:, pl.ds(0, query_wide)], pre_p.at[1, :, pl.ds(0, query_wide)])
    to_x[1] = to_neighbour(1, handed)
    comm.third(G1)
    comm.reuse(2)
    got_nor.wait_recv()
    left_rows(nor_t, nor_s)
    own_q.wait()
    got_q.wait_recv()
    product(Q, pre_p, 0, lhs, r)
    comm.begin(Q)
    comm.reuse(4)
    product_down(D2, 2 * d_wide)
    comm.first(U1)
    merge_portion(1, to_x[1])
    rest = pl.ds(query_wide, kv_heads * 128)
    own_kv = store(7, pre.at[:, rest], pre_p.at[0, :, rest])
    got_kv = hand(13, pre.at[:, rest], pre_p.at[1, :, rest])

    need_x = fetch(0, x_in, cot)
    steps = pre.shape[1] // tile_w
    load3(5, first_w, raw_a, 0, tile_w).start()
    for j in range(steps):
        load3(5, first_w, raw_a, j * tile_w, tile_w).wait()
        assemble(raw_a, w_a, tile_w)
        if j + 1 < steps:
            load3(5, first_w, raw_a, (j + 1) * tile_w, tile_w).start()

        def back_in(at, j=j):
            piece = dot_t(pre[at, j * tile_w : (j + 1) * tile_w], w_a[...])
            acc[at, :] = piece if j == 0 else acc[at, :] + piece

        over_rows(back_in, 256)
    comm.first(O)
    own_kv.wait()
    got_kv.wait_recv()
    product(KV, pre_p, query_wide, lhs, r)
    comm.begin(KV)
    product(GAIN, pre_p, query_wide + key_wide - 128, lhs, r, size=128)
    comm.second(U1)
    need_x.wait()

    def norm_one(at, dy1):
        x = cot[at, :].astype(f32)
        inverse = lax.rsqrt(jnp.mean(x * x, -1, keepdims=True) + EPSILON)
        grad = acc[at, :]
        gsum[0:1, :] += jnp.sum(grad * (x * inverse), 0, keepdims=True)
        e = grad * gains[0:1, :]
        total = dy1 + inverse * (
            e - x * (inverse * inverse) * jnp.mean(e * x, -1, keepdims=True)
        )
        queries[at, :] = total.astype(bf)

    stream(dy1_h, norm_one)
    store(8, queries, grad_out)
    comm.first(D2)
    comm.first(Q)

    gsib = gain_set[0]
    columns = jnp.concatenate([gsum[...], jnp.zeros((120, width), f32)], 0).T
    gcol[0] = columns.reshape(gcol.shape[1:]).astype(bf)
    got_gain = hand(14, gcol.at[0], gcol.at[1])
    comm.second(O)
    got_gain.wait_recv()
    for a in range(2):
        for b in range(2):
            y = lax.rem(me.y + b, 2)
            x = lax.rem(me.x + a, 2)
            if chunks[GAIN][5] == "yx":
                y, x = lax.rem(me.y + a, 2), lax.rem(me.x + b, 2)
            for z in range(me.Z):
                at = ((z * 2 + y) * 2 + x) * 2 + me.c
                gsib[a, b, z, :, 128:] = gcol[0, at] + gcol[1, at]
    comm.begin(GAIN)
    comm.first(KV)
    comm.second(D2)
    comm.second(Q)

    need_mixed = fetch(1, mixed_in, acc)
    need_mixed.wait()
    last_loads = lambda j: [
        pltpu.make_async_copy(
            down_w.at[pl.ds(j * wide, wide), :], wd.at[j % 2], load_sem.at[2]
        ),
        pltpu.make_async_copy(
            hidden_in.at[:, pl.ds(j * wide, wide)], fac_a.at[j % 2], load_sem.at[3]
        ),
    ]
    for copy in last_loads(0):
        copy.start()
    for j in range(tiles):
        for copy in last_loads(j):
            copy.wait()
        if j + 1 < tiles:
            for copy in last_loads(j + 1):
                copy.start()

        def add_down(at, j=j):
            acc[at, :] = acc[at, :] + plain_dot(fac_a[j % 2, at, :], wd[j % 2])

        over_rows(add_down, 256)
        if j == 0:
            comm.third(U1)
        if j == 1:
            comm.second(KV)
        if j == 2:
            comm.first(GAIN)
        if j == 3:
            comm.third(O)
            comm.third(D2)
        if j == 4:
            comm.third(Q)
        if j == 5:
            comm.second(GAIN)

    def round_result(at):
        low_t[at, :] = acc[at, :].astype(bf)

    got_low.wait_send()
    over_rows(round_result)
    store(9, low_t, result_out)
    comm.third(KV)
    comm.third(GAIN)
    for copy in passes:
        if copy is not got_low:
            copy.wait_send()
    for copy in stores:
        if not any(copy is p for p in (own_dy, own_low, own_q, own_kv)):
            copy.wait()


class _Both:
    def __init__(self, here, there):
        self.here, self.there, self.sent, self.settled = here, there, False, False

    def wait(self):
        if not self.sent:
            self.here.wait()
            self.there.wait_send()
        self.sent = True

    def settle(self):
        self.wait()
        if not self.settled:
            self.there.wait_recv()
        self.settled = True


def backward(saved, transposed, dy, x, kv_heads, group, batches):
    first_w, out_w, gate_w, up_w, down_w = saved[:5]
    queries, both_all, _, logs, mixed, _ = saved[5:11]
    hidden, slope, silu, bias, cos_tables, sin_tables = saved[11:]
    tokens, width = x.shape
    rows = tokens // batches
    Z = lax.axis_size("dp") // 2
    X = lax.axis_size("fsdp") // 2
    n, r, first_wide = first_w.shape
    rd = down_w.shape[1]
    key_wide = kv_heads * 128
    query_wide = kv_heads * group * HD
    used = query_wide + key_wide
    length = both_all.shape[1]
    features = hidden.shape[1]
    half = features // 2
    d_wide = width * 2 // 5 // 256 * 256
    wide, t = 512, 256
    bf, f32 = jnp.bfloat16, jnp.float32
    shape = jax.ShapeDtypeStruct
    vmem, dma = pltpu.VMEM, pltpu.SemaphoreType.DMA

    def four(depth, size):
        return [
            vmem((2, 2, Z, depth, size), bf),
            vmem((2, Z, depth, size), bf),
            vmem((Z, depth, size), bf),
            vmem((Z - 1, depth, size), bf),
        ]

    outs = [
        shape((tokens, width), bf),
        shape((tokens, width), bf),
        shape((r, first_wide), f32),
        shape((r, width), f32),
        shape((r, features), f32),
        shape((r, features), f32),
        shape((rd, width), f32),
        shape((Z, 2, X, rd, tokens), bf),
        shape((Z, 2, X, r, tokens), bf),
        shape((Z, 2, X, r, tokens), bf),
        shape((Z, 2, X, r, tokens), bf),
        shape((2, tokens, width), bf),
        shape((2, tokens, features), bf),
        shape((2, tokens, features), bf),
        shape((2, tokens, width), bf),
        shape((2, tokens, used), bf),
        shape((tokens, width), f32),
    ]
    any_space = pl.BlockSpec(memory_space=pl.ANY)
    in_vmem = pl.BlockSpec(memory_space=pltpu.VMEM)
    scratch = sum([four(r, half) for _ in range(3)], [])
    scratch += four(rd, d_wide) + four(rd, d_wide) + four(r, 256)
    scratch += [
        vmem((2, Z * rd, 2 * tokens), bf),
        vmem((4 * Z * r, 2 * tokens), bf),
        vmem((4, Z, r, tokens), bf),
        vmem((3, 2, tokens, t), bf),
        vmem((tokens, width), f32),
        vmem((2, 64, width), f32),
        vmem((tokens, width), bf),
        vmem((tokens, width), bf),
        vmem((tokens, query_wide), bf),
        vmem((tokens, query_wide), bf),
        vmem((tokens, used), bf),
        vmem((batches, length, key_wide), bf),
        vmem((batches, length, key_wide), bf),
        vmem((tokens, length), bias.dtype),
        vmem((tokens, 128), f32),
        vmem((2, tokens, 128), f32),
        vmem((2, tokens, 128), f32),
        vmem((2, batches, rows, key_wide), bf),
        vmem((batches, rows, key_wide), bf),
        vmem((n, r, key_wide), bf),
        vmem((width, key_wide), bf),
        vmem((2, wide, width), bf),
        vmem((2, tokens, wide), bf),
        vmem((2, tokens, wide), bf),
        vmem((tokens, wide), bf),
        vmem((tokens, wide), bf),
        vmem((8, width), f32),
        vmem((8, width), f32),
        vmem((2, n, r, 128), bf),
        dma((11, 2 + Z)),
        dma((11, 2 + Z)),
        pltpu.SemaphoreType.REGULAR((5,)),
        dma((15,)),
        dma((15,)),
        dma((2 * (features // wide),)),
        dma((2 * (features // wide),)),
        dma((12,)),
        dma((8 * Z,)),
        dma((10,)),
        dma((3, 2)),
        dma((3,)),
    ]
    return pl.pallas_call(
        functools.partial(backward_kernel, (batches, rows, kv_heads, group, used)),
        out_shape=outs,
        in_specs=[any_space] * 21,
        out_specs=[any_space] * 2 + [in_vmem] * 5 + [any_space] * 10,
        scratch_shapes=scratch,
        compiler_params=pltpu.CompilerParams(
            collective_id=2, has_side_effects=True, vmem_limit_bytes=63 * 2**20
        ),
    )(
        dy,
        first_w,
        out_w,
        gate_w,
        up_w,
        down_w.reshape(-1, width),
        queries,
        both_all,
        logs,
        mixed,
        hidden,
        slope,
        silu,
        bias,
        cos_tables,
        sin_tables,
        *transposed,
        x,
    )


def half_of(full):
    return full.astype(jnp.bfloat16)


def rotary_pairs(places, tokens, score_scale):
    cos_table, sin_table = rope_tables(places.reshape(tokens))
    ones, zeros = jnp.ones((tokens, HD), jnp.float32), jnp.zeros((tokens, HD), jnp.float32)
    cos_pair = jnp.concatenate([cos_table, cos_table], -1)
    sin_pair = jnp.concatenate([-sin_table, sin_table], -1)
    cos_tables = jnp.stack(
        [
            jnp.concatenate([cos_pair, cos_pair], -1) * score_scale,
            jnp.concatenate([cos_pair, ones], -1),
        ]
    )
    sin_tables = jnp.stack(
        [
            jnp.concatenate([sin_pair, sin_pair], -1) * score_scale,
            jnp.concatenate([sin_pair, zeros], -1),
        ]
    )
    return cos_tables, sin_tables


def forward_plain(shards, x, places, kv_heads, group, batches):
    tokens = x.shape[0]
    rows = tokens // batches
    length = rows * lax.axis_size("fsdp")
    query_features = kv_heads * group * HD
    used = query_features + kv_heads * 128
    fulls = gather(shards, ("yxc", "xyc", "yxc", "xyc", "yxc"), 1, 5)
    first_pack, out_full, gate_full, up_full, _ = (f.reshape(-1, f.shape[-1]) for f in fulls)
    gains = first_pack[:, used : used + 2].astype(jnp.float32).T
    query_index = lax.axis_index("fsdp") * rows + jnp.arange(rows, dtype=jnp.int32)
    key_index = jnp.arange(length, dtype=jnp.int32)
    x_float = x.astype(jnp.float32)
    cos_tables, sin_tables = rotary_pairs(places, tokens, HD**-0.5)
    doc_start = query_index[None, :] - places.reshape(batches, rows)
    allowed = (key_index[None, None, :] <= query_index[None, :, None]) & (
        key_index[None, None, :] >= doc_start[:, :, None]
    )
    bias = jnp.where(allowed, 0.0, NEGATIVE)
    attn_inverse = lax.rsqrt(jnp.mean(x_float * x_float, -1, keepdims=True) + EPSILON)
    normed = (x_float * attn_inverse * gains[0]).astype(jnp.bfloat16)
    projected = project(normed, first_pack[:, :used], cos_tables, sin_tables, kv_heads * 128)
    both_rows = projected[:, query_features:].reshape(batches, rows, -1)
    both_all = lax.all_gather(both_rows, "fsdp", axis=1, tiled=True)
    attended, logs = attend(projected, both_all, bias, kv_heads, group)
    mixed = x_float + plain_dot(attended, out_full)
    mlp_inverse = lax.rsqrt(jnp.mean(mixed * mixed, -1, keepdims=True) + EPSILON)
    normed_mlp = (mixed * mlp_inverse * gains[1]).astype(jnp.bfloat16)
    gate_pre = plain_dot(normed_mlp, gate_full)
    up_proj = plain_dot(normed_mlp, up_full)
    gate_sig = jax.nn.sigmoid(gate_pre)
    silu = gate_pre * gate_sig
    slope = up_proj * gate_sig * (1.0 + gate_pre * (1.0 - gate_sig))
    low = jnp.bfloat16
    return list(fulls) + [
        projected[:, :query_features],
        both_all,
        attended,
        logs,
        mixed,
        normed_mlp,
        (silu * up_proj).astype(low),
        slope.astype(low),
        silu.astype(low),
        bias.reshape(tokens, length),
        cos_tables,
        sin_tables,
    ]


def backward_plain(saved, cotangent, x_low, kv_heads, group, batches):
    tokens, width = x_low.shape
    rows = tokens // batches
    key_features = kv_heads * HD
    query_features = kv_heads * group * HD
    used = query_features + 2 * key_features
    x_float = x_low.astype(jnp.float32)
    first_pack, out_full, gate_full, up_full, down_full = (
        f.reshape(-1, f.shape[-1]) for f in saved[:5]
    )
    queries, both_all, attended, logs, mixed, normed_mlp = saved[5:11]
    hidden, slope, silu, bias, cos_tables, sin_tables = saved[11:]
    projection = first_pack[:, :used]
    gains = first_pack[:, used : used + 2].astype(jnp.float32).T
    attn_gain_f = gains[0]
    mlp_gain_f = gains[1]
    attn_inverse = lax.rsqrt(jnp.mean(x_float * x_float, -1, keepdims=True) + EPSILON)
    normed = (x_float * attn_inverse * attn_gain_f).astype(jnp.bfloat16)
    mlp_inverse = lax.rsqrt(jnp.mean(mixed * mixed, -1, keepdims=True) + EPSILON)
    output = (mixed + plain_dot(hidden, down_full)).astype(jnp.bfloat16)

    cot_low = cotangent
    cot_float = cot_low.astype(jnp.float32)
    grad_down = half_of(left_dot(hidden, cot_low))
    grad_hidden = right_dot(cot_low, down_full)
    grad_gate_pre = (grad_hidden * slope.astype(jnp.float32)).astype(jnp.bfloat16)
    grad_up_pre = (grad_hidden * silu.astype(jnp.float32)).astype(jnp.bfloat16)
    grad_gate = half_of(left_dot(normed_mlp, grad_gate_pre))
    grad_up = half_of(left_dot(normed_mlp, grad_up_pre))
    grad_normed_mlp = right_dot(grad_gate_pre, gate_full) + right_dot(grad_up_pre, up_full)
    grad_mlp_gain = jnp.sum(grad_normed_mlp * mixed * mlp_inverse, 0)
    grad_mixed = cot_float + norm_back(grad_normed_mlp * mlp_gain_f, mixed, mlp_inverse)
    grad_mixed_low = grad_mixed.astype(jnp.bfloat16)
    grad_out = half_of(left_dot(attended, grad_mixed_low))
    grad_attended = right_dot(grad_mixed_low, out_full).astype(jnp.bfloat16)
    grad_query_pre, portions = attend_back(
        queries,
        grad_attended,
        both_all,
        bias.reshape(batches, rows, -1),
        logs,
        cos_tables,
        sin_tables,
        group,
    )
    sums = lax.psum_scatter(portions, "fsdp", scatter_dimension=1, tiled=True)
    sums = sums.astype(jnp.float32).reshape(tokens, kv_heads, 128)
    turned = jnp.concatenate([sums[..., 32:64], sums[..., :32], sums[..., 64:]], -1)
    grad_pair_pre = (sums * cos_tables[1][:, None] - turned * sin_tables[1][:, None]).astype(
        jnp.bfloat16
    )
    grad_pre = jnp.concatenate(
        [grad_query_pre, grad_pair_pre.reshape(tokens, 2 * key_features)], -1
    )
    grad_projection = left_dot(normed, grad_pre)
    grad_normed = right_dot(grad_pre, projection)
    grad_attn_gain = jnp.sum(grad_normed * x_float * attn_inverse, 0)
    grad_input = grad_mixed + norm_back(grad_normed * attn_gain_f, x_float, attn_inverse)
    gain_columns = jnp.stack([grad_attn_gain, grad_mlp_gain], -1)
    gain_columns = jnp.pad(gain_columns, ((0, 0), (0, 126)))
    grad_first = half_of(jnp.concatenate([grad_projection, gain_columns], 1))
    grad_down, grad_gate, grad_up, grad_out, last = scatter(
        (grad_down, grad_gate, grad_up, grad_out, grad_first), ("xy", "yx", "xy", "yx", "xy"), 2
    )
    return (
        output,
        grad_input.astype(jnp.bfloat16),
        last,
        grad_out,
        grad_gate,
        grad_up,
        grad_down,
    )


def on_device(
    inputs,
    positions,
    cotangent,
    attn_gain,
    w_query,
    key_matrix,
    value_matrix,
    w_out,
    mlp_gain,
    w_gate,
    w_up,
    w_down,
):
    batches, _, rows, width = inputs.shape
    shard = w_query.shape[0]
    query_features = w_query.shape[1]
    key_features = key_matrix.shape[1]
    kv_heads = key_features // HD
    group = query_features // key_features
    tokens = batches * rows
    used = query_features + 2 * key_features

    extras = jnp.zeros((shard, 128), jnp.bfloat16)
    extras = extras.at[:, 0].set(attn_gain).at[:, 1].set(mlp_gain)
    pairs = jnp.concatenate(
        [key_matrix.reshape(shard, kv_heads, HD), value_matrix.reshape(shard, kv_heads, HD)], -1
    )
    first_shard = jnp.concatenate([w_query, pairs.reshape(shard, -1), extras], axis=1)
    shards = (first_shard, w_out, w_gate, w_up, w_down)
    x_low = inputs.reshape(tokens, width)
    cot_low = cotangent.reshape(tokens, width)
    fits = shard % 8 == 0 and lax.axis_size("fsdp") == 4 and rows % 256 == 0
    saved = (forward if fits else forward_plain)(
        shards, x_low, positions.reshape(tokens, 1), kv_heads, group, batches
    )
    if fits:
        by_place = (lax.axis_size("dp") // 2, 2, lax.axis_size("fsdp") // 2, 2, -1, tokens)
        transposed = [t.reshape(by_place) for t in saved[17:]]
        found = backward(saved[:17], transposed, cot_low, x_low, kv_heads, group, batches)
    else:
        found = backward_plain(saved, cot_low, x_low, kv_heads, group, batches)
    output, grad_input, last, grad_out, grad_gate, grad_up, grad_down = found[:7]
    last_pairs = last[:, query_features:used].reshape(shard, kv_heads, 2, HD)
    return (
        output.reshape(inputs.shape),
        grad_input.reshape(inputs.shape),
        last[:, used],
        last[:, :query_features],
        last_pairs[:, :, 0].reshape(shard, key_features),
        last_pairs[:, :, 1].reshape(shard, key_features),
        grad_out,
        last[:, used + 1],
        grad_gate,
        grad_up,
        grad_down,
    )


def solution(mesh):
    tokens = P(None, "dp", "fsdp", None)
    vector = P(BOTH)
    matrix = P(BOTH, None)
    weights = (vector, matrix, matrix, matrix, matrix, vector, matrix, matrix, matrix)
    return jax.shard_map(
        on_device,
        mesh=mesh,
        in_specs=(tokens, P(None, "dp", "fsdp"), tokens) + weights,
        out_specs=(tokens, tokens) + weights,
        check_vma=False,
    )
```

```python
import functools

import jax
import jax.numpy as jnp
from jax import lax
from jax.experimental import pallas as pl
from jax.experimental.pallas import tpu as pltpu
from jax.sharding import PartitionSpec as P

HD = 64
EPSILON = 1e-05
NEGATIVE = -1e30
ROPE_BASE = 10000.0
BOTH = ("dp", "fsdp")


def rope_tables(places):
    half = HD // 2
    freqs = ROPE_BASE ** (-jnp.arange(half).astype(jnp.float32) / half)
    angles = places.astype(jnp.float32)[:, None] * freqs[None, :]
    return (jnp.cos(angles), jnp.sin(angles))


def plain_dot(left, right):
    return jnp.dot(left, right, preferred_element_type=jnp.float32)


def left_dot(left, right):
    return lax.dot_general(
        left, right, (((0,), (0,)), ((), ())), preferred_element_type=jnp.float32
    )


def right_dot(left, right):
    return lax.dot_general(
        left, right, (((1,), (1,)), ((), ())), preferred_element_type=jnp.float32
    )


def norm_back(grad_normed, inputs_float, inverse):
    return inverse * (
        grad_normed
        - inputs_float * inverse * inverse * jnp.mean(grad_normed * inputs_float, -1, keepdims=True)
    )


class Place:
    def __init__(self):
        self.Z=lax.axis_size("dp")//2; self.X=lax.axis_size("fsdp")//2
        dp=lax.axis_index("dp"); fs=lax.axis_index("fsdp")
        self.z=dp//2; self.y=dp%2; self.x=fs//2; self.c=fs%2
    def device(self,s=0,dy=0,dx=0,dc=0):
        return (lax.rem(self.z+s,self.Z)*2+lax.rem(self.y+dy,2), lax.rem(self.x+dx,self.X)*2+lax.rem(self.c+dc,2))
    def slot(self,s,dy,dx,dc):
        return ((lax.rem(self.z+self.Z-s,self.Z)*2+lax.rem(self.y+dy,2))*self.X+lax.rem(self.x+dx,self.X))*2+lax.rem(self.c+dc,2)

MESH = pl.DeviceIdType.MESH

def greet(me):
    barrier=pltpu.get_barrier_semaphore()
    friends=[me.device(s=s) for s in range(1,me.Z)]+[me.device(dy=1),me.device(dx=1),me.device(dc=1)]
    for f in friends:
        pl.semaphore_signal(barrier,inc=1,device_id=f,device_id_type=MESH)
    pl.semaphore_wait(barrier,len(friends))

def gather_kernel(Z, orders, ahead, *refs):
    K=len(orders)
    shards=refs[:K]; outs=refs[K:2*K]; local,send,recv=refs[2*K:]
    me=Place()
    greet(me)
    dims={"y":1,"x":2,"c":3}
    def sem(rel):
        return ((rel[0]*2+rel[1])*2+rel[2])*2+rel[3]
    started=[]
    def start(k,rel,to):
        if isinstance(to,int):
            target=me.device(s=to); landed=(to,0,0,0)
        else:
            landed=list(rel); landed[dims[to]]=1; landed=tuple(landed)
            target=me.device(**{"d"+to:1})
        slot=me.slot(*rel)
        src=shards[k] if rel==(0,0,0,0) else outs[k].at[slot]
        cp=pltpu.make_async_remote_copy(src_ref=src,dst_ref=outs[k].at[slot],send_sem=send.at[k,sem(landed)],recv_sem=recv.at[k,sem(landed)],device_id=target,device_id_type=MESH)
        cp.start()
        table[(k,landed)]=cp
    table={}
    own=[]
    def first(k):
        cp=pltpu.make_async_copy(shards[k],outs[k].at[me.slot(0,0,0,0)],local.at[k]); cp.start(); own.append(cp)
        for s in range(1,Z): start(k,(0,0,0,0),s)
        for d in orders[k]: start(k,(0,0,0,0),d)
    def arrive(k,rel,rest):
        table[(k,rel)].wait_recv()
        for d in rest: start(k,rel,d)
    def rel_of(s,o,a,b=0,c=0):
        r=[s,0,0,0]; r[dims[o[0]]]=a; r[dims[o[1]]]=b; r[dims[o[2]]]=c
        return tuple(r)
    for k in range(min(ahead,K)): first(k)
    for t in range(K+3):
        if t+ahead<K: first(t+ahead)
        k=t
        if k<K:
            o=orders[k]
            for s in range(1,Z): arrive(k,rel_of(s,o,0),o)
        k=t-1
        if 0<=k<K:
            o=orders[k]
            for s in range(Z): arrive(k,rel_of(s,o,1),o[1:])
        k=t-2
        if 0<=k<K:
            o=orders[k]
            for s in range(Z):
                for a in range(2): arrive(k,rel_of(s,o,a,1),o[2:])
        k=t-3
        if 0<=k<K:
            o=orders[k]
            for s in range(Z):
                for a in range(2):
                    for b in range(2): arrive(k,rel_of(s,o,a,b,1),"")
    for cp in own: cp.wait()
    for cp in table.values(): cp.wait_send()

def gather(shards, orders, cid, ahead=2):
    n=lax.axis_size("dp")*lax.axis_size("fsdp"); Z=lax.axis_size("dp")//2; K=len(shards)
    return pl.pallas_call(functools.partial(gather_kernel,Z,orders,ahead),
        out_shape=[jax.ShapeDtypeStruct((n,)+s.shape,s.dtype) for s in shards],
        in_specs=[pl.BlockSpec(memory_space=pl.ANY)]*K,
        out_specs=[pl.BlockSpec(memory_space=pl.ANY)]*K,
        scratch_shapes=[pltpu.SemaphoreType.DMA((K,)),pltpu.SemaphoreType.DMA((K,8*Z)),pltpu.SemaphoreType.DMA((K,8*Z))],
        compiler_params=pltpu.CompilerParams(collective_id=cid,has_side_effects=True))(*shards)


class Gathering:
    def __init__(self, me, chunks, local, send, recv):
        self.me, self.chunks = me, chunks
        self.local, self.send, self.recv = local, send, recv
        self.table, self.own = {}, []

    def start(self, k, rel, to):
        shard, full, cols, _ = self.chunks[k]
        me = self.me
        if isinstance(to, int):
            target, landed = me.device(s=to), (to, 0, 0, 0)
        else:
            landed = list(rel)
            landed["zyxc".index(to)] = 1
            landed = tuple(landed)
            target = me.device(**{"d" + to: 1})
        slot = me.slot(*rel)
        here = full.at[slot, :, cols]
        at = ((landed[0] * 2 + landed[1]) * 2 + landed[2]) * 2 + landed[3]
        copy = pltpu.make_async_remote_copy(
            src_ref=shard.at[:, cols] if rel == (0, 0, 0, 0) else here,
            dst_ref=here,
            send_sem=self.send.at[k, at],
            recv_sem=self.recv.at[k, at],
            device_id=target,
            device_id_type=MESH,
        )
        copy.start()
        self.table[(k, landed)] = copy

    def begin(self, k):
        shard, full, cols, order = self.chunks[k]
        copy = pltpu.make_async_copy(
            shard.at[:, cols], full.at[self.me.slot(0, 0, 0, 0), :, cols], self.local.at[k]
        )
        copy.start()
        self.own.append((k, copy))
        for s in range(1, self.me.Z):
            self.start(k, (0, 0, 0, 0), s)
        for d in order:
            self.start(k, (0, 0, 0, 0), d)

    def step(self, k, stage):
        order = self.chunks[k][3]
        where = ["zyxc".index(d) for d in order]
        for s in range(1 if stage == 0 else 0, self.me.Z):
            for bits in range(1 << max(stage - 1, 0)):
                rel = [s, 0, 0, 0]
                for i in range(stage - 1):
                    rel[where[i]] = bits >> i & 1
                if stage:
                    rel[where[stage - 1]] = 1
                rel = tuple(rel)
                self.table[(k, rel)].wait_recv()
                for d in order[stage:]:
                    self.start(k, rel, d)
        if stage == 3:
            for at, copy in self.own:
                if at == k:
                    copy.wait()

    def finish(self):
        for copy in self.table.values():
            copy.wait_send()


def forward_kernel(sizes, *refs):
    batches, rows, kv_heads, group, used = sizes
    (first_s, out_s, gate_s, up_s, down_s, x_ref, place_ref, freq_ref) = refs[:8]
    (first_w, out_w, gate_w, up_w, down_w, q_out, kv_out, o_out, log_out) = refs[8:17]
    (mixed_out, h2_out, hidden_out, slope_out, silu_out, bias_out, cos_out, sin_out) = refs[17:25]
    (hid_turned, h2_turned, att_turned, nor_turned) = refs[25:29]
    (raw_a, raw_b, w_a, w_b, normed, queries, kv_all, attended, logs, mixed, h2) = refs[29:40]
    (hidden, slope, silu, bias, cos_t, sin_t, gains) = refs[40:47]
    (hid_t, h2_t, att_t, nor_t) = refs[47:51]
    (local, send, recv, kv_send, kv_recv, load_sem, store_sem) = refs[51:]
    me = Place()
    greet(me)
    whole = slice(None)
    half = down_w.shape[2] // 2
    comm = Gathering(
        me,
        (
            (first_s, first_w, whole, "xyc"),
            (out_s, out_w, whole, "yxc"),
            (gate_s, gate_w, whole, "yxc"),
            (up_s, up_w, whole, "xyc"),
            (down_s, down_w, pl.ds(0, half), "yxc"),
            (down_s, down_w, pl.ds(half, half), "xyc"),
        ),
        local,
        send,
        recv,
    )
    tokens, width = x_ref.shape
    length = kv_all.shape[1]
    stores = []

    def store(i, src, dst):
        copy = pltpu.make_async_copy(src, dst, store_sem.at[i])
        copy.start()
        stores.append(copy)

    def over_rows(body, step=64):
        def one(i, carry):
            body(pl.ds(pl.multiple_of(i * step, step), step))
            return carry

        lax.fori_loop(0, tokens // step, one, 0)

    def load(full, raw, col, size, i):
        return pltpu.make_async_copy(
            full.at[:, :, pl.ds(col, size)], raw.at[:, :, pl.ds(0, size)], load_sem.at[i]
        )

    def assemble(raw, flat, size):
        n, r, _ = raw.shape
        pair = 2 * r

        def one(i, carry):
            piece = raw[pl.ds(2 * i, 2), :, pl.ds(0, size)].astype(jnp.float32)
            flat[pl.ds(pl.multiple_of(pair * i, 16), pair), pl.ds(0, size)] = piece.reshape(
                pair, size
            ).astype(jnp.bfloat16)
            return carry

        lax.fori_loop(0, n // 2, one, 0)

    def turn_rows(src, dst, base, size):
        for i in range(size // 256):
            at = slice(base + i * 256, base + (i + 1) * 256)
            dst[at, :] = src[:, at].astype(jnp.float32).T.astype(jnp.bfloat16)

    comm.begin(0)
    comm.begin(1)
    comm.begin(2)

    scale = HD**-0.5
    lane = lax.broadcasted_iota(jnp.int32, (64, 128), 1)
    second = lax.rem(lane, HD) >= HD // 2
    is_value = lane >= HD

    def tables(at):
        angle = place_ref[at, :].astype(jnp.float32) * freq_ref[...]
        c, s = jnp.cos(angle), jnp.sin(angle)
        s = jnp.where(second, s, -s)
        cos_t[0, at, :] = c * scale
        sin_t[0, at, :] = s * scale
        cos_t[1, at, :] = jnp.where(is_value, 1.0, c)
        sin_t[1, at, :] = jnp.where(is_value, 0.0, s)

    over_rows(tables)
    first_row = lax.axis_index("fsdp") * rows

    def masks(at):
        token = at.start
        inside = lax.rem(token, rows)
        query = first_row + inside + lax.broadcasted_iota(jnp.int32, (64, length), 0)
        key = lax.broadcasted_iota(jnp.int32, (64, length), 1)
        start = query - place_ref[at, :]
        allowed = (key <= query) & (key >= start)
        bias[at, :] = jnp.where(allowed, 0.0, NEGATIVE).astype(jnp.bfloat16)

    over_rows(masks)
    store(0, bias, bias_out)
    store(1, cos_t, cos_out)
    store(2, sin_t, sin_out)

    comm.step(0, 0)
    comm.begin(3)
    comm.step(1, 0)
    comm.step(0, 1)
    comm.step(2, 0)
    comm.step(1, 1)
    comm.step(0, 2)
    comm.step(3, 0)
    comm.step(2, 1)
    comm.step(1, 2)
    comm.step(0, 3)

    tile = raw_a.shape[2]
    load(first_w, raw_a, used, 128, 0).start()
    load(first_w, raw_b, 0, tile, 1).start()
    load(first_w, raw_a, used, 128, 0).wait()
    assemble(raw_a, w_a, 128)
    gains[...] = w_a[:, :128].astype(jnp.float32).T[:8]
    load(first_w, raw_a, used - tile, tile, 0).start()

    def norm_one(at):
        x = x_ref[at, :].astype(jnp.float32)
        inverse = lax.rsqrt(jnp.mean(x * x, -1, keepdims=True) + EPSILON)
        normed[at, :] = (x * inverse * gains[0:1, :]).astype(jnp.bfloat16)

    over_rows(norm_one)

    def turn(flat, kind, put, step=256):
        def body(at):
            u = plain_dot(normed[at, :], flat[...])
            for j in range(tile // 128):
                piece = u[:, j * 128 : (j + 1) * 128]
                piece = piece * cos_t[kind, at, :] + swap_halves(piece) * sin_t[kind, at, :]
                put(at, j, piece.astype(jnp.bfloat16))

        over_rows(body, step)

    slot = (me.x * 2 + me.c) * rows

    def put_pair(at, j, piece):
        token = at.start
        b = token // rows
        row = pl.multiple_of(slot + lax.rem(token, rows), 256)
        kv_all[b, pl.ds(row, 256), j * 128 : (j + 1) * 128] = piece

    load(first_w, raw_a, used - tile, tile, 0).wait()
    assemble(raw_a, w_a, tile)
    turn(w_a, 1, put_pair)

    def share(i, dx, to):
        row = (lax.rem(me.x + dx, 2) * 2 + me.c) * rows
        block = kv_all.at[:, pl.ds(pl.multiple_of(row, 256), rows), :]
        copy = pltpu.make_async_remote_copy(
            src_ref=block,
            dst_ref=block,
            send_sem=kv_send.at[i],
            recv_sem=kv_recv.at[i],
            device_id=me.device(**{"d" + to: 1}),
            device_id_type=MESH,
        )
        copy.start()
        return copy

    to_x = share(0, 0, "x")
    to_c = share(1, 0, "c")
    comm.step(3, 1)
    comm.begin(4)
    for j in range(queries.shape[1] // tile):
        raw, flat = ((raw_b, w_b), (raw_a, w_a))[j % 2]
        if (j + 1) * tile < queries.shape[1]:
            load(first_w, (raw_a, raw_b)[j % 2], (j + 1) * tile, tile, j % 2).start()
        load(first_w, raw, j * tile, tile, 1 - j % 2).wait()
        assemble(raw, flat, tile)

        def put_query(at, i, piece, j=j):
            queries[at, j * tile + i * 128 : j * tile + (i + 1) * 128] = piece

        turn(flat, 0, put_query)
        if j == 0:
            comm.step(2, 2)
            comm.begin(5)
    store(3, queries, q_out)
    turn_rows(normed, nor_t, 0, width)
    store(12, nor_t, nor_turned)
    comm.step(1, 3)
    to_x.wait_recv()
    to_far = share(2, 1, "c")
    to_c.wait_recv()
    to_far.wait_recv()
    store(4, kv_all, kv_out)

    logs[...] = jnp.zeros_like(logs)
    lanes = lax.broadcasted_iota(jnp.int32, (rows, 128), 1)
    sides_mask = lane_masks(rows)

    def head(i, carry):
        b = i // kv_heads
        h = lax.rem(i, kv_heads)
        at = pl.ds(pl.multiple_of(b * rows, 256), rows)
        kv = kv_all[b, :, pl.ds(pl.multiple_of(h * 128, 128), 128)]
        sides = (kv, swapped(kv))
        shift = bias[at, :].astype(jnp.float32)
        log_piece = logs[at, :]
        for pair in range(group // 2):
            cols = pl.ds(pl.multiple_of(h * group * HD + pair * 128, 128), 128)
            q = queries[at, cols]
            found = []
            for side in range(2):
                scores = dot_t(q * sides_mask[side], sides[side]) + shift
                top = jnp.max(scores, -1, keepdims=True)
                powers = jnp.exp(scores - top)
                total = jnp.sum(powers, -1, keepdims=True)
                probs = (powers * (1.0 / total)).astype(jnp.bfloat16)
                found.append(plain_dot(probs, sides[1 - side]))
                log_piece = jnp.where(
                    lanes == h * group + pair * 2 + side, top + jnp.log(total), log_piece
                )
            attended[at, cols] = jnp.where(lanes < HD, found[0], found[1]).astype(jnp.bfloat16)
        logs[at, :] = log_piece
        return carry

    count = batches * kv_heads
    pumps = [(3, 2), (4, 0), (2, 3), (5, 0), (4, 1), (5, 1)]
    done = 0
    for i in range(6):
        upto = (2, 4, 6, 8, 9, 10)[i] * count // 10
        lax.fori_loop(done, upto, head, 0)
        done = upto
        comm.step(*pumps[i])
    store(5, attended, o_out)
    store(6, logs, log_out)

    steps = width // tile
    load(out_w, raw_a, 0, tile, 0).start()
    for j in range(steps):
        raw, flat = ((raw_a, w_a), (raw_b, w_b))[j % 2]
        if j + 1 < steps:
            load(out_w, (raw_b, raw_a)[j % 2], (j + 1) * tile, tile, 1 - j % 2).start()
        load(out_w, raw, j * tile, tile, j % 2).wait()
        assemble(raw, flat, tile)

        def add_in(at, flat=flat, j=j):
            cols = slice(j * tile, (j + 1) * tile)
            mixed[at, cols] = x_ref[at, cols].astype(jnp.float32) + plain_dot(
                attended[at, :], flat[...]
            )

        over_rows(add_in, 256)

    def norm_two(at):
        y = mixed[at, :]
        inverse = lax.rsqrt(jnp.mean(y * y, -1, keepdims=True) + EPSILON)
        h2[at, :] = (y * inverse * gains[1:2, :]).astype(jnp.bfloat16)

    over_rows(norm_two)
    store(7, mixed, mixed_out)
    store(8, h2, h2_out)
    turn_rows(attended, att_t, 0, attended.shape[1])
    store(13, att_t, att_turned)
    turn_rows(h2, h2_t, 0, width)
    store(14, h2_t, h2_turned)
    comm.step(3, 3)

    wide = 512
    features = hidden.shape[1]
    pumps = {1: (4, 2), 3: (5, 2), 5: (4, 3)}
    load(gate_w, raw_a, 0, wide, 0).start()
    load(up_w, raw_b, 0, wide, 1).start()
    for j in range(features // wide):
        load(gate_w, raw_a, j * wide, wide, 0).wait()
        assemble(raw_a, w_a, wide)
        load(up_w, raw_b, j * wide, wide, 1).wait()
        assemble(raw_b, w_b, wide)
        if (j + 1) * wide < features:
            load(gate_w, raw_a, (j + 1) * wide, wide, 0).start()
            load(up_w, raw_b, (j + 1) * wide, wide, 1).start()

        def units(at, j=j):
            cols = slice(j * wide, (j + 1) * wide)
            g = plain_dot(h2[at, :], w_a[:, :wide])
            u = plain_dot(h2[at, :], w_b[:, :wide])
            sig = jax.nn.sigmoid(g)
            soft = g * sig
            hidden[at, cols] = (soft * u).astype(jnp.bfloat16)
            silu[at, cols] = soft.astype(jnp.bfloat16)
            slope[at, cols] = (u * (sig * (1.0 + g * (1.0 - sig)))).astype(jnp.bfloat16)

        over_rows(units, 256)
        turn_rows(hidden, hid_t, j * wide, wide)
        cols = pl.ds(j * wide, wide)
        store(16 + 4 * j, hidden.at[:, cols], hidden_out.at[:, cols])
        store(17 + 4 * j, silu.at[:, cols], silu_out.at[:, cols])
        store(18 + 4 * j, slope.at[:, cols], slope_out.at[:, cols])
        store(19 + 4 * j, hid_t.at[cols, :], hid_turned.at[cols, :])
        if j in pumps:
            comm.step(*pumps[j])
    comm.step(5, 3)
    for copy in (to_x, to_c, to_far):
        copy.wait_send()
    comm.finish()
    for copy in stores:
        copy.wait()


def forward(shards, x, places, kv_heads, group, batches):
    first_s, out_s, gate_s, up_s, down_s = shards
    n = lax.axis_size("dp") * lax.axis_size("fsdp")
    Z = lax.axis_size("dp") // 2
    tokens, width = x.shape
    rows = tokens // batches
    length = rows * lax.axis_size("fsdp")
    key_wide = kv_heads * 128
    query_wide = kv_heads * group * HD
    used = query_wide + key_wide
    features = gate_s.shape[1]
    r = first_s.shape[0]
    freqs = ROPE_BASE ** (-jnp.arange(HD // 2).astype(jnp.float32) / (HD // 2))
    freqs = jnp.tile(freqs, 4)[None]
    bf, f32 = jnp.bfloat16, jnp.float32
    shape = jax.ShapeDtypeStruct
    outs = [shape((n,) + s.shape, s.dtype) for s in shards] + [
        shape((tokens, query_wide), bf),
        shape((batches, length, key_wide), bf),
        shape((tokens, query_wide), bf),
        shape((tokens, 128), f32),
        shape((tokens, width), f32),
        shape((tokens, width), bf),
        shape((tokens, features), bf),
        shape((tokens, features), bf),
        shape((tokens, features), bf),
        shape((tokens, length), bf),
        shape((2, tokens, 128), f32),
        shape((2, tokens, 128), f32),
        shape((features, tokens), bf),
        shape((width, tokens), bf),
        shape((query_wide, tokens), bf),
        shape((width, tokens), bf),
    ]
    vmem = pltpu.VMEM
    scratch = [
        vmem((n, r, key_wide), bf),
        vmem((n, r, key_wide), bf),
        vmem((width, key_wide), bf),
        vmem((width, key_wide), bf),
        vmem((tokens, width), bf),
        vmem((tokens, query_wide), bf),
        vmem((batches, length, key_wide), bf),
        vmem((tokens, query_wide), bf),
        vmem((tokens, 128), f32),
        vmem((tokens, width), f32),
        vmem((tokens, width), bf),
        vmem((tokens, features), bf),
        vmem((tokens, features), bf),
        vmem((tokens, features), bf),
        vmem((tokens, length), bf),
        vmem((2, tokens, 128), f32),
        vmem((2, tokens, 128), f32),
        vmem((8, width), f32),
        vmem((features, tokens), bf),
        vmem((width, tokens), bf),
        vmem((query_wide, tokens), bf),
        vmem((width, tokens), bf),
        pltpu.SemaphoreType.DMA((6,)),
        pltpu.SemaphoreType.DMA((6, 8 * Z)),
        pltpu.SemaphoreType.DMA((6, 8 * Z)),
        pltpu.SemaphoreType.DMA((3,)),
        pltpu.SemaphoreType.DMA((3,)),
        pltpu.SemaphoreType.DMA((2,)),
        pltpu.SemaphoreType.DMA((16 + 4 * (features // 512),)),
    ]
    any_space = pl.BlockSpec(memory_space=pl.ANY)
    in_vmem = pl.BlockSpec(memory_space=pltpu.VMEM)
    return pl.pallas_call(
        functools.partial(forward_kernel, (batches, rows, kv_heads, group, used)),
        out_shape=outs,
        in_specs=[any_space] * 5 + [in_vmem] * 3,
        out_specs=[any_space] * len(outs),
        scratch_shapes=scratch,
        compiler_params=pltpu.CompilerParams(
            collective_id=1, has_side_effects=True, vmem_limit_bytes=63 * 2**20
        ),
        cost_estimate=pl.CostEstimate(
            flops=2 * tokens * width * (used + width + 2 * features),
            bytes_accessed=4 * n * r * (used + width + 3 * features),
            transcendentals=tokens * features,
        ),
    )(*shards, x, places, freqs)


def tile_of(N):
    for t in (512,384,256,128):
        if N%t==0: return t
    return N

def scatter_kernel(Z, orders, ahead, dims_, *refs):
    K=len(orders)
    parts=refs[:K]; outs=refs[K:2*K]
    sc=refs[2*K:]
    first_buf=sc[:K]; one_buf=sc[K:2*K]; two_buf=sc[2*K:3*K]; last_buf=sc[3*K:4*K]
    shapes=sorted(set(dims_))
    stage=[sc[4*K+shapes.index(d)] for d in dims_]
    local,send,recv=sc[4*K+len(shapes):]
    me=Place()
    greet(me)
    copies={}
    def ship(k,name,index,src,dst,target):
        cp=pltpu.make_async_remote_copy(src_ref=src,dst_ref=dst,send_sem=send.at[k,index],recv_sem=recv.at[k,index],device_id=target,device_id_type=MESH)
        cp.start(); copies[(k,name)]=cp
    def part(k,a,b,other):
        o=orders[k]
        rel={o[0]:a,o[1]:b}
        y=lax.rem(me.y+rel["y"],2); x=lax.rem(me.x+rel["x"],me.X); c=lax.rem(me.c+other,2)
        return parts[k].at[:,y,x,c]
    order4=((1,1),(1,0),(0,1),(0,0))
    locals_={}
    def first(k):
        for i,(a,b) in enumerate(order4):
            ship(k,("c",a,b),i,part(k,a,b,1),first_buf[k].at[a,b],me.device(dc=1))
    def bring(k,i):
        a,b=order4[i]
        cp=pltpu.make_async_copy(part(k,a,b,0),stage[k].at[i%2],local.at[k,i%2]); cp.start(); locals_[(k,i)]=cp
    def add(dst,src,k):
        _,r,N=dims_[k]
        t=tile_of(N)
        def body(i,_):
            zi=i//(N//t); j=i%(N//t)
            cols=pl.ds(pl.multiple_of(j*t,128),t)
            dst[zi,:,cols]=dst[zi,:,cols]+src[zi,:,cols]
            return 0
        lax.fori_loop(0,Z*(N//t),body,0)
    def step_c(k):
        bring(k,0); bring(k,1)
        for i,(a,b) in enumerate(order4):
            copies[(k,("c",a,b))].wait_recv()
            locals_[(k,i)].wait()
            add(first_buf[k].at[a,b],stage[k].at[i%2],k)
            if i+2<4: bring(k,i+2)
            if a==1:
                ship(k,("1",b),4+b,first_buf[k].at[1,b],one_buf[k].at[b],me.device(**{"d"+orders[k][0]:1}))
    def step_1(k):
        for b in (1,0):
            copies[(k,("1",b))].wait_recv()
            add(first_buf[k].at[0,b],one_buf[k].at[b],k)
            if b==1:
                ship(k,"2",6,first_buf[k].at[0,1],two_buf[k],me.device(**{"d"+orders[k][1]:1}))
    def step_2(k):
        copies[(k,"2")].wait_recv()
        add(first_buf[k].at[0,0],two_buf[k],k)
        for s in range(1,Z):
            ship(k,("z",s),6+s,first_buf[k].at[0,0,lax.rem(me.z+s,Z)],last_buf[k].at[s-1],me.device(s=s))
    def step_z(k):
        _,r,N=dims_[k]
        for s in range(1,Z): copies[(k,("z",s))].wait_recv()
        t=tile_of(N)
        mine=first_buf[k].at[0,0,me.z]
        def body(j,_):
            cols=pl.ds(pl.multiple_of(j*t,128),t)
            total=mine[:,cols].astype(jnp.float32)
            for s in range(1,Z): total=total+last_buf[k][s-1,:,cols].astype(jnp.float32)
            outs[k][:,cols]=total
            return 0
        lax.fori_loop(0,N//t,body,0)
    for k in range(min(ahead,K)): first(k)
    for t in range(K+3):
        if t+ahead<K: first(t+ahead)
        if t<K: step_c(t)
        if 0<=t-1<K: step_1(t-1)
        if 0<=t-2<K: step_2(t-2)
        if 0<=t-3<K: step_z(t-3)
    for cp in copies.values(): cp.wait_send()

def scatter(parts, orders, cid, ahead=2):
    n=lax.axis_size("dp")*lax.axis_size("fsdp"); Z=lax.axis_size("dp")//2; X=lax.axis_size("fsdp")//2; K=len(parts)
    dims_=[(n,p.shape[0]//n,p.shape[1]) for p in parts]
    parts=[p.reshape(Z,2,X,2,p.shape[0]//n,p.shape[1]) for p in parts]
    bf=jnp.bfloat16
    sc=[pltpu.VMEM((2,2,Z,r,N),bf) for _,r,N in dims_]+[pltpu.VMEM((2,Z,r,N),bf) for _,r,N in dims_]+[pltpu.VMEM((Z,r,N),bf) for _,r,N in dims_]+[pltpu.VMEM((Z-1,r,N),bf) for _,r,N in dims_]+[pltpu.VMEM((2,Z,r,N),bf) for _,r,N in sorted(set(dims_))]
    return pl.pallas_call(functools.partial(scatter_kernel,Z,orders,ahead,dims_),
        out_shape=[jax.ShapeDtypeStruct((r,N),jnp.float32) for _,r,N in dims_],
        in_specs=[pl.BlockSpec(memory_space=pl.ANY)]*K,
        out_specs=[pl.BlockSpec(memory_space=pltpu.VMEM)]*K,
        scratch_shapes=sc+[pltpu.SemaphoreType.DMA((K,2)),pltpu.SemaphoreType.DMA((K,6+Z)),pltpu.SemaphoreType.DMA((K,6+Z))],
        compiler_params=pltpu.CompilerParams(collective_id=cid,has_side_effects=True,vmem_limit_bytes=63*2**20))(*parts)


def dot_t(left, right):
    return lax.dot_general(
        left, right, (((1,), (1,)), ((), ())), preferred_element_type=jnp.float32
    )


def swap_halves(u):
    lane = lax.broadcasted_iota(jnp.int32, u.shape, 1)
    down = pltpu.roll(u, 32, 1)
    up = pltpu.roll(u, 96, 1)
    return jnp.where(lax.rem(lane, 64) < 32, up, down)


def project_kernel(h_ref, w_ref, cos_ref, sin_ref, out_ref):
    u = plain_dot(h_ref[...], w_ref[...])
    for j in range(u.shape[1] // 128):
        piece = u[:, j * 128 : (j + 1) * 128]
        turned = piece * cos_ref[0] + swap_halves(piece) * sin_ref[0]
        out_ref[:, j * 128 : (j + 1) * 128] = turned.astype(jnp.bfloat16)


def project(normed, weight, cos_tables, sin_tables, width):
    tokens, depth = normed.shape
    steps = weight.shape[1] // width
    return pl.pallas_call(
        project_kernel,
        grid=(steps,),
        in_specs=[
            pl.BlockSpec((tokens, depth), lambda j: (0, 0)),
            pl.BlockSpec((depth, width), lambda j: (0, j)),
            pl.BlockSpec((1, tokens, 128), lambda j: (j // (steps - 1), 0, 0)),
            pl.BlockSpec((1, tokens, 128), lambda j: (j // (steps - 1), 0, 0)),
        ],
        out_specs=pl.BlockSpec((tokens, width), lambda j: (0, j)),
        out_shape=jax.ShapeDtypeStruct((tokens, steps * width), jnp.bfloat16),
        compiler_params=pltpu.CompilerParams(vmem_limit_bytes=48 * 2**20),
        cost_estimate=pl.CostEstimate(
            flops=2 * tokens * depth * weight.shape[1],
            bytes_accessed=2 * depth * weight.shape[1],
            transcendentals=0,
        ),
    )(normed, weight, cos_tables, sin_tables)


def lane_masks(rows):
    lane = lax.broadcasted_iota(jnp.int32, (rows, 128), 1)
    low_side = (lane < 64).astype(jnp.float32)
    return low_side.astype(jnp.bfloat16), (1.0 - low_side).astype(jnp.bfloat16)


def swapped(kv):
    return pltpu.roll(kv.astype(jnp.float32), 64, 1).astype(jnp.bfloat16)


def attend_kernel(group, q_ref, kv_ref, bias_ref, o_ref, log_ref):
    kv = kv_ref[0]
    sides = (kv, swapped(kv))
    rows = q_ref.shape[0]
    masks = lane_masks(rows)
    lane = lax.broadcasted_iota(jnp.int32, (rows, 128), 1)
    logs = jnp.zeros((rows, 128), jnp.float32)
    bias = bias_ref[0]
    for pair in range(group // 2):
        cols = slice(pair * 128, pair * 128 + 128)
        q = q_ref[:, cols]
        found = []
        for half in range(2):
            scores = dot_t(q * masks[half], sides[half]) + bias
            top = jnp.max(scores, -1, keepdims=True)
            powers = jnp.exp(scores - top)
            total = jnp.sum(powers, -1, keepdims=True)
            probs = (powers * (1.0 / total)).astype(jnp.bfloat16)
            found.append(plain_dot(probs, sides[1 - half]))
            logs = jnp.where(lane == pair * 2 + half, top + jnp.log(total), logs)
        o_ref[:, cols] = jnp.where(lane < 64, found[0], found[1]).astype(jnp.bfloat16)
    log_ref[...] = logs


def attend(projected, both_all, bias, kv_heads, group):
    batches, length, _ = both_all.shape
    rows = projected.shape[0] // batches
    wide = group * HD
    return pl.pallas_call(
        functools.partial(attend_kernel, group),
        grid=(batches, kv_heads),
        in_specs=[
            pl.BlockSpec((rows, wide), lambda b, h: (b, h)),
            pl.BlockSpec((1, length, 128), lambda b, h: (b, 0, h)),
            pl.BlockSpec((1, rows, length), lambda b, h: (b, 0, 0)),
        ],
        out_specs=[
            pl.BlockSpec((rows, wide), lambda b, h: (b, h)),
            pl.BlockSpec((rows, 128), lambda b, h: (b, h)),
        ],
        out_shape=[
            jax.ShapeDtypeStruct((batches * rows, kv_heads * wide), jnp.bfloat16),
            jax.ShapeDtypeStruct((batches * rows, kv_heads * 128), jnp.float32),
        ],
        compiler_params=pltpu.CompilerParams(vmem_limit_bytes=48 * 2**20),
    )(projected, both_all, bias)


def attend_back_kernel(
    group, q_ref, do_ref, kv_ref, bias_ref, log_ref, cos_ref, sin_ref, dq_ref, dkv_ref
):
    kv = kv_ref[0]
    sides = (kv, swapped(kv))
    rows = q_ref.shape[0]
    length = kv.shape[0]
    masks = lane_masks(rows)
    lane = lax.broadcasted_iota(jnp.int32, (rows, 128), 1)
    bias = bias_ref[0]
    key_sum = jnp.zeros((128, length), jnp.float32)
    value_sum = jnp.zeros((128, length), jnp.float32)
    for pair in range(group // 2):
        cols = slice(pair * 128, pair * 128 + 128)
        q = q_ref[:, cols]
        do = do_ref[:, cols]
        found = []
        for half in range(2):
            q_half = q * masks[half]
            do_half = do * masks[half]
            at = pair * 2 + half
            log_total = log_ref[:, at : at + 1]
            probs = jnp.exp(dot_t(q_half, sides[half]) + bias - log_total)
            grad_probs = dot_t(do_half, sides[1 - half])
            row_dot = jnp.sum(probs * grad_probs, -1, keepdims=True)
            grad_scores = (probs * (grad_probs - row_dot)).astype(jnp.bfloat16)
            found.append(plain_dot(grad_scores, sides[half]))
            key_sum = key_sum + left_dot(q_half, grad_scores)
            value_sum = value_sum + left_dot(do_half, probs.astype(jnp.bfloat16))
        dq = jnp.where(lane < 64, found[0], found[1])
        dq = dq * cos_ref[0] - swap_halves(dq) * sin_ref[0]
        dq_ref[:, cols] = dq.astype(jnp.bfloat16)
    both = jnp.concatenate(
        [key_sum[:64] + key_sum[64:], value_sum[:64] + value_sum[64:]], 0
    )
    dkv_ref[0] = both.T.astype(jnp.bfloat16)


def attend_back(projected, grad_attended, both_all, bias, logs, cos_tables, sin_tables, group):
    batches, length, _ = both_all.shape
    rows = projected.shape[0] // batches
    wide = group * HD
    kv_heads = both_all.shape[2] // 128
    return pl.pallas_call(
        functools.partial(attend_back_kernel, group),
        grid=(batches, kv_heads),
        in_specs=[
            pl.BlockSpec((rows, wide), lambda b, h: (b, h)),
            pl.BlockSpec((rows, wide), lambda b, h: (b, h)),
            pl.BlockSpec((1, length, 128), lambda b, h: (b, 0, h)),
            pl.BlockSpec((1, rows, length), lambda b, h: (b, 0, 0)),
            pl.BlockSpec((rows, 128), lambda b, h: (b, h)),
            pl.BlockSpec((1, rows, 128), lambda b, h: (0, b, 0)),
            pl.BlockSpec((1, rows, 128), lambda b, h: (0, b, 0)),
        ],
        out_specs=[
            pl.BlockSpec((rows, wide), lambda b, h: (b, h)),
            pl.BlockSpec((1, length, 128), lambda b, h: (b, 0, h)),
        ],
        out_shape=[
            jax.ShapeDtypeStruct((batches * rows, kv_heads * wide), jnp.bfloat16),
            jax.ShapeDtypeStruct((batches, length, kv_heads * 128), jnp.bfloat16),
        ],
        compiler_params=pltpu.CompilerParams(vmem_limit_bytes=48 * 2**20),
    )(projected, grad_attended, both_all, bias, logs, cos_tables, sin_tables)


class Scattering:
    def __init__(self, me, chunks, send, recv, free):
        self.me, self.chunks = me, chunks
        self.send, self.recv, self.free = send, recv, free
        self.copies = {}
        self.friends = [me.device(s=s) for s in range(1, me.Z)]
        self.friends += [me.device(dy=1), me.device(dx=1), me.device(dc=1)]

    def ship(self, k, name, index, src, dst, target):
        copy = pltpu.make_async_remote_copy(
            src_ref=src,
            dst_ref=dst,
            send_sem=self.send.at[k, index],
            recv_sem=self.recv.at[k, index],
            device_id=target,
            device_id_type=MESH,
        )
        copy.start()
        self.copies[(k, name)] = copy

    def add(self, dst, src, wide, base):
        depth = dst.shape[0]
        t = tile_of(wide)
        count = wide // t

        def body(i, carry):
            at = i // count
            cols = pl.ds(pl.multiple_of(base + lax.rem(i, count) * t, 128), t)
            dst[at, :, cols] = dst[at, :, cols] + src[at, :, cols]
            return carry

        lax.fori_loop(0, depth * count, body, 0)

    def buffers(self, k):
        own, one, two, last, wide = self.chunks[k][:5]
        cols = pl.ds(self.chunks[k][9], wide)
        return own, one, two, last, wide, cols

    def begin(self, k):
        own, one, two, last, wide, cols = self.buffers(k)
        order = self.chunks[k][5]
        for b in (1, 0):
            self.ship(
                k,
                ("1", b),
                b,
                own.at[1, b, :, :, cols],
                one.at[b, :, :, cols],
                self.me.device(**{"d" + order[0]: 1}),
            )

    def first(self, k):
        own, one, two, last, wide, cols = self.buffers(k)
        order = self.chunks[k][5]
        for b in (1, 0):
            self.copies[(k, ("1", b))].wait_recv()
            self.add(own.at[0, b], one.at[b], wide, self.chunks[k][9])
            if b == 1:
                self.ship(
                    k,
                    "2",
                    2,
                    own.at[0, 1, :, :, cols],
                    two.at[:, :, cols],
                    self.me.device(**{"d" + order[1]: 1}),
                )

    def second(self, k):
        own, one, two, last, wide, cols = self.buffers(k)
        me = self.me
        self.copies[(k, "2")].wait_recv()
        self.add(own.at[0, 0], two, wide, self.chunks[k][9])
        for s in range(1, me.Z):
            self.ship(
                k,
                ("z", s),
                2 + s,
                own.at[0, 0, lax.rem(me.z + s, me.Z), :, cols],
                last.at[s - 1, :, cols],
                me.device(s=s),
            )

    def third(self, k):
        own, one, two, last, wide, cols = self.buffers(k)
        me = self.me
        _, out, base, group, off = self.chunks[k][5:]
        for s in range(1, me.Z):
            self.copies[(k, ("z", s))].wait_recv()
        t = tile_of(wide)

        def body(j, carry):
            here = pl.ds(pl.multiple_of(off + j * t, 128), t)
            there = pl.ds(pl.multiple_of(base + j * t, 128), t)
            total = own[0, 0, me.z, :, here].astype(jnp.float32)
            for s in range(1, me.Z):
                total = total + last[s - 1, :, here].astype(jnp.float32)
            out[:, there] = total
            return carry

        lax.fori_loop(0, wide // t, body, 0)
        for (at, _), copy in self.copies.items():
            if at == k:
                copy.wait_send()
        if group is not None:
            for friend in self.friends:
                pl.semaphore_signal(
                    self.free.at[group], inc=1, device_id=friend, device_id_type=MESH
                )

    def reuse(self, group):
        pl.semaphore_wait(self.free.at[group], len(self.friends))


def backward_kernel(sizes, *refs):
    batches, rows, kv_heads, group, used = sizes
    (dy_ref, first_w, out_w, gate_w, up_w, down_w) = refs[:6]
    (q_in, kv_in, log_in, mixed_in, hidden_in, slope_in, silu_in, bias_in, cos_in, sin_in) = refs[6:16]
    (hid_t, h2_t, att_t, nor_t, x_in) = refs[16:21]
    outs = refs[21:36]
    (result_out, grad_out, g_first, g_out, g_gate, g_up, g_down) = outs[:7]
    (hid_s, h2_s, att_s, nor_s, dy_p, gate_p, up_p, dm_p) = outs[7:]
    pre_p, dy1_h = refs[36:38]
    sc = list(refs[38:])
    take = lambda n: [sc.pop(0) for _ in range(n)]
    sets = [take(4) for _ in range(3)]
    down_sets = [take(4) for _ in range(2)]
    gain_set = take(4)
    (lhs_d, lhs, lraw, rhs, acc, part, cot, low_t, queries, grads, pre) = take(11)
    (kv_all, dkv, bias, logs, cos_t, sin_t, dkv_r, dkv_x) = take(8)
    (raw_a, w_a, wd, fac_a, fac_b, dgt, dut, gains, gsum, gcol) = take(10)
    (send, recv, free, x_send, x_recv, t_send, t_recv, load_sem, lhs_sem, store_sem, own_sem, part_sem) = take(12)
    me = Place()
    greet(me)
    tokens, width = cot.shape
    length = kv_all.shape[1]
    features = hidden_in.shape[1]
    wide = dgt.shape[1]
    tiles = features // wide
    scale = HD**-0.5
    sibling = me.device(dc=1)
    f32, bf = jnp.float32, jnp.bfloat16
    r = lhs.shape[0] // (4 * me.Z)
    rd = lhs_d.shape[1] // me.Z
    big = sets[0][0].shape[-1]
    half = features // 2
    key_wide = kv_heads * 128
    query_wide = pre.shape[1] - key_wide
    d_wide = down_sets[0][0].shape[-1]
    d_rest = width - 2 * d_wide
    chunks = (
        (*down_sets[0], d_wide, "xy", g_down, 0, 4, 0),
        (*down_sets[1], d_wide, "yx", g_down, d_wide, None, 0),
        (*sets[0], half, "xy", g_gate, 0, 0, 0),
        (*sets[1], half, "yx", g_up, 0, 1, 0),
        (*sets[2], half, "xy", g_gate, half, 2, 0),
        (*sets[0], half, "yx", g_up, half, None, 0),
        (*sets[1], width, "xy", g_out, 0, None, 0),
        (*sets[2], query_wide, "yx", g_first, 0, None, 0),
        (*sets[2], key_wide - 128, "yx", g_first, query_wide, None, query_wide),
        (*gain_set, 256, "yx", g_first, query_wide + key_wide - 128, None, 0),
        (*down_sets[0], d_rest, "yx", g_down, 2 * d_wide, None, 0),
    )
    D0, D1, G0, U0, G1, U1, O, Q, KV, GAIN, D2 = range(11)
    comm = Scattering(me, chunks, send, recv, free)

    def over_rows(body, step=64):
        def one(i, carry):
            body(pl.ds(pl.multiple_of(i * step, step), step))
            return carry

        lax.fori_loop(0, tokens // step, one, 0)

    passes = []

    def hand(i, src, dst):
        copy = pltpu.make_async_remote_copy(
            src_ref=src,
            dst_ref=dst,
            send_sem=x_send.at[i],
            recv_sem=x_recv.at[i],
            device_id=sibling,
            device_id_type=MESH,
        )
        copy.start()
        passes.append(copy)
        return copy

    other = lax.rem(me.c + 1, 2)
    got_hid = hand(0, hid_t.at[:, :, :, other], hid_s)
    got_dy = hand(1, dy_ref, dy_p.at[1])
    got_h2 = hand(2, h2_t.at[:, :, :, other], h2_s)
    got_att = hand(3, att_t.at[:, :, :, other], att_s)
    got_nor = hand(4, nor_t.at[:, :, :, other], nor_s)

    def fetch(i, src, dst):
        copy = pltpu.make_async_copy(src, dst, load_sem.at[i])
        copy.start()
        return copy

    stores = []

    def store(i, src, dst):
        copy = pltpu.make_async_copy(src, dst, store_sem.at[i])
        copy.start()
        stores.append(copy)
        return copy

    need_cot = fetch(0, dy_ref, cot)
    own_dy = store(0, dy_ref, dy_p.at[0])
    def block(ref, a, b, order, c=None):
        rel = {order[0]: a, order[1]: b}
        y = lax.rem(me.y + rel["y"], 2)
        x = lax.rem(me.x + rel["x"], 2)
        return ref.at[:, y, x] if c is None else ref.at[:, y, x, c]

    def left_rows(own_t, sib_t):
        for side, ref in ((0, own_t), (1, sib_t)):
            loads = []
            for i in range(4):
                src = block(ref, i // 2, i % 2, "xy", me.c if side == 0 else None)
                copy = pltpu.make_async_copy(src, lraw.at[i], lhs_sem.at[i])
                copy.start()
                loads.append(copy)
            for copy in loads:
                copy.wait()

            def one(i, carry, side=side):
                for j in range(me.Z // 2):
                    piece = lraw[i, 2 * j : 2 * j + 2].astype(f32).reshape(2 * r, tokens)
                    at = pl.multiple_of((i * me.Z + 2 * j) * r, 16)
                    lhs[pl.ds(at, 2 * r), side * tokens : (side + 1) * tokens] = piece.astype(bf)
                return carry

            lax.fori_loop(0, 4, one, 0)

    def down_rows(k, i, slot):
        copies = []
        for side, ref in ((0, hid_t), (1, hid_s)):
            src = block(ref, i // 2, i % 2, chunks[k][5], me.c if side == 0 else None)
            for z in range(me.Z):
                copies.append(
                    pltpu.make_async_copy(
                        src.at[z],
                        lhs_d.at[slot, pl.ds(z * rd, rd), pl.ds(side * tokens, tokens)],
                        lhs_sem.at[(slot * 2 + side) * me.Z + z],
                    )
                )
        return copies

    def product_down(k, base, right=None):
        own, wide_k = chunks[k][0], chunks[k][4]
        for copy in down_rows(k, 3, 0):
            copy.start()
        for n, i in enumerate((3, 2, 1, 0)):
            slot = n % 2
            if i > 0:
                for copy in down_rows(k, i - 1, 1 - slot):
                    copy.start()
            for copy in down_rows(k, i, slot):
                copy.wait()
            left = lhs_d.at[slot]
            if right is None:
                product(k, dy_p, base, left, rd, (i,))
            else:

                def body(j, carry, i=i, left=left):
                    cols = pl.ds(pl.multiple_of(base + j * 256, 256), 256)
                    here = pl.ds(pl.multiple_of(j * 256, 256), 256)
                    total = plain_dot(left[:, :tokens], right[0][:, cols]) + plain_dot(
                        left[:, tokens:], right[1][:, cols]
                    )
                    own[i // 2, i % 2, :, :, here] = total.reshape(me.Z, rd, 256).astype(bf)
                    return carry

                lax.fori_loop(0, wide_k // 256, body, 0)
        comm.begin(k)

    def product(k, pair, base, left, depth, blocks=(0, 1, 2, 3), size=None):
        own, wide_k = chunks[k][0], size or chunks[k][4]
        t = rhs.shape[3] if wide_k % rhs.shape[3] == 0 else 128
        count = wide_k // t
        span = len(blocks)

        def tile(j, slot):
            cols = pl.ds(pl.multiple_of(base + j * t, 128), t)
            return [
                pltpu.make_async_copy(
                    pair.at[side, :, cols],
                    rhs.at[slot, side, :, pl.ds(0, t)],
                    own_sem.at[slot, side],
                )
                for side in range(2)
            ]

        depth_of = rhs.shape[0]
        for j in range(min(depth_of - 1, count)):
            for copy in tile(j, j):
                copy.start()

        def body(j, carry):
            slot = lax.rem(j, depth_of)
            ahead = j + depth_of - 1

            @pl.when(ahead < count)
            def _():
                for copy in tile(ahead, lax.rem(ahead, depth_of)):
                    copy.start()

            for copy in tile(j, slot):
                copy.wait()
            cols = pl.ds(pl.multiple_of(chunks[k][9] + j * t, 128), t)
            total = plain_dot(left[:, :tokens], rhs[slot, 0, :, :t]) + plain_dot(
                left[:, tokens:], rhs[slot, 1, :, :t]
            )
            total = total.reshape(span, me.Z, depth, t).astype(bf)
            for q, at in enumerate(blocks):
                if chunks[k][5] == "xy" or span == 1:
                    own[at // 2, at % 2, :, :, cols] = total[q]
                else:
                    own[at % 2, at // 2, :, :, cols] = total[q]
            return carry

        lax.fori_loop(0, count, body, 0)

    def load3(i, full, raw, col, size):
        return pltpu.make_async_copy(
            full.at[:, :, pl.ds(col, size)], raw.at[:, :, pl.ds(0, size)], load_sem.at[i]
        )

    def assemble(raw, flat, size):
        n, depth, _ = raw.shape
        pair = 2 * depth

        def one(i, carry):
            piece = raw[pl.ds(2 * i, 2), :, pl.ds(0, size)].astype(f32)
            flat[pl.ds(pl.multiple_of(pair * i, 16), pair), pl.ds(0, size)] = piece.reshape(
                pair, size
            ).astype(bf)
            return carry

        lax.fori_loop(0, n // 2, one, 0)

    def tile_loads(j):
        at = pl.ds(j * wide, wide)
        return [
            pltpu.make_async_copy(down_w.at[at, :], wd.at[j % 2], load_sem.at[2]),
            pltpu.make_async_copy(slope_in.at[:, at], fac_a.at[j % 2], load_sem.at[3]),
            pltpu.make_async_copy(silu_in.at[:, at], fac_b.at[j % 2], load_sem.at[4]),
        ]

    gate_tile = lambda j: load3(5, gate_w, raw_a, j * wide, wide)
    up_tile = lambda j: load3(6, up_w, raw_a, j * wide, wide)
    head_pack = load3(7, first_w, raw_a, used, 128)
    head_pack.start()
    head_pack.wait()
    assemble(raw_a, w_a, 128)
    gains[...] = w_a[:, :128].astype(f32).T[:8]
    for copy in tile_loads(0) + [gate_tile(0)]:
        copy.start()
    need_cot.wait()
    own_dy.wait()
    tile_sends = [None] * tiles

    def arrive(low, high):
        for j in range(low, high):
            for copy in tile_sends[j]:
                copy.settle()

    for j in range(tiles):
        slot = j % 2
        for copy in tile_loads(j):
            copy.wait()
        if j + 1 < tiles:
            for copy in tile_loads(j + 1):
                copy.start()
        gate_tile(j).wait()
        assemble(raw_a, w_a, wide)
        up_tile(j).start()
        if j >= 1:
            for copy in tile_sends[j - 1]:
                copy.wait()

        def units(at, slot=slot, j=j):
            grad_hidden = dot_t(cot[at, :], wd[slot])
            dg = (grad_hidden * fac_a[slot, at, :].astype(f32)).astype(bf)
            du = (grad_hidden * fac_b[slot, at, :].astype(f32)).astype(bf)
            dgt[at, :] = dg
            dut[at, :] = du
            piece = dot_t(dg, w_a[:, :wide])
            acc[at, :] = piece if j == 0 else acc[at, :] + piece

        over_rows(units, 256)
        cols = pl.ds(j * wide, wide)
        sends = []
        for i, (src, dst) in enumerate(((dgt, gate_p), (dut, up_p))):
            here = pltpu.make_async_copy(
                src, dst.at[0, :, cols], store_sem.at[1 + i]
            )
            there = pltpu.make_async_remote_copy(
                src_ref=src,
                dst_ref=dst.at[1, :, cols],
                send_sem=t_send.at[2 * j + i],
                recv_sem=t_recv.at[2 * j + i],
                device_id=sibling,
                device_id_type=MESH,
            )
            here.start()
            there.start()
            sends.append(_Both(here, there))
        tile_sends[j] = sends
        up_tile(j).wait()
        assemble(raw_a, w_a, wide)
        if j + 1 < tiles:
            gate_tile(j + 1).start()

        def units_up(at):
            acc[at, :] = acc[at, :] + dot_t(dut[at, :], w_a[:, :wide])

        over_rows(units_up, 256)
        if j == 0:
            got_dy.wait_recv()
            need_sib = fetch(1, dy_p.at[1], low_t)
            got_hid.wait_recv()
            need_sib.wait()
            product_down(D0, 0, (cot, low_t))
        if j == 1:
            product_down(D1, d_wide, (cot, low_t))
        if j == 3:
            got_h2.wait_recv()
            left_rows(h2_t, h2_s)
            arrive(0, 4)
            product(G0, gate_p, 0, lhs, r)
            comm.begin(G0)
            product(U0, up_p, 0, lhs, r)
            comm.begin(U0)
        if j == 4:
            comm.first(D0)
        if j == 5:
            comm.first(D1)
    arrive(4, tiles)
    product(G1, gate_p, half, lhs, r)
    comm.begin(G1)

    gsum[...] = jnp.zeros_like(gsum)

    def stream(src, body):
        def piece(i, slot):
            at = pl.ds(pl.multiple_of(i * 64, 64), 64)
            return pltpu.make_async_copy(src.at[at, :], part.at[slot], part_sem.at[slot])

        piece(0, 0).start()

        def one(i, carry):
            slot = lax.rem(i, 2)

            @pl.when(i + 1 < tokens // 64)
            def _():
                piece(i + 1, lax.rem(i + 1, 2)).start()

            piece(i, slot).wait()
            body(pl.ds(pl.multiple_of(i * 64, 64), 64), part[slot])
            return carry

        lax.fori_loop(0, tokens // 64, one, 0)

    def norm_two(at, y):
        inverse = lax.rsqrt(jnp.mean(y * y, -1, keepdims=True) + EPSILON)
        grad = acc[at, :]
        gsum[1:2, :] += jnp.sum(grad * (y * inverse), 0, keepdims=True)
        e = grad * gains[1:2, :]
        dy1 = cot[at, :].astype(f32) + inverse * (
            e - y * (inverse * inverse) * jnp.mean(e * y, -1, keepdims=True)
        )
        acc[at, :] = dy1
        low_t[at, :] = dy1.astype(bf)

    stream(mixed_in, norm_two)
    keep_dy1 = pltpu.make_async_copy(acc, dy1_h, part_sem.at[2])
    keep_dy1.start()
    own_low = store(5, low_t, dm_p.at[0])
    got_low = hand(5, low_t, dm_p.at[1])

    need_q = fetch(0, q_in, queries)
    need_kv = fetch(1, kv_in, kv_all)
    need = [
        fetch(8, bias_in, bias),
        fetch(9, log_in, logs),
        fetch(10, cos_in, cos_t),
        fetch(11, sin_in, sin_t),
    ]
    tile_w = raw_a.shape[2]
    steps = width // tile_w
    load3(5, out_w, raw_a, 0, tile_w).start()
    keep_dy1.wait()
    for j in range(steps):
        load3(5, out_w, raw_a, j * tile_w, tile_w).wait()
        assemble(raw_a, w_a, tile_w)
        if j + 1 < steps:
            load3(5, out_w, raw_a, (j + 1) * tile_w, tile_w).start()

        def back_out(at, j=j):
            piece = dot_t(low_t[at, j * tile_w : (j + 1) * tile_w], w_a[...])
            if j > 0:
                piece = acc[at, :] + piece
            if j + 1 < steps:
                acc[at, :] = piece
            else:
                grads[at, :] = piece.astype(bf)

        over_rows(back_out, 256)
    comm.second(D0)
    comm.first(G0)
    comm.second(D1)

    need_q.wait()
    need_kv.wait()
    for copy in need:
        copy.wait()
    def portion(dx, c):
        row = (lax.rem(me.x + dx, 2) * 2 + c) * rows
        return pl.ds(pl.multiple_of(row, 256), rows)

    def to_sibling(b):
        return [
            hand(6 + 2 * b + dx, dkv.at[b, portion(dx, other), :], dkv_r.at[dx, b])
            for dx in (1, 0)
        ]

    def gather_portion(b, dx):
        place = portion(dx, me.c)

        def body(j, carry):
            at = pl.ds(pl.multiple_of(j * 64, 64), 64)
            there = pl.ds(pl.multiple_of(place.start + j * 64, 64), 64)
            total = dkv_r[dx, b, at, :].astype(f32) + dkv[b, there, :].astype(f32)
            dkv_r[dx, b, at, :] = total.astype(bf)
            return carry

        lax.fori_loop(0, rows // 64, body, 0)

    def to_neighbour(b, handed):
        handed[0].wait_recv()
        gather_portion(b, 1)
        copy = pltpu.make_async_remote_copy(
            src_ref=dkv_r.at[1, b],
            dst_ref=dkv_x.at[b],
            send_sem=x_send.at[10 + b],
            recv_sem=x_recv.at[10 + b],
            device_id=me.device(dx=1),
            device_id_type=MESH,
        )
        copy.start()
        passes.append(copy)
        handed[1].wait_recv()
        gather_portion(b, 0)
        return copy

    def merge_portion(b, copy):
        copy.wait_recv()

        def merge(j, carry):
            at = pl.ds(pl.multiple_of(j * 64, 64), 64)
            token = pl.ds(pl.multiple_of(b * rows + j * 64, 64), 64)
            for h in range(kv_heads):
                cols = slice(h * 128, (h + 1) * 128)
                total = dkv_r[0, b, at, cols].astype(f32) + dkv_x[b, at, cols].astype(f32)
                total = total * cos_t[1, token, :] - swap_halves(total) * sin_t[1, token, :]
                pre[token, query_wide + h * 128 : query_wide + (h + 1) * 128] = total.astype(bf)
            return carry

        lax.fori_loop(0, rows // 64, merge, 0)

    to_x = [None] * batches
    lanes = lax.broadcasted_iota(jnp.int32, (rows, 128), 1)
    sides_mask = lane_masks(rows)

    def head(i, carry):
        b = i // kv_heads
        h = lax.rem(i, kv_heads)
        at = pl.ds(pl.multiple_of(b * rows, 256), rows)
        here = pl.ds(pl.multiple_of(h * 128, 128), 128)
        kv = kv_all[b, :, here]
        sides = (kv, swapped(kv))
        shift = bias[at, :].astype(f32)
        key_sum = jnp.zeros((128, length), f32)
        value_sum = jnp.zeros((128, length), f32)
        log_piece = logs[at, :]
        for pair in range(group // 2):
            cols = pl.ds(pl.multiple_of(h * group * HD + pair * 128, 128), 128)
            q = queries[at, cols]
            do = grads[at, cols]
            found = []
            for side in range(2):
                q_half = q * sides_mask[side]
                do_half = do * sides_mask[side]
                head_at = pair * 2 + side
                log_total = jnp.sum(
                    jnp.where(lanes == h * group + head_at, log_piece, 0.0), -1, keepdims=True
                )
                probs = jnp.exp(dot_t(q_half, sides[side]) + shift - log_total)
                grad_probs = dot_t(do_half, sides[1 - side])
                row_dot = jnp.sum(probs * grad_probs, -1, keepdims=True)
                grad_scores = (probs * (grad_probs - row_dot)).astype(bf)
                found.append(plain_dot(grad_scores, sides[side]))
                key_sum = key_sum + left_dot(q_half, grad_scores)
                value_sum = value_sum + left_dot(do_half, probs.astype(bf))
            dq = jnp.where(lanes < HD, found[0], found[1])
            dq = dq * cos_t[0, at, :] - swap_halves(dq) * sin_t[0, at, :]
            pre[at, cols] = dq.astype(bf)
        both = jnp.concatenate(
            [key_sum[:HD] + key_sum[HD:], value_sum[:HD] + value_sum[HD:]], 0
        )
        dkv[b, :, here] = both.T.astype(bf)
        return carry

    count = batches * kv_heads
    lax.fori_loop(0, 2, head, 0)
    comm.first(U0)
    comm.third(D0)
    own_low.wait()
    got_low.wait_recv()
    lax.fori_loop(2, 5, head, 0)
    comm.third(D1)
    comm.second(G0)
    handed = to_sibling(0)
    comm.first(G1)
    lax.fori_loop(5, 8, head, 0)
    comm.second(U0)
    comm.third(G0)
    comm.reuse(0)
    product(U1, up_p, half, lhs, r)
    comm.begin(U1)
    to_x[0] = to_neighbour(0, handed)
    lax.fori_loop(8, count, head, 0)
    comm.third(U0)
    comm.second(G1)
    merge_portion(0, to_x[0])
    comm.reuse(1)
    got_att.wait_recv()
    left_rows(att_t, att_s)
    product(O, dm_p, 0, lhs, r)
    comm.begin(O)
    handed = to_sibling(1)
    own_q = store(6, pre.at[:, pl.ds(0, query_wide)], pre_p.at[0, :, pl.ds(0, query_wide)])
    got_q = hand(12, pre.at[:, pl.ds(0, query_wide)], pre_p.at[1, :, pl.ds(0, query_wide)])
    to_x[1] = to_neighbour(1, handed)
    comm.third(G1)
    comm.reuse(2)
    got_nor.wait_recv()
    left_rows(nor_t, nor_s)
    own_q.wait()
    got_q.wait_recv()
    product(Q, pre_p, 0, lhs, r)
    comm.begin(Q)
    comm.reuse(4)
    product_down(D2, 2 * d_wide)
    comm.first(U1)
    merge_portion(1, to_x[1])
    rest = pl.ds(query_wide, kv_heads * 128)
    own_kv = store(7, pre.at[:, rest], pre_p.at[0, :, rest])
    got_kv = hand(13, pre.at[:, rest], pre_p.at[1, :, rest])

    need_x = fetch(0, x_in, cot)
    steps = pre.shape[1] // tile_w
    load3(5, first_w, raw_a, 0, tile_w).start()
    for j in range(steps):
        load3(5, first_w, raw_a, j * tile_w, tile_w).wait()
        assemble(raw_a, w_a, tile_w)
        if j + 1 < steps:
            load3(5, first_w, raw_a, (j + 1) * tile_w, tile_w).start()

        def back_in(at, j=j):
            piece = dot_t(pre[at, j * tile_w : (j + 1) * tile_w], w_a[...])
            acc[at, :] = piece if j == 0 else acc[at, :] + piece

        over_rows(back_in, 256)
    comm.first(O)
    own_kv.wait()
    got_kv.wait_recv()
    product(KV, pre_p, query_wide, lhs, r)
    comm.begin(KV)
    product(GAIN, pre_p, query_wide + key_wide - 128, lhs, r, size=128)
    comm.second(U1)
    need_x.wait()

    def norm_one(at, dy1):
        x = cot[at, :].astype(f32)
        inverse = lax.rsqrt(jnp.mean(x * x, -1, keepdims=True) + EPSILON)
        grad = acc[at, :]
        gsum[0:1, :] += jnp.sum(grad * (x * inverse), 0, keepdims=True)
        e = grad * gains[0:1, :]
        total = dy1 + inverse * (
            e - x * (inverse * inverse) * jnp.mean(e * x, -1, keepdims=True)
        )
        queries[at, :] = total.astype(bf)

    stream(dy1_h, norm_one)
    store(8, queries, grad_out)
    comm.first(D2)
    comm.first(Q)

    gsib = gain_set[0]
    columns = jnp.concatenate([gsum[...], jnp.zeros((120, width), f32)], 0).T
    gcol[0] = columns.reshape(gcol.shape[1:]).astype(bf)
    got_gain = hand(14, gcol.at[0], gcol.at[1])
    comm.second(O)
    got_gain.wait_recv()
    for a in range(2):
        for b in range(2):
            y = lax.rem(me.y + b, 2)
            x = lax.rem(me.x + a, 2)
            if chunks[GAIN][5] == "yx":
                y, x = lax.rem(me.y + a, 2), lax.rem(me.x + b, 2)
            for z in range(me.Z):
                at = ((z * 2 + y) * 2 + x) * 2 + me.c
                gsib[a, b, z, :, 128:] = gcol[0, at] + gcol[1, at]
    comm.begin(GAIN)
    comm.first(KV)
    comm.second(D2)
    comm.second(Q)

    need_mixed = fetch(1, mixed_in, acc)
    need_mixed.wait()
    last_loads = lambda j: [
        pltpu.make_async_copy(
            down_w.at[pl.ds(j * wide, wide), :], wd.at[j % 2], load_sem.at[2]
        ),
        pltpu.make_async_copy(
            hidden_in.at[:, pl.ds(j * wide, wide)], fac_a.at[j % 2], load_sem.at[3]
        ),
    ]
    for copy in last_loads(0):
        copy.start()
    for j in range(tiles):
        for copy in last_loads(j):
            copy.wait()
        if j + 1 < tiles:
            for copy in last_loads(j + 1):
                copy.start()

        def add_down(at, j=j):
            acc[at, :] = acc[at, :] + plain_dot(fac_a[j % 2, at, :], wd[j % 2])

        over_rows(add_down, 256)
        if j == 0:
            comm.third(U1)
        if j == 1:
            comm.second(KV)
        if j == 2:
            comm.first(GAIN)
        if j == 3:
            comm.third(O)
            comm.third(D2)
        if j == 4:
            comm.third(Q)
        if j == 5:
            comm.second(GAIN)

    def round_result(at):
        low_t[at, :] = acc[at, :].astype(bf)

    got_low.wait_send()
    over_rows(round_result)
    store(9, low_t, result_out)
    comm.third(KV)
    comm.third(GAIN)
    for copy in passes:
        if copy is not got_low:
            copy.wait_send()
    for copy in stores:
        if not any(copy is p for p in (own_dy, own_low, own_q, own_kv)):
            copy.wait()


class _Both:
    def __init__(self, here, there):
        self.here, self.there, self.sent, self.settled = here, there, False, False

    def wait(self):
        if not self.sent:
            self.here.wait()
            self.there.wait_send()
        self.sent = True

    def settle(self):
        self.wait()
        if not self.settled:
            self.there.wait_recv()
        self.settled = True


def backward(saved, transposed, dy, x, kv_heads, group, batches):
    first_w, out_w, gate_w, up_w, down_w = saved[:5]
    queries, both_all, _, logs, mixed, _ = saved[5:11]
    hidden, slope, silu, bias, cos_tables, sin_tables = saved[11:]
    tokens, width = x.shape
    rows = tokens // batches
    Z = lax.axis_size("dp") // 2
    X = lax.axis_size("fsdp") // 2
    n, r, first_wide = first_w.shape
    rd = down_w.shape[1]
    key_wide = kv_heads * 128
    query_wide = kv_heads * group * HD
    used = query_wide + key_wide
    length = both_all.shape[1]
    features = hidden.shape[1]
    half = features // 2
    d_wide = width * 2 // 5 // 256 * 256
    wide, t = 512, 256
    bf, f32 = jnp.bfloat16, jnp.float32
    shape = jax.ShapeDtypeStruct
    vmem, dma = pltpu.VMEM, pltpu.SemaphoreType.DMA

    def four(depth, size):
        return [
            vmem((2, 2, Z, depth, size), bf),
            vmem((2, Z, depth, size), bf),
            vmem((Z, depth, size), bf),
            vmem((Z - 1, depth, size), bf),
        ]

    outs = [
        shape((tokens, width), bf),
        shape((tokens, width), bf),
        shape((r, first_wide), f32),
        shape((r, width), f32),
        shape((r, features), f32),
        shape((r, features), f32),
        shape((rd, width), f32),
        shape((Z, 2, X, rd, tokens), bf),
        shape((Z, 2, X, r, tokens), bf),
        shape((Z, 2, X, r, tokens), bf),
        shape((Z, 2, X, r, tokens), bf),
        shape((2, tokens, width), bf),
        shape((2, tokens, features), bf),
        shape((2, tokens, features), bf),
        shape((2, tokens, width), bf),
        shape((2, tokens, used), bf),
        shape((tokens, width), f32),
    ]
    any_space = pl.BlockSpec(memory_space=pl.ANY)
    in_vmem = pl.BlockSpec(memory_space=pltpu.VMEM)
    scratch = sum([four(r, half) for _ in range(3)], [])
    scratch += four(rd, d_wide) + four(rd, d_wide) + four(r, 256)
    scratch += [
        vmem((2, Z * rd, 2 * tokens), bf),
        vmem((4 * Z * r, 2 * tokens), bf),
        vmem((4, Z, r, tokens), bf),
        vmem((3, 2, tokens, t), bf),
        vmem((tokens, width), f32),
        vmem((2, 64, width), f32),
        vmem((tokens, width), bf),
        vmem((tokens, width), bf),
        vmem((tokens, query_wide), bf),
        vmem((tokens, query_wide), bf),
        vmem((tokens, used), bf),
        vmem((batches, length, key_wide), bf),
        vmem((batches, length, key_wide), bf),
        vmem((tokens, length), bias.dtype),
        vmem((tokens, 128), f32),
        vmem((2, tokens, 128), f32),
        vmem((2, tokens, 128), f32),
        vmem((2, batches, rows, key_wide), bf),
        vmem((batches, rows, key_wide), bf),
        vmem((n, r, key_wide), bf),
        vmem((width, key_wide), bf),
        vmem((2, wide, width), bf),
        vmem((2, tokens, wide), bf),
        vmem((2, tokens, wide), bf),
        vmem((tokens, wide), bf),
        vmem((tokens, wide), bf),
        vmem((8, width), f32),
        vmem((8, width), f32),
        vmem((2, n, r, 128), bf),
        dma((11, 2 + Z)),
        dma((11, 2 + Z)),
        pltpu.SemaphoreType.REGULAR((5,)),
        dma((15,)),
        dma((15,)),
        dma((2 * (features // wide),)),
        dma((2 * (features // wide),)),
        dma((12,)),
        dma((8 * Z,)),
        dma((10,)),
        dma((3, 2)),
        dma((3,)),
    ]
    return pl.pallas_call(
        functools.partial(backward_kernel, (batches, rows, kv_heads, group, used)),
        out_shape=outs,
        in_specs=[any_space] * 21,
        out_specs=[any_space] * 2 + [in_vmem] * 5 + [any_space] * 10,
        scratch_shapes=scratch,
        compiler_params=pltpu.CompilerParams(
            collective_id=2, has_side_effects=True, vmem_limit_bytes=63 * 2**20
        ),
    )(
        dy,
        first_w,
        out_w,
        gate_w,
        up_w,
        down_w.reshape(-1, width),
        queries,
        both_all,
        logs,
        mixed,
        hidden,
        slope,
        silu,
        bias,
        cos_tables,
        sin_tables,
        *transposed,
        x,
    )


def half_of(full):
    return full.astype(jnp.bfloat16)


def rotary_pairs(places, tokens, score_scale):
    cos_table, sin_table = rope_tables(places.reshape(tokens))
    ones, zeros = jnp.ones((tokens, HD), jnp.float32), jnp.zeros((tokens, HD), jnp.float32)
    cos_pair = jnp.concatenate([cos_table, cos_table], -1)
    sin_pair = jnp.concatenate([-sin_table, sin_table], -1)
    cos_tables = jnp.stack(
        [
            jnp.concatenate([cos_pair, cos_pair], -1) * score_scale,
            jnp.concatenate([cos_pair, ones], -1),
        ]
    )
    sin_tables = jnp.stack(
        [
            jnp.concatenate([sin_pair, sin_pair], -1) * score_scale,
            jnp.concatenate([sin_pair, zeros], -1),
        ]
    )
    return cos_tables, sin_tables


def forward_plain(shards, x, places, kv_heads, group, batches):
    tokens = x.shape[0]
    rows = tokens // batches
    length = rows * lax.axis_size("fsdp")
    query_features = kv_heads * group * HD
    used = query_features + kv_heads * 128
    fulls = gather(shards, ("yxc", "xyc", "yxc", "xyc", "yxc"), 1, 5)
    first_pack, out_full, gate_full, up_full, _ = (f.reshape(-1, f.shape[-1]) for f in fulls)
    gains = first_pack[:, used : used + 2].astype(jnp.float32).T
    query_index = lax.axis_index("fsdp") * rows + jnp.arange(rows, dtype=jnp.int32)
    key_index = jnp.arange(length, dtype=jnp.int32)
    x_float = x.astype(jnp.float32)
    cos_tables, sin_tables = rotary_pairs(places, tokens, HD**-0.5)
    doc_start = query_index[None, :] - places.reshape(batches, rows)
    allowed = (key_index[None, None, :] <= query_index[None, :, None]) & (
        key_index[None, None, :] >= doc_start[:, :, None]
    )
    bias = jnp.where(allowed, 0.0, NEGATIVE)
    attn_inverse = lax.rsqrt(jnp.mean(x_float * x_float, -1, keepdims=True) + EPSILON)
    normed = (x_float * attn_inverse * gains[0]).astype(jnp.bfloat16)
    projected = project(normed, first_pack[:, :used], cos_tables, sin_tables, kv_heads * 128)
    both_rows = projected[:, query_features:].reshape(batches, rows, -1)
    both_all = lax.all_gather(both_rows, "fsdp", axis=1, tiled=True)
    attended, logs = attend(projected, both_all, bias, kv_heads, group)
    mixed = x_float + plain_dot(attended, out_full)
    mlp_inverse = lax.rsqrt(jnp.mean(mixed * mixed, -1, keepdims=True) + EPSILON)
    normed_mlp = (mixed * mlp_inverse * gains[1]).astype(jnp.bfloat16)
    gate_pre = plain_dot(normed_mlp, gate_full)
    up_proj = plain_dot(normed_mlp, up_full)
    gate_sig = jax.nn.sigmoid(gate_pre)
    silu = gate_pre * gate_sig
    slope = up_proj * gate_sig * (1.0 + gate_pre * (1.0 - gate_sig))
    low = jnp.bfloat16
    return list(fulls) + [
        projected[:, :query_features],
        both_all,
        attended,
        logs,
        mixed,
        normed_mlp,
        (silu * up_proj).astype(low),
        slope.astype(low),
        silu.astype(low),
        bias.reshape(tokens, length),
        cos_tables,
        sin_tables,
    ]


def backward_plain(saved, cotangent, x_low, kv_heads, group, batches):
    tokens, width = x_low.shape
    rows = tokens // batches
    key_features = kv_heads * HD
    query_features = kv_heads * group * HD
    used = query_features + 2 * key_features
    x_float = x_low.astype(jnp.float32)
    first_pack, out_full, gate_full, up_full, down_full = (
        f.reshape(-1, f.shape[-1]) for f in saved[:5]
    )
    queries, both_all, attended, logs, mixed, normed_mlp = saved[5:11]
    hidden, slope, silu, bias, cos_tables, sin_tables = saved[11:]
    projection = first_pack[:, :used]
    gains = first_pack[:, used : used + 2].astype(jnp.float32).T
    attn_gain_f = gains[0]
    mlp_gain_f = gains[1]
    attn_inverse = lax.rsqrt(jnp.mean(x_float * x_float, -1, keepdims=True) + EPSILON)
    normed = (x_float * attn_inverse * attn_gain_f).astype(jnp.bfloat16)
    mlp_inverse = lax.rsqrt(jnp.mean(mixed * mixed, -1, keepdims=True) + EPSILON)
    output = (mixed + plain_dot(hidden, down_full)).astype(jnp.bfloat16)

    cot_low = cotangent
    cot_float = cot_low.astype(jnp.float32)
    grad_down = half_of(left_dot(hidden, cot_low))
    grad_hidden = right_dot(cot_low, down_full)
    grad_gate_pre = (grad_hidden * slope.astype(jnp.float32)).astype(jnp.bfloat16)
    grad_up_pre = (grad_hidden * silu.astype(jnp.float32)).astype(jnp.bfloat16)
    grad_gate = half_of(left_dot(normed_mlp, grad_gate_pre))
    grad_up = half_of(left_dot(normed_mlp, grad_up_pre))
    grad_normed_mlp = right_dot(grad_gate_pre, gate_full) + right_dot(grad_up_pre, up_full)
    grad_mlp_gain = jnp.sum(grad_normed_mlp * mixed * mlp_inverse, 0)
    grad_mixed = cot_float + norm_back(grad_normed_mlp * mlp_gain_f, mixed, mlp_inverse)
    grad_mixed_low = grad_mixed.astype(jnp.bfloat16)
    grad_out = half_of(left_dot(attended, grad_mixed_low))
    grad_attended = right_dot(grad_mixed_low, out_full).astype(jnp.bfloat16)
    grad_query_pre, portions = attend_back(
        queries,
        grad_attended,
        both_all,
        bias.reshape(batches, rows, -1),
        logs,
        cos_tables,
        sin_tables,
        group,
    )
    sums = lax.psum_scatter(portions, "fsdp", scatter_dimension=1, tiled=True)
    sums = sums.astype(jnp.float32).reshape(tokens, kv_heads, 128)
    turned = jnp.concatenate([sums[..., 32:64], sums[..., :32], sums[..., 64:]], -1)
    grad_pair_pre = (sums * cos_tables[1][:, None] - turned * sin_tables[1][:, None]).astype(
        jnp.bfloat16
    )
    grad_pre = jnp.concatenate(
        [grad_query_pre, grad_pair_pre.reshape(tokens, 2 * key_features)], -1
    )
    grad_projection = left_dot(normed, grad_pre)
    grad_normed = right_dot(grad_pre, projection)
    grad_attn_gain = jnp.sum(grad_normed * x_float * attn_inverse, 0)
    grad_input = grad_mixed + norm_back(grad_normed * attn_gain_f, x_float, attn_inverse)
    gain_columns = jnp.stack([grad_attn_gain, grad_mlp_gain], -1)
    gain_columns = jnp.pad(gain_columns, ((0, 0), (0, 126)))
    grad_first = half_of(jnp.concatenate([grad_projection, gain_columns], 1))
    grad_down, grad_gate, grad_up, grad_out, last = scatter(
        (grad_down, grad_gate, grad_up, grad_out, grad_first), ("xy", "yx", "xy", "yx", "xy"), 2
    )
    return (
        output,
        grad_input.astype(jnp.bfloat16),
        last,
        grad_out,
        grad_gate,
        grad_up,
        grad_down,
    )


def on_device(
    inputs,
    positions,
    cotangent,
    attn_gain,
    w_query,
    key_matrix,
    value_matrix,
    w_out,
    mlp_gain,
    w_gate,
    w_up,
    w_down,
):
    batches, _, rows, width = inputs.shape
    shard = w_query.shape[0]
    query_features = w_query.shape[1]
    key_features = key_matrix.shape[1]
    kv_heads = key_features // HD
    group = query_features // key_features
    tokens = batches * rows
    used = query_features + 2 * key_features

    extras = jnp.zeros((shard, 128), jnp.bfloat16)
    extras = extras.at[:, 0].set(attn_gain).at[:, 1].set(mlp_gain)
    pairs = jnp.concatenate(
        [key_matrix.reshape(shard, kv_heads, HD), value_matrix.reshape(shard, kv_heads, HD)], -1
    )
    first_shard = jnp.concatenate([w_query, pairs.reshape(shard, -1), extras], axis=1)
    shards = (first_shard, w_out, w_gate, w_up, w_down)
    x_low = inputs.reshape(tokens, width)
    cot_low = cotangent.reshape(tokens, width)
    fits = shard % 8 == 0 and lax.axis_size("fsdp") == 4 and rows % 256 == 0
    saved = (forward if fits else forward_plain)(
        shards, x_low, positions.reshape(tokens, 1), kv_heads, group, batches
    )
    if fits:
        by_place = (lax.axis_size("dp") // 2, 2, lax.axis_size("fsdp") // 2, 2, -1, tokens)
        transposed = [t.reshape(by_place) for t in saved[17:]]
        found = backward(saved[:17], transposed, cot_low, x_low, kv_heads, group, batches)
    else:
        found = backward_plain(saved, cot_low, x_low, kv_heads, group, batches)
    output, grad_input, last, grad_out, grad_gate, grad_up, grad_down = found[:7]
    last_pairs = last[:, query_features:used].reshape(shard, kv_heads, 2, HD)
    return (
        output.reshape(inputs.shape),
        grad_input.reshape(inputs.shape),
        last[:, used],
        last[:, :query_features],
        last_pairs[:, :, 0].reshape(shard, key_features),
        last_pairs[:, :, 1].reshape(shard, key_features),
        grad_out,
        last[:, used + 1],
        grad_gate,
        grad_up,
        grad_down,
    )


def solution(mesh):
    tokens = P(None, "dp", "fsdp", None)
    vector = P(BOTH)
    matrix = P(BOTH, None)
    weights = (vector, matrix, matrix, matrix, matrix, vector, matrix, matrix, matrix)
    return jax.shard_map(
        on_device,
        mesh=mesh,
        in_specs=(tokens, P(None, "dp", "fsdp"), tokens) + weights,
        out_specs=(tokens, tokens) + weights,
        check_vma=False,
    )
```

```python
import functools

import jax
import jax.numpy as jnp
from jax import lax
from jax.experimental import pallas as pl
from jax.experimental.pallas import tpu as pltpu
from jax.sharding import PartitionSpec as P

HD = 64
EPSILON = 1e-05
NEGATIVE = -1e30
ROPE_BASE = 10000.0
BOTH = ("dp", "fsdp")


def rope_tables(places):
    half = HD // 2
    freqs = ROPE_BASE ** (-jnp.arange(half).astype(jnp.float32) / half)
    angles = places.astype(jnp.float32)[:, None] * freqs[None, :]
    return (jnp.cos(angles), jnp.sin(angles))


def plain_dot(left, right):
    return jnp.dot(left, right, preferred_element_type=jnp.float32)


def left_dot(left, right):
    return lax.dot_general(
        left, right, (((0,), (0,)), ((), ())), preferred_element_type=jnp.float32
    )


def right_dot(left, right):
    return lax.dot_general(
        left, right, (((1,), (1,)), ((), ())), preferred_element_type=jnp.float32
    )


def norm_back(grad_normed, inputs_float, inverse):
    return inverse * (
        grad_normed
        - inputs_float * inverse * inverse * jnp.mean(grad_normed * inputs_float, -1, keepdims=True)
    )


class Place:
    def __init__(self):
        self.Z=lax.axis_size("dp")//2; self.X=lax.axis_size("fsdp")//2
        dp=lax.axis_index("dp"); fs=lax.axis_index("fsdp")
        self.z=dp//2; self.y=dp%2; self.x=fs//2; self.c=fs%2
    def device(self,s=0,dy=0,dx=0,dc=0):
        return (lax.rem(self.z+s,self.Z)*2+lax.rem(self.y+dy,2), lax.rem(self.x+dx,self.X)*2+lax.rem(self.c+dc,2))
    def slot(self,s,dy,dx,dc):
        return ((lax.rem(self.z+self.Z-s,self.Z)*2+lax.rem(self.y+dy,2))*self.X+lax.rem(self.x+dx,self.X))*2+lax.rem(self.c+dc,2)

MESH = pl.DeviceIdType.MESH

def greet(me):
    barrier=pltpu.get_barrier_semaphore()
    friends=[me.device(s=s) for s in range(1,me.Z)]+[me.device(dy=1),me.device(dx=1),me.device(dc=1)]
    for f in friends:
        pl.semaphore_signal(barrier,inc=1,device_id=f,device_id_type=MESH)
    pl.semaphore_wait(barrier,len(friends))

def gather_kernel(Z, orders, ahead, *refs):
    K=len(orders)
    shards=refs[:K]; outs=refs[K:2*K]; local,send,recv=refs[2*K:]
    me=Place()
    greet(me)
    dims={"y":1,"x":2,"c":3}
    def sem(rel):
        return ((rel[0]*2+rel[1])*2+rel[2])*2+rel[3]
    started=[]
    def start(k,rel,to):
        if isinstance(to,int):
            target=me.device(s=to); landed=(to,0,0,0)
        else:
            landed=list(rel); landed[dims[to]]=1; landed=tuple(landed)
            target=me.device(**{"d"+to:1})
        slot=me.slot(*rel)
        src=shards[k] if rel==(0,0,0,0) else outs[k].at[slot]
        cp=pltpu.make_async_remote_copy(src_ref=src,dst_ref=outs[k].at[slot],send_sem=send.at[k,sem(landed)],recv_sem=recv.at[k,sem(landed)],device_id=target,device_id_type=MESH)
        cp.start()
        table[(k,landed)]=cp
    table={}
    own=[]
    def first(k):
        cp=pltpu.make_async_copy(shards[k],outs[k].at[me.slot(0,0,0,0)],local.at[k]); cp.start(); own.append(cp)
        for s in range(1,Z): start(k,(0,0,0,0),s)
        for d in orders[k]: start(k,(0,0,0,0),d)
    def arrive(k,rel,rest):
        table[(k,rel)].wait_recv()
        for d in rest: start(k,rel,d)
    def rel_of(s,o,a,b=0,c=0):
        r=[s,0,0,0]; r[dims[o[0]]]=a; r[dims[o[1]]]=b; r[dims[o[2]]]=c
        return tuple(r)
    for k in range(min(ahead,K)): first(k)
    for t in range(K+3):
        if t+ahead<K: first(t+ahead)
        k=t
        if k<K:
            o=orders[k]
            for s in range(1,Z): arrive(k,rel_of(s,o,0),o)
        k=t-1
        if 0<=k<K:
            o=orders[k]
            for s in range(Z): arrive(k,rel_of(s,o,1),o[1:])
        k=t-2
        if 0<=k<K:
            o=orders[k]
            for s in range(Z):
                for a in range(2): arrive(k,rel_of(s,o,a,1),o[2:])
        k=t-3
        if 0<=k<K:
            o=orders[k]
            for s in range(Z):
                for a in range(2):
                    for b in range(2): arrive(k,rel_of(s,o,a,b,1),"")
    for cp in own: cp.wait()
    for cp in table.values(): cp.wait_send()

def gather(shards, orders, cid, ahead=2):
    n=lax.axis_size("dp")*lax.axis_size("fsdp"); Z=lax.axis_size("dp")//2; K=len(shards)
    return pl.pallas_call(functools.partial(gather_kernel,Z,orders,ahead),
        out_shape=[jax.ShapeDtypeStruct((n,)+s.shape,s.dtype) for s in shards],
        in_specs=[pl.BlockSpec(memory_space=pl.ANY)]*K,
        out_specs=[pl.BlockSpec(memory_space=pl.ANY)]*K,
        scratch_shapes=[pltpu.SemaphoreType.DMA((K,)),pltpu.SemaphoreType.DMA((K,8*Z)),pltpu.SemaphoreType.DMA((K,8*Z))],
        compiler_params=pltpu.CompilerParams(collective_id=cid,has_side_effects=True))(*shards)


class Gathering:
    def __init__(self, me, chunks, local, send, recv):
        self.me, self.chunks = me, chunks
        self.local, self.send, self.recv = local, send, recv
        self.table, self.own = {}, []

    def start(self, k, rel, to):
        shard, full, cols, _ = self.chunks[k]
        me = self.me
        if isinstance(to, int):
            target, landed = me.device(s=to), (to, 0, 0, 0)
        else:
            landed = list(rel)
            landed["zyxc".index(to)] = 1
            landed = tuple(landed)
            target = me.device(**{"d" + to: 1})
        slot = me.slot(*rel)
        here = full.at[slot, :, cols]
        at = ((landed[0] * 2 + landed[1]) * 2 + landed[2]) * 2 + landed[3]
        copy = pltpu.make_async_remote_copy(
            src_ref=shard.at[:, cols] if rel == (0, 0, 0, 0) else here,
            dst_ref=here,
            send_sem=self.send.at[k, at],
            recv_sem=self.recv.at[k, at],
            device_id=target,
            device_id_type=MESH,
        )
        copy.start()
        self.table[(k, landed)] = copy

    def begin(self, k):
        shard, full, cols, order = self.chunks[k]
        copy = pltpu.make_async_copy(
            shard.at[:, cols], full.at[self.me.slot(0, 0, 0, 0), :, cols], self.local.at[k]
        )
        copy.start()
        self.own.append((k, copy))
        for s in range(1, self.me.Z):
            self.start(k, (0, 0, 0, 0), s)
        for d in order:
            self.start(k, (0, 0, 0, 0), d)

    def step(self, k, stage):
        order = self.chunks[k][3]
        where = ["zyxc".index(d) for d in order]
        for s in range(1 if stage == 0 else 0, self.me.Z):
            for bits in range(1 << max(stage - 1, 0)):
                rel = [s, 0, 0, 0]
                for i in range(stage - 1):
                    rel[where[i]] = bits >> i & 1
                if stage:
                    rel[where[stage - 1]] = 1
                rel = tuple(rel)
                self.table[(k, rel)].wait_recv()
                for d in order[stage:]:
                    self.start(k, rel, d)
        if stage == 3:
            for at, copy in self.own:
                if at == k:
                    copy.wait()

    def finish(self):
        for copy in self.table.values():
            copy.wait_send()


def forward_kernel(sizes, *refs):
    batches, rows, kv_heads, group, used = sizes
    (first_s, out_s, gate_s, up_s, down_s, x_ref, place_ref, freq_ref) = refs[:8]
    (first_w, out_w, gate_w, up_w, down_w, q_out, kv_out, o_out, log_out) = refs[8:17]
    (mixed_out, h2_out, hidden_out, slope_out, silu_out, bias_out, cos_out, sin_out) = refs[17:25]
    (hid_turned, h2_turned, att_turned, nor_turned) = refs[25:29]
    (raw_a, raw_b, w_a, w_b, normed, queries, kv_all, attended, logs, mixed, h2) = refs[29:40]
    (hidden, slope, silu, bias, cos_t, sin_t, gains) = refs[40:47]
    (hid_t, h2_t, att_t, nor_t) = refs[47:51]
    (local, send, recv, kv_send, kv_recv, load_sem, store_sem) = refs[51:]
    me = Place()
    greet(me)
    whole = slice(None)
    half = down_w.shape[2] // 2
    comm = Gathering(
        me,
        (
            (first_s, first_w, whole, "xyc"),
            (out_s, out_w, whole, "yxc"),
            (gate_s, gate_w, whole, "yxc"),
            (up_s, up_w, whole, "xyc"),
            (down_s, down_w, pl.ds(0, half), "yxc"),
            (down_s, down_w, pl.ds(half, half), "xyc"),
        ),
        local,
        send,
        recv,
    )
    tokens, width = x_ref.shape
    length = kv_all.shape[1]
    stores = []

    def store(i, src, dst):
        copy = pltpu.make_async_copy(src, dst, store_sem.at[i])
        copy.start()
        stores.append(copy)

    def over_rows(body, step=64):
        def one(i, carry):
            body(pl.ds(pl.multiple_of(i * step, step), step))
            return carry

        lax.fori_loop(0, tokens // step, one, 0)

    def load(full, raw, col, size, i):
        return pltpu.make_async_copy(
            full.at[:, :, pl.ds(col, size)], raw.at[:, :, pl.ds(0, size)], load_sem.at[i]
        )

    def assemble(raw, flat, size):
        n, r, _ = raw.shape
        pair = 2 * r

        def one(i, carry):
            piece = raw[pl.ds(2 * i, 2), :, pl.ds(0, size)].astype(jnp.float32)
            flat[pl.ds(pl.multiple_of(pair * i, 16), pair), pl.ds(0, size)] = piece.reshape(
                pair, size
            ).astype(jnp.bfloat16)
            return carry

        lax.fori_loop(0, n // 2, one, 0)

    def turn_rows(src, dst, base, size):
        for i in range(size // 256):
            at = slice(base + i * 256, base + (i + 1) * 256)
            dst[at, :] = src[:, at].astype(jnp.float32).T.astype(jnp.bfloat16)

    comm.begin(0)
    comm.begin(1)
    comm.begin(2)

    scale = HD**-0.5
    lane = lax.broadcasted_iota(jnp.int32, (64, 128), 1)
    second = lax.rem(lane, HD) >= HD // 2
    is_value = lane >= HD

    def tables(at):
        angle = place_ref[at, :].astype(jnp.float32) * freq_ref[...]
        c, s = jnp.cos(angle), jnp.sin(angle)
        s = jnp.where(second, s, -s)
        cos_t[0, at, :] = c * scale
        sin_t[0, at, :] = s * scale
        cos_t[1, at, :] = jnp.where(is_value, 1.0, c)
        sin_t[1, at, :] = jnp.where(is_value, 0.0, s)

    over_rows(tables)
    first_row = lax.axis_index("fsdp") * rows

    def masks(at):
        token = at.start
        inside = lax.rem(token, rows)
        query = first_row + inside + lax.broadcasted_iota(jnp.int32, (64, length), 0)
        key = lax.broadcasted_iota(jnp.int32, (64, length), 1)
        start = query - place_ref[at, :]
        allowed = (key <= query) & (key >= start)
        bias[at, :] = jnp.where(allowed, 0.0, NEGATIVE).astype(jnp.bfloat16)

    over_rows(masks)
    store(0, bias, bias_out)
    store(1, cos_t, cos_out)
    store(2, sin_t, sin_out)

    comm.step(0, 0)
    comm.begin(3)
    comm.step(1, 0)
    comm.step(0, 1)
    comm.step(2, 0)
    comm.step(1, 1)
    comm.step(0, 2)
    comm.step(3, 0)
    comm.step(2, 1)
    comm.step(1, 2)
    comm.step(0, 3)

    tile = raw_a.shape[2]
    load(first_w, raw_a, used, 128, 0).start()
    load(first_w, raw_b, 0, tile, 1).start()
    load(first_w, raw_a, used, 128, 0).wait()
    assemble(raw_a, w_a, 128)
    gains[...] = w_a[:, :128].astype(jnp.float32).T[:8]
    load(first_w, raw_a, used - tile, tile, 0).start()

    def norm_one(at):
        x = x_ref[at, :].astype(jnp.float32)
        inverse = lax.rsqrt(jnp.mean(x * x, -1, keepdims=True) + EPSILON)
        normed[at, :] = (x * inverse * gains[0:1, :]).astype(jnp.bfloat16)

    over_rows(norm_one)

    def turn(flat, kind, put, step=256):
        def body(at):
            u = plain_dot(normed[at, :], flat[...])
            for j in range(tile // 128):
                piece = u[:, j * 128 : (j + 1) * 128]
                piece = piece * cos_t[kind, at, :] + swap_halves(piece) * sin_t[kind, at, :]
                put(at, j, piece.astype(jnp.bfloat16))

        over_rows(body, step)

    slot = (me.x * 2 + me.c) * rows

    def put_pair(at, j, piece):
        token = at.start
        b = token // rows
        row = pl.multiple_of(slot + lax.rem(token, rows), 256)
        kv_all[b, pl.ds(row, 256), j * 128 : (j + 1) * 128] = piece

    load(first_w, raw_a, used - tile, tile, 0).wait()
    assemble(raw_a, w_a, tile)
    turn(w_a, 1, put_pair)

    def share(i, dx, to):
        row = (lax.rem(me.x + dx, 2) * 2 + me.c) * rows
        block = kv_all.at[:, pl.ds(pl.multiple_of(row, 256), rows), :]
        copy = pltpu.make_async_remote_copy(
            src_ref=block,
            dst_ref=block,
            send_sem=kv_send.at[i],
            recv_sem=kv_recv.at[i],
            device_id=me.device(**{"d" + to: 1}),
            device_id_type=MESH,
        )
        copy.start()
        return copy

    to_x = share(0, 0, "x")
    to_c = share(1, 0, "c")
    comm.step(3, 1)
    comm.begin(4)
    for j in range(queries.shape[1] // tile):
        raw, flat = ((raw_b, w_b), (raw_a, w_a))[j % 2]
        if (j + 1) * tile < queries.shape[1]:
            load(first_w, (raw_a, raw_b)[j % 2], (j + 1) * tile, tile, j % 2).start()
        load(first_w, raw, j * tile, tile, 1 - j % 2).wait()
        assemble(raw, flat, tile)

        def put_query(at, i, piece, j=j):
            queries[at, j * tile + i * 128 : j * tile + (i + 1) * 128] = piece

        turn(flat, 0, put_query)
        if j == 0:
            comm.step(2, 2)
            comm.begin(5)
    store(3, queries, q_out)
    turn_rows(normed, nor_t, 0, width)
    store(12, nor_t, nor_turned)
    comm.step(1, 3)
    to_x.wait_recv()
    to_far = share(2, 1, "c")
    to_c.wait_recv()
    to_far.wait_recv()
    store(4, kv_all, kv_out)

    logs[...] = jnp.zeros_like(logs)
    lanes = lax.broadcasted_iota(jnp.int32, (rows, 128), 1)
    sides_mask = lane_masks(rows)

    def head(i, carry):
        b = i // kv_heads
        h = lax.rem(i, kv_heads)
        at = pl.ds(pl.multiple_of(b * rows, 256), rows)
        kv = kv_all[b, :, pl.ds(pl.multiple_of(h * 128, 128), 128)]
        sides = (kv, swapped(kv))
        shift = bias[at, :].astype(jnp.float32)
        log_piece = logs[at, :]
        for pair in range(group // 2):
            cols = pl.ds(pl.multiple_of(h * group * HD + pair * 128, 128), 128)
            q = queries[at, cols]
            found = []
            for side in range(2):
                scores = dot_t(q * sides_mask[side], sides[side]) + shift
                top = jnp.max(scores, -1, keepdims=True)
                powers = jnp.exp(scores - top)
                total = jnp.sum(powers, -1, keepdims=True)
                probs = (powers * (1.0 / total)).astype(jnp.bfloat16)
                found.append(plain_dot(probs, sides[1 - side]))
                log_piece = jnp.where(
                    lanes == h * group + pair * 2 + side, top + jnp.log(total), log_piece
                )
            attended[at, cols] = jnp.where(lanes < HD, found[0], found[1]).astype(jnp.bfloat16)
        logs[at, :] = log_piece
        return carry

    count = batches * kv_heads
    pumps = [(3, 2), (4, 0), (2, 3), (5, 0), (4, 1), (5, 1)]
    done = 0
    for i in range(6):
        upto = (2, 4, 6, 8, 9, 10)[i] * count // 10
        lax.fori_loop(done, upto, head, 0)
        done = upto
        comm.step(*pumps[i])
    store(5, attended, o_out)
    store(6, logs, log_out)

    steps = width // tile
    load(out_w, raw_a, 0, tile, 0).start()
    for j in range(steps):
        raw, flat = ((raw_a, w_a), (raw_b, w_b))[j % 2]
        if j + 1 < steps:
            load(out_w, (raw_b, raw_a)[j % 2], (j + 1) * tile, tile, 1 - j % 2).start()
        load(out_w, raw, j * tile, tile, j % 2).wait()
        assemble(raw, flat, tile)

        def add_in(at, flat=flat, j=j):
            cols = slice(j * tile, (j + 1) * tile)
            mixed[at, cols] = x_ref[at, cols].astype(jnp.float32) + plain_dot(
                attended[at, :], flat[...]
            )

        over_rows(add_in, 256)

    def norm_two(at):
        y = mixed[at, :]
        inverse = lax.rsqrt(jnp.mean(y * y, -1, keepdims=True) + EPSILON)
        h2[at, :] = (y * inverse * gains[1:2, :]).astype(jnp.bfloat16)

    over_rows(norm_two)
    store(7, mixed, mixed_out)
    store(8, h2, h2_out)
    turn_rows(attended, att_t, 0, attended.shape[1])
    store(13, att_t, att_turned)
    turn_rows(h2, h2_t, 0, width)
    store(14, h2_t, h2_turned)
    comm.step(3, 3)

    wide = 512
    features = hidden.shape[1]
    pumps = {1: (4, 2), 3: (5, 2), 5: (4, 3)}
    load(gate_w, raw_a, 0, wide, 0).start()
    load(up_w, raw_b, 0, wide, 1).start()
    for j in range(features // wide):
        load(gate_w, raw_a, j * wide, wide, 0).wait()
        assemble(raw_a, w_a, wide)
        load(up_w, raw_b, j * wide, wide, 1).wait()
        assemble(raw_b, w_b, wide)
        if (j + 1) * wide < features:
            load(gate_w, raw_a, (j + 1) * wide, wide, 0).start()
            load(up_w, raw_b, (j + 1) * wide, wide, 1).start()

        def units(at, j=j):
            cols = slice(j * wide, (j + 1) * wide)
            g = plain_dot(h2[at, :], w_a[:, :wide])
            u = plain_dot(h2[at, :], w_b[:, :wide])
            sig = jax.nn.sigmoid(g)
            soft = g * sig
            hidden[at, cols] = (soft * u).astype(jnp.bfloat16)
            silu[at, cols] = soft.astype(jnp.bfloat16)
            slope[at, cols] = (u * (sig * (1.0 + g * (1.0 - sig)))).astype(jnp.bfloat16)

        over_rows(units, 256)
        turn_rows(hidden, hid_t, j * wide, wide)
        cols = pl.ds(j * wide, wide)
        store(16 + 4 * j, hidden.at[:, cols], hidden_out.at[:, cols])
        store(17 + 4 * j, silu.at[:, cols], silu_out.at[:, cols])
        store(18 + 4 * j, slope.at[:, cols], slope_out.at[:, cols])
        store(19 + 4 * j, hid_t.at[cols, :], hid_turned.at[cols, :])
        if j in pumps:
            comm.step(*pumps[j])
    comm.step(5, 3)
    for copy in (to_x, to_c, to_far):
        copy.wait_send()
    comm.finish()
    for copy in stores:
        copy.wait()


def forward(shards, x, places, kv_heads, group, batches):
    first_s, out_s, gate_s, up_s, down_s = shards
    n = lax.axis_size("dp") * lax.axis_size("fsdp")
    Z = lax.axis_size("dp") // 2
    tokens, width = x.shape
    rows = tokens // batches
    length = rows * lax.axis_size("fsdp")
    key_wide = kv_heads * 128
    query_wide = kv_heads * group * HD
    used = query_wide + key_wide
    features = gate_s.shape[1]
    r = first_s.shape[0]
    freqs = ROPE_BASE ** (-jnp.arange(HD // 2).astype(jnp.float32) / (HD // 2))
    freqs = jnp.tile(freqs, 4)[None]
    bf, f32 = jnp.bfloat16, jnp.float32
    shape = jax.ShapeDtypeStruct
    outs = [shape((n,) + s.shape, s.dtype) for s in shards] + [
        shape((tokens, query_wide), bf),
        shape((batches, length, key_wide), bf),
        shape((tokens, query_wide), bf),
        shape((tokens, 128), f32),
        shape((tokens, width), f32),
        shape((tokens, width), bf),
        shape((tokens, features), bf),
        shape((tokens, features), bf),
        shape((tokens, features), bf),
        shape((tokens, length), bf),
        shape((2, tokens, 128), f32),
        shape((2, tokens, 128), f32),
        shape((features, tokens), bf),
        shape((width, tokens), bf),
        shape((query_wide, tokens), bf),
        shape((width, tokens), bf),
    ]
    vmem = pltpu.VMEM
    scratch = [
        vmem((n, r, key_wide), bf),
        vmem((n, r, key_wide), bf),
        vmem((width, key_wide), bf),
        vmem((width, key_wide), bf),
        vmem((tokens, width), bf),
        vmem((tokens, query_wide), bf),
        vmem((batches, length, key_wide), bf),
        vmem((tokens, query_wide), bf),
        vmem((tokens, 128), f32),
        vmem((tokens, width), f32),
        vmem((tokens, width), bf),
        vmem((tokens, features), bf),
        vmem((tokens, features), bf),
        vmem((tokens, features), bf),
        vmem((tokens, length), bf),
        vmem((2, tokens, 128), f32),
        vmem((2, tokens, 128), f32),
        vmem((8, width), f32),
        vmem((features, tokens), bf),
        vmem((width, tokens), bf),
        vmem((query_wide, tokens), bf),
        vmem((width, tokens), bf),
        pltpu.SemaphoreType.DMA((6,)),
        pltpu.SemaphoreType.DMA((6, 8 * Z)),
        pltpu.SemaphoreType.DMA((6, 8 * Z)),
        pltpu.SemaphoreType.DMA((3,)),
        pltpu.SemaphoreType.DMA((3,)),
        pltpu.SemaphoreType.DMA((2,)),
        pltpu.SemaphoreType.DMA((16 + 4 * (features // 512),)),
    ]
    any_space = pl.BlockSpec(memory_space=pl.ANY)
    in_vmem = pl.BlockSpec(memory_space=pltpu.VMEM)
    return pl.pallas_call(
        functools.partial(forward_kernel, (batches, rows, kv_heads, group, used)),
        out_shape=outs,
        in_specs=[any_space] * 5 + [in_vmem] * 3,
        out_specs=[any_space] * len(outs),
        scratch_shapes=scratch,
        compiler_params=pltpu.CompilerParams(
            collective_id=1, has_side_effects=True, vmem_limit_bytes=63 * 2**20
        ),
        cost_estimate=pl.CostEstimate(
            flops=2 * tokens * width * (used + width + 2 * features),
            bytes_accessed=4 * n * r * (used + width + 3 * features),
            transcendentals=tokens * features,
        ),
    )(*shards, x, places, freqs)


def tile_of(N):
    for t in (512,384,256,128):
        if N%t==0: return t
    return N

def scatter_kernel(Z, orders, ahead, dims_, *refs):
    K=len(orders)
    parts=refs[:K]; outs=refs[K:2*K]
    sc=refs[2*K:]
    first_buf=sc[:K]; one_buf=sc[K:2*K]; two_buf=sc[2*K:3*K]; last_buf=sc[3*K:4*K]
    shapes=sorted(set(dims_))
    stage=[sc[4*K+shapes.index(d)] for d in dims_]
    local,send,recv=sc[4*K+len(shapes):]
    me=Place()
    greet(me)
    copies={}
    def ship(k,name,index,src,dst,target):
        cp=pltpu.make_async_remote_copy(src_ref=src,dst_ref=dst,send_sem=send.at[k,index],recv_sem=recv.at[k,index],device_id=target,device_id_type=MESH)
        cp.start(); copies[(k,name)]=cp
    def part(k,a,b,other):
        o=orders[k]
        rel={o[0]:a,o[1]:b}
        y=lax.rem(me.y+rel["y"],2); x=lax.rem(me.x+rel["x"],me.X); c=lax.rem(me.c+other,2)
        return parts[k].at[:,y,x,c]
    order4=((1,1),(1,0),(0,1),(0,0))
    locals_={}
    def first(k):
        for i,(a,b) in enumerate(order4):
            ship(k,("c",a,b),i,part(k,a,b,1),first_buf[k].at[a,b],me.device(dc=1))
    def bring(k,i):
        a,b=order4[i]
        cp=pltpu.make_async_copy(part(k,a,b,0),stage[k].at[i%2],local.at[k,i%2]); cp.start(); locals_[(k,i)]=cp
    def add(dst,src,k):
        _,r,N=dims_[k]
        t=tile_of(N)
        def body(i,_):
            zi=i//(N//t); j=i%(N//t)
            cols=pl.ds(pl.multiple_of(j*t,128),t)
            dst[zi,:,cols]=dst[zi,:,cols]+src[zi,:,cols]
            return 0
        lax.fori_loop(0,Z*(N//t),body,0)
    def step_c(k):
        bring(k,0); bring(k,1)
        for i,(a,b) in enumerate(order4):
            copies[(k,("c",a,b))].wait_recv()
            locals_[(k,i)].wait()
            add(first_buf[k].at[a,b],stage[k].at[i%2],k)
            if i+2<4: bring(k,i+2)
            if a==1:
                ship(k,("1",b),4+b,first_buf[k].at[1,b],one_buf[k].at[b],me.device(**{"d"+orders[k][0]:1}))
    def step_1(k):
        for b in (1,0):
            copies[(k,("1",b))].wait_recv()
            add(first_buf[k].at[0,b],one_buf[k].at[b],k)
            if b==1:
                ship(k,"2",6,first_buf[k].at[0,1],two_buf[k],me.device(**{"d"+orders[k][1]:1}))
    def step_2(k):
        copies[(k,"2")].wait_recv()
        add(first_buf[k].at[0,0],two_buf[k],k)
        for s in range(1,Z):
            ship(k,("z",s),6+s,first_buf[k].at[0,0,lax.rem(me.z+s,Z)],last_buf[k].at[s-1],me.device(s=s))
    def step_z(k):
        _,r,N=dims_[k]
        for s in range(1,Z): copies[(k,("z",s))].wait_recv()
        t=tile_of(N)
        mine=first_buf[k].at[0,0,me.z]
        def body(j,_):
            cols=pl.ds(pl.multiple_of(j*t,128),t)
            total=mine[:,cols].astype(jnp.float32)
            for s in range(1,Z): total=total+last_buf[k][s-1,:,cols].astype(jnp.float32)
            outs[k][:,cols]=total
            return 0
        lax.fori_loop(0,N//t,body,0)
    for k in range(min(ahead,K)): first(k)
    for t in range(K+3):
        if t+ahead<K: first(t+ahead)
        if t<K: step_c(t)
        if 0<=t-1<K: step_1(t-1)
        if 0<=t-2<K: step_2(t-2)
        if 0<=t-3<K: step_z(t-3)
    for cp in copies.values(): cp.wait_send()

def scatter(parts, orders, cid, ahead=2):
    n=lax.axis_size("dp")*lax.axis_size("fsdp"); Z=lax.axis_size("dp")//2; X=lax.axis_size("fsdp")//2; K=len(parts)
    dims_=[(n,p.shape[0]//n,p.shape[1]) for p in parts]
    parts=[p.reshape(Z,2,X,2,p.shape[0]//n,p.shape[1]) for p in parts]
    bf=jnp.bfloat16
    sc=[pltpu.VMEM((2,2,Z,r,N),bf) for _,r,N in dims_]+[pltpu.VMEM((2,Z,r,N),bf) for _,r,N in dims_]+[pltpu.VMEM((Z,r,N),bf) for _,r,N in dims_]+[pltpu.VMEM((Z-1,r,N),bf) for _,r,N in dims_]+[pltpu.VMEM((2,Z,r,N),bf) for _,r,N in sorted(set(dims_))]
    return pl.pallas_call(functools.partial(scatter_kernel,Z,orders,ahead,dims_),
        out_shape=[jax.ShapeDtypeStruct((r,N),jnp.float32) for _,r,N in dims_],
        in_specs=[pl.BlockSpec(memory_space=pl.ANY)]*K,
        out_specs=[pl.BlockSpec(memory_space=pltpu.VMEM)]*K,
        scratch_shapes=sc+[pltpu.SemaphoreType.DMA((K,2)),pltpu.SemaphoreType.DMA((K,6+Z)),pltpu.SemaphoreType.DMA((K,6+Z))],
        compiler_params=pltpu.CompilerParams(collective_id=cid,has_side_effects=True,vmem_limit_bytes=63*2**20))(*parts)


def dot_t(left, right):
    return lax.dot_general(
        left, right, (((1,), (1,)), ((), ())), preferred_element_type=jnp.float32
    )


def swap_halves(u):
    lane = lax.broadcasted_iota(jnp.int32, u.shape, 1)
    down = pltpu.roll(u, 32, 1)
    up = pltpu.roll(u, 96, 1)
    return jnp.where(lax.rem(lane, 64) < 32, up, down)


def project_kernel(h_ref, w_ref, cos_ref, sin_ref, out_ref):
    u = plain_dot(h_ref[...], w_ref[...])
    for j in range(u.shape[1] // 128):
        piece = u[:, j * 128 : (j + 1) * 128]
        turned = piece * cos_ref[0] + swap_halves(piece) * sin_ref[0]
        out_ref[:, j * 128 : (j + 1) * 128] = turned.astype(jnp.bfloat16)


def project(normed, weight, cos_tables, sin_tables, width):
    tokens, depth = normed.shape
    steps = weight.shape[1] // width
    return pl.pallas_call(
        project_kernel,
        grid=(steps,),
        in_specs=[
            pl.BlockSpec((tokens, depth), lambda j: (0, 0)),
            pl.BlockSpec((depth, width), lambda j: (0, j)),
            pl.BlockSpec((1, tokens, 128), lambda j: (j // (steps - 1), 0, 0)),
            pl.BlockSpec((1, tokens, 128), lambda j: (j // (steps - 1), 0, 0)),
        ],
        out_specs=pl.BlockSpec((tokens, width), lambda j: (0, j)),
        out_shape=jax.ShapeDtypeStruct((tokens, steps * width), jnp.bfloat16),
        compiler_params=pltpu.CompilerParams(vmem_limit_bytes=48 * 2**20),
        cost_estimate=pl.CostEstimate(
            flops=2 * tokens * depth * weight.shape[1],
            bytes_accessed=2 * depth * weight.shape[1],
            transcendentals=0,
        ),
    )(normed, weight, cos_tables, sin_tables)


def lane_masks(rows):
    lane = lax.broadcasted_iota(jnp.int32, (rows, 128), 1)
    low_side = (lane < 64).astype(jnp.float32)
    return low_side.astype(jnp.bfloat16), (1.0 - low_side).astype(jnp.bfloat16)


def swapped(kv):
    return pltpu.roll(kv.astype(jnp.float32), 64, 1).astype(jnp.bfloat16)


def attend_kernel(group, q_ref, kv_ref, bias_ref, o_ref, log_ref):
    kv = kv_ref[0]
    sides = (kv, swapped(kv))
    rows = q_ref.shape[0]
    masks = lane_masks(rows)
    lane = lax.broadcasted_iota(jnp.int32, (rows, 128), 1)
    logs = jnp.zeros((rows, 128), jnp.float32)
    bias = bias_ref[0]
    for pair in range(group // 2):
        cols = slice(pair * 128, pair * 128 + 128)
        q = q_ref[:, cols]
        found = []
        for half in range(2):
            scores = dot_t(q * masks[half], sides[half]) + bias
            top = jnp.max(scores, -1, keepdims=True)
            powers = jnp.exp(scores - top)
            total = jnp.sum(powers, -1, keepdims=True)
            probs = (powers * (1.0 / total)).astype(jnp.bfloat16)
            found.append(plain_dot(probs, sides[1 - half]))
            logs = jnp.where(lane == pair * 2 + half, top + jnp.log(total), logs)
        o_ref[:, cols] = jnp.where(lane < 64, found[0], found[1]).astype(jnp.bfloat16)
    log_ref[...] = logs


def attend(projected, both_all, bias, kv_heads, group):
    batches, length, _ = both_all.shape
    rows = projected.shape[0] // batches
    wide = group * HD
    return pl.pallas_call(
        functools.partial(attend_kernel, group),
        grid=(batches, kv_heads),
        in_specs=[
            pl.BlockSpec((rows, wide), lambda b, h: (b, h)),
            pl.BlockSpec((1, length, 128), lambda b, h: (b, 0, h)),
            pl.BlockSpec((1, rows, length), lambda b, h: (b, 0, 0)),
        ],
        out_specs=[
            pl.BlockSpec((rows, wide), lambda b, h: (b, h)),
            pl.BlockSpec((rows, 128), lambda b, h: (b, h)),
        ],
        out_shape=[
            jax.ShapeDtypeStruct((batches * rows, kv_heads * wide), jnp.bfloat16),
            jax.ShapeDtypeStruct((batches * rows, kv_heads * 128), jnp.float32),
        ],
        compiler_params=pltpu.CompilerParams(vmem_limit_bytes=48 * 2**20),
    )(projected, both_all, bias)


def attend_back_kernel(
    group, q_ref, do_ref, kv_ref, bias_ref, log_ref, cos_ref, sin_ref, dq_ref, dkv_ref
):
    kv = kv_ref[0]
    sides = (kv, swapped(kv))
    rows = q_ref.shape[0]
    length = kv.shape[0]
    masks = lane_masks(rows)
    lane = lax.broadcasted_iota(jnp.int32, (rows, 128), 1)
    bias = bias_ref[0]
    key_sum = jnp.zeros((128, length), jnp.float32)
    value_sum = jnp.zeros((128, length), jnp.float32)
    for pair in range(group // 2):
        cols = slice(pair * 128, pair * 128 + 128)
        q = q_ref[:, cols]
        do = do_ref[:, cols]
        found = []
        for half in range(2):
            q_half = q * masks[half]
            do_half = do * masks[half]
            at = pair * 2 + half
            log_total = log_ref[:, at : at + 1]
            probs = jnp.exp(dot_t(q_half, sides[half]) + bias - log_total)
            grad_probs = dot_t(do_half, sides[1 - half])
            row_dot = jnp.sum(probs * grad_probs, -1, keepdims=True)
            grad_scores = (probs * (grad_probs - row_dot)).astype(jnp.bfloat16)
            found.append(plain_dot(grad_scores, sides[half]))
            key_sum = key_sum + left_dot(q_half, grad_scores)
            value_sum = value_sum + left_dot(do_half, probs.astype(jnp.bfloat16))
        dq = jnp.where(lane < 64, found[0], found[1])
        dq = dq * cos_ref[0] - swap_halves(dq) * sin_ref[0]
        dq_ref[:, cols] = dq.astype(jnp.bfloat16)
    both = jnp.concatenate(
        [key_sum[:64] + key_sum[64:], value_sum[:64] + value_sum[64:]], 0
    )
    dkv_ref[0] = both.T.astype(jnp.bfloat16)


def attend_back(projected, grad_attended, both_all, bias, logs, cos_tables, sin_tables, group):
    batches, length, _ = both_all.shape
    rows = projected.shape[0] // batches
    wide = group * HD
    kv_heads = both_all.shape[2] // 128
    return pl.pallas_call(
        functools.partial(attend_back_kernel, group),
        grid=(batches, kv_heads),
        in_specs=[
            pl.BlockSpec((rows, wide), lambda b, h: (b, h)),
            pl.BlockSpec((rows, wide), lambda b, h: (b, h)),
            pl.BlockSpec((1, length, 128), lambda b, h: (b, 0, h)),
            pl.BlockSpec((1, rows, length), lambda b, h: (b, 0, 0)),
            pl.BlockSpec((rows, 128), lambda b, h: (b, h)),
            pl.BlockSpec((1, rows, 128), lambda b, h: (0, b, 0)),
            pl.BlockSpec((1, rows, 128), lambda b, h: (0, b, 0)),
        ],
        out_specs=[
            pl.BlockSpec((rows, wide), lambda b, h: (b, h)),
            pl.BlockSpec((1, length, 128), lambda b, h: (b, 0, h)),
        ],
        out_shape=[
            jax.ShapeDtypeStruct((batches * rows, kv_heads * wide), jnp.bfloat16),
            jax.ShapeDtypeStruct((batches, length, kv_heads * 128), jnp.bfloat16),
        ],
        compiler_params=pltpu.CompilerParams(vmem_limit_bytes=48 * 2**20),
    )(projected, grad_attended, both_all, bias, logs, cos_tables, sin_tables)


class Scattering:
    def __init__(self, me, chunks, send, recv, free):
        self.me, self.chunks = me, chunks
        self.send, self.recv, self.free = send, recv, free
        self.copies = {}
        self.friends = [me.device(s=s) for s in range(1, me.Z)]
        self.friends += [me.device(dy=1), me.device(dx=1), me.device(dc=1)]

    def ship(self, k, name, index, src, dst, target):
        copy = pltpu.make_async_remote_copy(
            src_ref=src,
            dst_ref=dst,
            send_sem=self.send.at[k, index],
            recv_sem=self.recv.at[k, index],
            device_id=target,
            device_id_type=MESH,
        )
        copy.start()
        self.copies[(k, name)] = copy

    def add(self, dst, src, wide, base):
        depth = dst.shape[0]
        t = tile_of(wide)
        count = wide // t

        def body(i, carry):
            at = i // count
            cols = pl.ds(pl.multiple_of(base + lax.rem(i, count) * t, 128), t)
            dst[at, :, cols] = dst[at, :, cols] + src[at, :, cols]
            return carry

        lax.fori_loop(0, depth * count, body, 0)

    def buffers(self, k):
        own, one, two, last, wide = self.chunks[k][:5]
        cols = pl.ds(self.chunks[k][9], wide)
        return own, one, two, last, wide, cols

    def begin(self, k):
        own, one, two, last, wide, cols = self.buffers(k)
        order = self.chunks[k][5]
        for b in (1, 0):
            self.ship(
                k,
                ("1", b),
                b,
                own.at[1, b, :, :, cols],
                one.at[b, :, :, cols],
                self.me.device(**{"d" + order[0]: 1}),
            )

    def first(self, k):
        own, one, two, last, wide, cols = self.buffers(k)
        order = self.chunks[k][5]
        for b in (1, 0):
            self.copies[(k, ("1", b))].wait_recv()
            self.add(own.at[0, b], one.at[b], wide, self.chunks[k][9])
            if b == 1:
                self.ship(
                    k,
                    "2",
                    2,
                    own.at[0, 1, :, :, cols],
                    two.at[:, :, cols],
                    self.me.device(**{"d" + order[1]: 1}),
                )

    def second(self, k):
        own, one, two, last, wide, cols = self.buffers(k)
        me = self.me
        self.copies[(k, "2")].wait_recv()
        self.add(own.at[0, 0], two, wide, self.chunks[k][9])
        for s in range(1, me.Z):
            self.ship(
                k,
                ("z", s),
                2 + s,
                own.at[0, 0, lax.rem(me.z + s, me.Z), :, cols],
                last.at[s - 1, :, cols],
                me.device(s=s),
            )

    def third(self, k):
        own, one, two, last, wide, cols = self.buffers(k)
        me = self.me
        _, out, base, group, off = self.chunks[k][5:]
        for s in range(1, me.Z):
            self.copies[(k, ("z", s))].wait_recv()
        t = tile_of(wide)

        def body(j, carry):
            here = pl.ds(pl.multiple_of(off + j * t, 128), t)
            there = pl.ds(pl.multiple_of(base + j * t, 128), t)
            total = own[0, 0, me.z, :, here].astype(jnp.float32)
            for s in range(1, me.Z):
                total = total + last[s - 1, :, here].astype(jnp.float32)
            out[:, there] = total
            return carry

        lax.fori_loop(0, wide // t, body, 0)
        for (at, _), copy in self.copies.items():
            if at == k:
                copy.wait_send()
        if group is not None:
            for friend in self.friends:
                pl.semaphore_signal(
                    self.free.at[group], inc=1, device_id=friend, device_id_type=MESH
                )

    def reuse(self, group):
        pl.semaphore_wait(self.free.at[group], len(self.friends))


def backward_kernel(sizes, *refs):
    batches, rows, kv_heads, group, used = sizes
    (dy_ref, first_w, out_w, gate_w, up_w, down_w) = refs[:6]
    (q_in, kv_in, log_in, mixed_in, hidden_in, slope_in, silu_in, bias_in, cos_in, sin_in) = refs[6:16]
    (hid_t, h2_t, att_t, nor_t, x_in) = refs[16:21]
    outs = refs[21:36]
    (result_out, grad_out, g_first, g_out, g_gate, g_up, g_down) = outs[:7]
    (hid_s, h2_s, att_s, nor_s, dy_p, gate_p, up_p, dm_p) = outs[7:]
    pre_p, dy1_h = refs[36:38]
    sc = list(refs[38:])
    take = lambda n: [sc.pop(0) for _ in range(n)]
    sets = [take(4) for _ in range(3)]
    down_sets = [take(4) for _ in range(2)]
    gain_set = take(4)
    (lhs_d, lhs, lraw, rhs, acc, part, cot, low_t, queries, grads, pre) = take(11)
    (kv_all, dkv, bias, logs, cos_t, sin_t, dkv_r, dkv_x) = take(8)
    (raw_a, w_a, wd, fac_a, fac_b, dgt, dut, gains, gsum, gcol) = take(10)
    (send, recv, free, x_send, x_recv, t_send, t_recv, load_sem, lhs_sem, store_sem, own_sem, part_sem) = take(12)
    me = Place()
    greet(me)
    tokens, width = cot.shape
    length = kv_all.shape[1]
    features = hidden_in.shape[1]
    wide = dgt.shape[1]
    tiles = features // wide
    scale = HD**-0.5
    sibling = me.device(dc=1)
    f32, bf = jnp.float32, jnp.bfloat16
    r = lhs.shape[0] // (4 * me.Z)
    rd = lhs_d.shape[1] // me.Z
    big = sets[0][0].shape[-1]
    half = features // 2
    key_wide = kv_heads * 128
    query_wide = pre.shape[1] - key_wide
    d_wide = down_sets[0][0].shape[-1]
    d_rest = width - 2 * d_wide
    chunks = (
        (*down_sets[0], d_wide, "xy", g_down, 0, 4, 0),
        (*down_sets[1], d_wide, "yx", g_down, d_wide, None, 0),
        (*sets[0], half, "xy", g_gate, 0, 0, 0),
        (*sets[1], half, "yx", g_up, 0, 1, 0),
        (*sets[2], half, "xy", g_gate, half, 2, 0),
        (*sets[0], half, "yx", g_up, half, None, 0),
        (*sets[1], width, "xy", g_out, 0, None, 0),
        (*sets[2], query_wide, "yx", g_first, 0, None, 0),
        (*sets[2], key_wide - 128, "yx", g_first, query_wide, None, query_wide),
        (*gain_set, 256, "yx", g_first, query_wide + key_wide - 128, None, 0),
        (*down_sets[0], d_rest, "yx", g_down, 2 * d_wide, None, 0),
    )
    D0, D1, G0, U0, G1, U1, O, Q, KV, GAIN, D2 = range(11)
    comm = Scattering(me, chunks, send, recv, free)

    def over_rows(body, step=64):
        def one(i, carry):
            body(pl.ds(pl.multiple_of(i * step, step), step))
            return carry

        lax.fori_loop(0, tokens // step, one, 0)

    passes = []

    def hand(i, src, dst):
        copy = pltpu.make_async_remote_copy(
            src_ref=src,
            dst_ref=dst,
            send_sem=x_send.at[i],
            recv_sem=x_recv.at[i],
            device_id=sibling,
            device_id_type=MESH,
        )
        copy.start()
        passes.append(copy)
        return copy

    other = lax.rem(me.c + 1, 2)
    got_hid = hand(0, hid_t.at[:, :, :, other], hid_s)
    got_dy = hand(1, dy_ref, dy_p.at[1])
    got_h2 = hand(2, h2_t.at[:, :, :, other], h2_s)
    got_att = hand(3, att_t.at[:, :, :, other], att_s)
    got_nor = hand(4, nor_t.at[:, :, :, other], nor_s)

    def fetch(i, src, dst):
        copy = pltpu.make_async_copy(src, dst, load_sem.at[i])
        copy.start()
        return copy

    stores = []

    def store(i, src, dst):
        copy = pltpu.make_async_copy(src, dst, store_sem.at[i])
        copy.start()
        stores.append(copy)
        return copy

    need_cot = fetch(0, dy_ref, cot)
    own_dy = store(0, dy_ref, dy_p.at[0])
    def block(ref, a, b, order, c=None):
        rel = {order[0]: a, order[1]: b}
        y = lax.rem(me.y + rel["y"], 2)
        x = lax.rem(me.x + rel["x"], 2)
        return ref.at[:, y, x] if c is None else ref.at[:, y, x, c]

    def left_rows(own_t, sib_t):
        for side, ref in ((0, own_t), (1, sib_t)):
            loads = []
            for i in range(4):
                src = block(ref, i // 2, i % 2, "xy", me.c if side == 0 else None)
                copy = pltpu.make_async_copy(src, lraw.at[i], lhs_sem.at[i])
                copy.start()
                loads.append(copy)
            for copy in loads:
                copy.wait()

            def one(i, carry, side=side):
                for j in range(me.Z // 2):
                    piece = lraw[i, 2 * j : 2 * j + 2].astype(f32).reshape(2 * r, tokens)
                    at = pl.multiple_of((i * me.Z + 2 * j) * r, 16)
                    lhs[pl.ds(at, 2 * r), side * tokens : (side + 1) * tokens] = piece.astype(bf)
                return carry

            lax.fori_loop(0, 4, one, 0)

    def down_rows(k, i, slot):
        copies = []
        for side, ref in ((0, hid_t), (1, hid_s)):
            src = block(ref, i // 2, i % 2, chunks[k][5], me.c if side == 0 else None)
            for z in range(me.Z):
                copies.append(
                    pltpu.make_async_copy(
                        src.at[z],
                        lhs_d.at[slot, pl.ds(z * rd, rd), pl.ds(side * tokens, tokens)],
                        lhs_sem.at[(slot * 2 + side) * me.Z + z],
                    )
                )
        return copies

    def product_down(k, base, right=None):
        own, wide_k = chunks[k][0], chunks[k][4]
        for copy in down_rows(k, 3, 0):
            copy.start()
        for n, i in enumerate((3, 2, 1, 0)):
            slot = n % 2
            if i > 0:
                for copy in down_rows(k, i - 1, 1 - slot):
                    copy.start()
            for copy in down_rows(k, i, slot):
                copy.wait()
            left = lhs_d.at[slot]
            if right is None:
                product(k, dy_p, base, left, rd, (i,))
            else:

                def body(j, carry, i=i, left=left):
                    cols = pl.ds(pl.multiple_of(base + j * 256, 256), 256)
                    here = pl.ds(pl.multiple_of(j * 256, 256), 256)
                    total = plain_dot(left[:, :tokens], right[0][:, cols]) + plain_dot(
                        left[:, tokens:], right[1][:, cols]
                    )
                    own[i // 2, i % 2, :, :, here] = total.reshape(me.Z, rd, 256).astype(bf)
                    return carry

                lax.fori_loop(0, wide_k // 256, body, 0)
        comm.begin(k)

    def product(k, pair, base, left, depth, blocks=(0, 1, 2, 3), size=None):
        own, wide_k = chunks[k][0], size or chunks[k][4]
        t = rhs.shape[3] if wide_k % rhs.shape[3] == 0 else 128
        count = wide_k // t
        span = len(blocks)

        def tile(j, slot):
            cols = pl.ds(pl.multiple_of(base + j * t, 128), t)
            return [
                pltpu.make_async_copy(
                    pair.at[side, :, cols],
                    rhs.at[slot, side, :, pl.ds(0, t)],
                    own_sem.at[slot, side],
                )
                for side in range(2)
            ]

        depth_of = rhs.shape[0]
        for j in range(min(depth_of - 1, count)):
            for copy in tile(j, j):
                copy.start()

        def body(j, carry):
            slot = lax.rem(j, depth_of)
            ahead = j + depth_of - 1

            @pl.when(ahead < count)
            def _():
                for copy in tile(ahead, lax.rem(ahead, depth_of)):
                    copy.start()

            for copy in tile(j, slot):
                copy.wait()
            cols = pl.ds(pl.multiple_of(chunks[k][9] + j * t, 128), t)
            total = plain_dot(left[:, :tokens], rhs[slot, 0, :, :t]) + plain_dot(
                left[:, tokens:], rhs[slot, 1, :, :t]
            )
            total = total.reshape(span, me.Z, depth, t).astype(bf)
            for q, at in enumerate(blocks):
                if chunks[k][5] == "xy" or span == 1:
                    own[at // 2, at % 2, :, :, cols] = total[q]
                else:
                    own[at % 2, at // 2, :, :, cols] = total[q]
            return carry

        lax.fori_loop(0, count, body, 0)

    def load3(i, full, raw, col, size):
        return pltpu.make_async_copy(
            full.at[:, :, pl.ds(col, size)], raw.at[:, :, pl.ds(0, size)], load_sem.at[i]
        )

    def assemble(raw, flat, size):
        n, depth, _ = raw.shape
        pair = 2 * depth

        def one(i, carry):
            piece = raw[pl.ds(2 * i, 2), :, pl.ds(0, size)].astype(f32)
            flat[pl.ds(pl.multiple_of(pair * i, 16), pair), pl.ds(0, size)] = piece.reshape(
                pair, size
            ).astype(bf)
            return carry

        lax.fori_loop(0, n // 2, one, 0)

    def tile_loads(j):
        at = pl.ds(j * wide, wide)
        return [
            pltpu.make_async_copy(down_w.at[at, :], wd.at[j % 2], load_sem.at[2]),
            pltpu.make_async_copy(slope_in.at[:, at], fac_a.at[j % 2], load_sem.at[3]),
            pltpu.make_async_copy(silu_in.at[:, at], fac_b.at[j % 2], load_sem.at[4]),
        ]

    gate_tile = lambda j: load3(5, gate_w, raw_a, j * wide, wide)
    up_tile = lambda j: load3(6, up_w, raw_a, j * wide, wide)
    head_pack = load3(7, first_w, raw_a, used, 128)
    head_pack.start()
    head_pack.wait()
    assemble(raw_a, w_a, 128)
    gains[...] = w_a[:, :128].astype(f32).T[:8]
    for copy in tile_loads(0) + [gate_tile(0)]:
        copy.start()
    need_cot.wait()
    own_dy.wait()
    tile_sends = [None] * tiles

    def arrive(low, high):
        for j in range(low, high):
            for copy in tile_sends[j]:
                copy.settle()

    for j in range(tiles):
        slot = j % 2
        for copy in tile_loads(j):
            copy.wait()
        if j + 1 < tiles:
            for copy in tile_loads(j + 1):
                copy.start()
        gate_tile(j).wait()
        assemble(raw_a, w_a, wide)
        up_tile(j).start()
        if j >= 1:
            for copy in tile_sends[j - 1]:
                copy.wait()

        def units(at, slot=slot, j=j):
            grad_hidden = dot_t(cot[at, :], wd[slot])
            dg = (grad_hidden * fac_a[slot, at, :].astype(f32)).astype(bf)
            du = (grad_hidden * fac_b[slot, at, :].astype(f32)).astype(bf)
            dgt[at, :] = dg
            dut[at, :] = du
            piece = dot_t(dg, w_a[:, :wide])
            acc[at, :] = piece if j == 0 else acc[at, :] + piece

        over_rows(units, 256)
        cols = pl.ds(j * wide, wide)
        sends = []
        for i, (src, dst) in enumerate(((dgt, gate_p), (dut, up_p))):
            here = pltpu.make_async_copy(
                src, dst.at[0, :, cols], store_sem.at[1 + i]
            )
            there = pltpu.make_async_remote_copy(
                src_ref=src,
                dst_ref=dst.at[1, :, cols],
                send_sem=t_send.at[2 * j + i],
                recv_sem=t_recv.at[2 * j + i],
                device_id=sibling,
                device_id_type=MESH,
            )
            here.start()
            there.start()
            sends.append(_Both(here, there))
        tile_sends[j] = sends
        up_tile(j).wait()
        assemble(raw_a, w_a, wide)
        if j + 1 < tiles:
            gate_tile(j + 1).start()

        def units_up(at):
            acc[at, :] = acc[at, :] + dot_t(dut[at, :], w_a[:, :wide])

        over_rows(units_up, 256)
        if j == 0:
            got_dy.wait_recv()
            need_sib = fetch(1, dy_p.at[1], low_t)
            got_hid.wait_recv()
            need_sib.wait()
            product_down(D0, 0, (cot, low_t))
        if j == 1:
            product_down(D1, d_wide, (cot, low_t))
        if j == 3:
            got_h2.wait_recv()
            left_rows(h2_t, h2_s)
            arrive(0, 4)
            product(G0, gate_p, 0, lhs, r)
            comm.begin(G0)
            product(U0, up_p, 0, lhs, r)
            comm.begin(U0)
        if j == 4:
            comm.first(D0)
        if j == 5:
            comm.first(D1)
    arrive(4, tiles)
    product(G1, gate_p, half, lhs, r)
    comm.begin(G1)

    gsum[...] = jnp.zeros_like(gsum)

    def stream(src, body):
        def piece(i, slot):
            at = pl.ds(pl.multiple_of(i * 64, 64), 64)
            return pltpu.make_async_copy(src.at[at, :], part.at[slot], part_sem.at[slot])

        piece(0, 0).start()

        def one(i, carry):
            slot = lax.rem(i, 2)

            @pl.when(i + 1 < tokens // 64)
            def _():
                piece(i + 1, lax.rem(i + 1, 2)).start()

            piece(i, slot).wait()
            body(pl.ds(pl.multiple_of(i * 64, 64), 64), part[slot])
            return carry

        lax.fori_loop(0, tokens // 64, one, 0)

    def norm_two(at, y):
        inverse = lax.rsqrt(jnp.mean(y * y, -1, keepdims=True) + EPSILON)
        grad = acc[at, :]
        gsum[1:2, :] += jnp.sum(grad * (y * inverse), 0, keepdims=True)
        e = grad * gains[1:2, :]
        dy1 = cot[at, :].astype(f32) + inverse * (
            e - y * (inverse * inverse) * jnp.mean(e * y, -1, keepdims=True)
        )
        acc[at, :] = dy1
        low_t[at, :] = dy1.astype(bf)

    stream(mixed_in, norm_two)
    keep_dy1 = pltpu.make_async_copy(acc, dy1_h, part_sem.at[2])
    keep_dy1.start()
    own_low = store(5, low_t, dm_p.at[0])
    got_low = hand(5, low_t, dm_p.at[1])

    need_q = fetch(0, q_in, queries)
    need_kv = fetch(1, kv_in, kv_all)
    need = [
        fetch(8, bias_in, bias),
        fetch(9, log_in, logs),
        fetch(10, cos_in, cos_t),
        fetch(11, sin_in, sin_t),
    ]
    tile_w = raw_a.shape[2]
    steps = width // tile_w
    load3(5, out_w, raw_a, 0, tile_w).start()
    keep_dy1.wait()
    for j in range(steps):
        load3(5, out_w, raw_a, j * tile_w, tile_w).wait()
        assemble(raw_a, w_a, tile_w)
        if j + 1 < steps:
            load3(5, out_w, raw_a, (j + 1) * tile_w, tile_w).start()

        def back_out(at, j=j):
            piece = dot_t(low_t[at, j * tile_w : (j + 1) * tile_w], w_a[...])
            if j > 0:
                piece = acc[at, :] + piece
            if j + 1 < steps:
                acc[at, :] = piece
            else:
                grads[at, :] = piece.astype(bf)

        over_rows(back_out, 256)
    comm.second(D0)
    comm.first(G0)

    need_q.wait()
    need_kv.wait()
    for copy in need:
        copy.wait()
    def portion(dx, c):
        row = (lax.rem(me.x + dx, 2) * 2 + c) * rows
        return pl.ds(pl.multiple_of(row, 256), rows)

    def to_sibling(b):
        return [
            hand(6 + 2 * b + dx, dkv.at[b, portion(dx, other), :], dkv_r.at[dx, b])
            for dx in (1, 0)
        ]

    def gather_portion(b, dx):
        place = portion(dx, me.c)

        def body(j, carry):
            at = pl.ds(pl.multiple_of(j * 64, 64), 64)
            there = pl.ds(pl.multiple_of(place.start + j * 64, 64), 64)
            total = dkv_r[dx, b, at, :].astype(f32) + dkv[b, there, :].astype(f32)
            dkv_r[dx, b, at, :] = total.astype(bf)
            return carry

        lax.fori_loop(0, rows // 64, body, 0)

    def to_neighbour(b, handed):
        handed[0].wait_recv()
        gather_portion(b, 1)
        copy = pltpu.make_async_remote_copy(
            src_ref=dkv_r.at[1, b],
            dst_ref=dkv_x.at[b],
            send_sem=x_send.at[10 + b],
            recv_sem=x_recv.at[10 + b],
            device_id=me.device(dx=1),
            device_id_type=MESH,
        )
        copy.start()
        passes.append(copy)
        handed[1].wait_recv()
        gather_portion(b, 0)
        return copy

    def merge_portion(b, copy):
        copy.wait_recv()

        def merge(j, carry):
            at = pl.ds(pl.multiple_of(j * 64, 64), 64)
            token = pl.ds(pl.multiple_of(b * rows + j * 64, 64), 64)
            for h in range(kv_heads):
                cols = slice(h * 128, (h + 1) * 128)
                total = dkv_r[0, b, at, cols].astype(f32) + dkv_x[b, at, cols].astype(f32)
                total = total * cos_t[1, token, :] - swap_halves(total) * sin_t[1, token, :]
                pre[token, query_wide + h * 128 : query_wide + (h + 1) * 128] = total.astype(bf)
            return carry

        lax.fori_loop(0, rows // 64, merge, 0)

    to_x = [None] * batches
    lanes = lax.broadcasted_iota(jnp.int32, (rows, 128), 1)
    sides_mask = lane_masks(rows)

    def head(i, carry):
        b = i // kv_heads
        h = lax.rem(i, kv_heads)
        at = pl.ds(pl.multiple_of(b * rows, 256), rows)
        here = pl.ds(pl.multiple_of(h * 128, 128), 128)
        kv = kv_all[b, :, here]
        sides = (kv, swapped(kv))
        shift = bias[at, :].astype(f32)
        key_sum = jnp.zeros((128, length), f32)
        value_sum = jnp.zeros((128, length), f32)
        log_piece = logs[at, :]
        for pair in range(group // 2):
            cols = pl.ds(pl.multiple_of(h * group * HD + pair * 128, 128), 128)
            q = queries[at, cols]
            do = grads[at, cols]
            found = []
            for side in range(2):
                q_half = q * sides_mask[side]
                do_half = do * sides_mask[side]
                head_at = pair * 2 + side
                log_total = jnp.sum(
                    jnp.where(lanes == h * group + head_at, log_piece, 0.0), -1, keepdims=True
                )
                probs = jnp.exp(dot_t(q_half, sides[side]) + shift - log_total)
                grad_probs = dot_t(do_half, sides[1 - side])
                row_dot = jnp.sum(probs * grad_probs, -1, keepdims=True)
                grad_scores = (probs * (grad_probs - row_dot)).astype(bf)
                found.append(plain_dot(grad_scores, sides[side]))
                key_sum = key_sum + left_dot(q_half, grad_scores)
                value_sum = value_sum + left_dot(do_half, probs.astype(bf))
            dq = jnp.where(lanes < HD, found[0], found[1])
            dq = dq * cos_t[0, at, :] - swap_halves(dq) * sin_t[0, at, :]
            pre[at, cols] = dq.astype(bf)
        both = jnp.concatenate(
            [key_sum[:HD] + key_sum[HD:], value_sum[:HD] + value_sum[HD:]], 0
        )
        dkv[b, :, here] = both.T.astype(bf)
        return carry

    count = batches * kv_heads
    lax.fori_loop(0, 2, head, 0)
    comm.second(D1)
    comm.first(U0)
    own_low.wait()
    got_low.wait_recv()
    lax.fori_loop(2, 5, head, 0)
    comm.third(D0)
    comm.second(G0)
    handed = to_sibling(0)
    comm.first(G1)
    lax.fori_loop(5, 8, head, 0)
    comm.third(D1)
    comm.second(U0)
    comm.third(G0)
    comm.reuse(0)
    product(U1, up_p, half, lhs, r)
    comm.begin(U1)
    to_x[0] = to_neighbour(0, handed)
    lax.fori_loop(8, count, head, 0)
    comm.third(U0)
    comm.second(G1)
    merge_portion(0, to_x[0])
    comm.reuse(1)
    got_att.wait_recv()
    left_rows(att_t, att_s)
    product(O, dm_p, 0, lhs, r)
    comm.begin(O)
    handed = to_sibling(1)
    own_q = store(6, pre.at[:, pl.ds(0, query_wide)], pre_p.at[0, :, pl.ds(0, query_wide)])
    got_q = hand(12, pre.at[:, pl.ds(0, query_wide)], pre_p.at[1, :, pl.ds(0, query_wide)])
    to_x[1] = to_neighbour(1, handed)
    comm.third(G1)
    comm.reuse(2)
    got_nor.wait_recv()
    left_rows(nor_t, nor_s)
    own_q.wait()
    got_q.wait_recv()
    product(Q, pre_p, 0, lhs, r)
    comm.begin(Q)
    comm.reuse(4)
    product_down(D2, 2 * d_wide)
    comm.first(U1)
    merge_portion(1, to_x[1])
    rest = pl.ds(query_wide, kv_heads * 128)
    own_kv = store(7, pre.at[:, rest], pre_p.at[0, :, rest])
    got_kv = hand(13, pre.at[:, rest], pre_p.at[1, :, rest])

    need_x = fetch(0, x_in, cot)
    steps = pre.shape[1] // tile_w
    load3(5, first_w, raw_a, 0, tile_w).start()
    for j in range(steps):
        load3(5, first_w, raw_a, j * tile_w, tile_w).wait()
        assemble(raw_a, w_a, tile_w)
        if j + 1 < steps:
            load3(5, first_w, raw_a, (j + 1) * tile_w, tile_w).start()

        def back_in(at, j=j):
            piece = dot_t(pre[at, j * tile_w : (j + 1) * tile_w], w_a[...])
            acc[at, :] = piece if j == 0 else acc[at, :] + piece

        over_rows(back_in, 256)
    comm.first(O)
    own_kv.wait()
    got_kv.wait_recv()
    product(KV, pre_p, query_wide, lhs, r)
    comm.begin(KV)
    product(GAIN, pre_p, query_wide + key_wide - 128, lhs, r, size=128)
    comm.second(U1)
    need_x.wait()

    def norm_one(at, dy1):
        x = cot[at, :].astype(f32)
        inverse = lax.rsqrt(jnp.mean(x * x, -1, keepdims=True) + EPSILON)
        grad = acc[at, :]
        gsum[0:1, :] += jnp.sum(grad * (x * inverse), 0, keepdims=True)
        e = grad * gains[0:1, :]
        total = dy1 + inverse * (
            e - x * (inverse * inverse) * jnp.mean(e * x, -1, keepdims=True)
        )
        queries[at, :] = total.astype(bf)

    stream(dy1_h, norm_one)
    store(8, queries, grad_out)
    comm.first(D2)
    comm.first(Q)

    gsib = gain_set[0]
    columns = jnp.concatenate([gsum[...], jnp.zeros((120, width), f32)], 0).T
    gcol[0] = columns.reshape(gcol.shape[1:]).astype(bf)
    got_gain = hand(14, gcol.at[0], gcol.at[1])
    comm.second(O)
    got_gain.wait_recv()
    for a in range(2):
        for b in range(2):
            y = lax.rem(me.y + b, 2)
            x = lax.rem(me.x + a, 2)
            if chunks[GAIN][5] == "yx":
                y, x = lax.rem(me.y + a, 2), lax.rem(me.x + b, 2)
            for z in range(me.Z):
                at = ((z * 2 + y) * 2 + x) * 2 + me.c
                gsib[a, b, z, :, 128:] = gcol[0, at] + gcol[1, at]
    comm.begin(GAIN)
    comm.first(KV)
    comm.second(D2)
    comm.second(Q)

    need_mixed = fetch(1, mixed_in, acc)
    need_mixed.wait()
    last_loads = lambda j: [
        pltpu.make_async_copy(
            down_w.at[pl.ds(j * wide, wide), :], wd.at[j % 2], load_sem.at[2]
        ),
        pltpu.make_async_copy(
            hidden_in.at[:, pl.ds(j * wide, wide)], fac_a.at[j % 2], load_sem.at[3]
        ),
    ]
    for copy in last_loads(0):
        copy.start()
    for j in range(tiles):
        for copy in last_loads(j):
            copy.wait()
        if j + 1 < tiles:
            for copy in last_loads(j + 1):
                copy.start()

        def add_down(at, j=j):
            acc[at, :] = acc[at, :] + plain_dot(fac_a[j % 2, at, :], wd[j % 2])

        over_rows(add_down, 256)
        if j == 0:
            comm.third(U1)
        if j == 1:
            comm.second(KV)
        if j == 2:
            comm.first(GAIN)
        if j == 3:
            comm.third(O)
            comm.third(D2)
        if j == 4:
            comm.third(Q)
        if j == 5:
            comm.second(GAIN)

    def round_result(at):
        low_t[at, :] = acc[at, :].astype(bf)

    got_low.wait_send()
    over_rows(round_result)
    store(9, low_t, result_out)
    comm.third(KV)
    comm.third(GAIN)
    for copy in passes:
        if copy is not got_low:
            copy.wait_send()
    for copy in stores:
        if not any(copy is p for p in (own_dy, own_low, own_q, own_kv)):
            copy.wait()


class _Both:
    def __init__(self, here, there):
        self.here, self.there, self.sent, self.settled = here, there, False, False

    def wait(self):
        if not self.sent:
            self.here.wait()
            self.there.wait_send()
        self.sent = True

    def settle(self):
        self.wait()
        if not self.settled:
            self.there.wait_recv()
        self.settled = True


def backward(saved, transposed, dy, x, kv_heads, group, batches):
    first_w, out_w, gate_w, up_w, down_w = saved[:5]
    queries, both_all, _, logs, mixed, _ = saved[5:11]
    hidden, slope, silu, bias, cos_tables, sin_tables = saved[11:]
    tokens, width = x.shape
    rows = tokens // batches
    Z = lax.axis_size("dp") // 2
    X = lax.axis_size("fsdp") // 2
    n, r, first_wide = first_w.shape
    rd = down_w.shape[1]
    key_wide = kv_heads * 128
    query_wide = kv_heads * group * HD
    used = query_wide + key_wide
    length = both_all.shape[1]
    features = hidden.shape[1]
    half = features // 2
    d_wide = width * 2 // 5 // 256 * 256
    wide, t = 512, 256
    bf, f32 = jnp.bfloat16, jnp.float32
    shape = jax.ShapeDtypeStruct
    vmem, dma = pltpu.VMEM, pltpu.SemaphoreType.DMA

    def four(depth, size):
        return [
            vmem((2, 2, Z, depth, size), bf),
            vmem((2, Z, depth, size), bf),
            vmem((Z, depth, size), bf),
            vmem((Z - 1, depth, size), bf),
        ]

    outs = [
        shape((tokens, width), bf),
        shape((tokens, width), bf),
        shape((r, first_wide), f32),
        shape((r, width), f32),
        shape((r, features), f32),
        shape((r, features), f32),
        shape((rd, width), f32),
        shape((Z, 2, X, rd, tokens), bf),
        shape((Z, 2, X, r, tokens), bf),
        shape((Z, 2, X, r, tokens), bf),
        shape((Z, 2, X, r, tokens), bf),
        shape((2, tokens, width), bf),
        shape((2, tokens, features), bf),
        shape((2, tokens, features), bf),
        shape((2, tokens, width), bf),
        shape((2, tokens, used), bf),
        shape((tokens, width), f32),
    ]
    any_space = pl.BlockSpec(memory_space=pl.ANY)
    in_vmem = pl.BlockSpec(memory_space=pltpu.VMEM)
    scratch = sum([four(r, half) for _ in range(3)], [])
    scratch += four(rd, d_wide) + four(rd, d_wide) + four(r, 256)
    scratch += [
        vmem((2, Z * rd, 2 * tokens), bf),
        vmem((4 * Z * r, 2 * tokens), bf),
        vmem((4, Z, r, tokens), bf),
        vmem((3, 2, tokens, t), bf),
        vmem((tokens, width), f32),
        vmem((2, 64, width), f32),
        vmem((tokens, width), bf),
        vmem((tokens, width), bf),
        vmem((tokens, query_wide), bf),
        vmem((tokens, query_wide), bf),
        vmem((tokens, used), bf),
        vmem((batches, length, key_wide), bf),
        vmem((batches, length, key_wide), bf),
        vmem((tokens, length), bias.dtype),
        vmem((tokens, 128), f32),
        vmem((2, tokens, 128), f32),
        vmem((2, tokens, 128), f32),
        vmem((2, batches, rows, key_wide), bf),
        vmem((batches, rows, key_wide), bf),
        vmem((n, r, key_wide), bf),
        vmem((width, key_wide), bf),
        vmem((2, wide, width), bf),
        vmem((2, tokens, wide), bf),
        vmem((2, tokens, wide), bf),
        vmem((tokens, wide), bf),
        vmem((tokens, wide), bf),
        vmem((8, width), f32),
        vmem((8, width), f32),
        vmem((2, n, r, 128), bf),
        dma((11, 2 + Z)),
        dma((11, 2 + Z)),
        pltpu.SemaphoreType.REGULAR((5,)),
        dma((15,)),
        dma((15,)),
        dma((2 * (features // wide),)),
        dma((2 * (features // wide),)),
        dma((12,)),
        dma((8 * Z,)),
        dma((10,)),
        dma((3, 2)),
        dma((3,)),
    ]
    return pl.pallas_call(
        functools.partial(backward_kernel, (batches, rows, kv_heads, group, used)),
        out_shape=outs,
        in_specs=[any_space] * 21,
        out_specs=[any_space] * 2 + [in_vmem] * 5 + [any_space] * 10,
        scratch_shapes=scratch,
        compiler_params=pltpu.CompilerParams(
            collective_id=2, has_side_effects=True, vmem_limit_bytes=63 * 2**20
        ),
    )(
        dy,
        first_w,
        out_w,
        gate_w,
        up_w,
        down_w.reshape(-1, width),
        queries,
        both_all,
        logs,
        mixed,
        hidden,
        slope,
        silu,
        bias,
        cos_tables,
        sin_tables,
        *transposed,
        x,
    )


def half_of(full):
    return full.astype(jnp.bfloat16)


def rotary_pairs(places, tokens, score_scale):
    cos_table, sin_table = rope_tables(places.reshape(tokens))
    ones, zeros = jnp.ones((tokens, HD), jnp.float32), jnp.zeros((tokens, HD), jnp.float32)
    cos_pair = jnp.concatenate([cos_table, cos_table], -1)
    sin_pair = jnp.concatenate([-sin_table, sin_table], -1)
    cos_tables = jnp.stack(
        [
            jnp.concatenate([cos_pair, cos_pair], -1) * score_scale,
            jnp.concatenate([cos_pair, ones], -1),
        ]
    )
    sin_tables = jnp.stack(
        [
            jnp.concatenate([sin_pair, sin_pair], -1) * score_scale,
            jnp.concatenate([sin_pair, zeros], -1),
        ]
    )
    return cos_tables, sin_tables


def forward_plain(shards, x, places, kv_heads, group, batches):
    tokens = x.shape[0]
    rows = tokens // batches
    length = rows * lax.axis_size("fsdp")
    query_features = kv_heads * group * HD
    used = query_features + kv_heads * 128
    fulls = gather(shards, ("yxc", "xyc", "yxc", "xyc", "yxc"), 1, 5)
    first_pack, out_full, gate_full, up_full, _ = (f.reshape(-1, f.shape[-1]) for f in fulls)
    gains = first_pack[:, used : used + 2].astype(jnp.float32).T
    query_index = lax.axis_index("fsdp") * rows + jnp.arange(rows, dtype=jnp.int32)
    key_index = jnp.arange(length, dtype=jnp.int32)
    x_float = x.astype(jnp.float32)
    cos_tables, sin_tables = rotary_pairs(places, tokens, HD**-0.5)
    doc_start = query_index[None, :] - places.reshape(batches, rows)
    allowed = (key_index[None, None, :] <= query_index[None, :, None]) & (
        key_index[None, None, :] >= doc_start[:, :, None]
    )
    bias = jnp.where(allowed, 0.0, NEGATIVE)
    attn_inverse = lax.rsqrt(jnp.mean(x_float * x_float, -1, keepdims=True) + EPSILON)
    normed = (x_float * attn_inverse * gains[0]).astype(jnp.bfloat16)
    projected = project(normed, first_pack[:, :used], cos_tables, sin_tables, kv_heads * 128)
    both_rows = projected[:, query_features:].reshape(batches, rows, -1)
    both_all = lax.all_gather(both_rows, "fsdp", axis=1, tiled=True)
    attended, logs = attend(projected, both_all, bias, kv_heads, group)
    mixed = x_float + plain_dot(attended, out_full)
    mlp_inverse = lax.rsqrt(jnp.mean(mixed * mixed, -1, keepdims=True) + EPSILON)
    normed_mlp = (mixed * mlp_inverse * gains[1]).astype(jnp.bfloat16)
    gate_pre = plain_dot(normed_mlp, gate_full)
    up_proj = plain_dot(normed_mlp, up_full)
    gate_sig = jax.nn.sigmoid(gate_pre)
    silu = gate_pre * gate_sig
    slope = up_proj * gate_sig * (1.0 + gate_pre * (1.0 - gate_sig))
    low = jnp.bfloat16
    return list(fulls) + [
        projected[:, :query_features],
        both_all,
        attended,
        logs,
        mixed,
        normed_mlp,
        (silu * up_proj).astype(low),
        slope.astype(low),
        silu.astype(low),
        bias.reshape(tokens, length),
        cos_tables,
        sin_tables,
    ]


def backward_plain(saved, cotangent, x_low, kv_heads, group, batches):
    tokens, width = x_low.shape
    rows = tokens // batches
    key_features = kv_heads * HD
    query_features = kv_heads * group * HD
    used = query_features + 2 * key_features
    x_float = x_low.astype(jnp.float32)
    first_pack, out_full, gate_full, up_full, down_full = (
        f.reshape(-1, f.shape[-1]) for f in saved[:5]
    )
    queries, both_all, attended, logs, mixed, normed_mlp = saved[5:11]
    hidden, slope, silu, bias, cos_tables, sin_tables = saved[11:]
    projection = first_pack[:, :used]
    gains = first_pack[:, used : used + 2].astype(jnp.float32).T
    attn_gain_f = gains[0]
    mlp_gain_f = gains[1]
    attn_inverse = lax.rsqrt(jnp.mean(x_float * x_float, -1, keepdims=True) + EPSILON)
    normed = (x_float * attn_inverse * attn_gain_f).astype(jnp.bfloat16)
    mlp_inverse = lax.rsqrt(jnp.mean(mixed * mixed, -1, keepdims=True) + EPSILON)
    output = (mixed + plain_dot(hidden, down_full)).astype(jnp.bfloat16)

    cot_low = cotangent
    cot_float = cot_low.astype(jnp.float32)
    grad_down = half_of(left_dot(hidden, cot_low))
    grad_hidden = right_dot(cot_low, down_full)
    grad_gate_pre = (grad_hidden * slope.astype(jnp.float32)).astype(jnp.bfloat16)
    grad_up_pre = (grad_hidden * silu.astype(jnp.float32)).astype(jnp.bfloat16)
    grad_gate = half_of(left_dot(normed_mlp, grad_gate_pre))
    grad_up = half_of(left_dot(normed_mlp, grad_up_pre))
    grad_normed_mlp = right_dot(grad_gate_pre, gate_full) + right_dot(grad_up_pre, up_full)
    grad_mlp_gain = jnp.sum(grad_normed_mlp * mixed * mlp_inverse, 0)
    grad_mixed = cot_float + norm_back(grad_normed_mlp * mlp_gain_f, mixed, mlp_inverse)
    grad_mixed_low = grad_mixed.astype(jnp.bfloat16)
    grad_out = half_of(left_dot(attended, grad_mixed_low))
    grad_attended = right_dot(grad_mixed_low, out_full).astype(jnp.bfloat16)
    grad_query_pre, portions = attend_back(
        queries,
        grad_attended,
        both_all,
        bias.reshape(batches, rows, -1),
        logs,
        cos_tables,
        sin_tables,
        group,
    )
    sums = lax.psum_scatter(portions, "fsdp", scatter_dimension=1, tiled=True)
    sums = sums.astype(jnp.float32).reshape(tokens, kv_heads, 128)
    turned = jnp.concatenate([sums[..., 32:64], sums[..., :32], sums[..., 64:]], -1)
    grad_pair_pre = (sums * cos_tables[1][:, None] - turned * sin_tables[1][:, None]).astype(
        jnp.bfloat16
    )
    grad_pre = jnp.concatenate(
        [grad_query_pre, grad_pair_pre.reshape(tokens, 2 * key_features)], -1
    )
    grad_projection = left_dot(normed, grad_pre)
    grad_normed = right_dot(grad_pre, projection)
    grad_attn_gain = jnp.sum(grad_normed * x_float * attn_inverse, 0)
    grad_input = grad_mixed + norm_back(grad_normed * attn_gain_f, x_float, attn_inverse)
    gain_columns = jnp.stack([grad_attn_gain, grad_mlp_gain], -1)
    gain_columns = jnp.pad(gain_columns, ((0, 0), (0, 126)))
    grad_first = half_of(jnp.concatenate([grad_projection, gain_columns], 1))
    grad_down, grad_gate, grad_up, grad_out, last = scatter(
        (grad_down, grad_gate, grad_up, grad_out, grad_first), ("xy", "yx", "xy", "yx", "xy"), 2
    )
    return (
        output,
        grad_input.astype(jnp.bfloat16),
        last,
        grad_out,
        grad_gate,
        grad_up,
        grad_down,
    )


def on_device(
    inputs,
    positions,
    cotangent,
    attn_gain,
    w_query,
    key_matrix,
    value_matrix,
    w_out,
    mlp_gain,
    w_gate,
    w_up,
    w_down,
):
    batches, _, rows, width = inputs.shape
    shard = w_query.shape[0]
    query_features = w_query.shape[1]
    key_features = key_matrix.shape[1]
    kv_heads = key_features // HD
    group = query_features // key_features
    tokens = batches * rows
    used = query_features + 2 * key_features

    extras = jnp.zeros((shard, 128), jnp.bfloat16)
    extras = extras.at[:, 0].set(attn_gain).at[:, 1].set(mlp_gain)
    pairs = jnp.concatenate(
        [key_matrix.reshape(shard, kv_heads, HD), value_matrix.reshape(shard, kv_heads, HD)], -1
    )
    first_shard = jnp.concatenate([w_query, pairs.reshape(shard, -1), extras], axis=1)
    shards = (first_shard, w_out, w_gate, w_up, w_down)
    x_low = inputs.reshape(tokens, width)
    cot_low = cotangent.reshape(tokens, width)
    fits = shard % 8 == 0 and lax.axis_size("fsdp") == 4 and rows % 256 == 0
    saved = (forward if fits else forward_plain)(
        shards, x_low, positions.reshape(tokens, 1), kv_heads, group, batches
    )
    if fits:
        by_place = (lax.axis_size("dp") // 2, 2, lax.axis_size("fsdp") // 2, 2, -1, tokens)
        transposed = [t.reshape(by_place) for t in saved[17:]]
        found = backward(saved[:17], transposed, cot_low, x_low, kv_heads, group, batches)
    else:
        found = backward_plain(saved, cot_low, x_low, kv_heads, group, batches)
    output, grad_input, last, grad_out, grad_gate, grad_up, grad_down = found[:7]
    last_pairs = last[:, query_features:used].reshape(shard, kv_heads, 2, HD)
    return (
        output.reshape(inputs.shape),
        grad_input.reshape(inputs.shape),
        last[:, used],
        last[:, :query_features],
        last_pairs[:, :, 0].reshape(shard, key_features),
        last_pairs[:, :, 1].reshape(shard, key_features),
        grad_out,
        last[:, used + 1],
        grad_gate,
        grad_up,
        grad_down,
    )


def solution(mesh):
    tokens = P(None, "dp", "fsdp", None)
    vector = P(BOTH)
    matrix = P(BOTH, None)
    weights = (vector, matrix, matrix, matrix, matrix, vector, matrix, matrix, matrix)
    return jax.shard_map(
        on_device,
        mesh=mesh,
        in_specs=(tokens, P(None, "dp", "fsdp"), tokens) + weights,
        out_specs=(tokens, tokens) + weights,
        check_vma=False,
    )
```
